128 devices in a mesh: section: 2 (over y_lo), ctx: 16 (over x, y_hi, core), fsdp: 4 (over z).
Axes of the slice: x: 4, y: 4 (y_hi: 2, y_lo: 2; y = y_hi * 2 + y_lo), z: 4, core: 2. Of those that a mesh axis runs over, the one named last changes fastest.
Arguments:
- inputs: bfloat16 [4, 4, 1024, 768], P(None, 'fsdp', 'ctx'), may hold values from -6 to 6
- cotangent: bfloat16 [4, 4, 1024, 768], P(None, 'fsdp', 'ctx'), may hold values from -6 to 6
- plan: int32 [4], replicated, may hold values from 0 to 3, each once
- block_table: int32 [32], replicated, may hold values from 0 to 31, each once
- attn_in: bfloat16 [2, 768, 2304], P('section', 'fsdp'), may hold values from -0.21875 to 0.21875
- attn_out: bfloat16 [2, 768, 768], P('section', 'fsdp'), may hold values from -1.25 to 1.25
- mlp_in: bfloat16 [2, 768, 3072], P('section', 'fsdp'), may hold values from -0.21875 to 0.21875
- mlp_out: bfloat16 [2, 3072, 768], P('section', 'fsdp'), may hold values from -0.15625 to 0.15625
- norm_gains: bfloat16 [2, 2, 768], P('section', None, 'fsdp'), may hold values from 0.5 to 1.5
- biases: bfloat16 [2, 6, 768], P('section', None, 'fsdp'), may hold values from -3 to 3
- mlp_bias: bfloat16 [2, 3072], P('section', 'fsdp'), may hold values from -3 to 3
Outputs:
- layer_out: bfloat16 [2, 4, 4, 1024, 768], P('section', None, 'fsdp', 'ctx')
- input_grad: bfloat16 [2, 4, 4, 1024, 768], P('section', None, 'fsdp', 'ctx')
- grad_attn_in: float32 [2, 768, 2304], P('section', 'fsdp')
- grad_attn_out: float32 [2, 768, 768], P('section', 'fsdp')
- grad_mlp_in: float32 [2, 768, 3072], P('section', 'fsdp')
- grad_mlp_out: float32 [2, 3072, 768], P('section', 'fsdp')
- grad_gains: float32 [2, 2, 768], P('section', None, 'fsdp')
- grad_biases: float32 [2, 6, 768], P('section', None, 'fsdp')
- grad_mlp_bias: float32 [2, 3072], P('section', 'fsdp')
The draws below stay inside these ranges and needn't reach their ends.
Inputs may be any that keep to these rules, and one draw needn't show every extreme that they name: `plan`: every micro-batch is taken at exactly one step. `block_table`: every block number occurs exactly once.
All inputs are finite; a program needn't handle non-finite values.
Results may differ from the reference program's by a relative error of at most 0.02.
Values may be sent and summed in bfloat16 or wider, within the bound.
No kernel may reach another device: no remote copies, remote signals or barrier semaphores. Data moves between devices by JAX's collectives and lax.ppermute only.
A program may use at most 256 MiB of HBM per device.

```python
import jax
import jax.numpy as jnp
from jax import lax

D = 768
HEADS = 12
FF = 3072
HDIM = 64
MICRO = 4
SEQ = 1024
BATCH = 4
LAYERS = 2
N_CTX = 16


def block_levels(key, extent, cuts, low, largest):
    level, own = 1.0, jax.random.fold_in(key, 6)
    for dim, blocks in cuts:
        heights = jnp.exp(jax.random.uniform(jax.random.fold_in(own, dim), (blocks,), jnp.float32, low / len(cuts), largest / len(cuts)))
        level = level * jnp.repeat(heights, extent[dim] // blocks).reshape([-1 if axis == dim else 1 for axis in range(len(extent))])
    return level


def scatter_about(rng, dims, width, most, cuts=(), kind=jnp.bfloat16):
    level = block_levels(rng, dims, cuts, -0.22, 0.18) if cuts else 1.0
    drawn = jax.random.normal(rng, dims, jnp.float32) * width * level
    return jnp.minimum(jnp.maximum(drawn, -most), most).astype(kind)


def setup_inputs(seed: int = 0) -> dict:
    keys = jax.random.split(jax.random.key(seed), 12)
    inputs = scatter_about(keys[0], (MICRO, BATCH, SEQ, D), 1.0, 6.0, ((1, 4), (2, 16)))
    cotangent = scatter_about(keys[1], (MICRO, BATCH, SEQ, D), 1.0, 6.0, ((1, 4), (2, 16)))
    plan = jax.random.permutation(keys[2], MICRO).astype(jnp.int32)
    block_table = jax.random.permutation(keys[3], 2 * N_CTX).astype(jnp.int32)
    attn_in = scatter_about(keys[4], (LAYERS, D, 3 * D), D ** -0.5, 0.21875, ((0, 2), (1, 4)))
    attn_out = scatter_about(keys[5], (LAYERS, D, D), (D // 32) ** -0.5, 1.25, ((0, 2), (1, 4)))
    mlp_in = scatter_about(keys[6], (LAYERS, D, FF), D ** -0.5, 0.21875, ((0, 2), (1, 4)))
    mlp_out = scatter_about(keys[7], (LAYERS, FF, D), (FF // 2) ** -0.5, 0.15625, ((0, 2), (1, 4)))
    norm_gains = jnp.clip(1.0 + 0.1 * jax.random.normal(keys[8], (LAYERS, 2, D), jnp.float32), 0.5, 1.5).astype(jnp.bfloat16)
    biases = scatter_about(keys[9], (LAYERS, 6, D), 0.3, 3.0, ((0, 2), (2, 4)))
    mlp_bias = scatter_about(keys[10], (LAYERS, FF), 0.3, 3.0, ((0, 2), (1, 4)))
    return {"inputs": inputs, "cotangent": cotangent, "plan": plan, "block_table": block_table, "attn_in": attn_in, "attn_out": attn_out, "mlp_in": mlp_in, "mlp_out": mlp_out, "norm_gains": norm_gains, "biases": biases, "mlp_bias": mlp_bias}


@jax.custom_vjp
def low(v):
    return lax.optimization_barrier(v.astype(jnp.bfloat16)).astype(jnp.float32)

@jax.custom_vjp
def low_back(v):
    return v

def low_keep(v):
    return (low(v), None)

def low_pass(kept, grad):
    return (grad,)

def back_keep(v):
    return (v, None)

def back_low(kept, grad):
    return (low(grad),)
low.defvjp(low_keep, low_pass)
low_back.defvjp(back_keep, back_low)
epsilon = 1e-05
neg_fill = -1e+30

def product(left_side, right_side, pattern):
    return jnp.einsum(pattern, left_side, right_side, precision=lax.Precision.HIGHEST)

def normalize(values, gain_row, shift_row):
    center = values - lax.optimization_barrier(jnp.mean(values, -1, keepdims=True))
    spread = lax.rsqrt(lax.optimization_barrier(jnp.mean(center * center, -1, keepdims=True)) + epsilon)
    return center * spread * gain_row + shift_row

def positions(block_table):
    block_len = SEQ // block_table.shape[0]
    offsets = jnp.arange(block_len, dtype=jnp.int32)
    return (block_table[:, None].astype(jnp.int32) * block_len + offsets[None, :]).reshape(-1).astype(jnp.int32)

def attention(queries, key_rows, values, places):
    query_block = min(512, SEQ)
    count_blocks = SEQ // query_block
    query_heads = queries.reshape(count_blocks, query_block, HEADS, HDIM)
    key_heads = key_rows.reshape(SEQ, HEADS, HDIM)
    value_heads = values.reshape(SEQ, HEADS, HDIM)
    query_places = places.reshape(count_blocks, query_block)

    def one_block(block_pair):
        block_rows, here_places = block_pair
        scores = low_back(product(block_rows, key_heads, 'qhd,khd->hqk') * HDIM ** (-0.5))
        allowed = here_places[:, None] >= places[None, :]
        scores = jnp.where(allowed[None], scores, neg_fill)
        weights = low(jax.nn.softmax(scores, axis=-1))
        return product(weights, value_heads, 'hqk,khd->qhd')
    result = lax.map(jax.checkpoint(one_block), (query_heads, query_places))
    return result.reshape(SEQ, D)

def layer(params, inputs, places):
    w_qkv, w_out, w_up, w_down, gain_rows, bias_rows, up_bias = params
    stream = low_back(inputs)
    normed = low(normalize(stream, gain_rows[0], bias_rows[0]))
    qkv_bias = jnp.concatenate([bias_rows[1], jnp.zeros_like(bias_rows[1]), bias_rows[2]])
    joined = product(normed, w_qkv, 'nsd,de->nse') + qkv_bias
    queries = low(low_back(joined[..., :D]))
    key_rows = low(low_back(joined[..., D:2 * D]))
    values = low(low_back(joined[..., 2 * D:]))
    mixed = lax.map(lambda triple: attention(triple[0], triple[1], triple[2], places), (queries, key_rows, values))
    mixed = low(low_back(mixed))
    branch = low_back(product(mixed, w_out, 'nsd,de->nse') + bias_rows[3])
    middle = stream + branch
    normed_two = low(normalize(middle, gain_rows[1], bias_rows[4]))
    hidden_pre = low_back(product(normed_two, w_up, 'nsd,df->nsf') + up_bias)
    active = low(jax.nn.gelu(hidden_pre))
    branch_two = low_back(product(active, w_down, 'nsf,fd->nsd') + bias_rows[5])
    return low(middle + branch_two)

def reference(inputs, cotangent, plan, block_table, attn_in, attn_out, mlp_in, mlp_out, norm_gains, biases, mlp_bias):
    places = positions(block_table)
    count_seqs = MICRO * BATCH
    stream = inputs[plan].astype(jnp.float32).reshape(count_seqs, SEQ, D)
    upstream = cotangent.astype(jnp.float32).reshape(count_seqs, SEQ, D)
    outputs = []
    pullers = []
    for layer_num in range(LAYERS):
        params = tuple((member[layer_num].astype(jnp.float32) for member in (attn_in, attn_out, mlp_in, mlp_out, norm_gains, biases, mlp_bias)))
        stream, puller = jax.vjp(lambda prm, val: layer(prm, val, places), params, stream)
        outputs.append(stream)
        pullers.append(puller)
    param_grads = [None] * LAYERS
    in_grads = [None] * LAYERS
    for layer_num in reversed(range(LAYERS)):
        param_grad, upstream = pullers[layer_num](upstream)
        param_grads[layer_num] = param_grad
        in_grads[layer_num] = upstream
    full_shape = (LAYERS, MICRO, BATCH, SEQ, D)
    layer_out = jnp.stack(outputs).reshape(full_shape).astype(jnp.bfloat16)
    input_grad = jnp.stack(in_grads).reshape(full_shape).astype(jnp.bfloat16)
    stacked = [jnp.stack([grad_set[index] for grad_set in param_grads]) for index in range(7)]
    return (layer_out, input_grad, stacked[0], stacked[1], stacked[2], stacked[3], stacked[4], stacked[5], stacked[6])
```

```python
import jax
import jax.numpy as jnp
from jax import lax
from jax.experimental import pallas as pl
from jax.experimental.pallas import tpu as pltpu
from jax.sharding import Mesh
from jax.sharding import PartitionSpec as P

HEADS = 12
HDIM = 64
GROUPS = 4
GROUP_HEADS = HEADS // GROUPS
WIDTH = GROUP_HEADS * HDIM
QUERY_BLOCK = 256
CTX = ("x", "yh", "core")

epsilon = 1e-05
neg_fill = -1e30


def dot(left_side, right_side, left_dim, right_dim):
    return lax.dot_general(
        left_side,
        right_side,
        (((left_dim,), (right_dim,)), ((), ())),
        preferred_element_type=jnp.float32,
    )


def head_columns(part, head):
    start = part * WIDTH + head * HDIM
    return slice(start, start + HDIM)


def attend_body(row_places, column_places, joined, mixed, log_total):
    rows = pl.ds(pl.multiple_of(pl.program_id(0) * QUERY_BLOCK, QUERY_BLOCK), QUERY_BLOCK)
    hidden = jnp.where(column_places[...] <= row_places[...], 0.0, neg_fill)
    parts = []
    for head in range(GROUP_HEADS):
        queries = joined[rows, head_columns(0, head)] * jnp.bfloat16(HDIM ** (-0.5))
        keys = joined[:, head_columns(1, head)]
        values = joined[:, head_columns(2, head)]
        scores = dot(keys, queries, 1, 1) + hidden
        top = jnp.max(scores, 0, keepdims=True)
        powers = jnp.exp(scores - top)
        total = jnp.sum(powers, 0, keepdims=True)
        parts.append(dot(values, powers.astype(jnp.bfloat16), 0, 0) / total)
        log_total[head : head + 1, :] = top + jnp.log(total)
    mixed[...] = jnp.concatenate(parts, 0).T.astype(jnp.bfloat16)


def attend(joined, row_places, column_places):
    count = joined.shape[0]
    return pl.pallas_call(
        attend_body,
        grid=(count // QUERY_BLOCK,),
        in_specs=[
            pl.BlockSpec((1, QUERY_BLOCK), lambda i: (0, i)),
            pl.BlockSpec((count, 1), lambda i: (0, 0)),
            pl.BlockSpec((count, 3 * WIDTH), lambda i: (0, 0)),
        ],
        out_specs=[
            pl.BlockSpec((QUERY_BLOCK, WIDTH), lambda i: (i, 0)),
            pl.BlockSpec((8, QUERY_BLOCK), lambda i: (0, i)),
        ],
        out_shape=[
            jax.ShapeDtypeStruct((count, WIDTH), jnp.bfloat16),
            jax.ShapeDtypeStruct((8, count), jnp.float32),
        ],
        compiler_params=pltpu.CompilerParams(vmem_limit_bytes=40 << 20),
        cost_estimate=pl.CostEstimate(
            flops=4 * count * count * WIDTH,
            bytes_accessed=8 * count * WIDTH,
            transcendentals=count * count * GROUP_HEADS,
        ),
    )(row_places, column_places, joined)


def attend_back_body(
    row_places, column_places, joined, grad_mixed, log_total, grad_joined, key_sums, value_sums
):
    step = pl.program_id(0)
    rows = pl.ds(pl.multiple_of(step * QUERY_BLOCK, QUERY_BLOCK), QUERY_BLOCK)

    @pl.when(step == 0)
    def _():
        key_sums[...] = jnp.zeros_like(key_sums)
        value_sums[...] = jnp.zeros_like(value_sums)

    hidden = jnp.where(column_places[...] <= row_places[...], 0.0, neg_fill)
    parts = []
    for head in range(GROUP_HEADS):
        queries = joined[rows, head_columns(0, head)] * jnp.bfloat16(HDIM ** (-0.5))
        keys = joined[:, head_columns(1, head)]
        values = joined[:, head_columns(2, head)]
        grads = grad_mixed[:, head_columns(0, head)]
        weights = jnp.exp(dot(keys, queries, 1, 1) + hidden - log_total[head : head + 1, :])
        grad_weights = dot(values, grads, 1, 1)
        inner_sum = jnp.sum(weights * grad_weights, 0, keepdims=True)
        grad_scores = (weights * (grad_weights - inner_sum)).astype(jnp.bfloat16)
        value_sums[head] += dot(weights.astype(jnp.bfloat16), grads, 1, 0)
        key_sums[head] += dot(grad_scores, queries, 1, 0)
        parts.append(dot(keys, grad_scores, 0, 0) * (HDIM ** (-0.5)))
    grad_joined[rows, :WIDTH] = jnp.concatenate(parts, 0).T.astype(jnp.bfloat16)

    @pl.when(step == pl.num_programs(0) - 1)
    def _():
        for head in range(GROUP_HEADS):
            grad_joined[:, head_columns(1, head)] = key_sums[head].astype(jnp.bfloat16)
            grad_joined[:, head_columns(2, head)] = value_sums[head].astype(jnp.bfloat16)


def attend_back(joined, grad_mixed, log_total, row_places, column_places):
    count = joined.shape[0]
    return pl.pallas_call(
        attend_back_body,
        grid=(count // QUERY_BLOCK,),
        in_specs=[
            pl.BlockSpec((1, QUERY_BLOCK), lambda i: (0, i)),
            pl.BlockSpec((count, 1), lambda i: (0, 0)),
            pl.BlockSpec((count, 3 * WIDTH), lambda i: (0, 0)),
            pl.BlockSpec((QUERY_BLOCK, WIDTH), lambda i: (i, 0)),
            pl.BlockSpec((8, QUERY_BLOCK), lambda i: (0, i)),
        ],
        out_specs=pl.BlockSpec((count, 3 * WIDTH), lambda i: (0, 0)),
        out_shape=jax.ShapeDtypeStruct((count, 3 * WIDTH), jnp.bfloat16),
        scratch_shapes=[
            pltpu.VMEM((GROUP_HEADS, count, HDIM), jnp.float32),
            pltpu.VMEM((GROUP_HEADS, count, HDIM), jnp.float32),
        ],
        compiler_params=pltpu.CompilerParams(vmem_limit_bytes=40 << 20),
        cost_estimate=pl.CostEstimate(
            flops=10 * count * count * WIDTH,
            bytes_accessed=16 * count * WIDTH,
            transcendentals=count * count * GROUP_HEADS,
        ),
    )(row_places, column_places, joined, grad_mixed, log_total)


def cross(left_side, right_side, pattern):
    return jnp.einsum(pattern, left_side, right_side, preferred_element_type=jnp.float32)


def normalize(values, gain_row, shift_row):
    center = values - jnp.mean(values, -1, keepdims=True)
    spread = lax.rsqrt(jnp.mean(center * center, -1, keepdims=True) + epsilon)
    unit_rows = center * spread
    return (unit_rows * gain_row + shift_row, unit_rows, spread)


def normalize_back(grad_out, unit_rows, spread, gain_row):
    grad_unit = grad_out * gain_row
    grad_in = spread * (
        grad_unit
        - jnp.mean(grad_unit, -1, keepdims=True)
        - unit_rows * jnp.mean(grad_unit * unit_rows, -1, keepdims=True)
    )
    return (grad_in, jnp.sum(grad_out * unit_rows, 0), jnp.sum(grad_out, 0))


def positions(block_table, block_len):
    offsets = jnp.arange(block_len, dtype=jnp.int32)
    return (block_table[:, None] * block_len + offsets[None, :]).reshape(-1)


def to_heads(rows, micro_count, parts):
    local = rows.shape[0] // micro_count
    split = rows.reshape(micro_count, local, parts, GROUPS, WIDTH).transpose(0, 3, 1, 2, 4)
    split = split.reshape(micro_count * GROUPS, local, parts * WIDTH)
    return lax.all_to_all(split, CTX, 0, 0, tiled=True).reshape(-1, parts * WIDTH)


def from_heads(columns, micro_count, parts):
    members = micro_count * GROUPS
    local = columns.shape[0] // members
    split = lax.all_to_all(columns.reshape(members, local, parts * WIDTH), CTX, 0, 0, tiled=True)
    split = split.reshape(micro_count, GROUPS, local, parts, WIDTH).transpose(0, 2, 3, 1, 4)
    return split.reshape(micro_count * local, parts * GROUPS * WIDTH)


def gather_weight(weight):
    return lax.all_gather(weight[0], "fsdp", axis=0, tiled=True)


def scatter_grad(grad):
    share = lax.psum_scatter(grad.astype(jnp.bfloat16), "fsdp", scatter_dimension=0, tiled=True)
    return lax.psum(share, CTX).astype(jnp.float32)[None]


def shards(
    inputs,
    cotangent,
    plan,
    block_table,
    attn_in,
    attn_out,
    mlp_in,
    mlp_out,
    norm_gains,
    biases,
    mlp_bias,
):
    shard = norm_gains.shape[2]
    small = jnp.concatenate([norm_gains[0], biases[0], mlp_bias.reshape(-1, shard)], 0)
    small_all = lax.all_gather(small, "fsdp", axis=0).astype(jnp.float32)
    w_qkv = gather_weight(attn_in)
    w_out = gather_weight(attn_out)
    w_up = gather_weight(mlp_in)
    w_down = gather_weight(mlp_out)
    model_width = w_out.shape[0]
    vector_rows = small_all[:, :8].transpose(1, 0, 2).reshape(8, model_width)
    gain_rows, bias_rows = vector_rows[:2], vector_rows[2:]
    up_bias = small_all[:, 8:].reshape(-1)
    qkv_bias = jnp.concatenate([bias_rows[1], jnp.zeros_like(bias_rows[1]), bias_rows[2]])

    micro_count, _, local_rows, _ = inputs.shape
    rows = micro_count * local_rows
    section_id = lax.axis_index("section")
    sections = lax.axis_size("section")
    places = positions(block_table, local_rows // 2)
    row_places, column_places = places[None, :], places[:, None]
    fresh = jnp.stack(
        [lax.dynamic_index_in_dim(inputs, plan[step], 0, keepdims=False) for step in range(micro_count)]
    ).reshape(rows, model_width)
    top_grad = cotangent.reshape(rows, model_width)

    def forward(entering):
        stream = entering.astype(jnp.float32)
        normed, unit_one, spread_one = normalize(stream, gain_rows[0], bias_rows[0])
        normed_low = normed.astype(jnp.bfloat16)
        joined = (cross(normed_low, w_qkv, "td,de->te") + qkv_bias).astype(jnp.bfloat16)
        joined_heads = to_heads(joined, micro_count, 3)
        mixed_heads, log_total = attend(joined_heads, row_places, column_places)
        mixed = from_heads(mixed_heads, micro_count, 1)
        middle = stream + (cross(mixed, w_out, "td,de->te") + bias_rows[3])
        normed_two, unit_two, spread_two = normalize(middle, gain_rows[1], bias_rows[4])
        normed_two_low = normed_two.astype(jnp.bfloat16)
        hidden_pre = cross(normed_two_low, w_up, "td,df->tf") + up_bias
        active_low = jax.nn.gelu(hidden_pre).astype(jnp.bfloat16)
        result = (middle + (cross(active_low, w_down, "tf,fd->td") + bias_rows[5])).astype(
            jnp.bfloat16
        )
        saved = (
            unit_one,
            spread_one,
            normed_low,
            joined_heads,
            log_total,
            mixed,
            unit_two,
            spread_two,
            normed_two_low,
            hidden_pre,
            active_low,
        )
        return result, saved

    def backward(grad_low, saved):
        (
            unit_one,
            spread_one,
            normed_low,
            joined_heads,
            log_total,
            mixed,
            unit_two,
            spread_two,
            normed_two_low,
            hidden_pre,
            active_low,
        ) = saved
        grad_top = grad_low.astype(jnp.float32)
        d_down = cross(active_low, grad_low, "tf,td->fd")
        d_shift_out = jnp.sum(grad_top, 0)
        grad_active = cross(grad_low, w_down, "td,fd->tf")
        _, gelu_pull = jax.vjp(jax.nn.gelu, hidden_pre)
        grad_hidden = gelu_pull(grad_active)[0].astype(jnp.bfloat16)
        d_up = cross(normed_two_low, grad_hidden, "td,tf->df")
        d_up_bias = jnp.sum(grad_hidden.astype(jnp.float32), 0)
        grad_normed_two = cross(grad_hidden, w_up, "tf,df->td")
        grad_norm_two, d_gain_two, d_shift_two = normalize_back(
            grad_normed_two, unit_two, spread_two, gain_rows[1]
        )
        grad_middle = grad_top + grad_norm_two
        grad_attn = grad_middle.astype(jnp.bfloat16)
        d_out = cross(mixed, grad_attn, "td,te->de")
        d_shift_attn = jnp.sum(grad_attn.astype(jnp.float32), 0)
        grad_mixed = cross(grad_attn, w_out, "te,de->td").astype(jnp.bfloat16)
        grad_mixed_heads = to_heads(grad_mixed, micro_count, 1)
        grad_heads = attend_back(
            joined_heads, grad_mixed_heads, log_total, row_places, column_places
        )
        grad_joined = from_heads(grad_heads, micro_count, 3)
        d_qkv = cross(normed_low, grad_joined, "td,te->de")
        joined_sums = jnp.sum(grad_joined.astype(jnp.float32), 0)
        grad_normed = cross(grad_joined, w_qkv, "te,de->td")
        grad_norm_one, d_gain_one, d_shift_one = normalize_back(
            grad_normed, unit_one, spread_one, gain_rows[0]
        )
        grad_in = (grad_middle + grad_norm_one).astype(jnp.bfloat16)
        vectors = jnp.stack(
            [
                d_gain_one,
                d_gain_two,
                d_shift_one,
                joined_sums[:model_width],
                joined_sums[2 * model_width :],
                d_shift_attn,
                d_shift_two,
                d_shift_out,
            ]
        )
        return grad_in, (d_qkv, d_out, d_up, d_down, vectors, d_up_bias)

    forward_pairs = [(i, i + 1) for i in range(sections - 1)]
    entering = fresh
    for _ in range(sections - 1):
        result, _ = forward(entering)
        received = lax.ppermute(result, "section", forward_pairs)
        entering = jnp.where(section_id == 0, fresh, received)
    layer_out, saved = forward(entering)

    back_pairs = [(i + 1, i) for i in range(sections - 1)]
    grad_low = top_grad
    for _ in range(sections - 1):
        result, _ = backward(grad_low, saved)
        received = lax.ppermute(result, "section", back_pairs)
        grad_low = jnp.where(section_id == sections - 1, top_grad, received)
    input_grad, (d_qkv, d_out, d_up, d_down, vectors, d_up_bias) = backward(grad_low, saved)

    vector_grads = jnp.concatenate([vectors, d_up_bias.reshape(-1, model_width)], 0)
    vector_grads = lax.psum(vector_grads, CTX + ("fsdp",))
    fsdp_id = lax.axis_index("fsdp")
    own_vectors = lax.dynamic_slice_in_dim(vector_grads[:8], fsdp_id * shard, shard, 1)
    up_len = mlp_bias.shape[1]
    own_up_bias = lax.dynamic_slice_in_dim(vector_grads[8:].reshape(-1), fsdp_id * up_len, up_len, 0)
    out_shape = (1, micro_count, 1, local_rows, model_width)
    return (
        layer_out.reshape(out_shape),
        input_grad.reshape(out_shape),
        scatter_grad(d_qkv),
        scatter_grad(d_out),
        scatter_grad(d_up),
        scatter_grad(d_down),
        own_vectors[None, :2],
        own_vectors[None, 2:],
        own_up_bias[None],
    )


def solution(mesh):
    fine = Mesh(
        mesh.devices.reshape(2, 4, 2, 2, 4), ("section", "x", "yh", "core", "fsdp")
    )
    rows = P(None, "fsdp", CTX, None)
    weight = P("section", "fsdp", None)
    vector = P("section", None, "fsdp")
    row = P("section", "fsdp")
    out_rows = P("section", None, "fsdp", CTX, None)
    return jax.shard_map(
        shards,
        mesh=fine,
        in_specs=(rows, rows, P(), P(), weight, weight, weight, weight, vector, vector, row),
        out_specs=(out_rows, out_rows, weight, weight, weight, weight, vector, vector, row),
        check_vma=False,
    )
```

```python
import jax
import jax.numpy as jnp
from jax import lax
from jax.experimental import pallas as pl
from jax.experimental.pallas import tpu as pltpu
from jax.sharding import Mesh
from jax.sharding import PartitionSpec as P

HEADS = 12
HDIM = 64
GROUPS = 4
GROUP_HEADS = HEADS // GROUPS
WIDTH = GROUP_HEADS * HDIM
QUERY_BLOCK = 256
EXTRA = 16
CTX = ("x", "yh", "core")

epsilon = 1e-05
neg_fill = -1e30


def dot(left_side, right_side, left_dim, right_dim):
    return lax.dot_general(
        left_side,
        right_side,
        (((left_dim,), (right_dim,)), ((), ())),
        preferred_element_type=jnp.float32,
    )


def head_columns(part, head):
    start = part * WIDTH + head * HDIM
    return slice(start, start + HDIM)


def attend_body(row_places, column_places, joined, mixed, log_total):
    rows = pl.ds(pl.multiple_of(pl.program_id(0) * QUERY_BLOCK, QUERY_BLOCK), QUERY_BLOCK)
    hidden = jnp.where(column_places[...] <= row_places[...], 0.0, neg_fill)
    parts = []
    for head in range(GROUP_HEADS):
        queries = joined[rows, head_columns(0, head)] * jnp.bfloat16(HDIM ** (-0.5))
        keys = joined[:, head_columns(1, head)]
        values = joined[:, head_columns(2, head)]
        scores = dot(keys, queries, 1, 1) + hidden
        top = jnp.max(scores, 0, keepdims=True)
        powers = jnp.exp(scores - top)
        total = jnp.sum(powers, 0, keepdims=True)
        parts.append(dot(values, powers.astype(jnp.bfloat16), 0, 0) / total)
        log_total[head : head + 1, :] = top + jnp.log(total)
    mixed[...] = jnp.concatenate(parts, 0).T.astype(jnp.bfloat16)


def attend(joined, row_places, column_places):
    count = joined.shape[0]
    return pl.pallas_call(
        attend_body,
        grid=(count // QUERY_BLOCK,),
        in_specs=[
            pl.BlockSpec((1, QUERY_BLOCK), lambda i: (0, i)),
            pl.BlockSpec((count, 1), lambda i: (0, 0)),
            pl.BlockSpec((count, 3 * WIDTH), lambda i: (0, 0)),
        ],
        out_specs=[
            pl.BlockSpec((QUERY_BLOCK, WIDTH), lambda i: (i, 0)),
            pl.BlockSpec((8, QUERY_BLOCK), lambda i: (0, i)),
        ],
        out_shape=[
            jax.ShapeDtypeStruct((count, WIDTH), jnp.bfloat16),
            jax.ShapeDtypeStruct((8, count), jnp.float32),
        ],
        compiler_params=pltpu.CompilerParams(vmem_limit_bytes=40 << 20),
        cost_estimate=pl.CostEstimate(
            flops=4 * count * count * WIDTH,
            bytes_accessed=8 * count * WIDTH,
            transcendentals=count * count * GROUP_HEADS,
        ),
    )(row_places, column_places, joined)


def attend_back_body(
    row_places, column_places, joined, grad_mixed, log_total, grad_joined, key_sums, value_sums
):
    step = pl.program_id(0)
    rows = pl.ds(pl.multiple_of(step * QUERY_BLOCK, QUERY_BLOCK), QUERY_BLOCK)

    @pl.when(step == 0)
    def _():
        key_sums[...] = jnp.zeros_like(key_sums)
        value_sums[...] = jnp.zeros_like(value_sums)

    hidden = jnp.where(column_places[...] <= row_places[...], 0.0, neg_fill)
    parts = []
    for head in range(GROUP_HEADS):
        queries = joined[rows, head_columns(0, head)] * jnp.bfloat16(HDIM ** (-0.5))
        keys = joined[:, head_columns(1, head)]
        values = joined[:, head_columns(2, head)]
        grads = grad_mixed[:, head_columns(0, head)]
        weights = jnp.exp(dot(keys, queries, 1, 1) + hidden - log_total[head : head + 1, :])
        grad_weights = dot(values, grads, 1, 1)
        inner_sum = jnp.sum(weights * grad_weights, 0, keepdims=True)
        grad_scores = (weights * (grad_weights - inner_sum)).astype(jnp.bfloat16)
        value_sums[head] += dot(weights.astype(jnp.bfloat16), grads, 1, 0)
        key_sums[head] += dot(grad_scores, queries, 1, 0)
        parts.append(dot(keys, grad_scores, 0, 0) * (HDIM ** (-0.5)))
    grad_joined[rows, :WIDTH] = jnp.concatenate(parts, 0).T.astype(jnp.bfloat16)

    @pl.when(step == pl.num_programs(0) - 1)
    def _():
        for head in range(GROUP_HEADS):
            grad_joined[:, head_columns(1, head)] = key_sums[head].astype(jnp.bfloat16)
            grad_joined[:, head_columns(2, head)] = value_sums[head].astype(jnp.bfloat16)


def attend_back(joined, grad_mixed, log_total, row_places, column_places):
    count = joined.shape[0]
    return pl.pallas_call(
        attend_back_body,
        grid=(count // QUERY_BLOCK,),
        in_specs=[
            pl.BlockSpec((1, QUERY_BLOCK), lambda i: (0, i)),
            pl.BlockSpec((count, 1), lambda i: (0, 0)),
            pl.BlockSpec((count, 3 * WIDTH), lambda i: (0, 0)),
            pl.BlockSpec((QUERY_BLOCK, WIDTH), lambda i: (i, 0)),
            pl.BlockSpec((8, QUERY_BLOCK), lambda i: (0, i)),
        ],
        out_specs=pl.BlockSpec((count, 3 * WIDTH), lambda i: (0, 0)),
        out_shape=jax.ShapeDtypeStruct((count, 3 * WIDTH), jnp.bfloat16),
        scratch_shapes=[
            pltpu.VMEM((GROUP_HEADS, count, HDIM), jnp.float32),
            pltpu.VMEM((GROUP_HEADS, count, HDIM), jnp.float32),
        ],
        compiler_params=pltpu.CompilerParams(vmem_limit_bytes=40 << 20),
        cost_estimate=pl.CostEstimate(
            flops=10 * count * count * WIDTH,
            bytes_accessed=16 * count * WIDTH,
            transcendentals=count * count * GROUP_HEADS,
        ),
    )(row_places, column_places, joined, grad_mixed, log_total)


def cross(left_side, right_side, pattern):
    return jnp.einsum(pattern, left_side, right_side, preferred_element_type=jnp.float32)


def normalize(values, gain_row, shift_row):
    center = values - jnp.mean(values, -1, keepdims=True)
    spread = lax.rsqrt(jnp.mean(center * center, -1, keepdims=True) + epsilon)
    unit_rows = center * spread
    return (unit_rows * gain_row + shift_row, unit_rows, spread)


def normalize_back(grad_out, unit_rows, spread, gain_row):
    grad_unit = grad_out * gain_row
    grad_in = spread * (
        grad_unit
        - jnp.mean(grad_unit, -1, keepdims=True)
        - unit_rows * jnp.mean(grad_unit * unit_rows, -1, keepdims=True)
    )
    return (grad_in, jnp.sum(grad_out * unit_rows, 0), jnp.sum(grad_out, 0))


def positions(block_table, block_len):
    offsets = jnp.arange(block_len, dtype=jnp.int32)
    return (block_table[:, None] * block_len + offsets[None, :]).reshape(-1)


def to_heads(rows, micro_count, parts):
    local = rows.shape[0] // micro_count
    split = rows.reshape(micro_count, local, parts, GROUPS, WIDTH).transpose(0, 3, 1, 2, 4)
    split = split.reshape(micro_count * GROUPS, local, parts * WIDTH)
    return lax.all_to_all(split, CTX, 0, 0, tiled=True).reshape(-1, parts * WIDTH)


def from_heads(columns, micro_count, parts):
    members = micro_count * GROUPS
    local = columns.shape[0] // members
    split = lax.all_to_all(columns.reshape(members, local, parts * WIDTH), CTX, 0, 0, tiled=True)
    split = split.reshape(micro_count, GROUPS, local, parts, WIDTH).transpose(0, 2, 3, 1, 4)
    return split.reshape(micro_count * local, parts * GROUPS * WIDTH)


def gather_weight(weight):
    half = weight.shape[1] // 2
    own = lax.dynamic_slice_in_dim(weight[0], lax.axis_index("core") * half, half, 0)
    return lax.all_gather(own, ("fsdp", "core"), axis=0, tiled=True)


def gather_small(value):
    count = lax.axis_size("fsdp")
    place = lax.axis_index("fsdp")
    whole = jnp.zeros((count,) + value.shape, value.dtype)
    for shift in range(count):
        pairs = [(source, (source + shift) % count) for source in range(count)]
        member = lax.ppermute(value, "fsdp", pairs) if shift else value
        whole = lax.dynamic_update_index_in_dim(whole, member, (place - shift) % count, 0)
    return whole


def scatter_grad(grad):
    return lax.psum_scatter(grad, ("fsdp", "core"), scatter_dimension=0, tiled=True)


def finish_grad(share, axes):
    total = lax.psum(share, axes)
    other = lax.ppermute(total, "core", [(0, 1), (1, 0)])
    first = lax.axis_index("core") == 0
    return jnp.stack([jnp.where(first, total, other), jnp.where(first, other, total)]).astype(
        jnp.float32
    )


def shards(
    inputs,
    cotangent,
    plan,
    block_table,
    attn_in,
    attn_out,
    mlp_in,
    mlp_out,
    norm_gains,
    biases,
    mlp_bias,
):
    shard = norm_gains.shape[2]
    small = jnp.concatenate([norm_gains[0], biases[0], mlp_bias.reshape(-1, shard)], 0)
    small_all = gather_small(small).astype(jnp.float32)
    w_qkv = gather_weight(attn_in)
    w_out = gather_weight(attn_out)
    w_up = gather_weight(mlp_in)
    w_down = gather_weight(mlp_out)
    model_width = w_out.shape[0]
    vector_rows = small_all[:, :8].transpose(1, 0, 2).reshape(8, model_width)
    gain_rows, bias_rows = vector_rows[:2], vector_rows[2:]
    up_bias = small_all[:, 8:].reshape(-1)
    qkv_bias = jnp.concatenate([bias_rows[1], jnp.zeros_like(bias_rows[1]), bias_rows[2]])

    micro_count, _, local_rows, _ = inputs.shape
    rows = micro_count * local_rows
    section_id = lax.axis_index("section")
    sections = lax.axis_size("section")
    places = positions(block_table, local_rows // 2)
    row_places, column_places = places[None, :], places[:, None]
    fresh = jnp.stack(
        [lax.dynamic_index_in_dim(inputs, plan[step], 0, keepdims=False) for step in range(micro_count)]
    ).reshape(rows, model_width)
    top_grad = cotangent.reshape(rows, model_width)

    def forward(entering):
        stream = entering.astype(jnp.float32)
        normed, unit_one, spread_one = normalize(stream, gain_rows[0], bias_rows[0])
        normed_low = normed.astype(jnp.bfloat16)
        joined = (cross(normed_low, w_qkv, "td,de->te") + qkv_bias).astype(jnp.bfloat16)
        joined_heads = to_heads(joined, micro_count, 3)
        mixed_heads, log_total = attend(joined_heads, row_places, column_places)
        mixed = from_heads(mixed_heads, micro_count, 1)
        middle = stream + (cross(mixed, w_out, "td,de->te") + bias_rows[3])
        normed_two, unit_two, spread_two = normalize(middle, gain_rows[1], bias_rows[4])
        normed_two_low = normed_two.astype(jnp.bfloat16)
        hidden_pre = cross(normed_two_low, w_up, "td,df->tf") + up_bias
        active_low = jax.nn.gelu(hidden_pre).astype(jnp.bfloat16)
        result = (middle + (cross(active_low, w_down, "tf,fd->td") + bias_rows[5])).astype(
            jnp.bfloat16
        )
        saved = (
            unit_one,
            spread_one,
            normed_low,
            joined_heads,
            log_total,
            mixed,
            unit_two,
            spread_two,
            normed_two_low,
            hidden_pre,
            active_low,
        )
        return result, saved

    def backward(grad_low, saved):
        (
            unit_one,
            spread_one,
            normed_low,
            joined_heads,
            log_total,
            mixed,
            unit_two,
            spread_two,
            normed_two_low,
            hidden_pre,
            active_low,
        ) = saved
        grad_top = grad_low.astype(jnp.float32)
        d_down = cross(active_low, grad_low, "tf,td->fd")
        d_shift_out = jnp.sum(grad_top, 0)
        grad_active = cross(grad_low, w_down, "td,fd->tf")
        _, gelu_pull = jax.vjp(jax.nn.gelu, hidden_pre)
        grad_hidden = gelu_pull(grad_active)[0].astype(jnp.bfloat16)
        d_up = cross(normed_two_low, grad_hidden, "td,tf->df")
        d_up_bias = jnp.sum(grad_hidden.astype(jnp.float32), 0)
        grad_normed_two = cross(grad_hidden, w_up, "tf,df->td")
        grad_norm_two, d_gain_two, d_shift_two = normalize_back(
            grad_normed_two, unit_two, spread_two, gain_rows[1]
        )
        grad_middle = grad_top + grad_norm_two
        grad_attn = grad_middle.astype(jnp.bfloat16)
        d_out = cross(mixed, grad_attn, "td,te->de")
        d_shift_attn = jnp.sum(grad_attn.astype(jnp.float32), 0)
        grad_mixed = cross(grad_attn, w_out, "te,de->td").astype(jnp.bfloat16)
        d_down, d_up, d_out = (value.astype(jnp.bfloat16) for value in (d_down, d_up, d_out))
        grad_mixed, d_down, d_up, d_out = lax.optimization_barrier(
            (grad_mixed, d_down, d_up, d_out)
        )
        grad_mixed_heads = to_heads(grad_mixed, micro_count, 1)
        grad_heads = attend_back(
            joined_heads, grad_mixed_heads, log_total, row_places, column_places
        )
        grad_joined = from_heads(grad_heads, micro_count, 3)
        d_qkv = cross(normed_low, grad_joined, "td,te->de")
        joined_sums = jnp.sum(grad_joined.astype(jnp.float32), 0)
        grad_normed = cross(grad_joined, w_qkv, "te,de->td")
        grad_norm_one, d_gain_one, d_shift_one = normalize_back(
            grad_normed, unit_one, spread_one, gain_rows[0]
        )
        grad_in = (grad_middle + grad_norm_one).astype(jnp.bfloat16)
        vectors = jnp.stack(
            [
                d_gain_one,
                d_gain_two,
                d_shift_one,
                joined_sums[:model_width],
                joined_sums[2 * model_width :],
                d_shift_attn,
                d_shift_two,
                d_shift_out,
            ]
        )
        return grad_in, (d_qkv, d_out, d_up, d_down, vectors, d_up_bias)

    forward_pairs = [(i, i + 1) for i in range(sections - 1)]
    entering = fresh
    for _ in range(sections - 1):
        result, _ = forward(entering)
        received = lax.ppermute(result, "section", forward_pairs)
        entering = jnp.where(section_id == 0, fresh, received)
    layer_out, saved = forward(entering)

    back_pairs = [(i + 1, i) for i in range(sections - 1)]
    grad_low = top_grad
    for _ in range(sections - 1):
        result, _ = backward(grad_low, saved)
        received = lax.ppermute(result, "section", back_pairs)
        grad_low = jnp.where(section_id == sections - 1, top_grad, received)
    input_grad, (d_qkv, d_out, d_up, d_down, vectors, d_up_bias) = backward(grad_low, saved)

    members = 2 * (model_width // shard)
    owner_row = jnp.concatenate(
        [
            vectors.reshape(8, -1, shard).transpose(1, 0, 2).reshape(-1, 1, 8 * shard),
            d_up_bias.reshape(-1, 1, mlp_bias.shape[1]),
        ],
        -1,
    )
    owner_row = jnp.pad(owner_row, ((0, 0), (0, 2 * EXTRA - 1), (0, 0)))
    owner_row = owner_row.reshape(members, EXTRA, -1)
    d_qkv = jnp.concatenate([d_qkv.reshape(members, shard // 2, -1), owner_row], 1)
    d_qkv = d_qkv.astype(jnp.bfloat16).reshape(-1, d_qkv.shape[-1])
    g_up = finish_grad(scatter_grad(d_up), ("yh", "x"))
    g_down = finish_grad(scatter_grad(d_down), ("yh", "x"))
    g_out = finish_grad(scatter_grad(d_out), ("x", "yh"))
    g_qkv = finish_grad(scatter_grad(d_qkv), ("x", "yh"))
    own_row = g_qkv[0, shard // 2]
    own_vectors = own_row[: 8 * shard].reshape(8, shard)
    own_up_bias = own_row[8 * shard :]
    g_qkv = g_qkv[:, : shard // 2]
    out_shape = (1, micro_count, 1, local_rows, model_width)
    return (
        layer_out.reshape(out_shape),
        input_grad.reshape(out_shape),
        g_qkv.reshape(1, -1, g_qkv.shape[-1]),
        g_out.reshape(1, -1, g_out.shape[-1]),
        g_up.reshape(1, -1, g_up.shape[-1]),
        g_down.reshape(1, -1, g_down.shape[-1]),
        own_vectors[None, :2],
        own_vectors[None, 2:],
        own_up_bias[None],
    )


def solution(mesh):
    fine = Mesh(
        mesh.devices.reshape(2, 4, 2, 2, 4), ("section", "x", "yh", "core", "fsdp")
    )
    rows = P(None, "fsdp", CTX, None)
    weight = P("section", "fsdp", None)
    vector = P("section", None, "fsdp")
    row = P("section", "fsdp")
    out_rows = P("section", None, "fsdp", CTX, None)
    return jax.shard_map(
        shards,
        mesh=fine,
        in_specs=(rows, rows, P(), P(), weight, weight, weight, weight, vector, vector, row),
        out_specs=(out_rows, out_rows, weight, weight, weight, weight, vector, vector, row),
        check_vma=False,
    )
```

```python
import jax
import jax.numpy as jnp
from jax import lax
from jax.experimental import pallas as pl
from jax.experimental.pallas import tpu as pltpu
from jax.sharding import Mesh
from jax.sharding import PartitionSpec as P

HEADS = 12
HDIM = 64
GROUPS = 4
GROUP_HEADS = HEADS // GROUPS
WIDTH = GROUP_HEADS * HDIM
QUERY_BLOCK = 256
EXTRA = 32
CTX = ("x", "yh", "core")

epsilon = 1e-05
neg_fill = -1e30


def dot(left_side, right_side, left_dim, right_dim):
    return lax.dot_general(
        left_side,
        right_side,
        (((left_dim,), (right_dim,)), ((), ())),
        preferred_element_type=jnp.float32,
    )


def head_columns(part, head):
    start = part * WIDTH + head * HDIM
    return slice(start, start + HDIM)


def attend_body(
    row_places, column_places, own, other, weight, bias, joined, mixed, log_total
):
    step = pl.program_id(0)
    half = own.shape[1]

    @pl.when(step == 0)
    def _():
        product = dot(own[...], weight[:half, :], 1, 0) + dot(other[...], weight[half:, :], 1, 0)
        joined[...] = (product + bias[...]).astype(jnp.bfloat16)

    rows = pl.ds(pl.multiple_of(step * QUERY_BLOCK, QUERY_BLOCK), QUERY_BLOCK)
    hidden = jnp.where(column_places[...] <= row_places[...], 0.0, neg_fill)
    parts = []
    for head in range(GROUP_HEADS):
        queries = joined[rows, head_columns(0, head)] * jnp.bfloat16(HDIM ** (-0.5))
        keys = joined[:, head_columns(1, head)]
        values = joined[:, head_columns(2, head)]
        scores = dot(keys, queries, 1, 1) + hidden
        top = jnp.max(scores, 0, keepdims=True)
        powers = jnp.exp(scores - top)
        total = jnp.sum(powers, 0, keepdims=True)
        parts.append(dot(values, powers.astype(jnp.bfloat16), 0, 0) / total)
        log_total[head : head + 1, :] = top + jnp.log(total)
    mixed[...] = jnp.concatenate(parts, 0).T.astype(jnp.bfloat16)


def whole(*shape):
    return pl.BlockSpec(shape, lambda i: (0,) * len(shape))


def attend(own, other, weight, bias, row_places, column_places):
    count, half = own.shape
    return pl.pallas_call(
        attend_body,
        grid=(count // QUERY_BLOCK,),
        in_specs=[
            pl.BlockSpec((1, QUERY_BLOCK), lambda i: (0, i)),
            whole(count, 1),
            whole(count, half),
            whole(count, half),
            whole(2 * half, 3 * WIDTH),
            whole(1, 3 * WIDTH),
        ],
        out_specs=[
            whole(count, 3 * WIDTH),
            pl.BlockSpec((QUERY_BLOCK, WIDTH), lambda i: (i, 0)),
            pl.BlockSpec((8, QUERY_BLOCK), lambda i: (0, i)),
        ],
        out_shape=[
            jax.ShapeDtypeStruct((count, 3 * WIDTH), jnp.bfloat16),
            jax.ShapeDtypeStruct((count, WIDTH), jnp.bfloat16),
            jax.ShapeDtypeStruct((8, count), jnp.float32),
        ],
        compiler_params=pltpu.CompilerParams(vmem_limit_bytes=48 << 20),
        cost_estimate=pl.CostEstimate(
            flops=4 * count * count * WIDTH,
            bytes_accessed=8 * count * WIDTH,
            transcendentals=count * count * GROUP_HEADS,
        ),
    )(row_places, column_places, own, other, weight, bias)


def attend_back_body(
    row_places,
    column_places,
    joined,
    grad_mixed,
    log_total,
    weight,
    grad_joined,
    grad_own,
    grad_other,
    key_sums,
    value_sums,
):
    step = pl.program_id(0)
    rows = pl.ds(pl.multiple_of(step * QUERY_BLOCK, QUERY_BLOCK), QUERY_BLOCK)

    @pl.when(step == 0)
    def _():
        key_sums[...] = jnp.zeros_like(key_sums)
        value_sums[...] = jnp.zeros_like(value_sums)

    hidden = jnp.where(column_places[...] <= row_places[...], 0.0, neg_fill)
    parts = []
    for head in range(GROUP_HEADS):
        queries = joined[rows, head_columns(0, head)] * jnp.bfloat16(HDIM ** (-0.5))
        keys = joined[:, head_columns(1, head)]
        values = joined[:, head_columns(2, head)]
        grads = grad_mixed[:, head_columns(0, head)]
        weights = jnp.exp(dot(keys, queries, 1, 1) + hidden - log_total[head : head + 1, :])
        grad_weights = dot(values, grads, 1, 1)
        inner_sum = jnp.sum(weights * grad_weights, 0, keepdims=True)
        grad_scores = (weights * (grad_weights - inner_sum)).astype(jnp.bfloat16)
        value_sums[head] += dot(weights.astype(jnp.bfloat16), grads, 1, 0)
        key_sums[head] += dot(grad_scores, queries, 1, 0)
        parts.append(dot(keys, grad_scores, 0, 0) * (HDIM ** (-0.5)))
    grad_joined[rows, :WIDTH] = jnp.concatenate(parts, 0).T.astype(jnp.bfloat16)

    @pl.when(step == pl.num_programs(0) - 1)
    def _():
        for head in range(GROUP_HEADS):
            grad_joined[:, head_columns(1, head)] = key_sums[head].astype(jnp.bfloat16)
            grad_joined[:, head_columns(2, head)] = value_sums[head].astype(jnp.bfloat16)
        half = grad_own.shape[1]
        grad_own[...] = dot(grad_joined[...], weight[:half, :], 1, 1).astype(jnp.bfloat16)
        grad_other[...] = dot(grad_joined[...], weight[half:, :], 1, 1).astype(jnp.bfloat16)


def attend_back(joined, grad_mixed, log_total, weight, row_places, column_places):
    count = joined.shape[0]
    half = weight.shape[0] // 2
    return pl.pallas_call(
        attend_back_body,
        grid=(count // QUERY_BLOCK,),
        in_specs=[
            pl.BlockSpec((1, QUERY_BLOCK), lambda i: (0, i)),
            whole(count, 1),
            whole(count, 3 * WIDTH),
            pl.BlockSpec((QUERY_BLOCK, WIDTH), lambda i: (i, 0)),
            pl.BlockSpec((8, QUERY_BLOCK), lambda i: (0, i)),
            whole(2 * half, 3 * WIDTH),
        ],
        out_specs=[whole(count, 3 * WIDTH), whole(count, half), whole(count, half)],
        out_shape=[
            jax.ShapeDtypeStruct((count, 3 * WIDTH), jnp.bfloat16),
            jax.ShapeDtypeStruct((count, half), jnp.bfloat16),
            jax.ShapeDtypeStruct((count, half), jnp.bfloat16),
        ],
        scratch_shapes=[
            pltpu.VMEM((GROUP_HEADS, count, HDIM), jnp.float32),
            pltpu.VMEM((GROUP_HEADS, count, HDIM), jnp.float32),
        ],
        compiler_params=pltpu.CompilerParams(vmem_limit_bytes=48 << 20),
        cost_estimate=pl.CostEstimate(
            flops=10 * count * count * WIDTH,
            bytes_accessed=16 * count * WIDTH,
            transcendentals=count * count * GROUP_HEADS,
        ),
    )(row_places, column_places, joined, grad_mixed, log_total, weight)


def cross(left_side, right_side, pattern):
    return jnp.einsum(pattern, left_side, right_side, preferred_element_type=jnp.float32)


def normalize(values, gain_row, shift_row):
    center = values - jnp.mean(values, -1, keepdims=True)
    spread = lax.rsqrt(jnp.mean(center * center, -1, keepdims=True) + epsilon)
    unit_rows = center * spread
    return (unit_rows * gain_row + shift_row, unit_rows, spread)


def normalize_back(grad_out, unit_rows, spread, gain_row):
    grad_unit = grad_out * gain_row
    grad_in = spread * (
        grad_unit
        - jnp.mean(grad_unit, -1, keepdims=True)
        - unit_rows * jnp.mean(grad_unit * unit_rows, -1, keepdims=True)
    )
    return (grad_in, jnp.sum(grad_out * unit_rows, 0), jnp.sum(grad_out, 0))


def positions(block_table, block_len):
    offsets = jnp.arange(block_len, dtype=jnp.int32)
    return (block_table[:, None] * block_len + offsets[None, :]).reshape(-1)


def exchange(value, axes):
    return lax.all_to_all(value, axes, 0, 0, tiled=True)


def swap(value):
    return lax.ppermute(value, "core", [(0, 1), (1, 0)])


def in_order(own, other):
    first = lax.axis_index("core") == 0
    return jnp.where(first, own, other), jnp.where(first, other, own)


def gather_weight(weight):
    half = weight.shape[1] // 2
    own = lax.dynamic_slice_in_dim(weight[0], lax.axis_index("core") * half, half, 0)
    return lax.all_gather(own, ("fsdp", "core"), axis=0, tiled=True)


def gather_small(value):
    count = lax.axis_size("fsdp")
    place = lax.axis_index("fsdp")
    gathered = jnp.zeros((count,) + value.shape, value.dtype)
    for shift in range(count):
        pairs = [(source, (source + shift) % count) for source in range(count)]
        member = lax.ppermute(value, "fsdp", pairs) if shift else value
        gathered = lax.dynamic_update_index_in_dim(gathered, member, (place - shift) % count, 0)
    return gathered


def sum_low(value):
    return jnp.sum(value.astype(jnp.float32), 0).astype(jnp.bfloat16)


def spread(value, axes):
    count = lax.axis_size(axes)
    return exchange(jnp.broadcast_to(value[None], (count,) + value.shape), axes)


def shards(
    inputs,
    cotangent,
    plan,
    block_table,
    attn_in,
    attn_out,
    mlp_in,
    mlp_out,
    norm_gains,
    biases,
    mlp_bias,
):
    shard = norm_gains.shape[2]
    core_id = lax.axis_index("core")
    group_id = lax.axis_index("yh") * 2 + core_id
    fsdp_id = lax.axis_index("fsdp")
    section_id = lax.axis_index("section")
    sections = lax.axis_size("section")
    fsdp_count = lax.axis_size("fsdp")

    small = jnp.concatenate([norm_gains[0], biases[0], mlp_bias.reshape(-1, shard)], 0)
    own_columns = lax.dynamic_index_in_dim(
        attn_in[0].reshape(shard, 3, GROUPS, WIDTH), group_id, 2, keepdims=False
    ).reshape(shard, 3 * WIDTH)
    w_group = gather_small(own_columns).reshape(-1, 3 * WIDTH)
    small_all = gather_small(small).astype(jnp.float32)
    w_out = gather_weight(attn_out)
    w_up = gather_weight(mlp_in)
    w_down = gather_weight(mlp_out)
    model_width = w_out.shape[0]
    half = model_width // 2
    w_group = jnp.concatenate(in_order(w_group[:half], w_group[half:]), 0)
    w_out_groups = w_out.reshape(GROUPS, WIDTH, model_width)
    vector_rows = small_all[:, :8].transpose(1, 0, 2).reshape(8, model_width)
    gain_rows, bias_rows = vector_rows[:2], vector_rows[2:]
    up_bias = small_all[:, 8:].reshape(-1)
    own_bias = lax.dynamic_index_in_dim(small_all, group_id, 0, keepdims=False)
    group_bias = jnp.concatenate([own_bias[3], jnp.zeros_like(own_bias[3]), own_bias[4]])[None]

    micro_count, _, local_rows, _ = inputs.shape
    rows = micro_count * local_rows
    places = positions(block_table, local_rows // 2)
    row_places, column_places = places[None, :], places[:, None]
    fresh = jnp.stack(
        [lax.dynamic_index_in_dim(inputs, plan[step], 0, keepdims=False) for step in range(micro_count)]
    ).reshape(rows, model_width)
    top_grad = cotangent.reshape(rows, model_width)
    head_shape = (micro_count, GROUPS, local_rows, WIDTH)

    def forward(entering):
        stream = entering.astype(jnp.float32)
        normed, unit_one, spread_one = normalize(stream, gain_rows[0], bias_rows[0])
        halves = normed.astype(jnp.bfloat16).reshape(micro_count, 1, local_rows, 2, half)
        halves = jnp.broadcast_to(
            halves.transpose(0, 1, 3, 2, 4), (micro_count, 2, 2, local_rows, half)
        )
        own = exchange(halves.reshape(-1, local_rows, half), CTX).reshape(-1, half)
        other = swap(own)
        joined, mixed_heads, log_total = attend(
            own, other, w_group, group_bias, row_places, column_places
        )
        mixed = exchange(mixed_heads.reshape(-1, local_rows, WIDTH), CTX).reshape(head_shape)
        attended = cross(mixed, w_out_groups, "mgtd,gde->mte").reshape(rows, model_width)
        middle = stream + (attended + bias_rows[3])
        normed_two, unit_two, spread_two = normalize(middle, gain_rows[1], bias_rows[4])
        normed_two_low = normed_two.astype(jnp.bfloat16)
        hidden_pre = cross(normed_two_low, w_up, "td,df->tf") + up_bias
        active_low = jax.nn.gelu(hidden_pre).astype(jnp.bfloat16)
        result = (middle + (cross(active_low, w_down, "tf,fd->td") + bias_rows[5])).astype(
            jnp.bfloat16
        )
        saved = (
            unit_one,
            spread_one,
            own,
            other,
            joined,
            log_total,
            mixed,
            unit_two,
            spread_two,
            normed_two_low,
            hidden_pre,
            active_low,
        )
        return result, saved

    def backward(grad_low, saved, last):
        (
            unit_one,
            spread_one,
            own,
            other,
            joined,
            log_total,
            mixed,
            unit_two,
            spread_two,
            normed_two_low,
            hidden_pre,
            active_low,
        ) = saved
        grad_top = grad_low.astype(jnp.float32)
        grad_active = cross(grad_low, w_down, "td,fd->tf")
        _, gelu_pull = jax.vjp(jax.nn.gelu, hidden_pre)
        grad_hidden = gelu_pull(grad_active)[0].astype(jnp.bfloat16)
        grad_normed_two = cross(grad_hidden, w_up, "tf,df->td")
        grad_norm_two, d_gain_two, d_shift_two = normalize_back(
            grad_normed_two, unit_two, spread_two, gain_rows[1]
        )
        grad_middle = grad_top + grad_norm_two
        grad_attn = grad_middle.astype(jnp.bfloat16)
        attn_parts = grad_attn.reshape(micro_count, local_rows, model_width)
        grad_mixed = cross(attn_parts, w_out_groups, "mte,gde->mgtd").astype(jnp.bfloat16)
        share = None
        if last:
            members = 2 * fsdp_count
            d_down = cross(active_low, grad_low, "tf,td->fd").astype(jnp.bfloat16)
            d_up = cross(normed_two_low, grad_hidden, "td,tf->df").astype(jnp.bfloat16)
            d_out = cross(mixed, attn_parts, "mgtd,mte->gde").astype(jnp.bfloat16)
            d_up = d_up.reshape(members, shard // 2, -1, model_width).transpose(0, 2, 1, 3)
            parts = [
                d_down.reshape(members, -1, model_width),
                d_up.reshape(members, -1, model_width),
                d_out.reshape(members, -1, model_width),
            ]
            parts.append(jnp.zeros((members, EXTRA, model_width), jnp.bfloat16))
            joint = jnp.concatenate(parts, 1)
            grad_mixed, joint = lax.optimization_barrier((grad_mixed, joint))
            share = lax.psum_scatter(
                joint.reshape(-1, model_width),
                ("fsdp", "core"),
                scatter_dimension=0,
                tiled=True,
            )
        grad_heads = exchange(grad_mixed.reshape(-1, local_rows, WIDTH), CTX).reshape(-1, WIDTH)
        grad_joined, grad_own, grad_other = attend_back(
            joined, grad_heads, log_total, w_group, row_places, column_places
        )
        received = swap(grad_other)
        summed = (grad_own.astype(jnp.float32) + received.astype(jnp.float32)).astype(jnp.bfloat16)
        returned = exchange(summed.reshape(-1, local_rows, half), CTX)
        returned = returned.reshape(micro_count, 2, 2, local_rows, half).astype(jnp.float32)
        grad_normed = (returned[:, 0] + returned[:, 1]).transpose(0, 2, 1, 3)
        grad_normed = grad_normed.reshape(rows, model_width)
        if last:
            grad_normed, share = lax.optimization_barrier((grad_normed, share))
        grad_norm_one, d_gain_one, d_shift_one = normalize_back(
            grad_normed, unit_one, spread_one, gain_rows[0]
        )
        grad_in = (grad_middle + grad_norm_one).astype(jnp.bfloat16)
        if not last:
            return grad_in
        d_qkv = jnp.concatenate(
            in_order(
                cross(own, grad_joined, "td,te->de").astype(jnp.bfloat16),
                cross(other, grad_joined, "td,te->de").astype(jnp.bfloat16),
            ),
            0,
        )
        joined_sums = jnp.sum(grad_joined.astype(jnp.float32), 0)
        vectors = jnp.stack(
            [
                d_gain_one,
                d_gain_two,
                d_shift_one,
                jnp.sum(grad_attn.astype(jnp.float32), 0),
                d_shift_two,
                jnp.sum(grad_top, 0),
            ]
        )
        d_up_bias = jnp.sum(grad_hidden.astype(jnp.float32), 0)
        return grad_in, share, d_qkv, joined_sums, vectors, d_up_bias

    forward_pairs = [(i, i + 1) for i in range(sections - 1)]
    entering = fresh
    for _ in range(sections - 1):
        result, _ = forward(entering)
        received = lax.ppermute(result, "section", forward_pairs)
        entering = jnp.where(section_id == 0, fresh, received)
    layer_out, saved = forward(entering)

    back_pairs = [(i + 1, i) for i in range(sections - 1)]
    grad_low = top_grad
    for _ in range(sections - 1):
        result = backward(grad_low, saved, False)
        received = lax.ppermute(result, "section", back_pairs)
        grad_low = jnp.where(section_id == sections - 1, top_grad, received)
    input_grad, share, d_qkv, joined_sums, vectors, d_up_bias = backward(grad_low, saved, True)

    pieces = 4 * fsdp_count
    qkv_piece = sum_low(exchange(d_qkv.reshape(pieces, -1, 3 * WIDTH), ("fsdp", "x")))
    qkv_all = spread(qkv_piece, CTX).reshape(4, GROUPS, -1, 3, WIDTH).transpose(0, 2, 3, 1, 4)
    g_qkv = qkv_all.reshape(1, shard, -1).astype(jnp.float32)

    joint_piece = sum_low(exchange(share.reshape(8, -1, model_width), ("x", "yh")))
    joint_all = spread(joint_piece, ("x", "yh")).reshape(-1, model_width)
    both = jnp.stack(in_order(joint_all, swap(joint_all))).astype(jnp.float32)
    down_rows = mlp_out.shape[1] // 2
    g_down = both[:, :down_rows].reshape(1, -1, model_width)
    g_up = both[:, down_rows : 2 * down_rows].reshape(2, -1, shard // 2, model_width)
    g_up = g_up.transpose(0, 2, 1, 3).reshape(1, shard, -1)
    g_out = both[:, 2 * down_rows : 2 * down_rows + shard // 2].reshape(1, shard, model_width)

    ours = jnp.arange(fsdp_count)[:, None] == group_id
    vector_parts = jnp.concatenate(
        [
            vectors.reshape(6, -1, shard).transpose(1, 0, 2).reshape(-1, 6 * shard),
            jnp.where(ours, joined_sums[None, :WIDTH], 0.0),
            jnp.where(ours, joined_sums[None, 2 * WIDTH :], 0.0),
            d_up_bias.reshape(fsdp_count, -1),
        ],
        1,
    )
    vector_sum = jnp.sum(exchange(vector_parts, "fsdp"), 0)
    vector_sum = jnp.sum(spread(vector_sum, CTX), 0)
    own_vectors = vector_sum[: 8 * shard].reshape(8, shard)
    own_up_bias = vector_sum[8 * shard :]
    order = (2, 6, 7, 3, 4, 5)
    g_biases = jnp.stack([own_vectors[place] for place in order])
    out_shape = (1, micro_count, 1, local_rows, model_width)
    return (
        layer_out.reshape(out_shape),
        input_grad.reshape(out_shape),
        g_qkv,
        g_out,
        g_up,
        g_down,
        own_vectors[None, :2],
        g_biases[None],
        own_up_bias[None],
    )


def solution(mesh):
    fine = Mesh(
        mesh.devices.reshape(2, 4, 2, 2, 4), ("section", "x", "yh", "core", "fsdp")
    )
    rows = P(None, "fsdp", CTX, None)
    weight = P("section", "fsdp", None)
    vector = P("section", None, "fsdp")
    row = P("section", "fsdp")
    out_rows = P("section", None, "fsdp", CTX, None)
    return jax.shard_map(
        shards,
        mesh=fine,
        in_specs=(rows, rows, P(), P(), weight, weight, weight, weight, vector, vector, row),
        out_specs=(out_rows, out_rows, weight, weight, weight, weight, vector, vector, row),
        check_vma=False,
    )
```

```python
import jax
import jax.numpy as jnp
from jax import lax
from jax.experimental import pallas as pl
from jax.experimental.pallas import tpu as pltpu
from jax.sharding import Mesh
from jax.sharding import PartitionSpec as P

HEADS = 12
HDIM = 64
GROUPS = 4
GROUP_HEADS = HEADS // GROUPS
WIDTH = GROUP_HEADS * HDIM
QUERY_BLOCK = 256
EXTRA = 32
JOINT_ROWS = 112
CTX = ("x", "yh", "core")

epsilon = 1e-05
neg_fill = -1e30


def dot(left_side, right_side, left_dim, right_dim):
    return lax.dot_general(
        left_side,
        right_side,
        (((left_dim,), (right_dim,)), ((), ())),
        preferred_element_type=jnp.float32,
    )


def head_columns(part, head):
    start = part * WIDTH + head * HDIM
    return slice(start, start + HDIM)


def attend_body(
    row_places, column_places, own, other, weight, bias, joined, mixed, log_total
):
    step = pl.program_id(0)
    half = own.shape[1]

    @pl.when(step == 0)
    def _():
        product = dot(own[...], weight[:half, :], 1, 0) + dot(other[...], weight[half:, :], 1, 0)
        joined[...] = (product + bias[...]).astype(jnp.bfloat16)

    rows = pl.ds(pl.multiple_of(step * QUERY_BLOCK, QUERY_BLOCK), QUERY_BLOCK)
    hidden = jnp.where(column_places[...] <= row_places[...], 0.0, neg_fill)
    parts = []
    for head in range(GROUP_HEADS):
        queries = joined[rows, head_columns(0, head)] * jnp.bfloat16(HDIM ** (-0.5))
        keys = joined[:, head_columns(1, head)]
        values = joined[:, head_columns(2, head)]
        scores = dot(keys, queries, 1, 1) + hidden
        top = jnp.max(scores, 0, keepdims=True)
        powers = jnp.exp(scores - top)
        total = jnp.sum(powers, 0, keepdims=True)
        parts.append(dot(values, powers.astype(jnp.bfloat16), 0, 0) / total)
        log_total[head : head + 1, :] = top + jnp.log(total)
    mixed[...] = jnp.concatenate(parts, 0).T.astype(jnp.bfloat16)


def whole(*shape):
    return pl.BlockSpec(shape, lambda i: (0,) * len(shape))


def attend(own, other, weight, bias, row_places, column_places):
    count, half = own.shape
    return pl.pallas_call(
        attend_body,
        grid=(count // QUERY_BLOCK,),
        in_specs=[
            pl.BlockSpec((1, QUERY_BLOCK), lambda i: (0, i)),
            whole(count, 1),
            whole(count, half),
            whole(count, half),
            whole(2 * half, 3 * WIDTH),
            whole(1, 3 * WIDTH),
        ],
        out_specs=[
            whole(count, 3 * WIDTH),
            pl.BlockSpec((QUERY_BLOCK, WIDTH), lambda i: (i, 0)),
            pl.BlockSpec((8, QUERY_BLOCK), lambda i: (0, i)),
        ],
        out_shape=[
            jax.ShapeDtypeStruct((count, 3 * WIDTH), jnp.bfloat16),
            jax.ShapeDtypeStruct((count, WIDTH), jnp.bfloat16),
            jax.ShapeDtypeStruct((8, count), jnp.float32),
        ],
        compiler_params=pltpu.CompilerParams(vmem_limit_bytes=48 << 20),
        cost_estimate=pl.CostEstimate(
            flops=4 * count * count * WIDTH,
            bytes_accessed=8 * count * WIDTH,
            transcendentals=count * count * GROUP_HEADS,
        ),
    )(row_places, column_places, own, other, weight, bias)


def attend_back_body(
    row_places,
    column_places,
    joined,
    grad_mixed,
    log_total,
    weight,
    grad_joined,
    grad_own,
    grad_other,
    key_sums,
    value_sums,
):
    step = pl.program_id(0)
    rows = pl.ds(pl.multiple_of(step * QUERY_BLOCK, QUERY_BLOCK), QUERY_BLOCK)

    @pl.when(step == 0)
    def _():
        key_sums[...] = jnp.zeros_like(key_sums)
        value_sums[...] = jnp.zeros_like(value_sums)

    hidden = jnp.where(column_places[...] <= row_places[...], 0.0, neg_fill)
    parts = []
    for head in range(GROUP_HEADS):
        queries = joined[rows, head_columns(0, head)] * jnp.bfloat16(HDIM ** (-0.5))
        keys = joined[:, head_columns(1, head)]
        values = joined[:, head_columns(2, head)]
        grads = grad_mixed[:, head_columns(0, head)]
        weights = jnp.exp(dot(keys, queries, 1, 1) + hidden - log_total[head : head + 1, :])
        grad_weights = dot(values, grads, 1, 1)
        inner_sum = jnp.sum(weights * grad_weights, 0, keepdims=True)
        grad_scores = (weights * (grad_weights - inner_sum)).astype(jnp.bfloat16)
        value_sums[head] += dot(weights.astype(jnp.bfloat16), grads, 1, 0)
        key_sums[head] += dot(grad_scores, queries, 1, 0)
        parts.append(dot(keys, grad_scores, 0, 0) * (HDIM ** (-0.5)))
    grad_joined[rows, :WIDTH] = jnp.concatenate(parts, 0).T.astype(jnp.bfloat16)

    @pl.when(step == pl.num_programs(0) - 1)
    def _():
        for head in range(GROUP_HEADS):
            grad_joined[:, head_columns(1, head)] = key_sums[head].astype(jnp.bfloat16)
            grad_joined[:, head_columns(2, head)] = value_sums[head].astype(jnp.bfloat16)
        half = grad_own.shape[1]
        grad_own[...] = dot(grad_joined[...], weight[:half, :], 1, 1).astype(jnp.bfloat16)
        grad_other[...] = dot(grad_joined[...], weight[half:, :], 1, 1).astype(jnp.bfloat16)


def attend_back(joined, grad_mixed, log_total, weight, row_places, column_places):
    count = joined.shape[0]
    half = weight.shape[0] // 2
    return pl.pallas_call(
        attend_back_body,
        grid=(count // QUERY_BLOCK,),
        in_specs=[
            pl.BlockSpec((1, QUERY_BLOCK), lambda i: (0, i)),
            whole(count, 1),
            whole(count, 3 * WIDTH),
            pl.BlockSpec((QUERY_BLOCK, WIDTH), lambda i: (i, 0)),
            pl.BlockSpec((8, QUERY_BLOCK), lambda i: (0, i)),
            whole(2 * half, 3 * WIDTH),
        ],
        out_specs=[whole(count, 3 * WIDTH), whole(count, half), whole(count, half)],
        out_shape=[
            jax.ShapeDtypeStruct((count, 3 * WIDTH), jnp.bfloat16),
            jax.ShapeDtypeStruct((count, half), jnp.bfloat16),
            jax.ShapeDtypeStruct((count, half), jnp.bfloat16),
        ],
        scratch_shapes=[
            pltpu.VMEM((GROUP_HEADS, count, HDIM), jnp.float32),
            pltpu.VMEM((GROUP_HEADS, count, HDIM), jnp.float32),
        ],
        compiler_params=pltpu.CompilerParams(vmem_limit_bytes=48 << 20),
        cost_estimate=pl.CostEstimate(
            flops=10 * count * count * WIDTH,
            bytes_accessed=16 * count * WIDTH,
            transcendentals=count * count * GROUP_HEADS,
        ),
    )(row_places, column_places, joined, grad_mixed, log_total, weight)


def weight_grads_body(
    active, grad_low, normed_two, grad_hidden, mixed, grad_attn, joint
):
    down_rows, up_rows = active.shape[1], normed_two.shape[0]
    width = grad_low.shape[1]
    joint[0, :down_rows, :] = dot(active[...], grad_low[...], 0, 0).astype(jnp.bfloat16)
    place = down_rows
    for panel in range(grad_hidden.shape[1] // width):
        product = dot(normed_two[...], grad_hidden[:, panel * width : (panel + 1) * width], 1, 0)
        joint[0, place : place + up_rows, :] = product.astype(jnp.bfloat16)
        place += up_rows
    joint[0, place : place + up_rows, :] = dot(mixed[...], grad_attn[...], 1, 0).astype(
        jnp.bfloat16
    )
    place += up_rows
    joint[0, place:, :] = jnp.zeros_like(joint[0, place:, :])


def weight_grads(active, grad_low, normed_two, grad_hidden, mixed, grad_attn, members):
    rows, hidden_width = active.shape
    width = grad_low.shape[1]
    down_rows, up_rows = hidden_width // members, width // members
    out_rows = 2 * down_rows + up_rows + EXTRA
    return pl.pallas_call(
        weight_grads_body,
        grid=(members,),
        in_specs=[
            pl.BlockSpec((rows, down_rows), lambda i: (0, i)),
            whole(rows, width),
            pl.BlockSpec((up_rows, rows), lambda i: (i, 0)),
            whole(rows, hidden_width),
            pl.BlockSpec((up_rows, rows), lambda i: (i, 0)),
            whole(rows, width),
        ],
        out_specs=pl.BlockSpec((1, out_rows, width), lambda i: (i, 0, 0)),
        out_shape=jax.ShapeDtypeStruct((members, out_rows, width), jnp.bfloat16),
        compiler_params=pltpu.CompilerParams(vmem_limit_bytes=48 << 20),
        cost_estimate=pl.CostEstimate(
            flops=2 * rows * width * (2 * hidden_width + width),
            bytes_accessed=2 * members * out_rows * width,
            transcendentals=0,
        ),
    )(active, grad_low, normed_two, grad_hidden, mixed, grad_attn)


def qkv_grads_body(core_id, own, other, grad_joined, pieces, sums):
    first_core = core_id[0] == 0
    grads = grad_joined[...]
    count, piece_rows = pieces.shape[0], pieces.shape[1] - 16
    per_half = count // 2
    own_grads = dot(own[...], grads, 0, 0).astype(jnp.bfloat16)
    other_grads = dot(other[...], grads, 0, 0).astype(jnp.bfloat16)
    halves = (
        jnp.where(first_core, own_grads, other_grads),
        jnp.where(first_core, other_grads, own_grads),
    )
    for index in range(count):
        start = (index % per_half) * piece_rows
        pieces[index, :piece_rows, :] = halves[index // per_half][start : start + piece_rows, :]
        pieces[index, piece_rows:, :] = jnp.zeros_like(pieces[index, piece_rows:, :])
    sums[...] = jnp.sum(grads.astype(jnp.float32), 0, keepdims=True)


def qkv_grads(core_id, own, other, grad_joined, count):
    rows, half = own.shape
    width = grad_joined.shape[1]
    piece_rows = 2 * half // count
    return pl.pallas_call(
        qkv_grads_body,
        in_specs=[pl.BlockSpec(memory_space=pltpu.SMEM)]
        + [pl.BlockSpec(memory_space=pltpu.VMEM)] * 3,
        out_specs=[pl.BlockSpec(memory_space=pltpu.VMEM)] * 2,
        out_shape=[
            jax.ShapeDtypeStruct((count, piece_rows + 16, width), jnp.bfloat16),
            jax.ShapeDtypeStruct((1, width), jnp.float32),
        ],
        compiler_params=pltpu.CompilerParams(vmem_limit_bytes=48 << 20),
        cost_estimate=pl.CostEstimate(
            flops=4 * rows * half * width, bytes_accessed=6 * rows * half, transcendentals=0
        ),
    )(core_id, own, other, grad_joined)


def unpack_body(core_id, own, other, g_qkv, g_out, g_up, g_down, vectors):
    first_core = core_id[0] == 0
    count = own.shape[0]
    width = own.shape[2]
    joint_rows = JOINT_ROWS
    piece_rows = own.shape[1] - joint_rows - 16
    up_rows = g_up.shape[0] // 2
    down_rows = g_down.shape[0] // 2
    sums = [None] * 4
    for core in range(2):
        pick = first_core if core == 0 else jnp.logical_not(first_core)
        joint = jnp.concatenate(
            [
                jnp.where(pick, own[i, :joint_rows, :], other[i, :joint_rows, :])
                for i in range(count)
            ],
            0,
        ).astype(jnp.float32)
        g_down[core * down_rows : (core + 1) * down_rows, :] = joint[:down_rows]
        place = down_rows
        for panel in range(g_up.shape[1] // width):
            g_up[core * up_rows : (core + 1) * up_rows, panel * width : (panel + 1) * width] = (
                joint[place : place + up_rows]
            )
            place += up_rows
        g_out[core * up_rows : (core + 1) * up_rows, :] = joint[place : place + up_rows]
        for i in range(count):
            x_id, group = i // 2, (i % 2) * 2 + core
            piece = jnp.where(pick, own[i, joint_rows:, :], other[i, joint_rows:, :])
            piece = piece.astype(jnp.float32)
            for part in range(3):
                start = part * width + group * WIDTH
                g_qkv[x_id * piece_rows : (x_id + 1) * piece_rows, start : start + WIDTH] = piece[
                    :piece_rows, part * WIDTH : (part + 1) * WIDTH
                ]
            row = piece[piece_rows : piece_rows + 1, :]
            sums[x_id] = row if sums[x_id] is None else sums[x_id] + row
    for x_id in range(4):
        vectors[x_id : x_id + 1, :] = sums[x_id]


def unpack(core_id, own, other, shard, hidden_width, hidden_shard):
    width = own.shape[2]
    return pl.pallas_call(
        unpack_body,
        in_specs=[pl.BlockSpec(memory_space=pltpu.SMEM)]
        + [pl.BlockSpec(memory_space=pltpu.VMEM)] * 2,
        out_specs=[pl.BlockSpec(memory_space=pltpu.VMEM)] * 5,
        out_shape=[
            jax.ShapeDtypeStruct((shard, 3 * width), jnp.float32),
            jax.ShapeDtypeStruct((shard, width), jnp.float32),
            jax.ShapeDtypeStruct((shard, hidden_width), jnp.float32),
            jax.ShapeDtypeStruct((hidden_shard, width), jnp.float32),
            jax.ShapeDtypeStruct((4, width), jnp.float32),
        ],
        compiler_params=pltpu.CompilerParams(vmem_limit_bytes=48 << 20),
        cost_estimate=pl.CostEstimate(flops=0, bytes_accessed=12 << 20, transcendentals=0),
    )(core_id, own, other)


def cross(left_side, right_side, pattern):
    return jnp.einsum(pattern, left_side, right_side, preferred_element_type=jnp.float32)


def normalize(values, gain_row, shift_row):
    center = values - jnp.mean(values, -1, keepdims=True)
    spread = lax.rsqrt(jnp.mean(center * center, -1, keepdims=True) + epsilon)
    unit_rows = center * spread
    return (unit_rows * gain_row + shift_row, unit_rows, spread)


def normalize_back(grad_out, unit_rows, spread, gain_row):
    grad_unit = grad_out * gain_row
    grad_in = spread * (
        grad_unit
        - jnp.mean(grad_unit, -1, keepdims=True)
        - unit_rows * jnp.mean(grad_unit * unit_rows, -1, keepdims=True)
    )
    return (grad_in, jnp.sum(grad_out * unit_rows, 0), jnp.sum(grad_out, 0))


def positions(block_table, block_len):
    offsets = jnp.arange(block_len, dtype=jnp.int32)
    return (block_table[:, None] * block_len + offsets[None, :]).reshape(-1)


def exchange(value, axes):
    return lax.all_to_all(value, axes, 0, 0, tiled=True)


def swap(value):
    return lax.ppermute(value, "core", [(0, 1), (1, 0)])


def in_order(own, other):
    first = lax.axis_index("core") == 0
    return jnp.where(first, own, other), jnp.where(first, other, own)


def gather_weight(weight):
    half = weight.shape[1] // 2
    own = lax.dynamic_slice_in_dim(weight[0], lax.axis_index("core") * half, half, 0)
    return lax.all_gather(own, ("fsdp", "core"), axis=0, tiled=True)


def sum_low(value):
    return jnp.sum(value.astype(jnp.float32), 0).astype(jnp.bfloat16)


def spread(value, axes):
    count = lax.axis_size(axes)
    return exchange(jnp.broadcast_to(value[None], (count,) + value.shape), axes)


def shards(
    inputs,
    cotangent,
    plan,
    block_table,
    attn_in,
    attn_out,
    mlp_in,
    mlp_out,
    norm_gains,
    biases,
    mlp_bias,
):
    shard = norm_gains.shape[2]
    core_id = lax.axis_index("core")
    group_id = lax.axis_index("yh") * 2 + core_id
    fsdp_id = lax.axis_index("fsdp")
    section_id = lax.axis_index("section")
    sections = lax.axis_size("section")
    fsdp_count = lax.axis_size("fsdp")

    small = jnp.concatenate([norm_gains[0], biases[0], mlp_bias.reshape(-1, shard)], 0)
    small = small.reshape(-1, 3 * WIDTH)
    own_columns = lax.dynamic_index_in_dim(
        attn_in[0].reshape(shard, 3, GROUPS, WIDTH), group_id, 2, keepdims=False
    ).reshape(shard, 3 * WIDTH)
    first_all = spread(
        jnp.concatenate(
            [own_columns, small, jnp.zeros((16 - small.shape[0], 3 * WIDTH), jnp.bfloat16)], 0
        ),
        "fsdp",
    )
    w_group = first_all[:, :shard].reshape(-1, 3 * WIDTH)
    small_all = first_all[:, shard : shard + small.shape[0]].reshape(fsdp_count, -1, shard)
    small_all = small_all.astype(jnp.float32)
    w_out = gather_weight(attn_out)
    w_up = gather_weight(mlp_in)
    w_down = gather_weight(mlp_out)
    model_width = w_out.shape[0]
    half = model_width // 2
    w_group = jnp.concatenate(in_order(w_group[:half], w_group[half:]), 0)
    w_out_groups = w_out.reshape(GROUPS, WIDTH, model_width)
    vector_rows = small_all[:, :8].transpose(1, 0, 2).reshape(8, model_width)
    gain_rows, bias_rows = vector_rows[:2], vector_rows[2:]
    up_bias = small_all[:, 8:].reshape(-1)
    own_bias = lax.dynamic_index_in_dim(small_all, group_id, 0, keepdims=False)
    group_bias = jnp.concatenate([own_bias[3], jnp.zeros_like(own_bias[3]), own_bias[4]])[None]

    micro_count, _, local_rows, _ = inputs.shape
    rows = micro_count * local_rows
    places = positions(block_table, local_rows // 2)
    row_places, column_places = places[None, :], places[:, None]
    fresh = jnp.stack(
        [lax.dynamic_index_in_dim(inputs, plan[step], 0, keepdims=False) for step in range(micro_count)]
    ).reshape(rows, model_width)
    top_grad = cotangent.reshape(rows, model_width)
    core_number = core_id.astype(jnp.int32)[None]
    head_shape = (micro_count, GROUPS, local_rows, WIDTH)

    def forward(entering):
        stream = entering.astype(jnp.float32)
        normed, unit_one, spread_one = normalize(stream, gain_rows[0], bias_rows[0])
        halves = normed.astype(jnp.bfloat16).reshape(micro_count, 1, local_rows, 2, half)
        halves = jnp.broadcast_to(
            halves.transpose(0, 1, 3, 2, 4), (micro_count, 2, 2, local_rows, half)
        )
        own = exchange(halves.reshape(-1, local_rows, half), CTX).reshape(-1, half)
        other = swap(own)
        joined, mixed_heads, log_total = attend(
            own, other, w_group, group_bias, row_places, column_places
        )
        mixed = exchange(mixed_heads.reshape(-1, local_rows, WIDTH), CTX).reshape(head_shape)
        attended = cross(mixed, w_out_groups, "mgtd,gde->mte").reshape(rows, model_width)
        middle = stream + (attended + bias_rows[3])
        normed_two, unit_two, spread_two = normalize(middle, gain_rows[1], bias_rows[4])
        normed_two_low = normed_two.astype(jnp.bfloat16)
        hidden_pre = cross(normed_two_low, w_up, "td,df->tf") + up_bias
        active_low = jax.nn.gelu(hidden_pre).astype(jnp.bfloat16)
        result = (middle + (cross(active_low, w_down, "tf,fd->td") + bias_rows[5])).astype(
            jnp.bfloat16
        )
        saved = (
            unit_one,
            spread_one,
            own,
            other,
            joined,
            log_total,
            mixed,
            unit_two,
            spread_two,
            normed_two_low,
            hidden_pre,
            active_low,
        )
        return result, saved

    def backward(grad_low, saved, last):
        (
            unit_one,
            spread_one,
            own,
            other,
            joined,
            log_total,
            mixed,
            unit_two,
            spread_two,
            normed_two_low,
            hidden_pre,
            active_low,
        ) = saved
        grad_top = grad_low.astype(jnp.float32)
        grad_active = cross(grad_low, w_down, "td,fd->tf")
        _, gelu_pull = jax.vjp(jax.nn.gelu, hidden_pre)
        grad_hidden = gelu_pull(grad_active)[0].astype(jnp.bfloat16)
        grad_normed_two = cross(grad_hidden, w_up, "tf,df->td")
        grad_norm_two, d_gain_two, d_shift_two = normalize_back(
            grad_normed_two, unit_two, spread_two, gain_rows[1]
        )
        grad_middle = grad_top + grad_norm_two
        grad_attn = grad_middle.astype(jnp.bfloat16)
        attn_parts = grad_attn.reshape(micro_count, local_rows, model_width)
        grad_mixed = cross(attn_parts, w_out_groups, "mte,gde->mgtd").astype(jnp.bfloat16)
        share = None
        grad_heads = exchange(grad_mixed.reshape(-1, local_rows, WIDTH), CTX).reshape(-1, WIDTH)
        if last:
            joint = weight_grads(
                active_low,
                grad_low,
                normed_two_low.T,
                grad_hidden,
                mixed.transpose(1, 3, 0, 2).reshape(model_width, rows),
                grad_attn,
                2 * fsdp_count,
            )
            grad_heads, joint = lax.optimization_barrier((grad_heads, joint))
            share = lax.psum_scatter(
                joint.reshape(-1, model_width),
                ("fsdp", "core"),
                scatter_dimension=0,
                tiled=True,
            )
        grad_joined, grad_own, grad_other = attend_back(
            joined, grad_heads, log_total, w_group, row_places, column_places
        )
        received = swap(grad_other)
        summed = (grad_own.astype(jnp.float32) + received.astype(jnp.float32)).astype(jnp.bfloat16)
        returned = exchange(summed.reshape(-1, local_rows, half), CTX)
        returned = returned.reshape(micro_count, 2, 2, local_rows, half).astype(jnp.float32)
        grad_normed = (returned[:, 0] + returned[:, 1]).transpose(0, 2, 1, 3)
        grad_normed = grad_normed.reshape(rows, model_width)
        grad_norm_one, d_gain_one, d_shift_one = normalize_back(
            grad_normed, unit_one, spread_one, gain_rows[0]
        )
        grad_in = (grad_middle + grad_norm_one).astype(jnp.bfloat16)
        if not last:
            return grad_in
        pieces, joined_sums = qkv_grads(core_number, own, other, grad_joined, 4 * fsdp_count)
        joined_sums = joined_sums[0]
        vectors = jnp.stack(
            [
                d_gain_one,
                d_gain_two,
                d_shift_one,
                jnp.sum(grad_attn.astype(jnp.float32), 0),
                d_shift_two,
                jnp.sum(grad_top, 0),
            ]
        )
        d_up_bias = jnp.sum(grad_hidden.astype(jnp.float32), 0)
        return grad_in, share, pieces, joined_sums, vectors, d_up_bias

    forward_pairs = [(i, i + 1) for i in range(sections - 1)]
    entering = fresh
    for _ in range(sections - 1):
        result, _ = forward(entering)
        received = lax.ppermute(result, "section", forward_pairs)
        entering = jnp.where(section_id == 0, fresh, received)
    layer_out, saved = forward(entering)

    back_pairs = [(i + 1, i) for i in range(sections - 1)]
    grad_low = top_grad
    for _ in range(sections - 1):
        result = backward(grad_low, saved, False)
        received = lax.ppermute(result, "section", back_pairs)
        grad_low = jnp.where(section_id == sections - 1, top_grad, received)
    input_grad, share, pieces, joined_sums, vectors, d_up_bias = backward(grad_low, saved, True)

    ours = jnp.arange(fsdp_count)[:, None] == group_id
    vector_parts = jnp.concatenate(
        [
            vectors.reshape(6, -1, shard).transpose(1, 0, 2).reshape(-1, 6 * shard),
            jnp.where(ours, joined_sums[None, :WIDTH], 0.0),
            jnp.where(ours, joined_sums[None, 2 * WIDTH :], 0.0),
            d_up_bias.reshape(fsdp_count, -1),
        ],
        1,
    )
    vector_parts = vector_parts.astype(jnp.bfloat16).reshape(4 * fsdp_count, 3 * WIDTH)
    pieces = pieces.at[:, pieces.shape[1] - 16, :].set(vector_parts)
    qkv_piece = sum_low(exchange(pieces, ("fsdp", "x")))
    qkv_piece = jnp.pad(qkv_piece, ((0, 0), (0, model_width - 3 * WIDTH)))
    joint_piece = sum_low(exchange(share.reshape(8, -1, model_width), ("x", "yh")))
    both = spread(jnp.concatenate([joint_piece, qkv_piece], 0), ("x", "yh"))
    g_qkv, g_out, g_up, g_down, vector_sum = unpack(
        core_number, both, swap(both), shard, mlp_in.shape[2], mlp_out.shape[1]
    )
    vector_sum = vector_sum[:, : 3 * WIDTH].reshape(-1)
    own_vectors = vector_sum[: 8 * shard].reshape(8, shard)
    own_up_bias = vector_sum[8 * shard :]
    order = (2, 6, 7, 3, 4, 5)
    g_biases = jnp.stack([own_vectors[place] for place in order])
    out_shape = (1, micro_count, 1, local_rows, model_width)
    return (
        layer_out.reshape(out_shape),
        input_grad.reshape(out_shape),
        g_qkv[None],
        g_out[None],
        g_up[None],
        g_down[None],
        own_vectors[None, :2],
        g_biases[None],
        own_up_bias[None],
    )


def solution(mesh):
    fine = Mesh(
        mesh.devices.reshape(2, 4, 2, 2, 4), ("section", "x", "yh", "core", "fsdp")
    )
    rows = P(None, "fsdp", CTX, None)
    weight = P("section", "fsdp", None)
    vector = P("section", None, "fsdp")
    row = P("section", "fsdp")
    out_rows = P("section", None, "fsdp", CTX, None)
    return jax.shard_map(
        shards,
        mesh=fine,
        in_specs=(rows, rows, P(), P(), weight, weight, weight, weight, vector, vector, row),
        out_specs=(out_rows, out_rows, weight, weight, weight, weight, vector, vector, row),
        check_vma=False,
    )
```

```python
import jax
import jax.numpy as jnp
from jax import lax
from jax.experimental import pallas as pl
from jax.experimental.pallas import tpu as pltpu
from jax.sharding import Mesh
from jax.sharding import PartitionSpec as P

HEADS = 12
HDIM = 64
GROUPS = 4
GROUP_HEADS = HEADS // GROUPS
WIDTH = GROUP_HEADS * HDIM
QUERY_BLOCK = 256
EXTRA = 32
JOINT_ROWS = 112
CTX = ("x", "yh", "core")

epsilon = 1e-05
neg_fill = -1e30


def dot(left_side, right_side, left_dim, right_dim):
    return lax.dot_general(
        left_side,
        right_side,
        (((left_dim,), (right_dim,)), ((), ())),
        preferred_element_type=jnp.float32,
    )


def head_columns(part, head):
    start = part * WIDTH + head * HDIM
    return slice(start, start + HDIM)


def attend_body(
    row_places, column_places, own, other, weight, bias, joined, mixed, log_total
):
    step = pl.program_id(0)
    half = own.shape[1]

    @pl.when(step == 0)
    def _():
        product = dot(own[...], weight[:half, :], 1, 0) + dot(other[...], weight[half:, :], 1, 0)
        joined[...] = (product + bias[...]).astype(jnp.bfloat16)

    rows = pl.ds(pl.multiple_of(step * QUERY_BLOCK, QUERY_BLOCK), QUERY_BLOCK)
    hidden = jnp.where(column_places[...] <= row_places[...], 0.0, neg_fill)
    parts = []
    for head in range(GROUP_HEADS):
        queries = joined[rows, head_columns(0, head)] * jnp.bfloat16(HDIM ** (-0.5))
        keys = joined[:, head_columns(1, head)]
        values = joined[:, head_columns(2, head)]
        scores = dot(keys, queries, 1, 1) + hidden
        top = jnp.max(scores, 0, keepdims=True)
        powers = jnp.exp(scores - top)
        total = jnp.sum(powers, 0, keepdims=True)
        parts.append(dot(values, powers.astype(jnp.bfloat16), 0, 0) / total)
        log_total[head : head + 1, :] = top + jnp.log(total)
    mixed[...] = jnp.concatenate(parts, 0).T.astype(jnp.bfloat16)


def whole(*shape):
    return pl.BlockSpec(shape, lambda i: (0,) * len(shape))


def attend(own, other, weight, bias, row_places, column_places):
    count, half = own.shape
    return pl.pallas_call(
        attend_body,
        grid=(count // QUERY_BLOCK,),
        in_specs=[
            pl.BlockSpec((1, QUERY_BLOCK), lambda i: (0, i)),
            whole(count, 1),
            whole(count, half),
            whole(count, half),
            whole(2 * half, 3 * WIDTH),
            whole(1, 3 * WIDTH),
        ],
        out_specs=[
            whole(count, 3 * WIDTH),
            pl.BlockSpec((QUERY_BLOCK, WIDTH), lambda i: (i, 0)),
            pl.BlockSpec((8, QUERY_BLOCK), lambda i: (0, i)),
        ],
        out_shape=[
            jax.ShapeDtypeStruct((count, 3 * WIDTH), jnp.bfloat16),
            jax.ShapeDtypeStruct((count, WIDTH), jnp.bfloat16),
            jax.ShapeDtypeStruct((8, count), jnp.float32),
        ],
        compiler_params=pltpu.CompilerParams(vmem_limit_bytes=48 << 20),
        cost_estimate=pl.CostEstimate(
            flops=4 * count * count * WIDTH,
            bytes_accessed=8 * count * WIDTH,
            transcendentals=count * count * GROUP_HEADS,
        ),
    )(row_places, column_places, own, other, weight, bias)


def attend_back_body(
    row_places,
    column_places,
    joined,
    grad_mixed,
    log_total,
    weight,
    grad_joined,
    grad_own,
    grad_other,
    key_sums,
    value_sums,
):
    step = pl.program_id(0)
    rows = pl.ds(pl.multiple_of(step * QUERY_BLOCK, QUERY_BLOCK), QUERY_BLOCK)

    @pl.when(step == 0)
    def _():
        key_sums[...] = jnp.zeros_like(key_sums)
        value_sums[...] = jnp.zeros_like(value_sums)

    hidden = jnp.where(column_places[...] <= row_places[...], 0.0, neg_fill)
    parts = []
    for head in range(GROUP_HEADS):
        queries = joined[rows, head_columns(0, head)] * jnp.bfloat16(HDIM ** (-0.5))
        keys = joined[:, head_columns(1, head)]
        values = joined[:, head_columns(2, head)]
        grads = grad_mixed[:, head_columns(0, head)]
        weights = jnp.exp(dot(keys, queries, 1, 1) + hidden - log_total[head : head + 1, :])
        grad_weights = dot(values, grads, 1, 1)
        inner_sum = jnp.sum(weights * grad_weights, 0, keepdims=True)
        grad_scores = (weights * (grad_weights - inner_sum)).astype(jnp.bfloat16)
        value_sums[head] += dot(weights.astype(jnp.bfloat16), grads, 1, 0)
        key_sums[head] += dot(grad_scores, queries, 1, 0)
        parts.append(dot(keys, grad_scores, 0, 0) * (HDIM ** (-0.5)))
    grad_joined[rows, :WIDTH] = jnp.concatenate(parts, 0).T.astype(jnp.bfloat16)

    @pl.when(step == pl.num_programs(0) - 1)
    def _():
        for head in range(GROUP_HEADS):
            grad_joined[:, head_columns(1, head)] = key_sums[head].astype(jnp.bfloat16)
            grad_joined[:, head_columns(2, head)] = value_sums[head].astype(jnp.bfloat16)
        half = grad_own.shape[1]
        grad_own[...] = dot(grad_joined[...], weight[:half, :], 1, 1).astype(jnp.bfloat16)
        grad_other[...] = dot(grad_joined[...], weight[half:, :], 1, 1).astype(jnp.bfloat16)


def attend_back(joined, grad_mixed, log_total, weight, row_places, column_places):
    count = joined.shape[0]
    half = weight.shape[0] // 2
    return pl.pallas_call(
        attend_back_body,
        grid=(count // QUERY_BLOCK,),
        in_specs=[
            pl.BlockSpec((1, QUERY_BLOCK), lambda i: (0, i)),
            whole(count, 1),
            whole(count, 3 * WIDTH),
            pl.BlockSpec((QUERY_BLOCK, WIDTH), lambda i: (i, 0)),
            pl.BlockSpec((8, QUERY_BLOCK), lambda i: (0, i)),
            whole(2 * half, 3 * WIDTH),
        ],
        out_specs=[whole(count, 3 * WIDTH), whole(count, half), whole(count, half)],
        out_shape=[
            jax.ShapeDtypeStruct((count, 3 * WIDTH), jnp.bfloat16),
            jax.ShapeDtypeStruct((count, half), jnp.bfloat16),
            jax.ShapeDtypeStruct((count, half), jnp.bfloat16),
        ],
        scratch_shapes=[
            pltpu.VMEM((GROUP_HEADS, count, HDIM), jnp.float32),
            pltpu.VMEM((GROUP_HEADS, count, HDIM), jnp.float32),
        ],
        compiler_params=pltpu.CompilerParams(vmem_limit_bytes=48 << 20),
        cost_estimate=pl.CostEstimate(
            flops=10 * count * count * WIDTH,
            bytes_accessed=16 * count * WIDTH,
            transcendentals=count * count * GROUP_HEADS,
        ),
    )(row_places, column_places, joined, grad_mixed, log_total, weight)


def weight_grads_body(
    active,
    active_other,
    grad_low,
    grad_low_other,
    normed_two,
    normed_two_other,
    grad_hidden,
    grad_hidden_other,
    mixed,
    mixed_other,
    grad_attn,
    grad_attn_other,
    joint,
):
    down_rows, up_rows = active.shape[1], normed_two.shape[0]
    width = grad_low.shape[1]
    product = dot(active[...], grad_low[...], 0, 0)
    product += dot(active_other[...], grad_low_other[...], 0, 0)
    joint[0, :down_rows, :] = product.astype(jnp.bfloat16)
    place = down_rows
    for panel in range(grad_hidden.shape[1] // width):
        columns = slice(panel * width, (panel + 1) * width)
        product = dot(normed_two[...], grad_hidden[:, columns], 1, 0)
        product += dot(normed_two_other[...], grad_hidden_other[:, columns], 1, 0)
        joint[0, place : place + up_rows, :] = product.astype(jnp.bfloat16)
        place += up_rows
    product = dot(mixed[...], grad_attn[...], 1, 0)
    product += dot(mixed_other[...], grad_attn_other[...], 1, 0)
    joint[0, place : place + up_rows, :] = product.astype(jnp.bfloat16)
    place += up_rows
    joint[0, place:, :] = jnp.zeros_like(joint[0, place:, :])


def weight_grads(pairs, members):
    (active, _), (grad_low, _), (normed_two, _), (grad_hidden, _) = pairs[:4]
    rows, hidden_width = grad_hidden.shape
    width = grad_low.shape[1]
    down_rows, up_rows = active.shape[1] // members, normed_two.shape[0] // members
    out_rows = 2 * down_rows + up_rows + EXTRA
    specs = [
        pl.BlockSpec((rows, down_rows), lambda i: (0, i)),
        whole(rows, width),
        pl.BlockSpec((up_rows, rows), lambda i: (i, 0)),
        whole(rows, hidden_width),
        pl.BlockSpec((up_rows, rows), lambda i: (i, 0)),
        whole(rows, width),
    ]
    return pl.pallas_call(
        weight_grads_body,
        grid=(members,),
        in_specs=[spec for spec in specs for _ in range(2)],
        out_specs=pl.BlockSpec((1, out_rows, width), lambda i: (i, 0, 0)),
        out_shape=jax.ShapeDtypeStruct((members, out_rows, width), jnp.bfloat16),
        compiler_params=pltpu.CompilerParams(vmem_limit_bytes=48 << 20),
        cost_estimate=pl.CostEstimate(
            flops=2 * rows * width * (2 * hidden_width + width),
            bytes_accessed=2 * members * out_rows * width,
            transcendentals=0,
        ),
    )(*[value for pair in pairs for value in pair])


def qkv_grads_body(core_id, own, other, grad_joined, pieces, sums):
    first_core = core_id[0] == 0
    grads = grad_joined[...]
    count, piece_rows = pieces.shape[0], pieces.shape[1] - 16
    per_half = count // 2
    own_grads = dot(own[...], grads, 0, 0).astype(jnp.bfloat16)
    other_grads = dot(other[...], grads, 0, 0).astype(jnp.bfloat16)
    halves = (
        jnp.where(first_core, own_grads, other_grads),
        jnp.where(first_core, other_grads, own_grads),
    )
    for index in range(count):
        start = (index % per_half) * piece_rows
        pieces[index, :piece_rows, :] = halves[index // per_half][start : start + piece_rows, :]
        pieces[index, piece_rows:, :] = jnp.zeros_like(pieces[index, piece_rows:, :])
    sums[...] = jnp.sum(grads.astype(jnp.float32), 0, keepdims=True)


def qkv_grads(core_id, own, other, grad_joined, count):
    rows, half = own.shape
    width = grad_joined.shape[1]
    piece_rows = 2 * half // count
    return pl.pallas_call(
        qkv_grads_body,
        in_specs=[pl.BlockSpec(memory_space=pltpu.SMEM)]
        + [pl.BlockSpec(memory_space=pltpu.VMEM)] * 3,
        out_specs=[pl.BlockSpec(memory_space=pltpu.VMEM)] * 2,
        out_shape=[
            jax.ShapeDtypeStruct((count, piece_rows + 16, width), jnp.bfloat16),
            jax.ShapeDtypeStruct((1, width), jnp.float32),
        ],
        compiler_params=pltpu.CompilerParams(vmem_limit_bytes=48 << 20),
        cost_estimate=pl.CostEstimate(
            flops=4 * rows * half * width, bytes_accessed=6 * rows * half, transcendentals=0
        ),
    )(core_id, own, other, grad_joined)


def unpack_body(core_id, own, other, g_qkv, g_out, g_up, g_down, vectors):
    first_core = core_id[0] == 0
    count = own.shape[0]
    width = own.shape[2]
    joint_rows = JOINT_ROWS
    piece_rows = own.shape[1] - joint_rows - 16
    up_rows = g_up.shape[0] // 2
    down_rows = g_down.shape[0] // 2
    sums = [None] * 4
    for core in range(2):
        pick = first_core if core == 0 else jnp.logical_not(first_core)
        joint = jnp.concatenate(
            [
                jnp.where(pick, own[i, :joint_rows, :], other[i, :joint_rows, :])
                for i in range(count)
            ],
            0,
        ).astype(jnp.float32)
        g_down[core * down_rows : (core + 1) * down_rows, :] = joint[:down_rows]
        place = down_rows
        for panel in range(g_up.shape[1] // width):
            g_up[core * up_rows : (core + 1) * up_rows, panel * width : (panel + 1) * width] = (
                joint[place : place + up_rows]
            )
            place += up_rows
        g_out[core * up_rows : (core + 1) * up_rows, :] = joint[place : place + up_rows]
        for i in range(count):
            x_id, group = i // 2, (i % 2) * 2 + core
            piece = jnp.where(pick, own[i, joint_rows:, :], other[i, joint_rows:, :])
            piece = piece.astype(jnp.float32)
            for part in range(3):
                start = part * width + group * WIDTH
                g_qkv[x_id * piece_rows : (x_id + 1) * piece_rows, start : start + WIDTH] = piece[
                    :piece_rows, part * WIDTH : (part + 1) * WIDTH
                ]
            row = piece[piece_rows : piece_rows + 1, :]
            sums[x_id] = row if sums[x_id] is None else sums[x_id] + row
    for x_id in range(4):
        vectors[x_id : x_id + 1, :] = sums[x_id]


def unpack(core_id, own, other, shard, hidden_width, hidden_shard):
    width = own.shape[2]
    return pl.pallas_call(
        unpack_body,
        in_specs=[pl.BlockSpec(memory_space=pltpu.SMEM)]
        + [pl.BlockSpec(memory_space=pltpu.VMEM)] * 2,
        out_specs=[pl.BlockSpec(memory_space=pltpu.VMEM)] * 5,
        out_shape=[
            jax.ShapeDtypeStruct((shard, 3 * width), jnp.float32),
            jax.ShapeDtypeStruct((shard, width), jnp.float32),
            jax.ShapeDtypeStruct((shard, hidden_width), jnp.float32),
            jax.ShapeDtypeStruct((hidden_shard, width), jnp.float32),
            jax.ShapeDtypeStruct((4, width), jnp.float32),
        ],
        compiler_params=pltpu.CompilerParams(vmem_limit_bytes=48 << 20),
        cost_estimate=pl.CostEstimate(flops=0, bytes_accessed=12 << 20, transcendentals=0),
    )(core_id, own, other)


def cross(left_side, right_side, pattern):
    return jnp.einsum(pattern, left_side, right_side, preferred_element_type=jnp.float32)


def normalize(values, gain_row, shift_row):
    center = values - jnp.mean(values, -1, keepdims=True)
    spread = lax.rsqrt(jnp.mean(center * center, -1, keepdims=True) + epsilon)
    unit_rows = center * spread
    return (unit_rows * gain_row + shift_row, unit_rows, spread)


def normalize_back(grad_out, unit_rows, spread, gain_row):
    grad_unit = grad_out * gain_row
    grad_in = spread * (
        grad_unit
        - jnp.mean(grad_unit, -1, keepdims=True)
        - unit_rows * jnp.mean(grad_unit * unit_rows, -1, keepdims=True)
    )
    return (grad_in, jnp.sum(grad_out * unit_rows, 0), jnp.sum(grad_out, 0))


def positions(block_table, block_len):
    offsets = jnp.arange(block_len, dtype=jnp.int32)
    return (block_table[:, None] * block_len + offsets[None, :]).reshape(-1)


def exchange(value, axes):
    return lax.all_to_all(value, axes, 0, 0, tiled=True)


def swap(value):
    return lax.ppermute(value, "core", [(0, 1), (1, 0)])


def in_order(own, other):
    first = lax.axis_index("core") == 0
    return jnp.where(first, own, other), jnp.where(first, other, own)


def gather_weights(attn_out, mlp_in, mlp_out):
    core_id = lax.axis_index("core")
    width = attn_out.shape[2]
    out_half, up_half, down_half = (
        lax.dynamic_slice_in_dim(
            weight[0], core_id * (weight.shape[1] // 2), weight.shape[1] // 2, 0
        )
        for weight in (attn_out, mlp_in, mlp_out)
    )
    panels = [up_half[:, start : start + width] for start in range(0, mlp_in.shape[2], width)]
    packed = jnp.concatenate([down_half] + panels + [out_half], 0)
    everyone = lax.all_gather(packed, ("fsdp", "core"), axis=0)
    down_rows, up_rows = down_half.shape[0], up_half.shape[0]
    w_down = everyone[:, :down_rows].reshape(-1, width)
    w_up = jnp.concatenate(
        [
            everyone[:, start : start + up_rows].reshape(-1, width)
            for start in range(down_rows, 2 * down_rows, up_rows)
        ],
        1,
    )
    w_out = everyone[:, 2 * down_rows :].reshape(-1, width)
    return w_out, w_up, w_down


def split_cores(value, axis):
    core_id = lax.axis_index("core")
    kept = lax.dynamic_index_in_dim(value, core_id, axis, keepdims=False)
    sent = lax.dynamic_index_in_dim(value, 1 - core_id, axis, keepdims=False)
    return kept, swap(sent)


def sum_low(value):
    return jnp.sum(value.astype(jnp.float32), 0).astype(jnp.bfloat16)


def spread(value, axes):
    count = lax.axis_size(axes)
    return exchange(jnp.broadcast_to(value[None], (count,) + value.shape), axes)


def shards(
    inputs,
    cotangent,
    plan,
    block_table,
    attn_in,
    attn_out,
    mlp_in,
    mlp_out,
    norm_gains,
    biases,
    mlp_bias,
):
    shard = norm_gains.shape[2]
    core_id = lax.axis_index("core")
    group_id = lax.axis_index("yh") * 2 + core_id
    fsdp_id = lax.axis_index("fsdp")
    section_id = lax.axis_index("section")
    sections = lax.axis_size("section")
    fsdp_count = lax.axis_size("fsdp")

    small = jnp.concatenate([norm_gains[0], biases[0], mlp_bias.reshape(-1, shard)], 0)
    small = small.reshape(-1, 3 * WIDTH)
    own_columns = lax.dynamic_index_in_dim(
        attn_in[0].reshape(shard, 3, GROUPS, WIDTH), group_id, 2, keepdims=False
    ).reshape(shard, 3 * WIDTH)
    first_all = spread(
        jnp.concatenate(
            [own_columns, small, jnp.zeros((16 - small.shape[0], 3 * WIDTH), jnp.bfloat16)], 0
        ),
        "fsdp",
    )
    w_group = first_all[:, :shard].reshape(-1, 3 * WIDTH)
    small_all = first_all[:, shard : shard + small.shape[0]].reshape(fsdp_count, -1, shard)
    small_all = small_all.astype(jnp.float32)
    w_out, w_up, w_down = gather_weights(attn_out, mlp_in, mlp_out)
    model_width = w_out.shape[0]
    half = model_width // 2
    w_group = jnp.concatenate(in_order(w_group[:half], w_group[half:]), 0)
    w_out_groups = w_out.reshape(GROUPS, WIDTH, model_width)
    vector_rows = small_all[:, :8].transpose(1, 0, 2).reshape(8, model_width)
    gain_rows, bias_rows = vector_rows[:2], vector_rows[2:]
    up_bias = small_all[:, 8:].reshape(-1)
    own_bias = lax.dynamic_index_in_dim(small_all, group_id, 0, keepdims=False)
    group_bias = jnp.concatenate([own_bias[3], jnp.zeros_like(own_bias[3]), own_bias[4]])[None]

    micro_count, _, local_rows, _ = inputs.shape
    rows = micro_count * local_rows
    places = positions(block_table, local_rows // 2)
    row_places, column_places = places[None, :], places[:, None]
    fresh = jnp.stack(
        [lax.dynamic_index_in_dim(inputs, plan[step], 0, keepdims=False) for step in range(micro_count)]
    ).reshape(rows, model_width)
    top_grad = cotangent.reshape(rows, model_width)
    core_number = core_id.astype(jnp.int32)[None]
    head_shape = (micro_count, GROUPS, local_rows, WIDTH)

    def forward(entering):
        stream = entering.astype(jnp.float32)
        normed, unit_one, spread_one = normalize(stream, gain_rows[0], bias_rows[0])
        halves = normed.astype(jnp.bfloat16).reshape(micro_count, 1, local_rows, 2, half)
        halves = jnp.broadcast_to(
            halves.transpose(0, 1, 3, 2, 4), (micro_count, 2, 2, local_rows, half)
        )
        own = exchange(halves.reshape(-1, local_rows, half), CTX).reshape(-1, half)
        other = swap(own)
        joined, mixed_heads, log_total = attend(
            own, other, w_group, group_bias, row_places, column_places
        )
        mixed = exchange(mixed_heads.reshape(-1, local_rows, WIDTH), CTX).reshape(head_shape)
        attended = cross(mixed, w_out_groups, "mgtd,gde->mte").reshape(rows, model_width)
        middle = stream + (attended + bias_rows[3])
        normed_two, unit_two, spread_two = normalize(middle, gain_rows[1], bias_rows[4])
        normed_two_low = normed_two.astype(jnp.bfloat16)
        hidden_pre = cross(normed_two_low, w_up, "td,df->tf") + up_bias
        active_low = jax.nn.gelu(hidden_pre).astype(jnp.bfloat16)
        result = (middle + (cross(active_low, w_down, "tf,fd->td") + bias_rows[5])).astype(
            jnp.bfloat16
        )
        saved = (
            unit_one,
            spread_one,
            own,
            other,
            joined,
            log_total,
            mixed,
            unit_two,
            spread_two,
            normed_two_low,
            hidden_pre,
            active_low,
        )
        return result, saved

    def backward(grad_low, saved, last):
        (
            unit_one,
            spread_one,
            own,
            other,
            joined,
            log_total,
            mixed,
            unit_two,
            spread_two,
            normed_two_low,
            hidden_pre,
            active_low,
        ) = saved
        grad_top = grad_low.astype(jnp.float32)
        grad_active = cross(grad_low, w_down, "td,fd->tf")
        _, gelu_pull = jax.vjp(jax.nn.gelu, hidden_pre)
        grad_hidden = gelu_pull(grad_active)[0].astype(jnp.bfloat16)
        grad_normed_two = cross(grad_hidden, w_up, "tf,df->td")
        grad_norm_two, d_gain_two, d_shift_two = normalize_back(
            grad_normed_two, unit_two, spread_two, gain_rows[1]
        )
        grad_middle = grad_top + grad_norm_two
        grad_attn = grad_middle.astype(jnp.bfloat16)
        attn_parts = grad_attn.reshape(micro_count, local_rows, model_width)
        grad_mixed = cross(attn_parts, w_out_groups, "mte,gde->mgtd").astype(jnp.bfloat16)
        share = None
        grad_heads = exchange(grad_mixed.reshape(-1, local_rows, WIDTH), CTX).reshape(-1, WIDTH)
        if last:
            active_pair = split_cores(active_low.reshape(rows, fsdp_count, 2, -1), 2)
            normed_pair = split_cores(normed_two_low.T.reshape(fsdp_count, 2, -1, rows), 1)
            mixed_pair = split_cores(
                mixed.transpose(1, 3, 0, 2).reshape(fsdp_count, 2, -1, rows), 1
            )
            joint = weight_grads(
                [
                    [value.reshape(rows, -1) for value in active_pair],
                    (grad_low, swap(grad_low)),
                    [value.reshape(-1, rows) for value in normed_pair],
                    (grad_hidden, swap(grad_hidden)),
                    [value.reshape(-1, rows) for value in mixed_pair],
                    (grad_attn, swap(grad_attn)),
                ],
                fsdp_count,
            )
            grad_heads, joint = lax.optimization_barrier((grad_heads, joint))
            share = lax.psum_scatter(
                joint.reshape(-1, model_width),
                "fsdp",
                scatter_dimension=0,
                tiled=True,
            )
        grad_joined, grad_own, grad_other = attend_back(
            joined, grad_heads, log_total, w_group, row_places, column_places
        )
        received = swap(grad_other)
        summed = (grad_own.astype(jnp.float32) + received.astype(jnp.float32)).astype(jnp.bfloat16)
        returned = exchange(summed.reshape(-1, local_rows, half), CTX)
        returned = returned.reshape(micro_count, 2, 2, local_rows, half).astype(jnp.float32)
        grad_normed = (returned[:, 0] + returned[:, 1]).transpose(0, 2, 1, 3)
        grad_normed = grad_normed.reshape(rows, model_width)
        grad_norm_one, d_gain_one, d_shift_one = normalize_back(
            grad_normed, unit_one, spread_one, gain_rows[0]
        )
        grad_in = (grad_middle + grad_norm_one).astype(jnp.bfloat16)
        if not last:
            return grad_in
        pieces, joined_sums = qkv_grads(core_number, own, other, grad_joined, 4 * fsdp_count)
        joined_sums = joined_sums[0]
        vectors = jnp.stack(
            [
                d_gain_one,
                d_gain_two,
                d_shift_one,
                jnp.sum(grad_attn.astype(jnp.float32), 0),
                d_shift_two,
                jnp.sum(grad_top, 0),
            ]
        )
        d_up_bias = jnp.sum(grad_hidden.astype(jnp.float32), 0)
        return grad_in, share, pieces, joined_sums, vectors, d_up_bias

    forward_pairs = [(i, i + 1) for i in range(sections - 1)]
    entering = fresh
    for _ in range(sections - 1):
        result, _ = forward(entering)
        received = lax.ppermute(result, "section", forward_pairs)
        entering = jnp.where(section_id == 0, fresh, received)
    layer_out, saved = forward(entering)

    back_pairs = [(i + 1, i) for i in range(sections - 1)]
    grad_low = top_grad
    for _ in range(sections - 1):
        result = backward(grad_low, saved, False)
        received = lax.ppermute(result, "section", back_pairs)
        grad_low = jnp.where(section_id == sections - 1, top_grad, received)
    input_grad, share, pieces, joined_sums, vectors, d_up_bias = backward(grad_low, saved, True)

    ours = jnp.arange(fsdp_count)[:, None] == group_id
    vector_parts = jnp.concatenate(
        [
            vectors.reshape(6, -1, shard).transpose(1, 0, 2).reshape(-1, 6 * shard),
            jnp.where(ours, joined_sums[None, :WIDTH], 0.0),
            jnp.where(ours, joined_sums[None, 2 * WIDTH :], 0.0),
            d_up_bias.reshape(fsdp_count, -1),
        ],
        1,
    )
    vector_parts = vector_parts.astype(jnp.bfloat16).reshape(4 * fsdp_count, 3 * WIDTH)
    pieces = pieces.at[:, pieces.shape[1] - 16, :].set(vector_parts)
    qkv_piece = sum_low(exchange(pieces, ("fsdp", "x")))
    qkv_piece = jnp.pad(qkv_piece, ((0, 0), (0, model_width - 3 * WIDTH)))
    joint_piece = sum_low(exchange(share.reshape(8, -1, model_width), ("x", "yh")))
    joint_piece, layer_out = lax.optimization_barrier((joint_piece, layer_out))
    both = spread(jnp.concatenate([joint_piece, qkv_piece], 0), ("x", "yh"))
    g_qkv, g_out, g_up, g_down, vector_sum = unpack(
        core_number, both, swap(both), shard, mlp_in.shape[2], mlp_out.shape[1]
    )
    vector_sum = vector_sum[:, : 3 * WIDTH].reshape(-1)
    own_vectors = vector_sum[: 8 * shard].reshape(8, shard)
    own_up_bias = vector_sum[8 * shard :]
    order = (2, 6, 7, 3, 4, 5)
    g_biases = jnp.stack([own_vectors[place] for place in order])
    out_shape = (1, micro_count, 1, local_rows, model_width)
    return (
        layer_out.reshape(out_shape),
        input_grad.reshape(out_shape),
        g_qkv[None],
        g_out[None],
        g_up[None],
        g_down[None],
        own_vectors[None, :2],
        g_biases[None],
        own_up_bias[None],
    )


def solution(mesh):
    fine = Mesh(
        mesh.devices.reshape(2, 4, 2, 2, 4), ("section", "x", "yh", "core", "fsdp")
    )
    rows = P(None, "fsdp", CTX, None)
    weight = P("section", "fsdp", None)
    vector = P("section", None, "fsdp")
    row = P("section", "fsdp")
    out_rows = P("section", None, "fsdp", CTX, None)
    return jax.shard_map(
        shards,
        mesh=fine,
        in_specs=(rows, rows, P(), P(), weight, weight, weight, weight, vector, vector, row),
        out_specs=(out_rows, out_rows, weight, weight, weight, weight, vector, vector, row),
        check_vma=False,
    )
```

```python
import jax
import jax.numpy as jnp
from jax import lax
from jax.experimental import pallas as pl
from jax.experimental.pallas import tpu as pltpu
from jax.sharding import Mesh
from jax.sharding import PartitionSpec as P

HEADS = 12
HDIM = 64
GROUPS = 4
GROUP_HEADS = HEADS // GROUPS
WIDTH = GROUP_HEADS * HDIM
QUERY_BLOCK = 256
EXTRA = 32
JOINT_ROWS = 112
CTX = ("x", "yh", "core")

epsilon = 1e-05
neg_fill = -1e30


def dot(left_side, right_side, left_dim, right_dim):
    return lax.dot_general(
        left_side,
        right_side,
        (((left_dim,), (right_dim,)), ((), ())),
        preferred_element_type=jnp.float32,
    )


def head_columns(part, head):
    start = part * WIDTH + head * HDIM
    return slice(start, start + HDIM)


def attend_body(
    row_places, column_places, own, other, weight, bias, joined, mixed, log_total
):
    step = pl.program_id(0)
    half = own.shape[1]

    @pl.when(step == 0)
    def _():
        product = dot(own[...], weight[:half, :], 1, 0) + dot(other[...], weight[half:, :], 1, 0)
        joined[...] = (product + bias[...]).astype(jnp.bfloat16)

    rows = pl.ds(pl.multiple_of(step * QUERY_BLOCK, QUERY_BLOCK), QUERY_BLOCK)
    hidden = jnp.where(column_places[...] <= row_places[...], 0.0, neg_fill)
    parts = []
    for head in range(GROUP_HEADS):
        queries = joined[rows, head_columns(0, head)] * jnp.bfloat16(HDIM ** (-0.5))
        keys = joined[:, head_columns(1, head)]
        values = joined[:, head_columns(2, head)]
        scores = dot(keys, queries, 1, 1) + hidden
        top = jnp.max(scores, 0, keepdims=True)
        powers = jnp.exp(scores - top)
        total = jnp.sum(powers, 0, keepdims=True)
        parts.append(dot(values, powers.astype(jnp.bfloat16), 0, 0) / total)
        log_total[head : head + 1, :] = top + jnp.log(total)
    mixed[...] = jnp.concatenate(parts, 0).T.astype(jnp.bfloat16)


def whole(*shape):
    return pl.BlockSpec(shape, lambda i: (0,) * len(shape))


def attend(own, other, weight, bias, row_places, column_places):
    count, half = own.shape
    return pl.pallas_call(
        attend_body,
        grid=(count // QUERY_BLOCK,),
        in_specs=[
            pl.BlockSpec((1, QUERY_BLOCK), lambda i: (0, i)),
            whole(count, 1),
            whole(count, half),
            whole(count, half),
            whole(2 * half, 3 * WIDTH),
            whole(1, 3 * WIDTH),
        ],
        out_specs=[
            whole(count, 3 * WIDTH),
            pl.BlockSpec((QUERY_BLOCK, WIDTH), lambda i: (i, 0)),
            pl.BlockSpec((8, QUERY_BLOCK), lambda i: (0, i)),
        ],
        out_shape=[
            jax.ShapeDtypeStruct((count, 3 * WIDTH), jnp.bfloat16),
            jax.ShapeDtypeStruct((count, WIDTH), jnp.bfloat16),
            jax.ShapeDtypeStruct((8, count), jnp.float32),
        ],
        compiler_params=pltpu.CompilerParams(vmem_limit_bytes=48 << 20),
        cost_estimate=pl.CostEstimate(
            flops=4 * count * count * WIDTH,
            bytes_accessed=8 * count * WIDTH,
            transcendentals=count * count * GROUP_HEADS,
        ),
    )(row_places, column_places, own, other, weight, bias)


def attend_back_body(
    row_places,
    column_places,
    joined,
    grad_mixed,
    log_total,
    weight,
    grad_joined,
    grad_own,
    grad_other,
    key_sums,
    value_sums,
):
    step = pl.program_id(0)
    rows = pl.ds(pl.multiple_of(step * QUERY_BLOCK, QUERY_BLOCK), QUERY_BLOCK)

    @pl.when(step == 0)
    def _():
        key_sums[...] = jnp.zeros_like(key_sums)
        value_sums[...] = jnp.zeros_like(value_sums)

    hidden = jnp.where(column_places[...] <= row_places[...], 0.0, neg_fill)
    parts = []
    for head in range(GROUP_HEADS):
        queries = joined[rows, head_columns(0, head)] * jnp.bfloat16(HDIM ** (-0.5))
        keys = joined[:, head_columns(1, head)]
        values = joined[:, head_columns(2, head)]
        grads = grad_mixed[:, head_columns(0, head)]
        weights = jnp.exp(dot(keys, queries, 1, 1) + hidden - log_total[head : head + 1, :])
        grad_weights = dot(values, grads, 1, 1)
        inner_sum = jnp.sum(weights * grad_weights, 0, keepdims=True)
        grad_scores = (weights * (grad_weights - inner_sum)).astype(jnp.bfloat16)
        value_sums[head] += dot(weights.astype(jnp.bfloat16), grads, 1, 0)
        key_sums[head] += dot(grad_scores, queries, 1, 0)
        parts.append(dot(keys, grad_scores, 0, 0) * (HDIM ** (-0.5)))
    grad_joined[rows, :WIDTH] = jnp.concatenate(parts, 0).T.astype(jnp.bfloat16)

    @pl.when(step == pl.num_programs(0) - 1)
    def _():
        for head in range(GROUP_HEADS):
            grad_joined[:, head_columns(1, head)] = key_sums[head].astype(jnp.bfloat16)
            grad_joined[:, head_columns(2, head)] = value_sums[head].astype(jnp.bfloat16)
        half = grad_own.shape[1]
        grad_own[...] = dot(grad_joined[...], weight[:half, :], 1, 1).astype(jnp.bfloat16)
        grad_other[...] = dot(grad_joined[...], weight[half:, :], 1, 1).astype(jnp.bfloat16)


def attend_back(joined, grad_mixed, log_total, weight, row_places, column_places):
    count = joined.shape[0]
    half = weight.shape[0] // 2
    return pl.pallas_call(
        attend_back_body,
        grid=(count // QUERY_BLOCK,),
        in_specs=[
            pl.BlockSpec((1, QUERY_BLOCK), lambda i: (0, i)),
            whole(count, 1),
            whole(count, 3 * WIDTH),
            pl.BlockSpec((QUERY_BLOCK, WIDTH), lambda i: (i, 0)),
            pl.BlockSpec((8, QUERY_BLOCK), lambda i: (0, i)),
            whole(2 * half, 3 * WIDTH),
        ],
        out_specs=[whole(count, 3 * WIDTH), whole(count, half), whole(count, half)],
        out_shape=[
            jax.ShapeDtypeStruct((count, 3 * WIDTH), jnp.bfloat16),
            jax.ShapeDtypeStruct((count, half), jnp.bfloat16),
            jax.ShapeDtypeStruct((count, half), jnp.bfloat16),
        ],
        scratch_shapes=[
            pltpu.VMEM((GROUP_HEADS, count, HDIM), jnp.float32),
            pltpu.VMEM((GROUP_HEADS, count, HDIM), jnp.float32),
        ],
        compiler_params=pltpu.CompilerParams(vmem_limit_bytes=48 << 20),
        cost_estimate=pl.CostEstimate(
            flops=10 * count * count * WIDTH,
            bytes_accessed=16 * count * WIDTH,
            transcendentals=count * count * GROUP_HEADS,
        ),
    )(row_places, column_places, joined, grad_mixed, log_total, weight)


def weight_grads_body(
    core_id,
    active,
    active_other,
    grad_low,
    grad_low_other,
    normed_two,
    normed_two_other,
    grad_hidden,
    grad_hidden_other,
    mixed,
    mixed_other,
    grad_attn,
    grad_attn_other,
    joint,
):
    down_rows, up_rows = active.shape[1], normed_two.shape[0]
    width = grad_low.shape[1]
    product = dot(active[...], grad_low[...], 0, 0)
    product += dot(active_other[...], grad_low_other[...], 0, 0)
    joint[0, :down_rows, :] = product.astype(jnp.bfloat16)
    place = down_rows
    for panel in range(grad_hidden.shape[1] // width):
        columns = slice(panel * width, (panel + 1) * width)
        product = dot(normed_two[...], grad_hidden[:, columns], 1, 0)
        product += dot(normed_two_other[...], grad_hidden_other[:, columns], 1, 0)
        joint[0, place : place + up_rows, :] = product.astype(jnp.bfloat16)
        place += up_rows
    product = dot(mixed[...], grad_attn[...], 1, 0)
    product += dot(mixed_other[...], grad_attn_other[...], 1, 0)
    joint[0, place : place + up_rows, :] = product.astype(jnp.bfloat16)
    place += up_rows
    joint[0, place:, :] = jnp.zeros_like(joint[0, place:, :])


def weight_grads(core_id, pairs, members):
    rows, hidden_width = pairs[0][0].shape
    width = pairs[1][0].shape[1]
    down_rows, up_rows = hidden_width // members // 2, width // members // 2
    out_rows = 2 * down_rows + up_rows + EXTRA
    flat = pl.BlockSpec((rows, width), lambda i, core: (0, 0))
    tall = pl.BlockSpec((up_rows, rows), lambda i, core: (2 * i + core[0], 0))
    specs = [
        pl.BlockSpec((rows, down_rows), lambda i, core: (0, 2 * i + core[0])),
        flat,
        tall,
        pl.BlockSpec((rows, hidden_width), lambda i, core: (0, 0)),
        tall,
        flat,
    ]
    return pl.pallas_call(
        weight_grads_body,
        grid_spec=pltpu.PrefetchScalarGridSpec(
            num_scalar_prefetch=1,
            grid=(members,),
            in_specs=[spec for spec in specs for _ in range(2)],
            out_specs=pl.BlockSpec((1, out_rows, width), lambda i, core: (i, 0, 0)),
        ),
        out_shape=jax.ShapeDtypeStruct((members, out_rows, width), jnp.bfloat16),
        compiler_params=pltpu.CompilerParams(vmem_limit_bytes=48 << 20),
        cost_estimate=pl.CostEstimate(
            flops=2 * rows * width * (2 * hidden_width + width),
            bytes_accessed=2 * members * out_rows * width,
            transcendentals=0,
        ),
    )(core_id, *[value for pair in pairs for value in pair])


def feed_forward_body(mixed, entering, packed, vectors, up_bias, result):
    members, width = packed.shape[0], packed.shape[2]
    panels = up_bias.shape[0]
    up_rows = width // members
    down_rows = panels * up_rows
    micro_count = mixed.shape[0] // GROUPS

    def weight_panel(start):
        return jnp.concatenate(
            [packed[member, start : start + up_rows, :] for member in range(members)], 0
        )

    w_out = weight_panel(2 * down_rows)
    middle = entering[...].astype(jnp.float32) + vectors[5:6, :]
    for group in range(GROUPS):
        part = jnp.concatenate([mixed[m * GROUPS + group] for m in range(micro_count)], 0)
        middle += dot(part, w_out[group * WIDTH : (group + 1) * WIDTH, :], 1, 0)
    normed, _, _ = normalize(middle, vectors[1:2, :], vectors[6:7, :])
    normed = normed.astype(jnp.bfloat16)
    parts = []
    for panel in range(panels):
        hidden = dot(normed, weight_panel(down_rows + panel * up_rows), 1, 0)
        hidden = hidden + up_bias[panel : panel + 1, :]
        parts.append(jax.nn.gelu(hidden).astype(jnp.bfloat16))
    active = jnp.concatenate(parts, 1)
    total = middle + vectors[7:8, :]
    for member in range(members):
        columns = slice(member * down_rows, (member + 1) * down_rows)
        total += dot(active[:, columns], packed[member, :down_rows, :], 1, 0)
    result[...] = total.astype(jnp.bfloat16)


def feed_forward(mixed, entering, packed, vectors, up_bias):
    rows, width = entering.shape
    return pl.pallas_call(
        feed_forward_body,
        in_specs=[pl.BlockSpec(memory_space=pltpu.VMEM)] * 5,
        out_specs=pl.BlockSpec(memory_space=pltpu.VMEM),
        out_shape=jax.ShapeDtypeStruct((rows, width), jnp.bfloat16),
        compiler_params=pltpu.CompilerParams(vmem_limit_bytes=48 << 20),
        cost_estimate=pl.CostEstimate(
            flops=18 * rows * width * width,
            bytes_accessed=18 * width * width,
            transcendentals=4 * rows * width,
        ),
    )(mixed, entering, packed, vectors, up_bias)


def qkv_grads_body(ids, own, other, grad_joined, *outs):
    pieces, sums, both = outs[:-2], outs[-2], outs[-1]
    first_core = ids[0] == 0
    grads = grad_joined[...]
    half = own.shape[1]
    own_grads = dot(own[...], grads, 0, 0).astype(jnp.bfloat16)
    other_grads = dot(other[...], grads, 0, 0).astype(jnp.bfloat16)
    both[:half, :] = jnp.where(first_core, own_grads, other_grads)
    both[half:, :] = jnp.where(first_core, other_grads, own_grads)
    count, piece_rows = len(pieces), pieces[0].shape[0]
    for shift in range(count):
        start = lax.rem(ids[1] + shift, count) * piece_rows
        pieces[shift][...] = both[pl.ds(pl.multiple_of(start, piece_rows), piece_rows), :]
    sums[...] = jnp.sum(grads.astype(jnp.float32), 0, keepdims=True)


def qkv_grads(ids, own, other, grad_joined, count):
    rows, half = own.shape
    width = grad_joined.shape[1]
    piece = jax.ShapeDtypeStruct((2 * half // count, width), jnp.bfloat16)
    return pl.pallas_call(
        qkv_grads_body,
        in_specs=[pl.BlockSpec(memory_space=pltpu.SMEM)]
        + [pl.BlockSpec(memory_space=pltpu.VMEM)] * 3,
        out_specs=[pl.BlockSpec(memory_space=pltpu.VMEM)] * (count + 1),
        out_shape=[piece] * count + [jax.ShapeDtypeStruct((1, width), jnp.float32)],
        scratch_shapes=[pltpu.VMEM((2 * half, width), jnp.bfloat16)],
        compiler_params=pltpu.CompilerParams(vmem_limit_bytes=48 << 20),
        cost_estimate=pl.CostEstimate(
            flops=4 * rows * half * width, bytes_accessed=6 * rows * half, transcendentals=0
        ),
    )(ids, own, other, grad_joined)


def unpack_body(core_id, own, other, g_qkv, g_out, g_up, g_down, vectors):
    first_core = core_id[0] == 0
    count = own.shape[0]
    width = own.shape[2]
    joint_rows = JOINT_ROWS
    piece_rows = own.shape[1] - joint_rows - 16
    up_rows = g_up.shape[0] // 2
    down_rows = g_down.shape[0] // 2
    sums = jnp.zeros(vectors.shape, jnp.float32)
    for core in range(2):
        pick = first_core if core == 0 else jnp.logical_not(first_core)
        joint = jnp.concatenate(
            [
                jnp.where(pick, own[i, :joint_rows, :], other[i, :joint_rows, :])
                for i in range(count)
            ],
            0,
        ).astype(jnp.float32)
        g_down[core * down_rows : (core + 1) * down_rows, :] = joint[:down_rows]
        place = down_rows
        for panel in range(g_up.shape[1] // width):
            g_up[core * up_rows : (core + 1) * up_rows, panel * width : (panel + 1) * width] = (
                joint[place : place + up_rows]
            )
            place += up_rows
        g_out[core * up_rows : (core + 1) * up_rows, :] = joint[place : place + up_rows]
        for i in range(count):
            x_id, group = i // 2, (i % 2) * 2 + core
            piece = jnp.where(pick, own[i, joint_rows:, :], other[i, joint_rows:, :])
            piece = piece.astype(jnp.float32)
            for part in range(3):
                start = part * width + group * WIDTH
                g_qkv[x_id * piece_rows : (x_id + 1) * piece_rows, start : start + WIDTH] = piece[
                    :piece_rows, part * WIDTH : (part + 1) * WIDTH
                ]
            sums += piece[piece_rows : piece_rows + 4, :]
    vectors[...] = sums


def unpack(core_id, own, other, shard, hidden_width, hidden_shard):
    width = own.shape[2]
    return pl.pallas_call(
        unpack_body,
        in_specs=[pl.BlockSpec(memory_space=pltpu.SMEM)]
        + [pl.BlockSpec(memory_space=pltpu.VMEM)] * 2,
        out_specs=[pl.BlockSpec(memory_space=pltpu.VMEM)] * 5,
        out_shape=[
            jax.ShapeDtypeStruct((shard, 3 * width), jnp.float32),
            jax.ShapeDtypeStruct((shard, width), jnp.float32),
            jax.ShapeDtypeStruct((shard, hidden_width), jnp.float32),
            jax.ShapeDtypeStruct((hidden_shard, width), jnp.float32),
            jax.ShapeDtypeStruct((4, width), jnp.float32),
        ],
        compiler_params=pltpu.CompilerParams(vmem_limit_bytes=48 << 20),
        cost_estimate=pl.CostEstimate(flops=0, bytes_accessed=12 << 20, transcendentals=0),
    )(core_id, own, other)


def cross(left_side, right_side, pattern):
    return jnp.einsum(pattern, left_side, right_side, preferred_element_type=jnp.float32)


def normalize(values, gain_row, shift_row):
    center = values - jnp.mean(values, -1, keepdims=True)
    spread = lax.rsqrt(jnp.mean(center * center, -1, keepdims=True) + epsilon)
    unit_rows = center * spread
    return (unit_rows * gain_row + shift_row, unit_rows, spread)


def normalize_back(grad_out, unit_rows, spread, gain_row):
    grad_unit = grad_out * gain_row
    grad_in = spread * (
        grad_unit
        - jnp.mean(grad_unit, -1, keepdims=True)
        - unit_rows * jnp.mean(grad_unit * unit_rows, -1, keepdims=True)
    )
    return (grad_in, jnp.sum(grad_out * unit_rows, 0), jnp.sum(grad_out, 0))


def positions(block_table, block_len):
    offsets = jnp.arange(block_len, dtype=jnp.int32)
    return (block_table[:, None] * block_len + offsets[None, :]).reshape(-1)


def exchange(value, axes):
    return lax.all_to_all(value, axes, 0, 0, tiled=True)


def swap(value):
    return lax.ppermute(value, "core", [(0, 1), (1, 0)])


def in_order(own, other):
    first = lax.axis_index("core") == 0
    return jnp.where(first, own, other), jnp.where(first, other, own)


def gather_weights(attn_out, mlp_in, mlp_out):
    core_id = lax.axis_index("core")
    width = attn_out.shape[2]
    out_half, up_half, down_half = (
        lax.dynamic_slice_in_dim(
            weight[0], core_id * (weight.shape[1] // 2), weight.shape[1] // 2, 0
        )
        for weight in (attn_out, mlp_in, mlp_out)
    )
    panels = [up_half[:, start : start + width] for start in range(0, mlp_in.shape[2], width)]
    packed = jnp.concatenate([down_half] + panels + [out_half], 0)
    everyone = lax.all_gather(packed, ("fsdp", "core"), axis=0)
    down_rows, up_rows = down_half.shape[0], up_half.shape[0]
    w_down = everyone[:, :down_rows].reshape(-1, width)
    w_up = jnp.concatenate(
        [
            everyone[:, start : start + up_rows].reshape(-1, width)
            for start in range(down_rows, 2 * down_rows, up_rows)
        ],
        1,
    )
    w_out = everyone[:, 2 * down_rows :].reshape(-1, width)
    return everyone, w_out, w_up, w_down


def ring_pairs(axis, shift):
    count = lax.axis_size(axis)
    return [(source, (source + shift) % count) for source in range(count)]


def gather_ring(value, axis, first):
    count = lax.axis_size(axis)
    members = [value] + [
        lax.ppermute(value, axis, ring_pairs(axis, -shift)) for shift in range(1, count)
    ]
    start = (first - lax.axis_index(axis)) % count
    doubled = jnp.concatenate(members + members, 0)
    rows = value.shape[0]
    return lax.dynamic_slice_in_dim(doubled, start * rows, count * rows, 0)


def sum_pieces(pieces, axis):
    total = pieces[0].astype(jnp.float32)
    for shift in range(1, len(pieces)):
        received = lax.ppermute(pieces[shift], axis, ring_pairs(axis, shift))
        total = total + received.astype(jnp.float32)
    return total.astype(jnp.bfloat16)


def sum_low(value):
    return jnp.sum(value.astype(jnp.float32), 0).astype(jnp.bfloat16)


def spread(value, axes):
    count = lax.axis_size(axes)
    return exchange(jnp.broadcast_to(value[None], (count,) + value.shape), axes)


def shards(
    inputs,
    cotangent,
    plan,
    block_table,
    attn_in,
    attn_out,
    mlp_in,
    mlp_out,
    norm_gains,
    biases,
    mlp_bias,
):
    shard = norm_gains.shape[2]
    core_id = lax.axis_index("core")
    group_id = lax.axis_index("yh") * 2 + core_id
    fsdp_id = lax.axis_index("fsdp")
    section_id = lax.axis_index("section")
    sections = lax.axis_size("section")
    fsdp_count = lax.axis_size("fsdp")

    small = jnp.concatenate([norm_gains[0], biases[0], mlp_bias.reshape(-1, shard)], 0)
    small = small.reshape(-1, 3 * WIDTH)
    own_columns = lax.dynamic_index_in_dim(
        attn_in[0].reshape(shard, 3, GROUPS, WIDTH), group_id, 2, keepdims=False
    ).reshape(shard, 3 * WIDTH)
    small_all = spread(small, "fsdp").reshape(fsdp_count, -1, shard).astype(jnp.float32)
    w_group = gather_ring(own_columns, "fsdp", 2 * core_id)
    packed, w_out, w_up, w_down = gather_weights(attn_out, mlp_in, mlp_out)
    model_width = w_out.shape[0]
    half = model_width // 2
    w_out_groups = w_out.reshape(GROUPS, WIDTH, model_width)
    vector_rows = small_all[:, :8].transpose(1, 0, 2).reshape(8, model_width)
    gain_rows, bias_rows = vector_rows[:2], vector_rows[2:]
    up_bias = small_all[:, 8:].reshape(-1)
    own_bias = lax.dynamic_index_in_dim(small_all, group_id, 0, keepdims=False)
    group_bias = jnp.concatenate([own_bias[3], jnp.zeros_like(own_bias[3]), own_bias[4]])[None]

    micro_count, _, local_rows, _ = inputs.shape
    rows = micro_count * local_rows
    places = positions(block_table, local_rows // 2)
    row_places, column_places = places[None, :], places[:, None]
    fresh = jnp.stack(
        [lax.dynamic_index_in_dim(inputs, plan[step], 0, keepdims=False) for step in range(micro_count)]
    ).reshape(rows, model_width)
    top_grad = cotangent.reshape(rows, model_width)
    core_number = core_id.astype(jnp.int32)[None]
    numbers = jnp.stack([core_id, fsdp_id]).astype(jnp.int32)
    head_shape = (micro_count, GROUPS, local_rows, WIDTH)

    def forward(entering, last):
        stream = entering.astype(jnp.float32)
        normed, unit_one, spread_one = normalize(stream, gain_rows[0], bias_rows[0])
        halves = normed.astype(jnp.bfloat16).reshape(micro_count, 1, local_rows, 2, half)
        halves = jnp.broadcast_to(
            halves.transpose(0, 1, 3, 2, 4), (micro_count, 2, 2, local_rows, half)
        )
        own = exchange(halves.reshape(-1, local_rows, half), CTX).reshape(-1, half)
        other = swap(own)
        joined, mixed_heads, log_total = attend(
            own, other, w_group, group_bias, row_places, column_places
        )
        mixed = exchange(mixed_heads.reshape(-1, local_rows, WIDTH), CTX)
        if not last:
            return feed_forward(
                mixed, entering, packed, vector_rows, up_bias.reshape(-1, model_width)
            )
        mixed = mixed.reshape(head_shape)
        attended = cross(mixed, w_out_groups, "mgtd,gde->mte").reshape(rows, model_width)
        middle = stream + (attended + bias_rows[3])
        normed_two, unit_two, spread_two = normalize(middle, gain_rows[1], bias_rows[4])
        normed_two_low = normed_two.astype(jnp.bfloat16)
        hidden_pre = cross(normed_two_low, w_up, "td,df->tf") + up_bias
        active_low = jax.nn.gelu(hidden_pre).astype(jnp.bfloat16)
        result = (middle + (cross(active_low, w_down, "tf,fd->td") + bias_rows[5])).astype(
            jnp.bfloat16
        )
        saved = (
            unit_one,
            spread_one,
            own,
            other,
            joined,
            log_total,
            mixed,
            unit_two,
            spread_two,
            normed_two_low,
            hidden_pre,
            active_low,
        )
        return result, saved

    def backward(grad_low, saved, last):
        (
            unit_one,
            spread_one,
            own,
            other,
            joined,
            log_total,
            mixed,
            unit_two,
            spread_two,
            normed_two_low,
            hidden_pre,
            active_low,
        ) = saved
        grad_top = grad_low.astype(jnp.float32)
        grad_active = cross(grad_low, w_down, "td,fd->tf")
        _, gelu_pull = jax.vjp(jax.nn.gelu, hidden_pre)
        grad_hidden = gelu_pull(grad_active)[0].astype(jnp.bfloat16)
        grad_normed_two = cross(grad_hidden, w_up, "tf,df->td")
        grad_norm_two, d_gain_two, d_shift_two = normalize_back(
            grad_normed_two, unit_two, spread_two, gain_rows[1]
        )
        grad_middle = grad_top + grad_norm_two
        grad_attn = grad_middle.astype(jnp.bfloat16)
        attn_parts = grad_attn.reshape(micro_count, local_rows, model_width)
        grad_mixed = cross(attn_parts, w_out_groups, "mte,gde->mgtd").astype(jnp.bfloat16)
        share = None
        grad_heads = exchange(grad_mixed.reshape(-1, local_rows, WIDTH), CTX).reshape(-1, WIDTH)
        if last:
            normed_tall = normed_two_low.T
            mixed_tall = mixed.transpose(1, 3, 0, 2).reshape(model_width, rows)
            members = (active_low, grad_low, normed_tall, grad_hidden, mixed_tall, grad_attn)
            joint = weight_grads(
                core_number, [(value, swap(value)) for value in members], fsdp_count
            )
            grad_heads, joint = lax.optimization_barrier((grad_heads, joint))
            share = lax.psum_scatter(
                joint.reshape(-1, model_width),
                "fsdp",
                scatter_dimension=0,
                tiled=True,
            )
        grad_joined, grad_own, grad_other = attend_back(
            joined, grad_heads, log_total, w_group, row_places, column_places
        )
        received = swap(grad_other)
        summed = (grad_own.astype(jnp.float32) + received.astype(jnp.float32)).astype(jnp.bfloat16)
        returned = exchange(summed.reshape(-1, local_rows, half), CTX)
        returned = returned.reshape(micro_count, 2, 2, local_rows, half).astype(jnp.float32)
        grad_normed = (returned[:, 0] + returned[:, 1]).transpose(0, 2, 1, 3)
        grad_normed = grad_normed.reshape(rows, model_width)
        grad_norm_one, d_gain_one, d_shift_one = normalize_back(
            grad_normed, unit_one, spread_one, gain_rows[0]
        )
        grad_in = (grad_middle + grad_norm_one).astype(jnp.bfloat16)
        if not last:
            return grad_in
        *pieces, joined_sums = qkv_grads(numbers, own, other, grad_joined, fsdp_count)
        joined_sums = joined_sums[0]
        qkv_share = sum_pieces(pieces, "fsdp")
        x_count = lax.axis_size("x")
        piece_rows = shard // x_count
        x_pieces = [
            lax.dynamic_slice_in_dim(
                qkv_share, (lax.axis_index("x") + shift) % x_count * piece_rows, piece_rows, 0
            )
            for shift in range(x_count)
        ]
        qkv_piece = sum_pieces(x_pieces, "x")
        vectors = jnp.stack(
            [
                d_gain_one,
                d_gain_two,
                d_shift_one,
                jnp.sum(grad_attn.astype(jnp.float32), 0),
                d_shift_two,
                jnp.sum(grad_top, 0),
            ]
        )
        d_up_bias = jnp.sum(grad_hidden.astype(jnp.float32), 0)
        return grad_in, share, qkv_piece, joined_sums, vectors, d_up_bias

    forward_pairs = [(i, i + 1) for i in range(sections - 1)]
    entering = fresh
    for _ in range(sections - 1):
        result = forward(entering, False)
        received = lax.ppermute(result, "section", forward_pairs)
        entering = jnp.where(section_id == 0, fresh, received)
    layer_out, saved = forward(entering, True)

    back_pairs = [(i + 1, i) for i in range(sections - 1)]
    grad_low = top_grad
    for _ in range(sections - 1):
        result = backward(grad_low, saved, False)
        received = lax.ppermute(result, "section", back_pairs)
        grad_low = jnp.where(section_id == sections - 1, top_grad, received)
    input_grad, share, qkv_piece, joined_sums, vectors, d_up_bias = backward(grad_low, saved, True)

    ours = jnp.arange(fsdp_count)[:, None] == group_id
    vector_parts = jnp.concatenate(
        [
            vectors.reshape(6, -1, shard).transpose(1, 0, 2).reshape(-1, 6 * shard),
            jnp.where(ours, joined_sums[None, :WIDTH], 0.0),
            jnp.where(ours, joined_sums[None, 2 * WIDTH :], 0.0),
            d_up_bias.reshape(fsdp_count, -1),
        ],
        1,
    )
    vector_parts = vector_parts.astype(jnp.bfloat16).reshape(fsdp_count, 4, 3 * WIDTH)
    vector_share = sum_low(exchange(vector_parts, "fsdp"))
    vector_share = jnp.pad(vector_share, ((0, 12), (0, 0)))
    qkv_piece = jnp.concatenate([qkv_piece, vector_share], 0)
    qkv_piece = jnp.pad(qkv_piece, ((0, 0), (0, model_width - 3 * WIDTH)))
    joint_piece = sum_low(exchange(share.reshape(8, -1, model_width), ("x", "yh")))
    joint_piece, layer_out = lax.optimization_barrier((joint_piece, layer_out))
    both = spread(jnp.concatenate([joint_piece, qkv_piece], 0), ("x", "yh"))
    g_qkv, g_out, g_up, g_down, vector_sum = unpack(
        core_number, both, swap(both), shard, mlp_in.shape[2], mlp_out.shape[1]
    )
    vector_sum = vector_sum[:, : 3 * WIDTH].reshape(-1)
    own_vectors = vector_sum[: 8 * shard].reshape(8, shard)
    own_up_bias = vector_sum[8 * shard :]
    order = (2, 6, 7, 3, 4, 5)
    g_biases = jnp.stack([own_vectors[place] for place in order])
    out_shape = (1, micro_count, 1, local_rows, model_width)
    return (
        layer_out.reshape(out_shape),
        input_grad.reshape(out_shape),
        g_qkv[None],
        g_out[None],
        g_up[None],
        g_down[None],
        own_vectors[None, :2],
        g_biases[None],
        own_up_bias[None],
    )


def solution(mesh):
    fine = Mesh(
        mesh.devices.reshape(2, 4, 2, 2, 4), ("section", "x", "yh", "core", "fsdp")
    )
    rows = P(None, "fsdp", CTX, None)
    weight = P("section", "fsdp", None)
    vector = P("section", None, "fsdp")
    row = P("section", "fsdp")
    out_rows = P("section", None, "fsdp", CTX, None)
    return jax.shard_map(
        shards,
        mesh=fine,
        in_specs=(rows, rows, P(), P(), weight, weight, weight, weight, vector, vector, row),
        out_specs=(out_rows, out_rows, weight, weight, weight, weight, vector, vector, row),
        check_vma=False,
    )
```

```python
import jax
import jax.numpy as jnp
from jax import lax
from jax.experimental import pallas as pl
from jax.experimental.pallas import tpu as pltpu
from jax.sharding import Mesh
from jax.sharding import PartitionSpec as P

HEADS = 12
HDIM = 64
GROUPS = 4
GROUP_HEADS = HEADS // GROUPS
WIDTH = GROUP_HEADS * HDIM
QUERY_BLOCK = 256
EXTRA = 32
JOINT_ROWS = 112
CTX = ("x", "yh", "core")

epsilon = 1e-05
neg_fill = -1e30


def dot(left_side, right_side, left_dim, right_dim):
    return lax.dot_general(
        left_side,
        right_side,
        (((left_dim,), (right_dim,)), ((), ())),
        preferred_element_type=jnp.float32,
    )


def head_columns(part, head):
    start = part * WIDTH + head * HDIM
    return slice(start, start + HDIM)


def whole(*shape):
    return pl.BlockSpec(shape, lambda i, *unused: (0,) * len(shape))


def sort_rows(target, source, table, back):
    blocks = table.shape[0]
    size = source.shape[0] // blocks
    for block in range(blocks):
        fixed = slice(block * size, (block + 1) * size)
        moved = pl.ds(pl.multiple_of(table[block] * size, size), size)
        if back:
            target[fixed, :] = source[moved, :]
        else:
            target[moved, :] = source[fixed, :]


def place_weight(target, members, ids):
    count, rows = len(members), members[0].shape[0]
    for shift, member in enumerate(members):
        place = lax.rem(ids[1] + shift - 2 * ids[0] + count, count)
        target[pl.ds(pl.multiple_of(place * rows, rows), rows), :] = member[...]


def mask_scores(scores):
    count = scores.shape[0] - QUERY_BLOCK
    tile = (QUERY_BLOCK, QUERY_BLOCK)
    visible = lax.broadcasted_iota(jnp.int32, tile, 0) <= lax.broadcasted_iota(jnp.int32, tile, 1)
    masked = jnp.where(visible, scores[count:], neg_fill)
    return jnp.concatenate([scores[:count], masked], 0) if count else masked


def attend_body(
    table, ids, own, other, w0, w1, w2, w3, bias, joined, mixed, log_total, weight, scratch, sorted_out
):
    step = pl.program_id(0)
    half = own.shape[1]

    @pl.when(step == 0)
    def _():
        place_weight(weight, (w0, w1, w2, w3), ids)
        product = dot(own[...], weight[:half, :], 1, 0) + dot(other[...], weight[half:, :], 1, 0)
        scratch[...] = (product + bias[...]).astype(jnp.bfloat16)
        sort_rows(joined, scratch, table, False)

    def block(index):
        rows = slice(index * QUERY_BLOCK, (index + 1) * QUERY_BLOCK)
        seen = slice(0, (index + 1) * QUERY_BLOCK)
        parts = []
        for head in range(GROUP_HEADS):
            queries = joined[rows, head_columns(0, head)] * jnp.bfloat16(HDIM ** (-0.5))
            keys = joined[seen, head_columns(1, head)]
            values = joined[seen, head_columns(2, head)]
            scores = mask_scores(dot(keys, queries, 1, 1))
            top = jnp.max(scores, 0, keepdims=True)
            powers = jnp.exp(scores - top)
            total = jnp.sum(powers, 0, keepdims=True)
            parts.append(dot(values, powers.astype(jnp.bfloat16), 0, 0) / total)
            log_total[head : head + 1, rows] = top + jnp.log(total)
        sorted_out[rows, :] = jnp.concatenate(parts, 0).T.astype(jnp.bfloat16)

    for index in range(own.shape[0] // QUERY_BLOCK):
        pl.when(step == index)(lambda index=index: block(index))

    @pl.when(step == pl.num_programs(0) - 1)
    def _():
        sort_rows(mixed, sorted_out, table, True)


def attend(table, ids, own, other, weights, bias):
    count, half = own.shape
    return pl.pallas_call(
        attend_body,
        grid_spec=pltpu.PrefetchScalarGridSpec(
            num_scalar_prefetch=2,
            grid=(count // QUERY_BLOCK,),
            in_specs=[whole(count, half)] * 2
            + [whole(*weight.shape) for weight in weights]
            + [whole(1, 3 * WIDTH)],
            out_specs=[whole(count, 3 * WIDTH), whole(count, WIDTH), whole(8, count)],
            scratch_shapes=[
                pltpu.VMEM((2 * half, 3 * WIDTH), jnp.bfloat16),
                pltpu.VMEM((count, 3 * WIDTH), jnp.bfloat16),
                pltpu.VMEM((count, WIDTH), jnp.bfloat16),
            ],
        ),
        out_shape=[
            jax.ShapeDtypeStruct((count, 3 * WIDTH), jnp.bfloat16),
            jax.ShapeDtypeStruct((count, WIDTH), jnp.bfloat16),
            jax.ShapeDtypeStruct((8, count), jnp.float32),
        ],
        compiler_params=pltpu.CompilerParams(vmem_limit_bytes=48 << 20),
        cost_estimate=pl.CostEstimate(
            flops=4 * count * count * WIDTH,
            bytes_accessed=8 * count * WIDTH,
            transcendentals=count * count * GROUP_HEADS,
        ),
    )(table, ids, own, other, *weights, bias)


def attend_back_body(
    table,
    ids,
    joined,
    grad_mixed,
    log_total,
    w0,
    w1,
    w2,
    w3,
    grad_joined,
    grad_own,
    grad_other,
    weight,
    sorted_grads,
    sorted_out,
    key_sums,
    value_sums,
):
    step = pl.program_id(0)
    half = grad_own.shape[1]

    @pl.when(step == 0)
    def _():
        place_weight(weight, (w0, w1, w2, w3), ids)
        sort_rows(sorted_grads, grad_mixed, table, False)
        key_sums[...] = jnp.zeros_like(key_sums)
        value_sums[...] = jnp.zeros_like(value_sums)

    def block(index):
        rows = slice(index * QUERY_BLOCK, (index + 1) * QUERY_BLOCK)
        seen = slice(0, (index + 1) * QUERY_BLOCK)
        parts = []
        for head in range(GROUP_HEADS):
            queries = joined[rows, head_columns(0, head)] * jnp.bfloat16(HDIM ** (-0.5))
            keys = joined[seen, head_columns(1, head)]
            values = joined[seen, head_columns(2, head)]
            grads = sorted_grads[rows, head_columns(0, head)]
            scores = mask_scores(dot(keys, queries, 1, 1))
            weights = jnp.exp(scores - log_total[head : head + 1, rows])
            grad_weights = dot(values, grads, 1, 1)
            inner_sum = jnp.sum(weights * grad_weights, 0, keepdims=True)
            grad_scores = (weights * (grad_weights - inner_sum)).astype(jnp.bfloat16)
            value_sums[head, seen, :] += dot(weights.astype(jnp.bfloat16), grads, 1, 0)
            key_sums[head, seen, :] += dot(grad_scores, queries, 1, 0)
            parts.append(dot(keys, grad_scores, 0, 0) * (HDIM ** (-0.5)))
        sorted_out[rows, :WIDTH] = jnp.concatenate(parts, 0).T.astype(jnp.bfloat16)

    for index in range(joined.shape[0] // QUERY_BLOCK):
        pl.when(step == index)(lambda index=index: block(index))

    @pl.when(step == pl.num_programs(0) - 1)
    def _():
        for head in range(GROUP_HEADS):
            sorted_out[:, head_columns(1, head)] = key_sums[head].astype(jnp.bfloat16)
            sorted_out[:, head_columns(2, head)] = value_sums[head].astype(jnp.bfloat16)
        sort_rows(grad_joined, sorted_out, table, True)
        grad_own[...] = dot(grad_joined[...], weight[:half, :], 1, 1).astype(jnp.bfloat16)
        grad_other[...] = dot(grad_joined[...], weight[half:, :], 1, 1).astype(jnp.bfloat16)


def attend_back(table, ids, joined, grad_mixed, log_total, weights):
    count = joined.shape[0]
    half = len(weights) * weights[0].shape[0] // 2
    return pl.pallas_call(
        attend_back_body,
        grid_spec=pltpu.PrefetchScalarGridSpec(
            num_scalar_prefetch=2,
            grid=(count // QUERY_BLOCK,),
            in_specs=[whole(count, 3 * WIDTH), whole(count, WIDTH), whole(8, count)]
            + [whole(*weight.shape) for weight in weights],
            out_specs=[whole(count, 3 * WIDTH), whole(count, half), whole(count, half)],
            scratch_shapes=[
                pltpu.VMEM((2 * half, 3 * WIDTH), jnp.bfloat16),
                pltpu.VMEM((count, WIDTH), jnp.bfloat16),
                pltpu.VMEM((count, 3 * WIDTH), jnp.bfloat16),
                pltpu.VMEM((GROUP_HEADS, count, HDIM), jnp.float32),
                pltpu.VMEM((GROUP_HEADS, count, HDIM), jnp.float32),
            ],
        ),
        out_shape=[
            jax.ShapeDtypeStruct((count, 3 * WIDTH), jnp.bfloat16),
            jax.ShapeDtypeStruct((count, half), jnp.bfloat16),
            jax.ShapeDtypeStruct((count, half), jnp.bfloat16),
        ],
        compiler_params=pltpu.CompilerParams(vmem_limit_bytes=48 << 20),
        cost_estimate=pl.CostEstimate(
            flops=10 * count * count * WIDTH,
            bytes_accessed=16 * count * WIDTH,
            transcendentals=count * count * GROUP_HEADS,
        ),
    )(table, ids, joined, grad_mixed, log_total, *weights)


def weight_grads_body(
    core_id,
    active,
    active_other,
    grad_low,
    grad_low_other,
    normed_two,
    normed_two_other,
    grad_hidden,
    grad_hidden_other,
    mixed,
    mixed_other,
    grad_attn,
    grad_attn_other,
    joint,
):
    down_rows, up_rows = active.shape[1], normed_two.shape[0]
    width = grad_low.shape[1]
    product = dot(active[...], grad_low[...], 0, 0)
    product += dot(active_other[...], grad_low_other[...], 0, 0)
    joint[0, :down_rows, :] = product.astype(jnp.bfloat16)
    place = down_rows
    for panel in range(grad_hidden.shape[1] // width):
        columns = slice(panel * width, (panel + 1) * width)
        product = dot(normed_two[...], grad_hidden[:, columns], 1, 0)
        product += dot(normed_two_other[...], grad_hidden_other[:, columns], 1, 0)
        joint[0, place : place + up_rows, :] = product.astype(jnp.bfloat16)
        place += up_rows
    product = dot(mixed[...], grad_attn[...], 1, 0)
    product += dot(mixed_other[...], grad_attn_other[...], 1, 0)
    joint[0, place : place + up_rows, :] = product.astype(jnp.bfloat16)
    place += up_rows
    joint[0, place:, :] = jnp.zeros_like(joint[0, place:, :])


def weight_grads(core_id, pairs, members):
    rows, hidden_width = pairs[0][0].shape
    width = pairs[1][0].shape[1]
    down_rows, up_rows = hidden_width // members // 2, width // members // 2
    out_rows = 2 * down_rows + up_rows + EXTRA
    flat = pl.BlockSpec((rows, width), lambda i, core: (0, 0))
    tall = pl.BlockSpec((up_rows, rows), lambda i, core: (2 * i + core[0], 0))
    specs = [
        pl.BlockSpec((rows, down_rows), lambda i, core: (0, 2 * i + core[0])),
        flat,
        tall,
        pl.BlockSpec((rows, hidden_width), lambda i, core: (0, 0)),
        tall,
        flat,
    ]
    return pl.pallas_call(
        weight_grads_body,
        grid_spec=pltpu.PrefetchScalarGridSpec(
            num_scalar_prefetch=1,
            grid=(members,),
            in_specs=[spec for spec in specs for _ in range(2)],
            out_specs=pl.BlockSpec((1, out_rows, width), lambda i, core: (i, 0, 0)),
        ),
        out_shape=jax.ShapeDtypeStruct((members, out_rows, width), jnp.bfloat16),
        compiler_params=pltpu.CompilerParams(vmem_limit_bytes=48 << 20),
        cost_estimate=pl.CostEstimate(
            flops=2 * rows * width * (2 * hidden_width + width),
            bytes_accessed=2 * members * out_rows * width,
            transcendentals=0,
        ),
    )(core_id, *[value for pair in pairs for value in pair])


def feed_forward_body(mixed, entering, packed, vectors, up_bias, result):
    members, width = packed.shape[0], packed.shape[2]
    panels = up_bias.shape[0]
    up_rows = width // members
    down_rows = panels * up_rows
    micro_count = mixed.shape[0] // GROUPS

    def weight_panel(start):
        return jnp.concatenate(
            [packed[member, start : start + up_rows, :] for member in range(members)], 0
        )

    w_out = weight_panel(2 * down_rows)
    middle = entering[...].astype(jnp.float32) + vectors[5:6, :]
    for group in range(GROUPS):
        part = jnp.concatenate([mixed[m * GROUPS + group] for m in range(micro_count)], 0)
        middle += dot(part, w_out[group * WIDTH : (group + 1) * WIDTH, :], 1, 0)
    normed, _, _ = normalize(middle, vectors[1:2, :], vectors[6:7, :])
    normed = normed.astype(jnp.bfloat16)
    parts = []
    for panel in range(panels):
        hidden = dot(normed, weight_panel(down_rows + panel * up_rows), 1, 0)
        hidden = hidden + up_bias[panel : panel + 1, :]
        parts.append(jax.nn.gelu(hidden).astype(jnp.bfloat16))
    active = jnp.concatenate(parts, 1)
    total = middle + vectors[7:8, :]
    for member in range(members):
        columns = slice(member * down_rows, (member + 1) * down_rows)
        total += dot(active[:, columns], packed[member, :down_rows, :], 1, 0)
    result[...] = total.astype(jnp.bfloat16)


def feed_forward(mixed, entering, packed, vectors, up_bias):
    rows, width = entering.shape
    return pl.pallas_call(
        feed_forward_body,
        in_specs=[pl.BlockSpec(memory_space=pltpu.VMEM)] * 5,
        out_specs=pl.BlockSpec(memory_space=pltpu.VMEM),
        out_shape=jax.ShapeDtypeStruct((rows, width), jnp.bfloat16),
        compiler_params=pltpu.CompilerParams(vmem_limit_bytes=48 << 20),
        cost_estimate=pl.CostEstimate(
            flops=18 * rows * width * width,
            bytes_accessed=18 * width * width,
            transcendentals=4 * rows * width,
        ),
    )(mixed, entering, packed, vectors, up_bias)


def qkv_grads_body(ids, own, other, grad_joined, *outs):
    pieces, sums, both = outs[:-2], outs[-2], outs[-1]
    first_core = ids[0] == 0
    grads = grad_joined[...]
    half = own.shape[1]
    own_grads = dot(own[...], grads, 0, 0).astype(jnp.bfloat16)
    other_grads = dot(other[...], grads, 0, 0).astype(jnp.bfloat16)
    both[:half, :] = jnp.where(first_core, own_grads, other_grads)
    both[half:, :] = jnp.where(first_core, other_grads, own_grads)
    count, piece_rows = len(pieces), pieces[0].shape[0]
    for shift in range(count):
        start = lax.rem(ids[1] + shift, count) * piece_rows
        pieces[shift][...] = both[pl.ds(pl.multiple_of(start, piece_rows), piece_rows), :]
    sums[...] = jnp.sum(grads.astype(jnp.float32), 0, keepdims=True)


def qkv_grads(ids, own, other, grad_joined, count):
    rows, half = own.shape
    width = grad_joined.shape[1]
    piece = jax.ShapeDtypeStruct((2 * half // count, width), jnp.bfloat16)
    return pl.pallas_call(
        qkv_grads_body,
        in_specs=[pl.BlockSpec(memory_space=pltpu.SMEM)]
        + [pl.BlockSpec(memory_space=pltpu.VMEM)] * 3,
        out_specs=[pl.BlockSpec(memory_space=pltpu.VMEM)] * (count + 1),
        out_shape=[piece] * count + [jax.ShapeDtypeStruct((1, width), jnp.float32)],
        scratch_shapes=[pltpu.VMEM((2 * half, width), jnp.bfloat16)],
        compiler_params=pltpu.CompilerParams(vmem_limit_bytes=48 << 20),
        cost_estimate=pl.CostEstimate(
            flops=4 * rows * half * width, bytes_accessed=6 * rows * half, transcendentals=0
        ),
    )(ids, own, other, grad_joined)


def unpack_body(core_id, own, other, g_qkv, g_out, g_up, g_down, vectors):
    first_core = core_id[0] == 0
    count = own.shape[0]
    width = own.shape[2]
    joint_rows = JOINT_ROWS
    piece_rows = own.shape[1] - joint_rows - 16
    up_rows = g_up.shape[0] // 2
    down_rows = g_down.shape[0] // 2
    sums = jnp.zeros(vectors.shape, jnp.float32)
    for core in range(2):
        pick = first_core if core == 0 else jnp.logical_not(first_core)
        joint = jnp.concatenate(
            [
                jnp.where(pick, own[i, :joint_rows, :], other[i, :joint_rows, :])
                for i in range(count)
            ],
            0,
        ).astype(jnp.float32)
        g_down[core * down_rows : (core + 1) * down_rows, :] = joint[:down_rows]
        place = down_rows
        for panel in range(g_up.shape[1] // width):
            g_up[core * up_rows : (core + 1) * up_rows, panel * width : (panel + 1) * width] = (
                joint[place : place + up_rows]
            )
            place += up_rows
        g_out[core * up_rows : (core + 1) * up_rows, :] = joint[place : place + up_rows]
        for i in range(count):
            x_id, group = i // 2, (i % 2) * 2 + core
            piece = jnp.where(pick, own[i, joint_rows:, :], other[i, joint_rows:, :])
            piece = piece.astype(jnp.float32)
            for part in range(3):
                start = part * width + group * WIDTH
                g_qkv[x_id * piece_rows : (x_id + 1) * piece_rows, start : start + WIDTH] = piece[
                    :piece_rows, part * WIDTH : (part + 1) * WIDTH
                ]
            sums += piece[piece_rows : piece_rows + 4, :]
    vectors[...] = sums


def unpack(core_id, own, other, shard, hidden_width, hidden_shard):
    width = own.shape[2]
    return pl.pallas_call(
        unpack_body,
        in_specs=[pl.BlockSpec(memory_space=pltpu.SMEM)]
        + [pl.BlockSpec(memory_space=pltpu.VMEM)] * 2,
        out_specs=[pl.BlockSpec(memory_space=pltpu.VMEM)] * 5,
        out_shape=[
            jax.ShapeDtypeStruct((shard, 3 * width), jnp.float32),
            jax.ShapeDtypeStruct((shard, width), jnp.float32),
            jax.ShapeDtypeStruct((shard, hidden_width), jnp.float32),
            jax.ShapeDtypeStruct((hidden_shard, width), jnp.float32),
            jax.ShapeDtypeStruct((4, width), jnp.float32),
        ],
        compiler_params=pltpu.CompilerParams(vmem_limit_bytes=48 << 20),
        cost_estimate=pl.CostEstimate(flops=0, bytes_accessed=12 << 20, transcendentals=0),
    )(core_id, own, other)


def cross(left_side, right_side, pattern):
    return jnp.einsum(pattern, left_side, right_side, preferred_element_type=jnp.float32)


def normalize(values, gain_row, shift_row):
    center = values - jnp.mean(values, -1, keepdims=True)
    spread = lax.rsqrt(jnp.mean(center * center, -1, keepdims=True) + epsilon)
    unit_rows = center * spread
    return (unit_rows * gain_row + shift_row, unit_rows, spread)


def normalize_back(grad_out, unit_rows, spread, gain_row):
    grad_unit = grad_out * gain_row
    grad_in = spread * (
        grad_unit
        - jnp.mean(grad_unit, -1, keepdims=True)
        - unit_rows * jnp.mean(grad_unit * unit_rows, -1, keepdims=True)
    )
    return (grad_in, jnp.sum(grad_out * unit_rows, 0), jnp.sum(grad_out, 0))


def exchange(value, axes):
    return lax.all_to_all(value, axes, 0, 0, tiled=True)


def swap(value):
    return lax.ppermute(value, "core", [(0, 1), (1, 0)])


def in_order(own, other):
    first = lax.axis_index("core") == 0
    return jnp.where(first, own, other), jnp.where(first, other, own)


def gather_weights(attn_out, mlp_in, mlp_out):
    core_id = lax.axis_index("core")
    width = attn_out.shape[2]
    out_half, up_half, down_half = (
        lax.dynamic_slice_in_dim(
            weight[0], core_id * (weight.shape[1] // 2), weight.shape[1] // 2, 0
        )
        for weight in (attn_out, mlp_in, mlp_out)
    )
    panels = [up_half[:, start : start + width] for start in range(0, mlp_in.shape[2], width)]
    packed = jnp.concatenate([down_half] + panels + [out_half], 0)
    everyone = lax.all_gather(packed, ("fsdp", "core"), axis=0)
    down_rows, up_rows = down_half.shape[0], up_half.shape[0]
    w_down = everyone[:, :down_rows].reshape(-1, width)
    w_up = jnp.concatenate(
        [
            everyone[:, start : start + up_rows].reshape(-1, width)
            for start in range(down_rows, 2 * down_rows, up_rows)
        ],
        1,
    )
    w_out = everyone[:, 2 * down_rows :].reshape(-1, width)
    return everyone, w_out, w_up, w_down


def ring_pairs(axis, shift):
    count = lax.axis_size(axis)
    return [(source, (source + shift) % count) for source in range(count)]


def gather_ring(value, axis):
    return [value] + [
        lax.ppermute(value, axis, ring_pairs(axis, -shift))
        for shift in range(1, lax.axis_size(axis))
    ]


def sum_pieces(pieces, axis):
    total = pieces[0].astype(jnp.float32)
    for shift in range(1, len(pieces)):
        received = lax.ppermute(pieces[shift], axis, ring_pairs(axis, shift))
        total = total + received.astype(jnp.float32)
    return total.astype(jnp.bfloat16)


def sum_low(value):
    return jnp.sum(value.astype(jnp.float32), 0).astype(jnp.bfloat16)


def spread(value, axes):
    count = lax.axis_size(axes)
    return exchange(jnp.broadcast_to(value[None], (count,) + value.shape), axes)


def shards(
    inputs,
    cotangent,
    plan,
    block_table,
    attn_in,
    attn_out,
    mlp_in,
    mlp_out,
    norm_gains,
    biases,
    mlp_bias,
):
    shard = norm_gains.shape[2]
    core_id = lax.axis_index("core")
    group_id = lax.axis_index("yh") * 2 + core_id
    fsdp_id = lax.axis_index("fsdp")
    section_id = lax.axis_index("section")
    sections = lax.axis_size("section")
    fsdp_count = lax.axis_size("fsdp")

    small = jnp.concatenate([norm_gains[0], biases[0], mlp_bias.reshape(-1, shard)], 0)
    small = small.reshape(-1, 3 * WIDTH)
    own_columns = lax.dynamic_index_in_dim(
        attn_in[0].reshape(shard, 3, GROUPS, WIDTH), group_id, 2, keepdims=False
    ).reshape(shard, 3 * WIDTH)
    small_all = spread(small, "fsdp").reshape(fsdp_count, -1, shard).astype(jnp.float32)
    own_columns, small_all = lax.optimization_barrier((own_columns, small_all))
    w_group = gather_ring(own_columns, "fsdp")
    packed, w_out, w_up, w_down = gather_weights(attn_out, mlp_in, mlp_out)
    model_width = w_out.shape[0]
    half = model_width // 2
    w_out_groups = w_out.reshape(GROUPS, WIDTH, model_width)
    vector_rows = small_all[:, :8].transpose(1, 0, 2).reshape(8, model_width)
    gain_rows, bias_rows = vector_rows[:2], vector_rows[2:]
    up_bias = small_all[:, 8:].reshape(-1)
    own_bias = lax.dynamic_index_in_dim(small_all, group_id, 0, keepdims=False)
    group_bias = jnp.concatenate([own_bias[3], jnp.zeros_like(own_bias[3]), own_bias[4]])[None]

    micro_count, _, local_rows, _ = inputs.shape
    rows = micro_count * local_rows
    fresh = jnp.stack(
        [lax.dynamic_index_in_dim(inputs, plan[step], 0, keepdims=False) for step in range(micro_count)]
    ).reshape(rows, model_width)
    top_grad = cotangent.reshape(rows, model_width)
    core_number = core_id.astype(jnp.int32)[None]
    numbers = jnp.stack([core_id, fsdp_id]).astype(jnp.int32)
    head_shape = (micro_count, GROUPS, local_rows, WIDTH)

    def forward(entering, last):
        stream = entering.astype(jnp.float32)
        normed, unit_one, spread_one = normalize(stream, gain_rows[0], bias_rows[0])
        halves = normed.astype(jnp.bfloat16).reshape(micro_count, 1, local_rows, 2, half)
        halves = jnp.broadcast_to(
            halves.transpose(0, 1, 3, 2, 4), (micro_count, 2, 2, local_rows, half)
        )
        own = exchange(halves.reshape(-1, local_rows, half), CTX).reshape(-1, half)
        other = swap(own)
        joined, mixed_heads, log_total = attend(
            block_table, numbers, own, other, w_group, group_bias
        )
        mixed = exchange(mixed_heads.reshape(-1, local_rows, WIDTH), CTX)
        if not last:
            return feed_forward(
                mixed, entering, packed, vector_rows, up_bias.reshape(-1, model_width)
            )
        mixed = mixed.reshape(head_shape)
        attended = cross(mixed, w_out_groups, "mgtd,gde->mte").reshape(rows, model_width)
        middle = stream + (attended + bias_rows[3])
        normed_two, unit_two, spread_two = normalize(middle, gain_rows[1], bias_rows[4])
        normed_two_low = normed_two.astype(jnp.bfloat16)
        hidden_pre = cross(normed_two_low, w_up, "td,df->tf") + up_bias
        active_low = jax.nn.gelu(hidden_pre).astype(jnp.bfloat16)
        result = (middle + (cross(active_low, w_down, "tf,fd->td") + bias_rows[5])).astype(
            jnp.bfloat16
        )
        saved = (
            unit_one,
            spread_one,
            own,
            other,
            joined,
            log_total,
            mixed,
            unit_two,
            spread_two,
            normed_two_low,
            hidden_pre,
            active_low,
        )
        return result, saved

    def backward(grad_low, saved, last):
        (
            unit_one,
            spread_one,
            own,
            other,
            joined,
            log_total,
            mixed,
            unit_two,
            spread_two,
            normed_two_low,
            hidden_pre,
            active_low,
        ) = saved
        grad_top = grad_low.astype(jnp.float32)
        grad_active = cross(grad_low, w_down, "td,fd->tf")
        _, gelu_pull = jax.vjp(jax.nn.gelu, hidden_pre)
        grad_hidden = gelu_pull(grad_active)[0].astype(jnp.bfloat16)
        grad_normed_two = cross(grad_hidden, w_up, "tf,df->td")
        grad_norm_two, d_gain_two, d_shift_two = normalize_back(
            grad_normed_two, unit_two, spread_two, gain_rows[1]
        )
        grad_middle = grad_top + grad_norm_two
        grad_attn = grad_middle.astype(jnp.bfloat16)
        attn_parts = grad_attn.reshape(micro_count, local_rows, model_width)
        grad_mixed = cross(attn_parts, w_out_groups, "mte,gde->mgtd").astype(jnp.bfloat16)
        share = None
        grad_heads = exchange(grad_mixed.reshape(-1, local_rows, WIDTH), CTX).reshape(-1, WIDTH)
        if last:
            normed_tall = normed_two_low.T
            mixed_tall = mixed.transpose(1, 3, 0, 2).reshape(model_width, rows)
            members = (active_low, grad_low, normed_tall, grad_hidden, mixed_tall, grad_attn)
            joint = weight_grads(
                core_number, [(value, swap(value)) for value in members], fsdp_count
            )
            grad_heads, joint = lax.optimization_barrier((grad_heads, joint))
            share = lax.psum_scatter(
                joint.reshape(-1, model_width),
                "fsdp",
                scatter_dimension=0,
                tiled=True,
            )
        grad_joined, grad_own, grad_other = attend_back(
            block_table, numbers, joined, grad_heads, log_total, w_group
        )
        received = swap(grad_other)
        summed = (grad_own.astype(jnp.float32) + received.astype(jnp.float32)).astype(jnp.bfloat16)
        returned = exchange(summed.reshape(-1, local_rows, half), CTX)
        returned = returned.reshape(micro_count, 2, 2, local_rows, half).astype(jnp.float32)
        grad_normed = (returned[:, 0] + returned[:, 1]).transpose(0, 2, 1, 3)
        grad_normed = grad_normed.reshape(rows, model_width)
        grad_norm_one, d_gain_one, d_shift_one = normalize_back(
            grad_normed, unit_one, spread_one, gain_rows[0]
        )
        grad_in = (grad_middle + grad_norm_one).astype(jnp.bfloat16)
        if not last:
            return grad_in
        *pieces, joined_sums = qkv_grads(numbers, own, other, grad_joined, fsdp_count)
        joined_sums = joined_sums[0]
        qkv_share = sum_pieces(pieces, "fsdp")
        x_count = lax.axis_size("x")
        piece_rows = shard // x_count
        x_pieces = [
            lax.dynamic_slice_in_dim(
                qkv_share, (lax.axis_index("x") + shift) % x_count * piece_rows, piece_rows, 0
            )
            for shift in range(x_count)
        ]
        qkv_piece = sum_pieces(x_pieces, "x")
        vectors = jnp.stack(
            [
                d_gain_one,
                d_gain_two,
                d_shift_one,
                jnp.sum(grad_attn.astype(jnp.float32), 0),
                d_shift_two,
                jnp.sum(grad_top, 0),
            ]
        )
        d_up_bias = jnp.sum(grad_hidden.astype(jnp.float32), 0)
        return grad_in, share, qkv_piece, joined_sums, vectors, d_up_bias

    forward_pairs = [(i, i + 1) for i in range(sections - 1)]
    entering = fresh
    for _ in range(sections - 1):
        result = forward(entering, False)
        received = lax.ppermute(result, "section", forward_pairs)
        entering = jnp.where(section_id == 0, fresh, received)
    layer_out, saved = forward(entering, True)

    back_pairs = [(i + 1, i) for i in range(sections - 1)]
    grad_low = top_grad
    for _ in range(sections - 1):
        result = backward(grad_low, saved, False)
        received = lax.ppermute(result, "section", back_pairs)
        grad_low = jnp.where(section_id == sections - 1, top_grad, received)
    input_grad, share, qkv_piece, joined_sums, vectors, d_up_bias = backward(grad_low, saved, True)

    ours = jnp.arange(fsdp_count)[:, None] == group_id
    vector_parts = jnp.concatenate(
        [
            vectors.reshape(6, -1, shard).transpose(1, 0, 2).reshape(-1, 6 * shard),
            jnp.where(ours, joined_sums[None, :WIDTH], 0.0),
            jnp.where(ours, joined_sums[None, 2 * WIDTH :], 0.0),
            d_up_bias.reshape(fsdp_count, -1),
        ],
        1,
    )
    vector_parts = vector_parts.astype(jnp.bfloat16).reshape(fsdp_count, 4, 3 * WIDTH)
    vector_share = sum_low(exchange(vector_parts, "fsdp"))
    vector_share = jnp.pad(vector_share, ((0, 12), (0, 0)))
    qkv_piece = jnp.concatenate([qkv_piece, vector_share], 0)
    qkv_piece = jnp.pad(qkv_piece, ((0, 0), (0, model_width - 3 * WIDTH)))
    share, qkv_piece = lax.optimization_barrier((share, qkv_piece))
    joint_piece = sum_low(exchange(share.reshape(8, -1, model_width), ("x", "yh")))
    joint_piece, layer_out = lax.optimization_barrier((joint_piece, layer_out))
    both = spread(jnp.concatenate([joint_piece, qkv_piece], 0), ("x", "yh"))
    g_qkv, g_out, g_up, g_down, vector_sum = unpack(
        core_number, both, swap(both), shard, mlp_in.shape[2], mlp_out.shape[1]
    )
    vector_sum = vector_sum[:, : 3 * WIDTH].reshape(-1)
    own_vectors = vector_sum[: 8 * shard].reshape(8, shard)
    own_up_bias = vector_sum[8 * shard :]
    order = (2, 6, 7, 3, 4, 5)
    g_biases = jnp.stack([own_vectors[place] for place in order])
    out_shape = (1, micro_count, 1, local_rows, model_width)
    return (
        layer_out.reshape(out_shape),
        input_grad.reshape(out_shape),
        g_qkv[None],
        g_out[None],
        g_up[None],
        g_down[None],
        own_vectors[None, :2],
        g_biases[None],
        own_up_bias[None],
    )


def solution(mesh):
    fine = Mesh(
        mesh.devices.reshape(2, 4, 2, 2, 4), ("section", "x", "yh", "core", "fsdp")
    )
    rows = P(None, "fsdp", CTX, None)
    weight = P("section", "fsdp", None)
    vector = P("section", None, "fsdp")
    row = P("section", "fsdp")
    out_rows = P("section", None, "fsdp", CTX, None)
    return jax.shard_map(
        shards,
        mesh=fine,
        in_specs=(rows, rows, P(), P(), weight, weight, weight, weight, vector, vector, row),
        out_specs=(out_rows, out_rows, weight, weight, weight, weight, vector, vector, row),
        check_vma=False,
    )
```

```python
import jax
import jax.numpy as jnp
from jax import lax
from jax.experimental import pallas as pl
from jax.experimental.pallas import tpu as pltpu
from jax.sharding import Mesh
from jax.sharding import PartitionSpec as P

HEADS = 12
HDIM = 64
GROUPS = 4
GROUP_HEADS = HEADS // GROUPS
WIDTH = GROUP_HEADS * HDIM
QUERY_BLOCK = 256
EXTRA = 32
JOINT_ROWS = 112
CTX = ("x", "yh", "core")

epsilon = 1e-05
neg_fill = -1e30
GELU_SCALE = (2.0 / 3.141592653589793) ** 0.5
GELU_CUBE = 0.044715


def dot(left_side, right_side, left_dim, right_dim):
    return lax.dot_general(
        left_side,
        right_side,
        (((left_dim,), (right_dim,)), ((), ())),
        preferred_element_type=jnp.float32,
    )


def head_columns(part, head):
    start = part * WIDTH + head * HDIM
    return slice(start, start + HDIM)


def whole(*shape):
    return pl.BlockSpec(shape, lambda i, *unused: (0,) * len(shape))


def sort_rows(target, source, table, back):
    blocks = table.shape[0]
    size = source.shape[0] // blocks
    for block in range(blocks):
        fixed = slice(block * size, (block + 1) * size)
        moved = pl.ds(pl.multiple_of(table[block] * size, size), size)
        if back:
            target[fixed, :] = source[moved, :]
        else:
            target[moved, :] = source[fixed, :]


def place_weight(target, members, ids):
    count, rows = len(members), members[0].shape[0]
    for shift, member in enumerate(members):
        place = lax.rem(ids[1] + shift - 2 * ids[0] + count, count)
        target[pl.ds(pl.multiple_of(place * rows, rows), rows), :] = member[...]


def mask_scores(scores):
    count = scores.shape[0] - QUERY_BLOCK
    tile = (QUERY_BLOCK, QUERY_BLOCK)
    visible = lax.broadcasted_iota(jnp.int32, tile, 0) <= lax.broadcasted_iota(jnp.int32, tile, 1)
    masked = jnp.where(visible, scores[count:], neg_fill)
    return jnp.concatenate([scores[:count], masked], 0) if count else masked


def attend_body(
    table, ids, own, other, w0, w1, w2, w3, bias, joined, mixed, log_total, weight, scratch, sorted_out
):
    step = pl.program_id(0)
    half = own.shape[1]

    @pl.when(step == 0)
    def _():
        place_weight(weight, (w0, w1, w2, w3), ids)
        product = dot(own[...], weight[:half, :], 1, 0) + dot(other[...], weight[half:, :], 1, 0)
        scratch[...] = (product + bias[...]).astype(jnp.bfloat16)
        sort_rows(joined, scratch, table, False)

    def block(index):
        rows = slice(index * QUERY_BLOCK, (index + 1) * QUERY_BLOCK)
        seen = slice(0, (index + 1) * QUERY_BLOCK)
        parts = []
        for head in range(GROUP_HEADS):
            queries = joined[rows, head_columns(0, head)] * jnp.bfloat16(HDIM ** (-0.5))
            keys = joined[seen, head_columns(1, head)]
            values = joined[seen, head_columns(2, head)]
            scores = mask_scores(dot(keys, queries, 1, 1))
            top = jnp.max(scores, 0, keepdims=True)
            powers = jnp.exp(scores - top)
            total = jnp.sum(powers, 0, keepdims=True)
            parts.append(dot(values, powers.astype(jnp.bfloat16), 0, 0) / total)
            log_total[head : head + 1, rows] = top + jnp.log(total)
        sorted_out[rows, :] = jnp.concatenate(parts, 0).T.astype(jnp.bfloat16)

    for index in range(own.shape[0] // QUERY_BLOCK):
        pl.when(step == index)(lambda index=index: block(index))

    @pl.when(step == pl.num_programs(0) - 1)
    def _():
        sort_rows(mixed, sorted_out, table, True)


def attend(table, ids, own, other, weights, bias):
    count, half = own.shape
    return pl.pallas_call(
        attend_body,
        grid_spec=pltpu.PrefetchScalarGridSpec(
            num_scalar_prefetch=2,
            grid=(count // QUERY_BLOCK,),
            in_specs=[whole(count, half)] * 2
            + [whole(*weight.shape) for weight in weights]
            + [whole(1, 3 * WIDTH)],
            out_specs=[whole(count, 3 * WIDTH), whole(count, WIDTH), whole(8, count)],
            scratch_shapes=[
                pltpu.VMEM((2 * half, 3 * WIDTH), jnp.bfloat16),
                pltpu.VMEM((count, 3 * WIDTH), jnp.bfloat16),
                pltpu.VMEM((count, WIDTH), jnp.bfloat16),
            ],
        ),
        out_shape=[
            jax.ShapeDtypeStruct((count, 3 * WIDTH), jnp.bfloat16),
            jax.ShapeDtypeStruct((count, WIDTH), jnp.bfloat16),
            jax.ShapeDtypeStruct((8, count), jnp.float32),
        ],
        compiler_params=pltpu.CompilerParams(vmem_limit_bytes=48 << 20),
        cost_estimate=pl.CostEstimate(
            flops=4 * count * count * WIDTH,
            bytes_accessed=8 * count * WIDTH,
            transcendentals=count * count * GROUP_HEADS,
        ),
    )(table, ids, own, other, *weights, bias)


def attend_back_body(
    table,
    ids,
    joined,
    grad_mixed,
    log_total,
    w0,
    w1,
    w2,
    w3,
    grad_joined,
    grad_own,
    grad_other,
    weight,
    sorted_grads,
    sorted_out,
    key_sums,
    value_sums,
):
    step = pl.program_id(0)
    half = grad_own.shape[1]

    @pl.when(step == 0)
    def _():
        place_weight(weight, (w0, w1, w2, w3), ids)
        sort_rows(sorted_grads, grad_mixed, table, False)
        key_sums[...] = jnp.zeros_like(key_sums)
        value_sums[...] = jnp.zeros_like(value_sums)

    def block(index):
        rows = slice(index * QUERY_BLOCK, (index + 1) * QUERY_BLOCK)
        seen = slice(0, (index + 1) * QUERY_BLOCK)
        parts = []
        for head in range(GROUP_HEADS):
            queries = joined[rows, head_columns(0, head)] * jnp.bfloat16(HDIM ** (-0.5))
            keys = joined[seen, head_columns(1, head)]
            values = joined[seen, head_columns(2, head)]
            grads = sorted_grads[rows, head_columns(0, head)]
            scores = mask_scores(dot(keys, queries, 1, 1))
            weights = jnp.exp(scores - log_total[head : head + 1, rows])
            grad_weights = dot(values, grads, 1, 1)
            inner_sum = jnp.sum(weights * grad_weights, 0, keepdims=True)
            grad_scores = (weights * (grad_weights - inner_sum)).astype(jnp.bfloat16)
            value_sums[head, seen, :] += dot(weights.astype(jnp.bfloat16), grads, 1, 0)
            key_sums[head, seen, :] += dot(grad_scores, queries, 1, 0)
            parts.append(dot(keys, grad_scores, 0, 0) * (HDIM ** (-0.5)))
        sorted_out[rows, :WIDTH] = jnp.concatenate(parts, 0).T.astype(jnp.bfloat16)

    for index in range(joined.shape[0] // QUERY_BLOCK):
        pl.when(step == index)(lambda index=index: block(index))

    @pl.when(step == pl.num_programs(0) - 1)
    def _():
        for head in range(GROUP_HEADS):
            sorted_out[:, head_columns(1, head)] = key_sums[head].astype(jnp.bfloat16)
            sorted_out[:, head_columns(2, head)] = value_sums[head].astype(jnp.bfloat16)
        sort_rows(grad_joined, sorted_out, table, True)
        grad_own[...] = dot(grad_joined[...], weight[:half, :], 1, 1).astype(jnp.bfloat16)
        grad_other[...] = dot(grad_joined[...], weight[half:, :], 1, 1).astype(jnp.bfloat16)


def attend_back(table, ids, joined, grad_mixed, log_total, weights):
    count = joined.shape[0]
    half = len(weights) * weights[0].shape[0] // 2
    return pl.pallas_call(
        attend_back_body,
        grid_spec=pltpu.PrefetchScalarGridSpec(
            num_scalar_prefetch=2,
            grid=(count // QUERY_BLOCK,),
            in_specs=[whole(count, 3 * WIDTH), whole(count, WIDTH), whole(8, count)]
            + [whole(*weight.shape) for weight in weights],
            out_specs=[whole(count, 3 * WIDTH), whole(count, half), whole(count, half)],
            scratch_shapes=[
                pltpu.VMEM((2 * half, 3 * WIDTH), jnp.bfloat16),
                pltpu.VMEM((count, WIDTH), jnp.bfloat16),
                pltpu.VMEM((count, 3 * WIDTH), jnp.bfloat16),
                pltpu.VMEM((GROUP_HEADS, count, HDIM), jnp.float32),
                pltpu.VMEM((GROUP_HEADS, count, HDIM), jnp.float32),
            ],
        ),
        out_shape=[
            jax.ShapeDtypeStruct((count, 3 * WIDTH), jnp.bfloat16),
            jax.ShapeDtypeStruct((count, half), jnp.bfloat16),
            jax.ShapeDtypeStruct((count, half), jnp.bfloat16),
        ],
        compiler_params=pltpu.CompilerParams(vmem_limit_bytes=48 << 20),
        cost_estimate=pl.CostEstimate(
            flops=10 * count * count * WIDTH,
            bytes_accessed=16 * count * WIDTH,
            transcendentals=count * count * GROUP_HEADS,
        ),
    )(table, ids, joined, grad_mixed, log_total, *weights)


def weight_grads_body(
    core_id,
    active,
    active_other,
    grad_low,
    grad_low_other,
    normed_two,
    normed_two_other,
    grad_hidden,
    grad_hidden_other,
    mixed,
    mixed_other,
    grad_attn,
    grad_attn_other,
    joint,
):
    down_rows, up_rows = active.shape[1], normed_two.shape[0]
    width = grad_low.shape[1]
    product = dot(active[...], grad_low[...], 0, 0)
    product += dot(active_other[...], grad_low_other[...], 0, 0)
    joint[0, :down_rows, :] = product.astype(jnp.bfloat16)
    place = down_rows
    for panel in range(grad_hidden.shape[1] // width):
        columns = slice(panel * width, (panel + 1) * width)
        product = dot(normed_two[...], grad_hidden[:, columns], 1, 0)
        product += dot(normed_two_other[...], grad_hidden_other[:, columns], 1, 0)
        joint[0, place : place + up_rows, :] = product.astype(jnp.bfloat16)
        place += up_rows
    product = dot(mixed[...], grad_attn[...], 1, 0)
    product += dot(mixed_other[...], grad_attn_other[...], 1, 0)
    joint[0, place : place + up_rows, :] = product.astype(jnp.bfloat16)
    place += up_rows
    joint[0, place:, :] = jnp.zeros_like(joint[0, place:, :])


def weight_grads(core_id, pairs, members):
    rows, hidden_width = pairs[0][0].shape
    width = pairs[1][0].shape[1]
    down_rows, up_rows = hidden_width // members // 2, width // members // 2
    out_rows = 2 * down_rows + up_rows + EXTRA
    flat = pl.BlockSpec((rows, width), lambda i, core: (0, 0))
    tall = pl.BlockSpec((up_rows, rows), lambda i, core: (2 * i + core[0], 0))
    specs = [
        pl.BlockSpec((rows, down_rows), lambda i, core: (0, 2 * i + core[0])),
        flat,
        tall,
        pl.BlockSpec((rows, hidden_width), lambda i, core: (0, 0)),
        tall,
        flat,
    ]
    return pl.pallas_call(
        weight_grads_body,
        grid_spec=pltpu.PrefetchScalarGridSpec(
            num_scalar_prefetch=1,
            grid=(members,),
            in_specs=[spec for spec in specs for _ in range(2)],
            out_specs=pl.BlockSpec((1, out_rows, width), lambda i, core: (i, 0, 0)),
        ),
        out_shape=jax.ShapeDtypeStruct((members, out_rows, width), jnp.bfloat16),
        compiler_params=pltpu.CompilerParams(vmem_limit_bytes=48 << 20),
        cost_estimate=pl.CostEstimate(
            flops=2 * rows * width * (2 * hidden_width + width),
            bytes_accessed=2 * members * out_rows * width,
            transcendentals=0,
        ),
    )(core_id, *[value for pair in pairs for value in pair])


def weight_panel(packed, start):
    members, width = packed.shape[0], packed.shape[2]
    rows = width // members
    return jnp.concatenate([packed[i, start : start + rows, :] for i in range(members)], 0)


def join_groups(mixed, group):
    micro_count = mixed.shape[0] // GROUPS
    return jnp.concatenate([mixed[m * GROUPS + group] for m in range(micro_count)], 0)


def attend_out(mixed, entering, packed, vectors, w_out):
    middle = entering[...].astype(jnp.float32) + vectors[5:6, :]
    for group in range(GROUPS):
        rows = slice(group * WIDTH, (group + 1) * WIDTH)
        middle += dot(join_groups(mixed, group), w_out[rows, :], 1, 0)
    return middle


def feed_forward_body(mixed, entering, packed, vectors, up_bias, result):
    members, width = packed.shape[0], packed.shape[2]
    panels = up_bias.shape[0]
    up_rows = width // members
    down_rows = panels * up_rows
    middle = attend_out(mixed, entering, packed, vectors, weight_panel(packed, 2 * down_rows))
    normed, _, _ = normalize(middle, vectors[1:2, :], vectors[6:7, :])
    normed = normed.astype(jnp.bfloat16)
    parts = []
    for panel in range(panels):
        hidden = dot(normed, weight_panel(packed, down_rows + panel * up_rows), 1, 0)
        hidden = hidden + up_bias[panel : panel + 1, :]
        parts.append(jax.nn.gelu(hidden).astype(jnp.bfloat16))
    active = jnp.concatenate(parts, 1)
    total = middle + vectors[7:8, :]
    for member in range(members):
        columns = slice(member * down_rows, (member + 1) * down_rows)
        total += dot(active[:, columns], packed[member, :down_rows, :], 1, 0)
    result[...] = total.astype(jnp.bfloat16)


def feed_forward(mixed, entering, packed, vectors, up_bias):
    rows, width = entering.shape
    return pl.pallas_call(
        feed_forward_body,
        in_specs=[pl.BlockSpec(memory_space=pltpu.VMEM)] * 5,
        out_specs=pl.BlockSpec(memory_space=pltpu.VMEM),
        out_shape=jax.ShapeDtypeStruct((rows, width), jnp.bfloat16),
        compiler_params=pltpu.CompilerParams(vmem_limit_bytes=48 << 20),
        cost_estimate=pl.CostEstimate(
            flops=18 * rows * width * width,
            bytes_accessed=18 * width * width,
            transcendentals=4 * rows * width,
        ),
    )(mixed, entering, packed, vectors, up_bias)


def feed_back_body(mixed, entering, packed, vectors, up_bias, grad_low, *outs):
    last = len(outs) == 6
    grad_mixed, grad_middle = outs[:2]
    members, width = packed.shape[0], packed.shape[2]
    panels = up_bias.shape[0]
    up_rows = width // members
    down_rows = panels * up_rows
    micro_count = mixed.shape[0] // GROUPS
    local_rows = mixed.shape[1]
    w_out = weight_panel(packed, 2 * down_rows)
    middle = attend_out(mixed, entering, packed, vectors, w_out)
    normed, unit, spread_two = normalize(middle, vectors[1:2, :], vectors[6:7, :])
    normed = normed.astype(jnp.bfloat16)
    grads = grad_low[...]
    grad_normed = jnp.zeros(middle.shape, jnp.float32)
    per_panel = members // panels
    for panel in range(panels):
        columns = slice(panel * width, (panel + 1) * width)
        w_up = weight_panel(packed, down_rows + panel * up_rows)
        hidden = dot(normed, w_up, 1, 0) + up_bias[panel : panel + 1, :]
        square = hidden * hidden
        bend = jnp.tanh(GELU_SCALE * (hidden + GELU_CUBE * (square * hidden)))
        slope = 0.5 * (1.0 + bend) + 0.5 * hidden * (1.0 - bend * bend) * (
            GELU_SCALE * (1.0 + 3.0 * GELU_CUBE * square)
        )
        w_down = jnp.concatenate(
            [packed[i, :down_rows, :] for i in range(panel * per_panel, (panel + 1) * per_panel)],
            0,
        )
        grad_hidden = (dot(grads, w_down, 1, 1) * slope).astype(jnp.bfloat16)
        grad_normed += dot(grad_hidden, w_up, 1, 1)
        if last:
            outs[2][:, columns] = grad_hidden
            outs[5][panel : panel + 1, :] = jnp.sum(
                grad_hidden.astype(jnp.float32), 0, keepdims=True
            )
        else:
            outs[2][:, columns] = (0.5 * hidden * (1.0 + bend)).astype(jnp.bfloat16)
    grad_top = grads.astype(jnp.float32)
    grad_norm, d_gain, d_shift = normalize_back(grad_normed, unit, spread_two, vectors[1:2, :])
    grad_sum = grad_top + grad_norm
    grad_middle[...] = grad_sum
    grad_attn = grad_sum.astype(jnp.bfloat16)
    for group in range(GROUPS):
        part = dot(grad_attn, w_out[group * WIDTH : (group + 1) * WIDTH, :], 1, 1)
        part = part.astype(jnp.bfloat16)
        for m in range(micro_count):
            grad_mixed[m * GROUPS + group] = part[m * local_rows : (m + 1) * local_rows]
    if last:
        outs[3][...] = grad_attn
        sums = outs[4]
        sums[0:1, :] = d_gain[None]
        sums[1:2, :] = d_shift[None]
        sums[2:3, :] = jnp.sum(grad_attn.astype(jnp.float32), 0, keepdims=True)
        sums[3:4, :] = jnp.sum(grad_top, 0, keepdims=True)
    else:
        outs[3][...] = normed.astype(jnp.float32).T.astype(jnp.bfloat16)
        for group in range(GROUPS):
            part = join_groups(mixed, group).astype(jnp.float32).T.astype(jnp.bfloat16)
            outs[4][group * WIDTH : (group + 1) * WIDTH, :] = part


def feed_back(mixed, entering, packed, vectors, up_bias, grad_low, last):
    rows, width = entering.shape
    hidden_width = up_bias.size
    shapes = [(mixed.shape, jnp.bfloat16), ((rows, width), jnp.float32)]
    shapes.append(((rows, hidden_width), jnp.bfloat16))
    if last:
        shapes.append(((rows, width), jnp.bfloat16))
        shapes += [((4, width), jnp.float32), (up_bias.shape, jnp.float32)]
    else:
        shapes += [((width, rows), jnp.bfloat16)] * 2
    return pl.pallas_call(
        feed_back_body,
        in_specs=[pl.BlockSpec(memory_space=pltpu.VMEM)] * 6,
        out_specs=[pl.BlockSpec(memory_space=pltpu.VMEM)] * len(shapes),
        out_shape=[jax.ShapeDtypeStruct(*shape) for shape in shapes],
        compiler_params=pltpu.CompilerParams(vmem_limit_bytes=56 << 20),
        cost_estimate=pl.CostEstimate(
            flops=28 * rows * width * width,
            bytes_accessed=24 * width * width,
            transcendentals=4 * rows * width,
        ),
    )(mixed, entering, packed, vectors, up_bias, grad_low)


def qkv_grads_body(ids, own, other, grad_joined, *outs):
    pieces, sums, both = outs[:-2], outs[-2], outs[-1]
    first_core = ids[0] == 0
    grads = grad_joined[...]
    half = own.shape[1]
    own_grads = dot(own[...], grads, 0, 0).astype(jnp.bfloat16)
    other_grads = dot(other[...], grads, 0, 0).astype(jnp.bfloat16)
    both[:half, :] = jnp.where(first_core, own_grads, other_grads)
    both[half:, :] = jnp.where(first_core, other_grads, own_grads)
    count, piece_rows = len(pieces), pieces[0].shape[0]
    for shift in range(count):
        start = lax.rem(ids[1] + shift, count) * piece_rows
        pieces[shift][...] = both[pl.ds(pl.multiple_of(start, piece_rows), piece_rows), :]
    sums[...] = jnp.sum(grads.astype(jnp.float32), 0, keepdims=True)


def qkv_grads(ids, own, other, grad_joined, count):
    rows, half = own.shape
    width = grad_joined.shape[1]
    piece = jax.ShapeDtypeStruct((2 * half // count, width), jnp.bfloat16)
    return pl.pallas_call(
        qkv_grads_body,
        in_specs=[pl.BlockSpec(memory_space=pltpu.SMEM)]
        + [pl.BlockSpec(memory_space=pltpu.VMEM)] * 3,
        out_specs=[pl.BlockSpec(memory_space=pltpu.VMEM)] * (count + 1),
        out_shape=[piece] * count + [jax.ShapeDtypeStruct((1, width), jnp.float32)],
        scratch_shapes=[pltpu.VMEM((2 * half, width), jnp.bfloat16)],
        compiler_params=pltpu.CompilerParams(vmem_limit_bytes=48 << 20),
        cost_estimate=pl.CostEstimate(
            flops=4 * rows * half * width, bytes_accessed=6 * rows * half, transcendentals=0
        ),
    )(ids, own, other, grad_joined)


def unpack_body(core_id, own, other, g_qkv, g_out, g_up, g_down, vectors):
    first_core = core_id[0] == 0
    count = own.shape[0]
    width = own.shape[2]
    joint_rows = JOINT_ROWS
    piece_rows = own.shape[1] - joint_rows - 16
    up_rows = g_up.shape[0] // 2
    down_rows = g_down.shape[0] // 2
    sums = jnp.zeros(vectors.shape, jnp.float32)
    for core in range(2):
        pick = first_core if core == 0 else jnp.logical_not(first_core)
        joint = jnp.concatenate(
            [
                jnp.where(pick, own[i, :joint_rows, :], other[i, :joint_rows, :])
                for i in range(count)
            ],
            0,
        ).astype(jnp.float32)
        g_down[core * down_rows : (core + 1) * down_rows, :] = joint[:down_rows]
        place = down_rows
        for panel in range(g_up.shape[1] // width):
            g_up[core * up_rows : (core + 1) * up_rows, panel * width : (panel + 1) * width] = (
                joint[place : place + up_rows]
            )
            place += up_rows
        g_out[core * up_rows : (core + 1) * up_rows, :] = joint[place : place + up_rows]
        for i in range(count):
            x_id, group = i // 2, (i % 2) * 2 + core
            piece = jnp.where(pick, own[i, joint_rows:, :], other[i, joint_rows:, :])
            piece = piece.astype(jnp.float32)
            for part in range(3):
                start = part * width + group * WIDTH
                g_qkv[x_id * piece_rows : (x_id + 1) * piece_rows, start : start + WIDTH] = piece[
                    :piece_rows, part * WIDTH : (part + 1) * WIDTH
                ]
            sums += piece[piece_rows : piece_rows + 4, :]
    vectors[...] = sums


def unpack(core_id, own, other, shard, hidden_width, hidden_shard):
    width = own.shape[2]
    return pl.pallas_call(
        unpack_body,
        in_specs=[pl.BlockSpec(memory_space=pltpu.SMEM)]
        + [pl.BlockSpec(memory_space=pltpu.VMEM)] * 2,
        out_specs=[pl.BlockSpec(memory_space=pltpu.VMEM)] * 5,
        out_shape=[
            jax.ShapeDtypeStruct((shard, 3 * width), jnp.float32),
            jax.ShapeDtypeStruct((shard, width), jnp.float32),
            jax.ShapeDtypeStruct((shard, hidden_width), jnp.float32),
            jax.ShapeDtypeStruct((hidden_shard, width), jnp.float32),
            jax.ShapeDtypeStruct((4, width), jnp.float32),
        ],
        compiler_params=pltpu.CompilerParams(vmem_limit_bytes=48 << 20),
        cost_estimate=pl.CostEstimate(flops=0, bytes_accessed=12 << 20, transcendentals=0),
    )(core_id, own, other)


def normalize(values, gain_row, shift_row):
    center = values - jnp.mean(values, -1, keepdims=True)
    spread = lax.rsqrt(jnp.mean(center * center, -1, keepdims=True) + epsilon)
    unit_rows = center * spread
    return (unit_rows * gain_row + shift_row, unit_rows, spread)


def normalize_back(grad_out, unit_rows, spread, gain_row):
    grad_unit = grad_out * gain_row
    grad_in = spread * (
        grad_unit
        - jnp.mean(grad_unit, -1, keepdims=True)
        - unit_rows * jnp.mean(grad_unit * unit_rows, -1, keepdims=True)
    )
    return (grad_in, jnp.sum(grad_out * unit_rows, 0), jnp.sum(grad_out, 0))


def exchange(value, axes):
    return lax.all_to_all(value, axes, 0, 0, tiled=True)


def swap(value):
    return lax.ppermute(value, "core", [(0, 1), (1, 0)])


def in_order(own, other):
    first = lax.axis_index("core") == 0
    return jnp.where(first, own, other), jnp.where(first, other, own)


def gather_weights(attn_out, mlp_in, mlp_out):
    core_id = lax.axis_index("core")
    width = attn_out.shape[2]
    out_half, up_half, down_half = (
        lax.dynamic_slice_in_dim(
            weight[0], core_id * (weight.shape[1] // 2), weight.shape[1] // 2, 0
        )
        for weight in (attn_out, mlp_in, mlp_out)
    )
    panels = [up_half[:, start : start + width] for start in range(0, mlp_in.shape[2], width)]
    packed = jnp.concatenate([down_half] + panels + [out_half], 0)
    return lax.all_gather(packed, ("fsdp", "core"), axis=0)


def ring_pairs(axis, shift):
    count = lax.axis_size(axis)
    return [(source, (source + shift) % count) for source in range(count)]


def gather_ring(value, axis):
    return [value] + [
        lax.ppermute(value, axis, ring_pairs(axis, -shift))
        for shift in range(1, lax.axis_size(axis))
    ]


def sum_pieces(pieces, axis):
    total = pieces[0].astype(jnp.float32)
    for shift in range(1, len(pieces)):
        received = lax.ppermute(pieces[shift], axis, ring_pairs(axis, shift))
        total = total + received.astype(jnp.float32)
    return total.astype(jnp.bfloat16)


def sum_low(value):
    return jnp.sum(value.astype(jnp.float32), 0).astype(jnp.bfloat16)


def spread(value, axes):
    count = lax.axis_size(axes)
    return exchange(jnp.broadcast_to(value[None], (count,) + value.shape), axes)


def shards(
    inputs,
    cotangent,
    plan,
    block_table,
    attn_in,
    attn_out,
    mlp_in,
    mlp_out,
    norm_gains,
    biases,
    mlp_bias,
):
    shard = norm_gains.shape[2]
    core_id = lax.axis_index("core")
    group_id = lax.axis_index("yh") * 2 + core_id
    fsdp_id = lax.axis_index("fsdp")
    section_id = lax.axis_index("section")
    sections = lax.axis_size("section")
    fsdp_count = lax.axis_size("fsdp")

    small = jnp.concatenate([norm_gains[0], biases[0], mlp_bias.reshape(-1, shard)], 0)
    small = small.reshape(-1, 3 * WIDTH)
    own_columns = lax.dynamic_index_in_dim(
        attn_in[0].reshape(shard, 3, GROUPS, WIDTH), group_id, 2, keepdims=False
    ).reshape(shard, 3 * WIDTH)
    small_all = spread(small, "fsdp").reshape(fsdp_count, -1, shard).astype(jnp.float32)
    w_group = gather_ring(own_columns, "fsdp")
    packed = gather_weights(attn_out, mlp_in, mlp_out)
    model_width = attn_out.shape[2]
    half = model_width // 2
    vector_rows = small_all[:, :8].transpose(1, 0, 2).reshape(8, model_width)
    gain_rows, bias_rows = vector_rows[:2], vector_rows[2:]
    up_rows = small_all[:, 8:].reshape(-1, model_width)
    own_bias = lax.dynamic_index_in_dim(small_all, group_id, 0, keepdims=False)
    group_bias = jnp.concatenate([own_bias[3], jnp.zeros_like(own_bias[3]), own_bias[4]])[None]

    micro_count, _, local_rows, _ = inputs.shape
    rows = micro_count * local_rows
    fresh = jnp.stack(
        [lax.dynamic_index_in_dim(inputs, plan[step], 0, keepdims=False) for step in range(micro_count)]
    ).reshape(rows, model_width)
    top_grad = cotangent.reshape(rows, model_width)
    core_number = core_id.astype(jnp.int32)[None]
    numbers = jnp.stack([core_id, fsdp_id]).astype(jnp.int32)

    def forward(entering):
        stream = entering.astype(jnp.float32)
        normed, unit_one, spread_one = normalize(stream, gain_rows[0], bias_rows[0])
        halves = normed.astype(jnp.bfloat16).reshape(micro_count, 1, local_rows, 2, half)
        halves = jnp.broadcast_to(
            halves.transpose(0, 1, 3, 2, 4), (micro_count, 2, 2, local_rows, half)
        )
        own = exchange(halves.reshape(-1, local_rows, half), CTX).reshape(-1, half)
        other = swap(own)
        joined, mixed_heads, log_total = attend(
            block_table, numbers, own, other, w_group, group_bias
        )
        mixed = exchange(mixed_heads.reshape(-1, local_rows, WIDTH), CTX)
        result = feed_forward(mixed, entering, packed, vector_rows, up_rows)
        return result, (entering, unit_one, spread_one, own, other, joined, log_total, mixed)

    def backward(grad_low, saved, kept):
        entering, unit_one, spread_one, own, other, joined, log_total, mixed = saved
        last = kept is not None
        grad_mixed, grad_middle, *extra = feed_back(
            mixed, entering, packed, vector_rows, up_rows, grad_low, last
        )
        grad_heads = exchange(grad_mixed.reshape(-1, local_rows, WIDTH), CTX).reshape(-1, WIDTH)
        if last:
            grad_hidden, grad_attn, sums, up_sums = extra
            active_low, normed_tall, mixed_tall = kept
            members = (active_low, grad_low, normed_tall, grad_hidden, mixed_tall, grad_attn)
            joint = weight_grads(
                core_number, [(value, swap(value)) for value in members], fsdp_count
            )
            grad_heads, joint = lax.optimization_barrier((grad_heads, joint))
            share = lax.psum_scatter(
                joint.reshape(-1, model_width),
                "fsdp",
                scatter_dimension=0,
                tiled=True,
            )
        grad_joined, grad_own, grad_other = attend_back(
            block_table, numbers, joined, grad_heads, log_total, w_group
        )
        received = swap(grad_other)
        summed = (grad_own.astype(jnp.float32) + received.astype(jnp.float32)).astype(jnp.bfloat16)
        returned = exchange(summed.reshape(-1, local_rows, half), CTX)
        returned = returned.reshape(micro_count, 2, 2, local_rows, half).astype(jnp.float32)
        grad_normed = (returned[:, 0] + returned[:, 1]).transpose(0, 2, 1, 3)
        grad_normed = grad_normed.reshape(rows, model_width)
        grad_norm_one, d_gain_one, d_shift_one = normalize_back(
            grad_normed, unit_one, spread_one, gain_rows[0]
        )
        grad_in = (grad_middle + grad_norm_one).astype(jnp.bfloat16)
        if not last:
            return grad_in, extra
        *pieces, joined_sums = qkv_grads(numbers, own, other, grad_joined, fsdp_count)
        joined_sums = joined_sums[0]
        qkv_share = sum_pieces(pieces, "fsdp")
        x_count = lax.axis_size("x")
        piece_rows = shard // x_count
        x_pieces = [
            lax.dynamic_slice_in_dim(
                qkv_share, (lax.axis_index("x") + shift) % x_count * piece_rows, piece_rows, 0
            )
            for shift in range(x_count)
        ]
        qkv_piece = sum_pieces(x_pieces, "x")
        vectors = jnp.stack([d_gain_one, sums[0], d_shift_one, sums[2], sums[1], sums[3]])
        d_up_bias = up_sums.reshape(-1)
        return grad_in, share, qkv_piece, joined_sums, vectors, d_up_bias

    forward_pairs = [(i, i + 1) for i in range(sections - 1)]
    entering = fresh
    for _ in range(sections - 1):
        result, _ = forward(entering)
        received = lax.ppermute(result, "section", forward_pairs)
        entering = jnp.where(section_id == 0, fresh, received)
    layer_out, saved = forward(entering)

    back_pairs = [(i + 1, i) for i in range(sections - 1)]
    grad_low = top_grad
    for _ in range(sections - 1):
        result, kept = backward(grad_low, saved, None)
        received = lax.ppermute(result, "section", back_pairs)
        grad_low = jnp.where(section_id == sections - 1, top_grad, received)
    input_grad, share, qkv_piece, joined_sums, vectors, d_up_bias = backward(grad_low, saved, kept)

    ours = jnp.arange(fsdp_count)[:, None] == group_id
    vector_parts = jnp.concatenate(
        [
            vectors.reshape(6, -1, shard).transpose(1, 0, 2).reshape(-1, 6 * shard),
            jnp.where(ours, joined_sums[None, :WIDTH], 0.0),
            jnp.where(ours, joined_sums[None, 2 * WIDTH :], 0.0),
            d_up_bias.reshape(fsdp_count, -1),
        ],
        1,
    )
    vector_parts = vector_parts.astype(jnp.bfloat16).reshape(fsdp_count, 4, 3 * WIDTH)
    vector_share = sum_low(exchange(vector_parts, "fsdp"))
    vector_share = jnp.pad(vector_share, ((0, 12), (0, 0)))
    qkv_piece = jnp.concatenate([qkv_piece, vector_share], 0)
    qkv_piece = jnp.pad(qkv_piece, ((0, 0), (0, model_width - 3 * WIDTH)))
    joint_piece = sum_low(exchange(share.reshape(8, -1, model_width), ("x", "yh")))
    joint_piece, layer_out = lax.optimization_barrier((joint_piece, layer_out))
    both = spread(jnp.concatenate([joint_piece, qkv_piece], 0), ("x", "yh"))
    g_qkv, g_out, g_up, g_down, vector_sum = unpack(
        core_number, both, swap(both), shard, mlp_in.shape[2], mlp_out.shape[1]
    )
    vector_sum = vector_sum[:, : 3 * WIDTH].reshape(-1)
    own_vectors = vector_sum[: 8 * shard].reshape(8, shard)
    own_up_bias = vector_sum[8 * shard :]
    order = (2, 6, 7, 3, 4, 5)
    g_biases = jnp.stack([own_vectors[place] for place in order])
    out_shape = (1, micro_count, 1, local_rows, model_width)
    return (
        layer_out.reshape(out_shape),
        input_grad.reshape(out_shape),
        g_qkv[None],
        g_out[None],
        g_up[None],
        g_down[None],
        own_vectors[None, :2],
        g_biases[None],
        own_up_bias[None],
    )


def solution(mesh):
    fine = Mesh(
        mesh.devices.reshape(2, 4, 2, 2, 4), ("section", "x", "yh", "core", "fsdp")
    )
    rows = P(None, "fsdp", CTX, None)
    weight = P("section", "fsdp", None)
    vector = P("section", None, "fsdp")
    row = P("section", "fsdp")
    out_rows = P("section", None, "fsdp", CTX, None)
    return jax.shard_map(
        shards,
        mesh=fine,
        in_specs=(rows, rows, P(), P(), weight, weight, weight, weight, vector, vector, row),
        out_specs=(out_rows, out_rows, weight, weight, weight, weight, vector, vector, row),
        check_vma=False,
    )
```

```python
import jax
import jax.numpy as jnp
from jax import lax
from jax.experimental import pallas as pl
from jax.experimental.pallas import tpu as pltpu
from jax.sharding import Mesh
from jax.sharding import PartitionSpec as P

HEADS = 12
HDIM = 64
GROUPS = 4
GROUP_HEADS = HEADS // GROUPS
WIDTH = GROUP_HEADS * HDIM
QUERY_BLOCK = 256
EXTRA = 32
JOINT_ROWS = 112
CTX = ("x", "yh", "core")

epsilon = 1e-05
neg_fill = -1e30
GELU_SCALE = (2.0 / 3.141592653589793) ** 0.5
GELU_CUBE = 0.044715


def dot(left_side, right_side, left_dim, right_dim):
    return lax.dot_general(
        left_side,
        right_side,
        (((left_dim,), (right_dim,)), ((), ())),
        preferred_element_type=jnp.float32,
    )


def head_columns(part, head):
    start = part * WIDTH + head * HDIM
    return slice(start, start + HDIM)


def whole(*shape):
    return pl.BlockSpec(shape, lambda i, *unused: (0,) * len(shape))


def sort_rows(target, source, table, back):
    blocks = table.shape[0]
    size = source.shape[0] // blocks
    for block in range(blocks):
        fixed = slice(block * size, (block + 1) * size)
        moved = pl.ds(pl.multiple_of(table[block] * size, size), size)
        if back:
            target[fixed, :] = source[moved, :]
        else:
            target[moved, :] = source[fixed, :]


def place_weight(target, members, ids):
    count, rows = len(members), members[0].shape[0]
    for shift, member in enumerate(members):
        place = lax.rem(ids[1] + shift - 2 * ids[0] + count, count)
        target[pl.ds(pl.multiple_of(place * rows, rows), rows), :] = member[...]


def mask_scores(scores):
    count = scores.shape[0] - QUERY_BLOCK
    tile = (QUERY_BLOCK, QUERY_BLOCK)
    visible = lax.broadcasted_iota(jnp.int32, tile, 0) <= lax.broadcasted_iota(jnp.int32, tile, 1)
    masked = jnp.where(visible, scores[count:], neg_fill)
    return jnp.concatenate([scores[:count], masked], 0) if count else masked


def attend_body(
    table, ids, own, other, w0, w1, w2, w3, bias, joined, mixed, log_total, weight, scratch, sorted_out
):
    step = pl.program_id(0)
    half = own.shape[1]

    @pl.when(step == 0)
    def _():
        place_weight(weight, (w0, w1, w2, w3), ids)
        product = dot(own[...], weight[:half, :], 1, 0) + dot(other[...], weight[half:, :], 1, 0)
        scratch[...] = (product + bias[...]).astype(jnp.bfloat16)
        sort_rows(joined, scratch, table, False)

    def block(index):
        rows = slice(index * QUERY_BLOCK, (index + 1) * QUERY_BLOCK)
        seen = slice(0, (index + 1) * QUERY_BLOCK)
        parts = []
        for head in range(GROUP_HEADS):
            queries = joined[rows, head_columns(0, head)] * jnp.bfloat16(HDIM ** (-0.5))
            keys = joined[seen, head_columns(1, head)]
            values = joined[seen, head_columns(2, head)]
            scores = mask_scores(dot(keys, queries, 1, 1))
            top = jnp.max(scores, 0, keepdims=True)
            powers = jnp.exp(scores - top)
            total = jnp.sum(powers, 0, keepdims=True)
            parts.append(dot(values, powers.astype(jnp.bfloat16), 0, 0) / total)
            log_total[head : head + 1, rows] = top + jnp.log(total)
        sorted_out[rows, :] = jnp.concatenate(parts, 0).T.astype(jnp.bfloat16)

    for index in range(own.shape[0] // QUERY_BLOCK):
        pl.when(step == index)(lambda index=index: block(index))

    @pl.when(step == pl.num_programs(0) - 1)
    def _():
        sort_rows(mixed, sorted_out, table, True)


def attend(table, ids, own, other, weights, bias):
    count, half = own.shape
    return pl.pallas_call(
        attend_body,
        grid_spec=pltpu.PrefetchScalarGridSpec(
            num_scalar_prefetch=2,
            grid=(count // QUERY_BLOCK,),
            in_specs=[whole(count, half)] * 2
            + [whole(*weight.shape) for weight in weights]
            + [whole(1, 3 * WIDTH)],
            out_specs=[whole(count, 3 * WIDTH), whole(count, WIDTH), whole(8, count)],
            scratch_shapes=[
                pltpu.VMEM((2 * half, 3 * WIDTH), jnp.bfloat16),
                pltpu.VMEM((count, 3 * WIDTH), jnp.bfloat16),
                pltpu.VMEM((count, WIDTH), jnp.bfloat16),
            ],
        ),
        out_shape=[
            jax.ShapeDtypeStruct((count, 3 * WIDTH), jnp.bfloat16),
            jax.ShapeDtypeStruct((count, WIDTH), jnp.bfloat16),
            jax.ShapeDtypeStruct((8, count), jnp.float32),
        ],
        compiler_params=pltpu.CompilerParams(vmem_limit_bytes=48 << 20),
        cost_estimate=pl.CostEstimate(
            flops=4 * count * count * WIDTH,
            bytes_accessed=8 * count * WIDTH,
            transcendentals=count * count * GROUP_HEADS,
        ),
    )(table, ids, own, other, *weights, bias)


def attend_back_body(
    table,
    ids,
    joined,
    grad_mixed,
    log_total,
    w0,
    w1,
    w2,
    w3,
    grad_joined,
    grad_own,
    grad_other,
    weight,
    sorted_grads,
    sorted_out,
    key_sums,
    value_sums,
):
    step = pl.program_id(0)
    half = grad_own.shape[1]

    @pl.when(step == 0)
    def _():
        place_weight(weight, (w0, w1, w2, w3), ids)
        sort_rows(sorted_grads, grad_mixed, table, False)
        key_sums[...] = jnp.zeros_like(key_sums)
        value_sums[...] = jnp.zeros_like(value_sums)

    def block(index):
        rows = slice(index * QUERY_BLOCK, (index + 1) * QUERY_BLOCK)
        seen = slice(0, (index + 1) * QUERY_BLOCK)
        parts = []
        for head in range(GROUP_HEADS):
            queries = joined[rows, head_columns(0, head)] * jnp.bfloat16(HDIM ** (-0.5))
            keys = joined[seen, head_columns(1, head)]
            values = joined[seen, head_columns(2, head)]
            grads = sorted_grads[rows, head_columns(0, head)]
            scores = mask_scores(dot(keys, queries, 1, 1))
            weights = jnp.exp(scores - log_total[head : head + 1, rows])
            grad_weights = dot(values, grads, 1, 1)
            inner_sum = jnp.sum(weights * grad_weights, 0, keepdims=True)
            grad_scores = (weights * (grad_weights - inner_sum)).astype(jnp.bfloat16)
            value_sums[head, seen, :] += dot(weights.astype(jnp.bfloat16), grads, 1, 0)
            key_sums[head, seen, :] += dot(grad_scores, queries, 1, 0)
            parts.append(dot(keys, grad_scores, 0, 0) * (HDIM ** (-0.5)))
        sorted_out[rows, :WIDTH] = jnp.concatenate(parts, 0).T.astype(jnp.bfloat16)

    for index in range(joined.shape[0] // QUERY_BLOCK):
        pl.when(step == index)(lambda index=index: block(index))

    @pl.when(step == pl.num_programs(0) - 1)
    def _():
        for head in range(GROUP_HEADS):
            sorted_out[:, head_columns(1, head)] = key_sums[head].astype(jnp.bfloat16)
            sorted_out[:, head_columns(2, head)] = value_sums[head].astype(jnp.bfloat16)
        sort_rows(grad_joined, sorted_out, table, True)
        grad_own[...] = dot(grad_joined[...], weight[:half, :], 1, 1).astype(jnp.bfloat16)
        grad_other[...] = dot(grad_joined[...], weight[half:, :], 1, 1).astype(jnp.bfloat16)


def attend_back(table, ids, joined, grad_mixed, log_total, weights):
    count = joined.shape[0]
    half = len(weights) * weights[0].shape[0] // 2
    return pl.pallas_call(
        attend_back_body,
        grid_spec=pltpu.PrefetchScalarGridSpec(
            num_scalar_prefetch=2,
            grid=(count // QUERY_BLOCK,),
            in_specs=[whole(count, 3 * WIDTH), whole(count, WIDTH), whole(8, count)]
            + [whole(*weight.shape) for weight in weights],
            out_specs=[whole(count, 3 * WIDTH), whole(count, half), whole(count, half)],
            scratch_shapes=[
                pltpu.VMEM((2 * half, 3 * WIDTH), jnp.bfloat16),
                pltpu.VMEM((count, WIDTH), jnp.bfloat16),
                pltpu.VMEM((count, 3 * WIDTH), jnp.bfloat16),
                pltpu.VMEM((GROUP_HEADS, count, HDIM), jnp.float32),
                pltpu.VMEM((GROUP_HEADS, count, HDIM), jnp.float32),
            ],
        ),
        out_shape=[
            jax.ShapeDtypeStruct((count, 3 * WIDTH), jnp.bfloat16),
            jax.ShapeDtypeStruct((count, half), jnp.bfloat16),
            jax.ShapeDtypeStruct((count, half), jnp.bfloat16),
        ],
        compiler_params=pltpu.CompilerParams(vmem_limit_bytes=48 << 20),
        cost_estimate=pl.CostEstimate(
            flops=10 * count * count * WIDTH,
            bytes_accessed=16 * count * WIDTH,
            transcendentals=count * count * GROUP_HEADS,
        ),
    )(table, ids, joined, grad_mixed, log_total, *weights)


def weight_grads_body(
    core_id,
    active,
    active_other,
    grad_low,
    grad_low_other,
    normed_two,
    normed_two_other,
    grad_hidden,
    grad_hidden_other,
    mixed,
    mixed_other,
    grad_attn,
    grad_attn_other,
    joint,
):
    down_rows, up_rows = active.shape[1], normed_two.shape[0]
    width = grad_low.shape[1]
    product = dot(active[...], grad_low[...], 0, 0)
    product += dot(active_other[...], grad_low_other[...], 0, 0)
    joint[0, :down_rows, :] = product.astype(jnp.bfloat16)
    place = down_rows
    for panel in range(grad_hidden.shape[1] // width):
        columns = slice(panel * width, (panel + 1) * width)
        product = dot(normed_two[...], grad_hidden[:, columns], 1, 0)
        product += dot(normed_two_other[...], grad_hidden_other[:, columns], 1, 0)
        joint[0, place : place + up_rows, :] = product.astype(jnp.bfloat16)
        place += up_rows
    product = dot(mixed[...], grad_attn[...], 1, 0)
    product += dot(mixed_other[...], grad_attn_other[...], 1, 0)
    joint[0, place : place + up_rows, :] = product.astype(jnp.bfloat16)
    place += up_rows
    joint[0, place:, :] = jnp.zeros_like(joint[0, place:, :])


def weight_grads(core_id, pairs, members):
    rows, hidden_width = pairs[0][0].shape
    width = pairs[1][0].shape[1]
    down_rows, up_rows = hidden_width // members // 2, width // members // 2
    out_rows = 2 * down_rows + up_rows + EXTRA
    flat = pl.BlockSpec((rows, width), lambda i, core: (0, 0))
    tall = pl.BlockSpec((up_rows, rows), lambda i, core: (2 * i + core[0], 0))
    specs = [
        pl.BlockSpec((rows, down_rows), lambda i, core: (0, 2 * i + core[0])),
        flat,
        tall,
        pl.BlockSpec((rows, hidden_width), lambda i, core: (0, 0)),
        tall,
        flat,
    ]
    return pl.pallas_call(
        weight_grads_body,
        grid_spec=pltpu.PrefetchScalarGridSpec(
            num_scalar_prefetch=1,
            grid=(members,),
            in_specs=[spec for spec in specs for _ in range(2)],
            out_specs=pl.BlockSpec((1, out_rows, width), lambda i, core: (i, 0, 0)),
        ),
        out_shape=jax.ShapeDtypeStruct((members, out_rows, width), jnp.bfloat16),
        compiler_params=pltpu.CompilerParams(vmem_limit_bytes=48 << 20),
        cost_estimate=pl.CostEstimate(
            flops=2 * rows * width * (2 * hidden_width + width),
            bytes_accessed=2 * members * out_rows * width,
            transcendentals=0,
        ),
    )(core_id, *[value for pair in pairs for value in pair])


def weight_panel(packed, start):
    members, width = packed.shape[0], packed.shape[2]
    rows = width // members
    return jnp.concatenate([packed[i, start : start + rows, :] for i in range(members)], 0)


def join_groups(mixed, group):
    micro_count = mixed.shape[0] // GROUPS
    return jnp.concatenate([mixed[m * GROUPS + group] for m in range(micro_count)], 0)


def attend_out(mixed, entering, packed, vectors, w_out):
    middle = entering[...].astype(jnp.float32) + vectors[5:6, :]
    for group in range(GROUPS):
        rows = slice(group * WIDTH, (group + 1) * WIDTH)
        middle += dot(join_groups(mixed, group), w_out[rows, :], 1, 0)
    return middle


def feed_forward_body(mixed, entering, packed, vectors, up_bias, result):
    members, width = packed.shape[0], packed.shape[2]
    panels = up_bias.shape[0]
    up_rows = width // members
    down_rows = panels * up_rows
    middle = attend_out(mixed, entering, packed, vectors, weight_panel(packed, 2 * down_rows))
    normed, _, _ = normalize(middle, vectors[1:2, :], vectors[6:7, :])
    normed = normed.astype(jnp.bfloat16)
    parts = []
    for panel in range(panels):
        hidden = dot(normed, weight_panel(packed, down_rows + panel * up_rows), 1, 0)
        hidden = hidden + up_bias[panel : panel + 1, :]
        parts.append(jax.nn.gelu(hidden).astype(jnp.bfloat16))
    active = jnp.concatenate(parts, 1)
    total = middle + vectors[7:8, :]
    for member in range(members):
        columns = slice(member * down_rows, (member + 1) * down_rows)
        total += dot(active[:, columns], packed[member, :down_rows, :], 1, 0)
    result[...] = total.astype(jnp.bfloat16)


def feed_forward(mixed, entering, packed, vectors, up_bias):
    rows, width = entering.shape
    return pl.pallas_call(
        feed_forward_body,
        in_specs=[pl.BlockSpec(memory_space=pltpu.VMEM)] * 5,
        out_specs=pl.BlockSpec(memory_space=pltpu.VMEM),
        out_shape=jax.ShapeDtypeStruct((rows, width), jnp.bfloat16),
        compiler_params=pltpu.CompilerParams(vmem_limit_bytes=48 << 20),
        cost_estimate=pl.CostEstimate(
            flops=18 * rows * width * width,
            bytes_accessed=18 * width * width,
            transcendentals=4 * rows * width,
        ),
    )(mixed, entering, packed, vectors, up_bias)


def feed_back_body(mixed, entering, packed, vectors, up_bias, grad_low, *outs):
    last = len(outs) == 6
    grad_mixed, grad_middle = outs[:2]
    members, width = packed.shape[0], packed.shape[2]
    panels = up_bias.shape[0]
    up_rows = width // members
    down_rows = panels * up_rows
    micro_count = mixed.shape[0] // GROUPS
    local_rows = mixed.shape[1]
    w_out = weight_panel(packed, 2 * down_rows)
    middle = attend_out(mixed, entering, packed, vectors, w_out)
    normed, unit, spread_two = normalize(middle, vectors[1:2, :], vectors[6:7, :])
    normed = normed.astype(jnp.bfloat16)
    grads = grad_low[...]
    grad_normed = jnp.zeros(middle.shape, jnp.float32)
    per_panel = members // panels
    for panel in range(panels):
        columns = slice(panel * width, (panel + 1) * width)
        w_up = weight_panel(packed, down_rows + panel * up_rows)
        hidden = dot(normed, w_up, 1, 0) + up_bias[panel : panel + 1, :]
        square = hidden * hidden
        bend = jnp.tanh(GELU_SCALE * (hidden + GELU_CUBE * (square * hidden)))
        slope = 0.5 * (1.0 + bend) + 0.5 * hidden * (1.0 - bend * bend) * (
            GELU_SCALE * (1.0 + 3.0 * GELU_CUBE * square)
        )
        w_down = jnp.concatenate(
            [packed[i, :down_rows, :] for i in range(panel * per_panel, (panel + 1) * per_panel)],
            0,
        )
        grad_hidden = (dot(grads, w_down, 1, 1) * slope).astype(jnp.bfloat16)
        grad_normed += dot(grad_hidden, w_up, 1, 1)
        if last:
            outs[2][:, columns] = grad_hidden
            outs[5][panel : panel + 1, :] = jnp.sum(
                grad_hidden.astype(jnp.float32), 0, keepdims=True
            )
        else:
            outs[2][:, columns] = (0.5 * hidden * (1.0 + bend)).astype(jnp.bfloat16)
    grad_top = grads.astype(jnp.float32)
    grad_norm, d_gain, d_shift = normalize_back(grad_normed, unit, spread_two, vectors[1:2, :])
    grad_sum = grad_top + grad_norm
    grad_middle[...] = grad_sum
    grad_attn = grad_sum.astype(jnp.bfloat16)
    for group in range(GROUPS):
        part = dot(grad_attn, w_out[group * WIDTH : (group + 1) * WIDTH, :], 1, 1)
        part = part.astype(jnp.bfloat16)
        for m in range(micro_count):
            grad_mixed[m * GROUPS + group] = part[m * local_rows : (m + 1) * local_rows]
    if last:
        outs[3][...] = grad_attn
        sums = outs[4]
        sums[0:1, :] = d_gain[None]
        sums[1:2, :] = d_shift[None]
        sums[2:3, :] = jnp.sum(grad_attn.astype(jnp.float32), 0, keepdims=True)
        sums[3:4, :] = jnp.sum(grad_top, 0, keepdims=True)
    else:
        outs[3][...] = normed.astype(jnp.float32).T.astype(jnp.bfloat16)
        for group in range(GROUPS):
            part = join_groups(mixed, group).astype(jnp.float32).T.astype(jnp.bfloat16)
            outs[4][group * WIDTH : (group + 1) * WIDTH, :] = part


def feed_back(mixed, entering, packed, vectors, up_bias, grad_low, last):
    rows, width = entering.shape
    hidden_width = up_bias.size
    shapes = [(mixed.shape, jnp.bfloat16), ((rows, width), jnp.float32)]
    shapes.append(((rows, hidden_width), jnp.bfloat16))
    if last:
        shapes.append(((rows, width), jnp.bfloat16))
        shapes += [((4, width), jnp.float32), (up_bias.shape, jnp.float32)]
    else:
        shapes += [((width, rows), jnp.bfloat16)] * 2
    return pl.pallas_call(
        feed_back_body,
        in_specs=[pl.BlockSpec(memory_space=pltpu.VMEM)] * 6,
        out_specs=[pl.BlockSpec(memory_space=pltpu.VMEM)] * len(shapes),
        out_shape=[jax.ShapeDtypeStruct(*shape) for shape in shapes],
        compiler_params=pltpu.CompilerParams(vmem_limit_bytes=56 << 20),
        cost_estimate=pl.CostEstimate(
            flops=28 * rows * width * width,
            bytes_accessed=24 * width * width,
            transcendentals=4 * rows * width,
        ),
    )(mixed, entering, packed, vectors, up_bias, grad_low)


def qkv_grads_body(ids, own, other, grad_joined, *outs):
    pieces, sums, both = outs[:-2], outs[-2], outs[-1]
    first_core = ids[0] == 0
    grads = grad_joined[...]
    half = own.shape[1]
    own_grads = dot(own[...], grads, 0, 0).astype(jnp.bfloat16)
    other_grads = dot(other[...], grads, 0, 0).astype(jnp.bfloat16)
    both[:half, :] = jnp.where(first_core, own_grads, other_grads)
    both[half:, :] = jnp.where(first_core, other_grads, own_grads)
    count, piece_rows = len(pieces), pieces[0].shape[0]
    for shift in range(count):
        start = lax.rem(ids[1] + shift, count) * piece_rows
        pieces[shift][...] = both[pl.ds(pl.multiple_of(start, piece_rows), piece_rows), :]
    sums[...] = jnp.sum(grads.astype(jnp.float32), 0, keepdims=True)


def qkv_grads(ids, own, other, grad_joined, count):
    rows, half = own.shape
    width = grad_joined.shape[1]
    piece = jax.ShapeDtypeStruct((2 * half // count, width), jnp.bfloat16)
    return pl.pallas_call(
        qkv_grads_body,
        in_specs=[pl.BlockSpec(memory_space=pltpu.SMEM)]
        + [pl.BlockSpec(memory_space=pltpu.VMEM)] * 3,
        out_specs=[pl.BlockSpec(memory_space=pltpu.VMEM)] * (count + 1),
        out_shape=[piece] * count + [jax.ShapeDtypeStruct((1, width), jnp.float32)],
        scratch_shapes=[pltpu.VMEM((2 * half, width), jnp.bfloat16)],
        compiler_params=pltpu.CompilerParams(vmem_limit_bytes=48 << 20),
        cost_estimate=pl.CostEstimate(
            flops=4 * rows * half * width, bytes_accessed=6 * rows * half, transcendentals=0
        ),
    )(ids, own, other, grad_joined)


def unpack_body(core_id, own, other, g_qkv, g_out, g_up, g_down, vectors):
    first_core = core_id[0] == 0
    count = own.shape[0]
    width = own.shape[2]
    joint_rows = JOINT_ROWS
    piece_rows = own.shape[1] - joint_rows - 16
    up_rows = g_up.shape[0] // 2
    down_rows = g_down.shape[0] // 2
    sums = jnp.zeros(vectors.shape, jnp.float32)
    for core in range(2):
        pick = first_core if core == 0 else jnp.logical_not(first_core)
        joint = jnp.concatenate(
            [
                jnp.where(pick, own[i, :joint_rows, :], other[i, :joint_rows, :])
                for i in range(count)
            ],
            0,
        ).astype(jnp.float32)
        g_down[core * down_rows : (core + 1) * down_rows, :] = joint[:down_rows]
        place = down_rows
        for panel in range(g_up.shape[1] // width):
            g_up[core * up_rows : (core + 1) * up_rows, panel * width : (panel + 1) * width] = (
                joint[place : place + up_rows]
            )
            place += up_rows
        g_out[core * up_rows : (core + 1) * up_rows, :] = joint[place : place + up_rows]
        for i in range(count):
            x_id, group = i // 2, (i % 2) * 2 + core
            piece = jnp.where(pick, own[i, joint_rows:, :], other[i, joint_rows:, :])
            piece = piece.astype(jnp.float32)
            for part in range(3):
                start = part * width + group * WIDTH
                g_qkv[x_id * piece_rows : (x_id + 1) * piece_rows, start : start + WIDTH] = piece[
                    :piece_rows, part * WIDTH : (part + 1) * WIDTH
                ]
            sums += piece[piece_rows : piece_rows + 4, :]
    vectors[...] = sums


def unpack(core_id, own, other, shard, hidden_width, hidden_shard):
    width = own.shape[2]
    return pl.pallas_call(
        unpack_body,
        in_specs=[pl.BlockSpec(memory_space=pltpu.SMEM)]
        + [pl.BlockSpec(memory_space=pltpu.VMEM)] * 2,
        out_specs=[pl.BlockSpec(memory_space=pltpu.VMEM)] * 5,
        out_shape=[
            jax.ShapeDtypeStruct((shard, 3 * width), jnp.float32),
            jax.ShapeDtypeStruct((shard, width), jnp.float32),
            jax.ShapeDtypeStruct((shard, hidden_width), jnp.float32),
            jax.ShapeDtypeStruct((hidden_shard, width), jnp.float32),
            jax.ShapeDtypeStruct((4, width), jnp.float32),
        ],
        compiler_params=pltpu.CompilerParams(vmem_limit_bytes=48 << 20),
        cost_estimate=pl.CostEstimate(flops=0, bytes_accessed=12 << 20, transcendentals=0),
    )(core_id, own, other)


def normalize(values, gain_row, shift_row):
    center = values - jnp.mean(values, -1, keepdims=True)
    spread = lax.rsqrt(jnp.mean(center * center, -1, keepdims=True) + epsilon)
    unit_rows = center * spread
    return (unit_rows * gain_row + shift_row, unit_rows, spread)


def normalize_back(grad_out, unit_rows, spread, gain_row):
    grad_unit = grad_out * gain_row
    grad_in = spread * (
        grad_unit
        - jnp.mean(grad_unit, -1, keepdims=True)
        - unit_rows * jnp.mean(grad_unit * unit_rows, -1, keepdims=True)
    )
    return (grad_in, jnp.sum(grad_out * unit_rows, 0), jnp.sum(grad_out, 0))


def exchange(value, axes):
    return lax.all_to_all(value, axes, 0, 0, tiled=True)


def swap(value):
    return lax.ppermute(value, "core", [(0, 1), (1, 0)])


def in_order(own, other):
    first = lax.axis_index("core") == 0
    return jnp.where(first, own, other), jnp.where(first, other, own)


def pack_weights(attn_out, mlp_in, mlp_out):
    core_id = lax.axis_index("core")
    width = attn_out.shape[2]
    out_half, up_half, down_half = (
        lax.dynamic_slice_in_dim(
            weight[0], core_id * (weight.shape[1] // 2), weight.shape[1] // 2, 0
        )
        for weight in (attn_out, mlp_in, mlp_out)
    )
    panels = [up_half[:, start : start + width] for start in range(0, mlp_in.shape[2], width)]
    return jnp.concatenate([down_half] + panels + [out_half], 0)


def ring_pairs(axis, shift):
    count = lax.axis_size(axis)
    return [(source, (source + shift) % count) for source in range(count)]


def gather_ring(value, axis):
    return [value] + [
        lax.ppermute(value, axis, ring_pairs(axis, -shift))
        for shift in range(1, lax.axis_size(axis))
    ]


def sum_pieces(pieces, axis):
    total = pieces[0].astype(jnp.float32)
    for shift in range(1, len(pieces)):
        received = lax.ppermute(pieces[shift], axis, ring_pairs(axis, shift))
        total = total + received.astype(jnp.float32)
    return total.astype(jnp.bfloat16)


def sum_low(value):
    return jnp.sum(value.astype(jnp.float32), 0).astype(jnp.bfloat16)


def spread(value, axes):
    count = lax.axis_size(axes)
    return exchange(jnp.broadcast_to(value[None], (count,) + value.shape), axes)


def shards(
    inputs,
    cotangent,
    plan,
    block_table,
    attn_in,
    attn_out,
    mlp_in,
    mlp_out,
    norm_gains,
    biases,
    mlp_bias,
):
    shard = norm_gains.shape[2]
    core_id = lax.axis_index("core")
    group_id = lax.axis_index("yh") * 2 + core_id
    fsdp_id = lax.axis_index("fsdp")
    section_id = lax.axis_index("section")
    sections = lax.axis_size("section")
    fsdp_count = lax.axis_size("fsdp")

    small = jnp.concatenate([norm_gains[0], biases[0], mlp_bias.reshape(-1, shard)], 0)
    small = small.reshape(-1, 3 * WIDTH)
    own_columns = lax.dynamic_index_in_dim(
        attn_in[0].reshape(shard, 3, GROUPS, WIDTH), group_id, 2, keepdims=False
    ).reshape(shard, 3 * WIDTH)
    small_all = spread(small, "fsdp").reshape(fsdp_count, -1, shard).astype(jnp.float32)
    w_group = gather_ring(own_columns, "fsdp")
    packed, w_group, small_all = lax.optimization_barrier(
        (pack_weights(attn_out, mlp_in, mlp_out), w_group, small_all)
    )
    packed = lax.all_gather(packed, ("fsdp", "core"), axis=0)
    model_width = attn_out.shape[2]
    half = model_width // 2
    vector_rows = small_all[:, :8].transpose(1, 0, 2).reshape(8, model_width)
    gain_rows, bias_rows = vector_rows[:2], vector_rows[2:]
    up_rows = small_all[:, 8:].reshape(-1, model_width)
    own_bias = lax.dynamic_index_in_dim(small_all, group_id, 0, keepdims=False)
    group_bias = jnp.concatenate([own_bias[3], jnp.zeros_like(own_bias[3]), own_bias[4]])[None]

    micro_count, _, local_rows, _ = inputs.shape
    rows = micro_count * local_rows
    fresh = jnp.stack(
        [lax.dynamic_index_in_dim(inputs, plan[step], 0, keepdims=False) for step in range(micro_count)]
    ).reshape(rows, model_width)
    top_grad = cotangent.reshape(rows, model_width)
    core_number = core_id.astype(jnp.int32)[None]
    numbers = jnp.stack([core_id, fsdp_id]).astype(jnp.int32)

    def forward(entering):
        stream = entering.astype(jnp.float32)
        normed, unit_one, spread_one = normalize(stream, gain_rows[0], bias_rows[0])
        halves = normed.astype(jnp.bfloat16).reshape(micro_count, 1, local_rows, 2, half)
        halves = jnp.broadcast_to(
            halves.transpose(0, 1, 3, 2, 4), (micro_count, 2, 2, local_rows, half)
        )
        own = exchange(halves.reshape(-1, local_rows, half), CTX).reshape(-1, half)
        other = swap(own)
        joined, mixed_heads, log_total = attend(
            block_table, numbers, own, other, w_group, group_bias
        )
        mixed = exchange(mixed_heads.reshape(-1, local_rows, WIDTH), CTX)
        result = feed_forward(mixed, entering, packed, vector_rows, up_rows)
        return result, (entering, unit_one, spread_one, own, other, joined, log_total, mixed)

    def backward(grad_low, saved, kept):
        entering, unit_one, spread_one, own, other, joined, log_total, mixed = saved
        last = kept is not None
        grad_mixed, grad_middle, *extra = feed_back(
            mixed, entering, packed, vector_rows, up_rows, grad_low, last
        )
        grad_heads = exchange(grad_mixed.reshape(-1, local_rows, WIDTH), CTX).reshape(-1, WIDTH)
        if last:
            grad_hidden, grad_attn, sums, up_sums = extra
            active_pair, normed_pair, mixed_pair = kept
            low_pair, hidden_pair, attn_pair = (
                (value, swap(value)) for value in (grad_low, grad_hidden, grad_attn)
            )
            joint = weight_grads(
                core_number,
                [active_pair, low_pair, normed_pair, hidden_pair, mixed_pair, attn_pair],
                fsdp_count,
            )
            grad_heads, joint = lax.optimization_barrier((grad_heads, joint))
            share = lax.psum_scatter(
                joint.reshape(-1, model_width),
                "fsdp",
                scatter_dimension=0,
                tiled=True,
            )
        grad_joined, grad_own, grad_other = attend_back(
            block_table, numbers, joined, grad_heads, log_total, w_group
        )
        received = swap(grad_other)
        summed = (grad_own.astype(jnp.float32) + received.astype(jnp.float32)).astype(jnp.bfloat16)
        returned = exchange(summed.reshape(-1, local_rows, half), CTX)
        if last:
            returned, own = lax.optimization_barrier((returned, own))
        returned = returned.reshape(micro_count, 2, 2, local_rows, half).astype(jnp.float32)
        grad_normed = (returned[:, 0] + returned[:, 1]).transpose(0, 2, 1, 3)
        grad_normed = grad_normed.reshape(rows, model_width)
        grad_norm_one, d_gain_one, d_shift_one = normalize_back(
            grad_normed, unit_one, spread_one, gain_rows[0]
        )
        grad_in = (grad_middle + grad_norm_one).astype(jnp.bfloat16)
        if not last:
            return grad_in, extra
        *pieces, joined_sums = qkv_grads(numbers, own, other, grad_joined, fsdp_count)
        joined_sums = joined_sums[0]
        qkv_share = sum_pieces(pieces, "fsdp")
        share, qkv_share = lax.optimization_barrier((share, qkv_share))
        x_count = lax.axis_size("x")
        piece_rows = shard // x_count
        x_pieces = [
            lax.dynamic_slice_in_dim(
                qkv_share, (lax.axis_index("x") + shift) % x_count * piece_rows, piece_rows, 0
            )
            for shift in range(x_count)
        ]
        qkv_piece = sum_pieces(x_pieces, "x")
        vectors = jnp.stack([d_gain_one, sums[0], d_shift_one, sums[2], sums[1], sums[3]])
        d_up_bias = up_sums.reshape(-1)
        return grad_in, share, qkv_piece, joined_sums, vectors, d_up_bias

    forward_pairs = [(i, i + 1) for i in range(sections - 1)]
    entering = fresh
    for _ in range(sections - 1):
        result, _ = forward(entering)
        received = lax.ppermute(result, "section", forward_pairs)
        entering = jnp.where(section_id == 0, fresh, received)
    layer_out, saved = forward(entering)

    back_pairs = [(i + 1, i) for i in range(sections - 1)]
    grad_low = top_grad
    for _ in range(sections - 1):
        result, kept = backward(grad_low, saved, None)
        received = lax.ppermute(result, "section", back_pairs)
        grad_low = jnp.where(section_id == sections - 1, top_grad, received)
        kept = [(value, swap(value)) for value in kept]
        grad_low, kept = lax.optimization_barrier((grad_low, kept))
    input_grad, share, qkv_piece, joined_sums, vectors, d_up_bias = backward(grad_low, saved, kept)

    ours = jnp.arange(fsdp_count)[:, None] == group_id
    vector_parts = jnp.concatenate(
        [
            vectors.reshape(6, -1, shard).transpose(1, 0, 2).reshape(-1, 6 * shard),
            jnp.where(ours, joined_sums[None, :WIDTH], 0.0),
            jnp.where(ours, joined_sums[None, 2 * WIDTH :], 0.0),
            d_up_bias.reshape(fsdp_count, -1),
        ],
        1,
    )
    vector_parts = vector_parts.astype(jnp.bfloat16).reshape(fsdp_count, 4, 3 * WIDTH)
    vector_share = sum_low(exchange(vector_parts, "fsdp"))
    vector_share = jnp.pad(vector_share, ((0, 12), (0, 0)))
    qkv_piece = jnp.concatenate([qkv_piece, vector_share], 0)
    qkv_piece = jnp.pad(qkv_piece, ((0, 0), (0, model_width - 3 * WIDTH)))
    joint_piece = sum_low(exchange(share.reshape(8, -1, model_width), ("x", "yh")))
    joint_piece, layer_out = lax.optimization_barrier((joint_piece, layer_out))
    both = spread(jnp.concatenate([joint_piece, qkv_piece], 0), ("x", "yh"))
    g_qkv, g_out, g_up, g_down, vector_sum = unpack(
        core_number, both, swap(both), shard, mlp_in.shape[2], mlp_out.shape[1]
    )
    vector_sum = vector_sum[:, : 3 * WIDTH].reshape(-1)
    own_vectors = vector_sum[: 8 * shard].reshape(8, shard)
    own_up_bias = vector_sum[8 * shard :]
    order = (2, 6, 7, 3, 4, 5)
    g_biases = jnp.stack([own_vectors[place] for place in order])
    out_shape = (1, micro_count, 1, local_rows, model_width)
    return (
        layer_out.reshape(out_shape),
        input_grad.reshape(out_shape),
        g_qkv[None],
        g_out[None],
        g_up[None],
        g_down[None],
        own_vectors[None, :2],
        g_biases[None],
        own_up_bias[None],
    )


def solution(mesh):
    fine = Mesh(
        mesh.devices.reshape(2, 4, 2, 2, 4), ("section", "x", "yh", "core", "fsdp")
    )
    rows = P(None, "fsdp", CTX, None)
    weight = P("section", "fsdp", None)
    vector = P("section", None, "fsdp")
    row = P("section", "fsdp")
    out_rows = P("section", None, "fsdp", CTX, None)
    return jax.shard_map(
        shards,
        mesh=fine,
        in_specs=(rows, rows, P(), P(), weight, weight, weight, weight, vector, vector, row),
        out_specs=(out_rows, out_rows, weight, weight, weight, weight, vector, vector, row),
        check_vma=False,
    )
```

```python
import functools

import jax
import jax.numpy as jnp
from jax import lax
from jax.experimental import pallas as pl
from jax.experimental.pallas import tpu as pltpu
from jax.sharding import Mesh
from jax.sharding import PartitionSpec as P

HEADS = 12
HDIM = 64
GROUPS = 4
GROUP_HEADS = HEADS // GROUPS
WIDTH = GROUP_HEADS * HDIM
QUERY_BLOCK = 256
EXTRA = 32
JOINT_ROWS = 112
CTX = ("x", "yh", "core")

epsilon = 1e-05
neg_fill = -1e30
GELU_SCALE = (2.0 / 3.141592653589793) ** 0.5
GELU_CUBE = 0.044715


def dot(left_side, right_side, left_dim, right_dim):
    return lax.dot_general(
        left_side,
        right_side,
        (((left_dim,), (right_dim,)), ((), ())),
        preferred_element_type=jnp.float32,
    )


def head_columns(part, head):
    start = part * WIDTH + head * HDIM
    return slice(start, start + HDIM)


def whole(*shape):
    return pl.BlockSpec(shape, lambda i, *unused: (0,) * len(shape))


def sort_rows(target, source, table, back):
    blocks = table.shape[0]
    size = source.shape[0] // blocks
    for block in range(blocks):
        fixed = slice(block * size, (block + 1) * size)
        moved = pl.ds(pl.multiple_of(table[block] * size, size), size)
        if back:
            target[fixed, :] = source[moved, :]
        else:
            target[moved, :] = source[fixed, :]


def place_weight(target, members, ids):
    count, rows = len(members), members[0].shape[0]
    for shift, member in enumerate(members):
        place = lax.rem(ids[1] + shift - 2 * ids[0] + count, count)
        target[pl.ds(pl.multiple_of(place * rows, rows), rows), :] = member[...]


def mask_scores(scores):
    count = scores.shape[0] - QUERY_BLOCK
    tile = (QUERY_BLOCK, QUERY_BLOCK)
    visible = lax.broadcasted_iota(jnp.int32, tile, 0) <= lax.broadcasted_iota(jnp.int32, tile, 1)
    masked = jnp.where(visible, scores[count:], neg_fill)
    return jnp.concatenate([scores[:count], masked], 0) if count else masked


def attend_body(
    table, ids, own, other, w0, w1, w2, w3, bias, joined, mixed, log_total, weight, scratch, sorted_out
):
    step = pl.program_id(0)
    half = own.shape[1]

    @pl.when(step == 0)
    def _():
        place_weight(weight, (w0, w1, w2, w3), ids)
        product = dot(own[...], weight[:half, :], 1, 0) + dot(other[...], weight[half:, :], 1, 0)
        scratch[...] = (product + bias[...]).astype(jnp.bfloat16)
        sort_rows(joined, scratch, table, False)

    def block(index):
        rows = slice(index * QUERY_BLOCK, (index + 1) * QUERY_BLOCK)
        seen = slice(0, (index + 1) * QUERY_BLOCK)
        parts = []
        for head in range(GROUP_HEADS):
            queries = joined[rows, head_columns(0, head)] * jnp.bfloat16(HDIM ** (-0.5))
            keys = joined[seen, head_columns(1, head)]
            values = joined[seen, head_columns(2, head)]
            scores = mask_scores(dot(keys, queries, 1, 1))
            top = jnp.max(scores, 0, keepdims=True)
            powers = jnp.exp(scores - top)
            total = jnp.sum(powers, 0, keepdims=True)
            parts.append(dot(values, powers.astype(jnp.bfloat16), 0, 0) / total)
            log_total[head : head + 1, rows] = top + jnp.log(total)
        sorted_out[rows, :] = jnp.concatenate(parts, 0).T.astype(jnp.bfloat16)

    for index in range(own.shape[0] // QUERY_BLOCK):
        pl.when(step == index)(lambda index=index: block(index))

    @pl.when(step == pl.num_programs(0) - 1)
    def _():
        sort_rows(mixed, sorted_out, table, True)


def attend(table, ids, own, other, weights, bias):
    count, half = own.shape
    return pl.pallas_call(
        attend_body,
        grid_spec=pltpu.PrefetchScalarGridSpec(
            num_scalar_prefetch=2,
            grid=(count // QUERY_BLOCK,),
            in_specs=[whole(count, half)] * 2
            + [whole(*weight.shape) for weight in weights]
            + [whole(1, 3 * WIDTH)],
            out_specs=[whole(count, 3 * WIDTH), whole(count, WIDTH), whole(8, count)],
            scratch_shapes=[
                pltpu.VMEM((2 * half, 3 * WIDTH), jnp.bfloat16),
                pltpu.VMEM((count, 3 * WIDTH), jnp.bfloat16),
                pltpu.VMEM((count, WIDTH), jnp.bfloat16),
            ],
        ),
        out_shape=[
            jax.ShapeDtypeStruct((count, 3 * WIDTH), jnp.bfloat16),
            jax.ShapeDtypeStruct((count, WIDTH), jnp.bfloat16),
            jax.ShapeDtypeStruct((8, count), jnp.float32),
        ],
        compiler_params=pltpu.CompilerParams(vmem_limit_bytes=48 << 20),
        cost_estimate=pl.CostEstimate(
            flops=4 * count * count * WIDTH,
            bytes_accessed=8 * count * WIDTH,
            transcendentals=count * count * GROUP_HEADS,
        ),
    )(table, ids, own, other, *weights, bias)


def attend_back_body(
    table,
    ids,
    joined,
    grad_mixed,
    log_total,
    w0,
    w1,
    w2,
    w3,
    grad_joined,
    grad_own,
    grad_other,
    weight,
    sorted_grads,
    sorted_out,
    key_sums,
    value_sums,
):
    step = pl.program_id(0)
    half = grad_own.shape[1]

    @pl.when(step == 0)
    def _():
        place_weight(weight, (w0, w1, w2, w3), ids)
        sort_rows(sorted_grads, grad_mixed, table, False)
        key_sums[...] = jnp.zeros_like(key_sums)
        value_sums[...] = jnp.zeros_like(value_sums)

    def block(index):
        rows = slice(index * QUERY_BLOCK, (index + 1) * QUERY_BLOCK)
        seen = slice(0, (index + 1) * QUERY_BLOCK)
        parts = []
        for head in range(GROUP_HEADS):
            queries = joined[rows, head_columns(0, head)] * jnp.bfloat16(HDIM ** (-0.5))
            keys = joined[seen, head_columns(1, head)]
            values = joined[seen, head_columns(2, head)]
            grads = sorted_grads[rows, head_columns(0, head)]
            scores = mask_scores(dot(keys, queries, 1, 1))
            weights = jnp.exp(scores - log_total[head : head + 1, rows])
            grad_weights = dot(values, grads, 1, 1)
            inner_sum = jnp.sum(weights * grad_weights, 0, keepdims=True)
            grad_scores = (weights * (grad_weights - inner_sum)).astype(jnp.bfloat16)
            value_sums[head, seen, :] += dot(weights.astype(jnp.bfloat16), grads, 1, 0)
            key_sums[head, seen, :] += dot(grad_scores, queries, 1, 0)
            parts.append(dot(keys, grad_scores, 0, 0) * (HDIM ** (-0.5)))
        sorted_out[rows, :WIDTH] = jnp.concatenate(parts, 0).T.astype(jnp.bfloat16)

    for index in range(joined.shape[0] // QUERY_BLOCK):
        pl.when(step == index)(lambda index=index: block(index))

    @pl.when(step == pl.num_programs(0) - 1)
    def _():
        for head in range(GROUP_HEADS):
            sorted_out[:, head_columns(1, head)] = key_sums[head].astype(jnp.bfloat16)
            sorted_out[:, head_columns(2, head)] = value_sums[head].astype(jnp.bfloat16)
        sort_rows(grad_joined, sorted_out, table, True)
        grad_own[...] = dot(grad_joined[...], weight[:half, :], 1, 1).astype(jnp.bfloat16)
        grad_other[...] = dot(grad_joined[...], weight[half:, :], 1, 1).astype(jnp.bfloat16)


def attend_back(table, ids, joined, grad_mixed, log_total, weights):
    count = joined.shape[0]
    half = len(weights) * weights[0].shape[0] // 2
    return pl.pallas_call(
        attend_back_body,
        grid_spec=pltpu.PrefetchScalarGridSpec(
            num_scalar_prefetch=2,
            grid=(count // QUERY_BLOCK,),
            in_specs=[whole(count, 3 * WIDTH), whole(count, WIDTH), whole(8, count)]
            + [whole(*weight.shape) for weight in weights],
            out_specs=[whole(count, 3 * WIDTH), whole(count, half), whole(count, half)],
            scratch_shapes=[
                pltpu.VMEM((2 * half, 3 * WIDTH), jnp.bfloat16),
                pltpu.VMEM((count, WIDTH), jnp.bfloat16),
                pltpu.VMEM((count, 3 * WIDTH), jnp.bfloat16),
                pltpu.VMEM((GROUP_HEADS, count, HDIM), jnp.float32),
                pltpu.VMEM((GROUP_HEADS, count, HDIM), jnp.float32),
            ],
        ),
        out_shape=[
            jax.ShapeDtypeStruct((count, 3 * WIDTH), jnp.bfloat16),
            jax.ShapeDtypeStruct((count, half), jnp.bfloat16),
            jax.ShapeDtypeStruct((count, half), jnp.bfloat16),
        ],
        compiler_params=pltpu.CompilerParams(vmem_limit_bytes=48 << 20),
        cost_estimate=pl.CostEstimate(
            flops=10 * count * count * WIDTH,
            bytes_accessed=16 * count * WIDTH,
            transcendentals=count * count * GROUP_HEADS,
        ),
    )(table, ids, joined, grad_mixed, log_total, *weights)


def weight_grads_body(
    core_id,
    active,
    active_other,
    grad_low,
    grad_low_other,
    normed_two,
    normed_two_other,
    grad_hidden,
    grad_hidden_other,
    mixed,
    mixed_other,
    grad_attn,
    grad_attn_other,
    joint,
):
    down_rows, up_rows = active.shape[1], normed_two.shape[0]
    width = grad_low.shape[1]
    product = dot(active[...], grad_low[...], 0, 0)
    product += dot(active_other[...], grad_low_other[...], 0, 0)
    joint[0, :down_rows, :] = product.astype(jnp.bfloat16)
    place = down_rows
    for panel in range(grad_hidden.shape[1] // width):
        columns = slice(panel * width, (panel + 1) * width)
        product = dot(normed_two[...], grad_hidden[:, columns], 1, 0)
        product += dot(normed_two_other[...], grad_hidden_other[:, columns], 1, 0)
        joint[0, place : place + up_rows, :] = product.astype(jnp.bfloat16)
        place += up_rows
    product = dot(mixed[...], grad_attn[...], 1, 0)
    product += dot(mixed_other[...], grad_attn_other[...], 1, 0)
    joint[0, place : place + up_rows, :] = product.astype(jnp.bfloat16)
    place += up_rows
    joint[0, place:, :] = jnp.zeros_like(joint[0, place:, :])


def weight_grads(core_id, pairs, members):
    rows, hidden_width = pairs[0][0].shape
    width = pairs[1][0].shape[1]
    down_rows, up_rows = hidden_width // members // 2, width // members // 2
    out_rows = 2 * down_rows + up_rows + EXTRA
    flat = pl.BlockSpec((rows, width), lambda i, core: (0, 0))
    tall = pl.BlockSpec((up_rows, rows), lambda i, core: (2 * i + core[0], 0))
    specs = [
        pl.BlockSpec((rows, down_rows), lambda i, core: (0, 2 * i + core[0])),
        flat,
        tall,
        pl.BlockSpec((rows, hidden_width), lambda i, core: (0, 0)),
        tall,
        flat,
    ]
    return pl.pallas_call(
        weight_grads_body,
        grid_spec=pltpu.PrefetchScalarGridSpec(
            num_scalar_prefetch=1,
            grid=(members,),
            in_specs=[spec for spec in specs for _ in range(2)],
            out_specs=pl.BlockSpec((1, out_rows, width), lambda i, core: (i, 0, 0)),
        ),
        out_shape=jax.ShapeDtypeStruct((members, out_rows, width), jnp.bfloat16),
        compiler_params=pltpu.CompilerParams(vmem_limit_bytes=48 << 20),
        cost_estimate=pl.CostEstimate(
            flops=2 * rows * width * (2 * hidden_width + width),
            bytes_accessed=2 * members * out_rows * width,
            transcendentals=0,
        ),
    )(core_id, *[value for pair in pairs for value in pair])


def weight_panel(packed, start):
    members, width = packed.shape[0], packed.shape[2]
    rows = width // members
    return jnp.concatenate([packed[i, start : start + rows, :] for i in range(members)], 0)


def join_groups(mixed, group):
    micro_count = mixed.shape[0] // GROUPS
    return jnp.concatenate([mixed[m * GROUPS + group] for m in range(micro_count)], 0)


def attend_out(mixed, entering, packed, vectors, w_out):
    middle = entering[...].astype(jnp.float32) + vectors[5:6, :]
    for group in range(GROUPS):
        rows = slice(group * WIDTH, (group + 1) * WIDTH)
        middle += dot(join_groups(mixed, group), w_out[rows, :], 1, 0)
    return middle


def feed_forward_body(mixed, entering, packed, vectors, up_bias, result):
    members, width = packed.shape[0], packed.shape[2]
    panels = up_bias.shape[0]
    up_rows = width // members
    down_rows = panels * up_rows
    middle = attend_out(mixed, entering, packed, vectors, weight_panel(packed, 2 * down_rows))
    normed, _, _ = normalize(middle, vectors[1:2, :], vectors[6:7, :])
    normed = normed.astype(jnp.bfloat16)
    parts = []
    for panel in range(panels):
        hidden = dot(normed, weight_panel(packed, down_rows + panel * up_rows), 1, 0)
        hidden = hidden + up_bias[panel : panel + 1, :]
        parts.append(jax.nn.gelu(hidden).astype(jnp.bfloat16))
    active = jnp.concatenate(parts, 1)
    total = middle + vectors[7:8, :]
    for member in range(members):
        columns = slice(member * down_rows, (member + 1) * down_rows)
        total += dot(active[:, columns], packed[member, :down_rows, :], 1, 0)
    result[...] = total.astype(jnp.bfloat16)


def feed_forward(mixed, entering, packed, vectors, up_bias):
    rows, width = entering.shape
    return pl.pallas_call(
        feed_forward_body,
        in_specs=[pl.BlockSpec(memory_space=pltpu.VMEM)] * 5,
        out_specs=pl.BlockSpec(memory_space=pltpu.VMEM),
        out_shape=jax.ShapeDtypeStruct((rows, width), jnp.bfloat16),
        compiler_params=pltpu.CompilerParams(vmem_limit_bytes=48 << 20),
        cost_estimate=pl.CostEstimate(
            flops=18 * rows * width * width,
            bytes_accessed=18 * width * width,
            transcendentals=4 * rows * width,
        ),
    )(mixed, entering, packed, vectors, up_bias)


def feed_back_body(mixed, entering, packed, vectors, up_bias, grad_low, *outs):
    last = len(outs) == 6
    grad_mixed, grad_middle = outs[:2]
    members, width = packed.shape[0], packed.shape[2]
    panels = up_bias.shape[0]
    up_rows = width // members
    down_rows = panels * up_rows
    micro_count = mixed.shape[0] // GROUPS
    local_rows = mixed.shape[1]
    w_out = weight_panel(packed, 2 * down_rows)
    middle = attend_out(mixed, entering, packed, vectors, w_out)
    normed, unit, spread_two = normalize(middle, vectors[1:2, :], vectors[6:7, :])
    normed = normed.astype(jnp.bfloat16)
    grads = grad_low[...]
    grad_normed = jnp.zeros(middle.shape, jnp.float32)
    per_panel = members // panels
    for panel in range(panels):
        columns = slice(panel * width, (panel + 1) * width)
        w_up = weight_panel(packed, down_rows + panel * up_rows)
        hidden = dot(normed, w_up, 1, 0) + up_bias[panel : panel + 1, :]
        square = hidden * hidden
        bend = jnp.tanh(GELU_SCALE * (hidden + GELU_CUBE * (square * hidden)))
        slope = 0.5 * (1.0 + bend) + 0.5 * hidden * (1.0 - bend * bend) * (
            GELU_SCALE * (1.0 + 3.0 * GELU_CUBE * square)
        )
        w_down = jnp.concatenate(
            [packed[i, :down_rows, :] for i in range(panel * per_panel, (panel + 1) * per_panel)],
            0,
        )
        grad_hidden = (dot(grads, w_down, 1, 1) * slope).astype(jnp.bfloat16)
        grad_normed += dot(grad_hidden, w_up, 1, 1)
        if last:
            outs[2][:, columns] = grad_hidden
            outs[5][panel : panel + 1, :] = jnp.sum(
                grad_hidden.astype(jnp.float32), 0, keepdims=True
            )
        else:
            outs[2][:, columns] = (0.5 * hidden * (1.0 + bend)).astype(jnp.bfloat16)
    grad_top = grads.astype(jnp.float32)
    grad_norm, d_gain, d_shift = normalize_back(grad_normed, unit, spread_two, vectors[1:2, :])
    grad_sum = grad_top + grad_norm
    grad_middle[...] = grad_sum
    grad_attn = grad_sum.astype(jnp.bfloat16)
    for group in range(GROUPS):
        part = dot(grad_attn, w_out[group * WIDTH : (group + 1) * WIDTH, :], 1, 1)
        part = part.astype(jnp.bfloat16)
        for m in range(micro_count):
            grad_mixed[m * GROUPS + group] = part[m * local_rows : (m + 1) * local_rows]
    if last:
        outs[3][...] = grad_attn
        sums = outs[4]
        sums[0:1, :] = d_gain[None]
        sums[1:2, :] = d_shift[None]
        sums[2:3, :] = jnp.sum(grad_attn.astype(jnp.float32), 0, keepdims=True)
        sums[3:4, :] = jnp.sum(grad_top, 0, keepdims=True)
    else:
        outs[3][...] = normed.astype(jnp.float32).T.astype(jnp.bfloat16)
        for group in range(GROUPS):
            part = join_groups(mixed, group).astype(jnp.float32).T.astype(jnp.bfloat16)
            outs[4][group * WIDTH : (group + 1) * WIDTH, :] = part


def feed_back(mixed, entering, packed, vectors, up_bias, grad_low, last):
    rows, width = entering.shape
    hidden_width = up_bias.size
    shapes = [(mixed.shape, jnp.bfloat16), ((rows, width), jnp.float32)]
    shapes.append(((rows, hidden_width), jnp.bfloat16))
    if last:
        shapes.append(((rows, width), jnp.bfloat16))
        shapes += [((4, width), jnp.float32), (up_bias.shape, jnp.float32)]
    else:
        shapes += [((width, rows), jnp.bfloat16)] * 2
    return pl.pallas_call(
        feed_back_body,
        in_specs=[pl.BlockSpec(memory_space=pltpu.VMEM)] * 6,
        out_specs=[pl.BlockSpec(memory_space=pltpu.VMEM)] * len(shapes),
        out_shape=[jax.ShapeDtypeStruct(*shape) for shape in shapes],
        compiler_params=pltpu.CompilerParams(vmem_limit_bytes=56 << 20),
        cost_estimate=pl.CostEstimate(
            flops=28 * rows * width * width,
            bytes_accessed=24 * width * width,
            transcendentals=4 * rows * width,
        ),
    )(mixed, entering, packed, vectors, up_bias, grad_low)


def qkv_grads_body(owners, ids, own, other, grad_joined, *outs):
    pieces, sums, both = outs[:-2], outs[-2], outs[-1]
    first_core = ids[0] == 0
    grads = grad_joined[...]
    half = own.shape[1]
    own_grads = dot(own[...], grads, 0, 0).astype(jnp.bfloat16)
    other_grads = dot(other[...], grads, 0, 0).astype(jnp.bfloat16)
    both[:half, :] = jnp.where(first_core, own_grads, other_grads)
    both[half:, :] = jnp.where(first_core, other_grads, own_grads)
    count = len(pieces)
    rows = pieces[0].shape[0] // owners
    for shift in range(count):
        place = lax.rem(ids[2] + shift, count) * rows
        for owner in range(owners):
            start = pl.multiple_of(owner * rows * count + place, rows)
            pieces[shift][owner * rows : (owner + 1) * rows, :] = both[pl.ds(start, rows), :]
    sums[...] = jnp.sum(grads.astype(jnp.float32), 0, keepdims=True)


def qkv_grads(ids, own, other, grad_joined, count, owners):
    rows, half = own.shape
    width = grad_joined.shape[1]
    piece = jax.ShapeDtypeStruct((2 * half // count, width), jnp.bfloat16)
    return pl.pallas_call(
        functools.partial(qkv_grads_body, owners),
        in_specs=[pl.BlockSpec(memory_space=pltpu.SMEM)]
        + [pl.BlockSpec(memory_space=pltpu.VMEM)] * 3,
        out_specs=[pl.BlockSpec(memory_space=pltpu.VMEM)] * (count + 1),
        out_shape=[piece] * count + [jax.ShapeDtypeStruct((1, width), jnp.float32)],
        scratch_shapes=[pltpu.VMEM((2 * half, width), jnp.bfloat16)],
        compiler_params=pltpu.CompilerParams(vmem_limit_bytes=48 << 20),
        cost_estimate=pl.CostEstimate(
            flops=4 * rows * half * width, bytes_accessed=6 * rows * half, transcendentals=0
        ),
    )(ids, own, other, grad_joined)


def unpack_body(core_id, own, other, g_qkv, g_out, g_up, g_down, vectors):
    first_core = core_id[0] == 0
    count = own.shape[0]
    width = own.shape[2]
    joint_rows = JOINT_ROWS
    piece_rows = own.shape[1] - joint_rows - 16
    up_rows = g_up.shape[0] // 2
    down_rows = g_down.shape[0] // 2
    sums = jnp.zeros(vectors.shape, jnp.float32)
    for core in range(2):
        pick = first_core if core == 0 else jnp.logical_not(first_core)
        joint = jnp.concatenate(
            [
                jnp.where(pick, own[i, :joint_rows, :], other[i, :joint_rows, :])
                for i in range(count)
            ],
            0,
        ).astype(jnp.float32)
        g_down[core * down_rows : (core + 1) * down_rows, :] = joint[:down_rows]
        place = down_rows
        for panel in range(g_up.shape[1] // width):
            g_up[core * up_rows : (core + 1) * up_rows, panel * width : (panel + 1) * width] = (
                joint[place : place + up_rows]
            )
            place += up_rows
        g_out[core * up_rows : (core + 1) * up_rows, :] = joint[place : place + up_rows]
        for i in range(count):
            x_id, group = i // 2, (i % 2) * 2 + core
            piece = jnp.where(pick, own[i, joint_rows:, :], other[i, joint_rows:, :])
            piece = piece.astype(jnp.float32)
            for part in range(3):
                start = part * width + group * WIDTH
                g_qkv[x_id * piece_rows : (x_id + 1) * piece_rows, start : start + WIDTH] = piece[
                    :piece_rows, part * WIDTH : (part + 1) * WIDTH
                ]
            sums += piece[piece_rows : piece_rows + 4, :]
    vectors[...] = sums


def unpack(core_id, own, other, shard, hidden_width, hidden_shard):
    width = own.shape[2]
    return pl.pallas_call(
        unpack_body,
        in_specs=[pl.BlockSpec(memory_space=pltpu.SMEM)]
        + [pl.BlockSpec(memory_space=pltpu.VMEM)] * 2,
        out_specs=[pl.BlockSpec(memory_space=pltpu.VMEM)] * 5,
        out_shape=[
            jax.ShapeDtypeStruct((shard, 3 * width), jnp.float32),
            jax.ShapeDtypeStruct((shard, width), jnp.float32),
            jax.ShapeDtypeStruct((shard, hidden_width), jnp.float32),
            jax.ShapeDtypeStruct((hidden_shard, width), jnp.float32),
            jax.ShapeDtypeStruct((4, width), jnp.float32),
        ],
        compiler_params=pltpu.CompilerParams(vmem_limit_bytes=48 << 20),
        cost_estimate=pl.CostEstimate(flops=0, bytes_accessed=12 << 20, transcendentals=0),
    )(core_id, own, other)


def normalize(values, gain_row, shift_row):
    center = values - jnp.mean(values, -1, keepdims=True)
    spread = lax.rsqrt(jnp.mean(center * center, -1, keepdims=True) + epsilon)
    unit_rows = center * spread
    return (unit_rows * gain_row + shift_row, unit_rows, spread)


def normalize_back(grad_out, unit_rows, spread, gain_row):
    grad_unit = grad_out * gain_row
    grad_in = spread * (
        grad_unit
        - jnp.mean(grad_unit, -1, keepdims=True)
        - unit_rows * jnp.mean(grad_unit * unit_rows, -1, keepdims=True)
    )
    return (grad_in, jnp.sum(grad_out * unit_rows, 0), jnp.sum(grad_out, 0))


def exchange(value, axes):
    return lax.all_to_all(value, axes, 0, 0, tiled=True)


def swap(value):
    return lax.ppermute(value, "core", [(0, 1), (1, 0)])


def in_order(own, other):
    first = lax.axis_index("core") == 0
    return jnp.where(first, own, other), jnp.where(first, other, own)


def pack_weights(attn_out, mlp_in, mlp_out):
    core_id = lax.axis_index("core")
    width = attn_out.shape[2]
    out_half, up_half, down_half = (
        lax.dynamic_slice_in_dim(
            weight[0], core_id * (weight.shape[1] // 2), weight.shape[1] // 2, 0
        )
        for weight in (attn_out, mlp_in, mlp_out)
    )
    panels = [up_half[:, start : start + width] for start in range(0, mlp_in.shape[2], width)]
    return jnp.concatenate([down_half] + panels + [out_half], 0)


def ring_pairs(axis, shift):
    count = lax.axis_size(axis)
    return [(source, (source + shift) % count) for source in range(count)]


def gather_ring(value, axis):
    return [value] + [
        lax.ppermute(value, axis, ring_pairs(axis, -shift))
        for shift in range(1, lax.axis_size(axis))
    ]


def sum_pieces(pieces, axis):
    total = pieces[0].astype(jnp.float32)
    for shift in range(1, len(pieces)):
        received = lax.ppermute(pieces[shift], axis, ring_pairs(axis, shift))
        total = total + received.astype(jnp.float32)
    return total.astype(jnp.bfloat16)


def sum_low(value):
    return jnp.sum(value.astype(jnp.float32), 0).astype(jnp.bfloat16)


def spread(value, axes):
    count = lax.axis_size(axes)
    return exchange(jnp.broadcast_to(value[None], (count,) + value.shape), axes)


def shards(
    inputs,
    cotangent,
    plan,
    block_table,
    attn_in,
    attn_out,
    mlp_in,
    mlp_out,
    norm_gains,
    biases,
    mlp_bias,
):
    shard = norm_gains.shape[2]
    core_id = lax.axis_index("core")
    group_id = lax.axis_index("yh") * 2 + core_id
    fsdp_id = lax.axis_index("fsdp")
    section_id = lax.axis_index("section")
    sections = lax.axis_size("section")
    fsdp_count = lax.axis_size("fsdp")

    small = jnp.concatenate([norm_gains[0], biases[0], mlp_bias.reshape(-1, shard)], 0)
    small = small.reshape(-1, 3 * WIDTH)
    own_columns = lax.dynamic_index_in_dim(
        attn_in[0].reshape(shard, 3, GROUPS, WIDTH), group_id, 2, keepdims=False
    ).reshape(shard, 3 * WIDTH)
    small_all = spread(small, "fsdp").reshape(fsdp_count, -1, shard).astype(jnp.float32)
    w_group = gather_ring(own_columns, "fsdp")
    packed = pack_weights(attn_out, mlp_in, mlp_out)
    packed = lax.all_gather(packed, ("fsdp", "core"), axis=0)
    model_width = attn_out.shape[2]
    half = model_width // 2
    vector_rows = small_all[:, :8].transpose(1, 0, 2).reshape(8, model_width)
    gain_rows, bias_rows = vector_rows[:2], vector_rows[2:]
    up_rows = small_all[:, 8:].reshape(-1, model_width)
    own_bias = lax.dynamic_index_in_dim(small_all, group_id, 0, keepdims=False)
    group_bias = jnp.concatenate([own_bias[3], jnp.zeros_like(own_bias[3]), own_bias[4]])[None]

    micro_count, _, local_rows, _ = inputs.shape
    rows = micro_count * local_rows
    fresh = jnp.stack(
        [lax.dynamic_index_in_dim(inputs, plan[step], 0, keepdims=False) for step in range(micro_count)]
    ).reshape(rows, model_width)
    top_grad = cotangent.reshape(rows, model_width)
    core_number = core_id.astype(jnp.int32)[None]
    numbers = jnp.stack([core_id, fsdp_id, lax.axis_index("x")]).astype(jnp.int32)

    def forward(entering):
        stream = entering.astype(jnp.float32)
        normed, unit_one, spread_one = normalize(stream, gain_rows[0], bias_rows[0])
        halves = normed.astype(jnp.bfloat16).reshape(micro_count, 1, local_rows, 2, half)
        halves = jnp.broadcast_to(
            halves.transpose(0, 1, 3, 2, 4), (micro_count, 2, 2, local_rows, half)
        )
        own = exchange(halves.reshape(-1, local_rows, half), CTX).reshape(-1, half)
        own, weights = lax.optimization_barrier((own, w_group))
        other = swap(own)
        joined, mixed_heads, log_total = attend(
            block_table, numbers, own, other, weights, group_bias
        )
        mixed = exchange(mixed_heads.reshape(-1, local_rows, WIDTH), CTX)
        result = feed_forward(mixed, entering, packed, vector_rows, up_rows)
        return result, (entering, unit_one, spread_one, own, other, joined, log_total, mixed)

    def backward(grad_low, saved, kept):
        entering, unit_one, spread_one, own, other, joined, log_total, mixed = saved
        last = kept is not None
        grad_mixed, grad_middle, *extra = feed_back(
            mixed, entering, packed, vector_rows, up_rows, grad_low, last
        )
        grad_heads = exchange(grad_mixed.reshape(-1, local_rows, WIDTH), CTX).reshape(-1, WIDTH)
        if last:
            grad_hidden, grad_attn, sums, up_sums = extra
            active_pair, normed_pair, mixed_pair = kept
            low_pair, hidden_pair, attn_pair = (
                (value, swap(value)) for value in (grad_low, grad_hidden, grad_attn)
            )
            joint = weight_grads(
                core_number,
                [active_pair, low_pair, normed_pair, hidden_pair, mixed_pair, attn_pair],
                fsdp_count,
            )
            grad_heads, joint = lax.optimization_barrier((grad_heads, joint))
            share = lax.psum_scatter(
                joint.reshape(-1, model_width),
                "fsdp",
                scatter_dimension=0,
                tiled=True,
            )
        grad_joined, grad_own, grad_other = attend_back(
            block_table, numbers, joined, grad_heads, log_total, w_group
        )
        received = swap(grad_other)
        summed = (grad_own.astype(jnp.float32) + received.astype(jnp.float32)).astype(jnp.bfloat16)
        returned = exchange(summed.reshape(-1, local_rows, half), CTX)
        returned = returned.reshape(micro_count, 2, 2, local_rows, half).astype(jnp.float32)
        grad_normed = (returned[:, 0] + returned[:, 1]).transpose(0, 2, 1, 3)
        grad_normed = grad_normed.reshape(rows, model_width)
        grad_norm_one, d_gain_one, d_shift_one = normalize_back(
            grad_normed, unit_one, spread_one, gain_rows[0]
        )
        grad_in = (grad_middle + grad_norm_one).astype(jnp.bfloat16)
        if not last:
            return grad_in, extra
        x_count = lax.axis_size("x")
        *pieces, joined_sums = qkv_grads(numbers, own, other, grad_joined, x_count, fsdp_count)
        joined_sums = joined_sums[0]
        qkv_share = sum_pieces(pieces, "x")
        share, qkv_share = lax.optimization_barrier((share, qkv_share))
        piece_rows = shard // x_count
        owner_pieces = [
            lax.dynamic_slice_in_dim(
                qkv_share, (fsdp_id + shift) % fsdp_count * piece_rows, piece_rows, 0
            )
            for shift in range(fsdp_count)
        ]
        qkv_piece = sum_pieces(owner_pieces, "fsdp")
        vectors = jnp.stack([d_gain_one, sums[0], d_shift_one, sums[2], sums[1], sums[3]])
        d_up_bias = up_sums.reshape(-1)
        return grad_in, share, qkv_piece, joined_sums, vectors, d_up_bias

    forward_pairs = [(i, i + 1) for i in range(sections - 1)]
    entering = fresh
    for _ in range(sections - 1):
        result, _ = forward(entering)
        received = lax.ppermute(result, "section", forward_pairs)
        entering = jnp.where(section_id == 0, fresh, received)
    layer_out, saved = forward(entering)

    back_pairs = [(i + 1, i) for i in range(sections - 1)]
    grad_low = top_grad
    for _ in range(sections - 1):
        result, kept = backward(grad_low, saved, None)
        received = lax.ppermute(result, "section", back_pairs)
        grad_low = jnp.where(section_id == sections - 1, top_grad, received)
        kept = [(value, swap(value)) for value in kept]
        grad_low, kept = lax.optimization_barrier((grad_low, kept))
    input_grad, share, qkv_piece, joined_sums, vectors, d_up_bias = backward(grad_low, saved, kept)

    ours = jnp.arange(fsdp_count)[:, None] == group_id
    vector_parts = jnp.concatenate(
        [
            vectors.reshape(6, -1, shard).transpose(1, 0, 2).reshape(-1, 6 * shard),
            jnp.where(ours, joined_sums[None, :WIDTH], 0.0),
            jnp.where(ours, joined_sums[None, 2 * WIDTH :], 0.0),
            d_up_bias.reshape(fsdp_count, -1),
        ],
        1,
    )
    vector_parts = vector_parts.astype(jnp.bfloat16).reshape(fsdp_count, 4, 3 * WIDTH)
    vector_share = sum_low(exchange(vector_parts, "fsdp"))
    vector_share = jnp.pad(vector_share, ((0, 12), (0, 0)))
    qkv_piece = jnp.concatenate([qkv_piece, vector_share], 0)
    qkv_piece = jnp.pad(qkv_piece, ((0, 0), (0, model_width - 3 * WIDTH)))
    joint_piece = sum_low(exchange(share.reshape(8, -1, model_width), ("x", "yh")))
    joint_piece, layer_out = lax.optimization_barrier((joint_piece, layer_out))
    both = spread(jnp.concatenate([joint_piece, qkv_piece], 0), ("x", "yh"))
    g_qkv, g_out, g_up, g_down, vector_sum = unpack(
        core_number, both, swap(both), shard, mlp_in.shape[2], mlp_out.shape[1]
    )
    vector_sum = vector_sum[:, : 3 * WIDTH].reshape(-1)
    own_vectors = vector_sum[: 8 * shard].reshape(8, shard)
    own_up_bias = vector_sum[8 * shard :]
    order = (2, 6, 7, 3, 4, 5)
    g_biases = jnp.stack([own_vectors[place] for place in order])
    out_shape = (1, micro_count, 1, local_rows, model_width)
    return (
        layer_out.reshape(out_shape),
        input_grad.reshape(out_shape),
        g_qkv[None],
        g_out[None],
        g_up[None],
        g_down[None],
        own_vectors[None, :2],
        g_biases[None],
        own_up_bias[None],
    )


def solution(mesh):
    fine = Mesh(
        mesh.devices.reshape(2, 4, 2, 2, 4), ("section", "x", "yh", "core", "fsdp")
    )
    rows = P(None, "fsdp", CTX, None)
    weight = P("section", "fsdp", None)
    vector = P("section", None, "fsdp")
    row = P("section", "fsdp")
    out_rows = P("section", None, "fsdp", CTX, None)
    return jax.shard_map(
        shards,
        mesh=fine,
        in_specs=(rows, rows, P(), P(), weight, weight, weight, weight, vector, vector, row),
        out_specs=(out_rows, out_rows, weight, weight, weight, weight, vector, vector, row),
        check_vma=False,
    )
```

```python
import functools

import jax
import jax.numpy as jnp
from jax import lax
from jax.experimental import pallas as pl
from jax.experimental.pallas import tpu as pltpu
from jax.sharding import Mesh
from jax.sharding import PartitionSpec as P

HEADS = 12
HDIM = 64
GROUPS = 4
GROUP_HEADS = HEADS // GROUPS
WIDTH = GROUP_HEADS * HDIM
QUERY_BLOCK = 256
EXTRA = 32
JOINT_ROWS = 112
CTX = ("x", "yh", "core")

epsilon = 1e-05
neg_fill = -1e30
GELU_SCALE = (2.0 / 3.141592653589793) ** 0.5
GELU_CUBE = 0.044715


def dot(left_side, right_side, left_dim, right_dim):
    return lax.dot_general(
        left_side,
        right_side,
        (((left_dim,), (right_dim,)), ((), ())),
        preferred_element_type=jnp.float32,
    )


def head_columns(part, head):
    start = part * WIDTH + head * HDIM
    return slice(start, start + HDIM)


def whole(*shape):
    return pl.BlockSpec(shape, lambda i, *unused: (0,) * len(shape))


def sort_rows(target, source, table, back):
    blocks = table.shape[0]
    size = source.shape[0] // blocks
    for block in range(blocks):
        fixed = slice(block * size, (block + 1) * size)
        moved = pl.ds(pl.multiple_of(table[block] * size, size), size)
        if back:
            target[fixed, :] = source[moved, :]
        else:
            target[moved, :] = source[fixed, :]


def place_weight(target, members, ids):
    count, rows = len(members), members[0].shape[0]
    for shift, member in enumerate(members):
        place = lax.rem(ids[1] + shift - 2 * ids[0] + count, count)
        target[pl.ds(pl.multiple_of(place * rows, rows), rows), :] = member[...]


def mask_scores(scores):
    count = scores.shape[0] - QUERY_BLOCK
    tile = (QUERY_BLOCK, QUERY_BLOCK)
    visible = lax.broadcasted_iota(jnp.int32, tile, 0) <= lax.broadcasted_iota(jnp.int32, tile, 1)
    masked = jnp.where(visible, scores[count:], neg_fill)
    return jnp.concatenate([scores[:count], masked], 0) if count else masked


def attend_body(
    table, ids, own, other, w0, w1, w2, w3, bias, joined, mixed, log_total, weight, scratch, sorted_out
):
    step = pl.program_id(0)
    half = own.shape[1]

    @pl.when(step == 0)
    def _():
        place_weight(weight, (w0, w1, w2, w3), ids)
        product = dot(own[...], weight[:half, :], 1, 0) + dot(other[...], weight[half:, :], 1, 0)
        scratch[...] = (product + bias[...]).astype(jnp.bfloat16)
        sort_rows(joined, scratch, table, False)

    def block(index):
        rows = slice(index * QUERY_BLOCK, (index + 1) * QUERY_BLOCK)
        seen = slice(0, (index + 1) * QUERY_BLOCK)
        parts = []
        for head in range(GROUP_HEADS):
            queries = joined[rows, head_columns(0, head)] * jnp.bfloat16(HDIM ** (-0.5))
            keys = joined[seen, head_columns(1, head)]
            values = joined[seen, head_columns(2, head)]
            scores = mask_scores(dot(keys, queries, 1, 1))
            top = jnp.max(scores, 0, keepdims=True)
            powers = jnp.exp(scores - top)
            total = jnp.sum(powers, 0, keepdims=True)
            parts.append(dot(values, powers.astype(jnp.bfloat16), 0, 0) / total)
            log_total[head : head + 1, rows] = top + jnp.log(total)
        sorted_out[rows, :] = jnp.concatenate(parts, 0).T.astype(jnp.bfloat16)

    for index in range(own.shape[0] // QUERY_BLOCK):
        pl.when(step == index)(lambda index=index: block(index))

    @pl.when(step == pl.num_programs(0) - 1)
    def _():
        sort_rows(mixed, sorted_out, table, True)


def attend(table, ids, own, other, weights, bias):
    count, half = own.shape
    return pl.pallas_call(
        attend_body,
        grid_spec=pltpu.PrefetchScalarGridSpec(
            num_scalar_prefetch=2,
            grid=(count // QUERY_BLOCK,),
            in_specs=[whole(count, half)] * 2
            + [whole(*weight.shape) for weight in weights]
            + [whole(1, 3 * WIDTH)],
            out_specs=[whole(count, 3 * WIDTH), whole(count, WIDTH), whole(8, count)],
            scratch_shapes=[
                pltpu.VMEM((2 * half, 3 * WIDTH), jnp.bfloat16),
                pltpu.VMEM((count, 3 * WIDTH), jnp.bfloat16),
                pltpu.VMEM((count, WIDTH), jnp.bfloat16),
            ],
        ),
        out_shape=[
            jax.ShapeDtypeStruct((count, 3 * WIDTH), jnp.bfloat16),
            jax.ShapeDtypeStruct((count, WIDTH), jnp.bfloat16),
            jax.ShapeDtypeStruct((8, count), jnp.float32),
        ],
        compiler_params=pltpu.CompilerParams(vmem_limit_bytes=48 << 20),
        cost_estimate=pl.CostEstimate(
            flops=4 * count * count * WIDTH,
            bytes_accessed=8 * count * WIDTH,
            transcendentals=count * count * GROUP_HEADS,
        ),
    )(table, ids, own, other, *weights, bias)


def attend_back_body(
    table,
    ids,
    joined,
    grad_mixed,
    log_total,
    w0,
    w1,
    w2,
    w3,
    grad_joined,
    grad_own,
    grad_other,
    weight,
    sorted_grads,
    sorted_out,
    key_sums,
    value_sums,
):
    step = pl.program_id(0)
    half = grad_own.shape[1]

    @pl.when(step == 0)
    def _():
        place_weight(weight, (w0, w1, w2, w3), ids)
        sort_rows(sorted_grads, grad_mixed, table, False)
        key_sums[...] = jnp.zeros_like(key_sums)
        value_sums[...] = jnp.zeros_like(value_sums)

    def block(index):
        rows = slice(index * QUERY_BLOCK, (index + 1) * QUERY_BLOCK)
        seen = slice(0, (index + 1) * QUERY_BLOCK)
        parts = []
        for head in range(GROUP_HEADS):
            queries = joined[rows, head_columns(0, head)] * jnp.bfloat16(HDIM ** (-0.5))
            keys = joined[seen, head_columns(1, head)]
            values = joined[seen, head_columns(2, head)]
            grads = sorted_grads[rows, head_columns(0, head)]
            scores = mask_scores(dot(keys, queries, 1, 1))
            weights = jnp.exp(scores - log_total[head : head + 1, rows])
            grad_weights = dot(values, grads, 1, 1)
            inner_sum = jnp.sum(weights * grad_weights, 0, keepdims=True)
            grad_scores = (weights * (grad_weights - inner_sum)).astype(jnp.bfloat16)
            value_sums[head, seen, :] += dot(weights.astype(jnp.bfloat16), grads, 1, 0)
            key_sums[head, seen, :] += dot(grad_scores, queries, 1, 0)
            parts.append(dot(keys, grad_scores, 0, 0) * (HDIM ** (-0.5)))
        sorted_out[rows, :WIDTH] = jnp.concatenate(parts, 0).T.astype(jnp.bfloat16)

    for index in range(joined.shape[0] // QUERY_BLOCK):
        pl.when(step == index)(lambda index=index: block(index))

    @pl.when(step == pl.num_programs(0) - 1)
    def _():
        for head in range(GROUP_HEADS):
            sorted_out[:, head_columns(1, head)] = key_sums[head].astype(jnp.bfloat16)
            sorted_out[:, head_columns(2, head)] = value_sums[head].astype(jnp.bfloat16)
        sort_rows(grad_joined, sorted_out, table, True)
        grad_own[...] = dot(grad_joined[...], weight[:half, :], 1, 1).astype(jnp.bfloat16)
        grad_other[...] = dot(grad_joined[...], weight[half:, :], 1, 1).astype(jnp.bfloat16)


def attend_back(table, ids, joined, grad_mixed, log_total, weights):
    count = joined.shape[0]
    half = len(weights) * weights[0].shape[0] // 2
    return pl.pallas_call(
        attend_back_body,
        grid_spec=pltpu.PrefetchScalarGridSpec(
            num_scalar_prefetch=2,
            grid=(count // QUERY_BLOCK,),
            in_specs=[whole(count, 3 * WIDTH), whole(count, WIDTH), whole(8, count)]
            + [whole(*weight.shape) for weight in weights],
            out_specs=[whole(count, 3 * WIDTH), whole(count, half), whole(count, half)],
            scratch_shapes=[
                pltpu.VMEM((2 * half, 3 * WIDTH), jnp.bfloat16),
                pltpu.VMEM((count, WIDTH), jnp.bfloat16),
                pltpu.VMEM((count, 3 * WIDTH), jnp.bfloat16),
                pltpu.VMEM((GROUP_HEADS, count, HDIM), jnp.float32),
                pltpu.VMEM((GROUP_HEADS, count, HDIM), jnp.float32),
            ],
        ),
        out_shape=[
            jax.ShapeDtypeStruct((count, 3 * WIDTH), jnp.bfloat16),
            jax.ShapeDtypeStruct((count, half), jnp.bfloat16),
            jax.ShapeDtypeStruct((count, half), jnp.bfloat16),
        ],
        compiler_params=pltpu.CompilerParams(vmem_limit_bytes=48 << 20),
        cost_estimate=pl.CostEstimate(
            flops=10 * count * count * WIDTH,
            bytes_accessed=16 * count * WIDTH,
            transcendentals=count * count * GROUP_HEADS,
        ),
    )(table, ids, joined, grad_mixed, log_total, *weights)


def weight_grads_body(
    core_id,
    active,
    active_other,
    grad_low,
    grad_low_other,
    normed_two,
    normed_two_other,
    grad_hidden,
    grad_hidden_other,
    mixed,
    mixed_other,
    grad_attn,
    grad_attn_other,
    joint,
):
    down_rows, up_rows = active.shape[1], normed_two.shape[0]
    width = grad_low.shape[1]
    product = dot(active[...], grad_low[...], 0, 0)
    product += dot(active_other[...], grad_low_other[...], 0, 0)
    joint[0, :down_rows, :] = product.astype(jnp.bfloat16)
    place = down_rows
    for panel in range(grad_hidden.shape[1] // width):
        columns = slice(panel * width, (panel + 1) * width)
        product = dot(normed_two[...], grad_hidden[:, columns], 1, 0)
        product += dot(normed_two_other[...], grad_hidden_other[:, columns], 1, 0)
        joint[0, place : place + up_rows, :] = product.astype(jnp.bfloat16)
        place += up_rows
    product = dot(mixed[...], grad_attn[...], 1, 0)
    product += dot(mixed_other[...], grad_attn_other[...], 1, 0)
    joint[0, place : place + up_rows, :] = product.astype(jnp.bfloat16)
    place += up_rows
    joint[0, place:, :] = jnp.zeros_like(joint[0, place:, :])


def weight_grads(core_id, pairs, members):
    rows, hidden_width = pairs[0][0].shape
    width = pairs[1][0].shape[1]
    down_rows, up_rows = hidden_width // members // 2, width // members // 2
    out_rows = 2 * down_rows + up_rows + EXTRA
    flat = pl.BlockSpec((rows, width), lambda i, core: (0, 0))
    tall = pl.BlockSpec((up_rows, rows), lambda i, core: (2 * i + core[0], 0))
    specs = [
        pl.BlockSpec((rows, down_rows), lambda i, core: (0, 2 * i + core[0])),
        flat,
        tall,
        pl.BlockSpec((rows, hidden_width), lambda i, core: (0, 0)),
        tall,
        flat,
    ]
    return pl.pallas_call(
        weight_grads_body,
        grid_spec=pltpu.PrefetchScalarGridSpec(
            num_scalar_prefetch=1,
            grid=(members,),
            in_specs=[spec for spec in specs for _ in range(2)],
            out_specs=pl.BlockSpec((1, out_rows, width), lambda i, core: (i, 0, 0)),
        ),
        out_shape=jax.ShapeDtypeStruct((members, out_rows, width), jnp.bfloat16),
        compiler_params=pltpu.CompilerParams(vmem_limit_bytes=48 << 20),
        cost_estimate=pl.CostEstimate(
            flops=2 * rows * width * (2 * hidden_width + width),
            bytes_accessed=2 * members * out_rows * width,
            transcendentals=0,
        ),
    )(core_id, *[value for pair in pairs for value in pair])


def weight_panel(packed, start):
    members, width = packed.shape[0], packed.shape[2]
    rows = width // members
    return jnp.concatenate([packed[i, start : start + rows, :] for i in range(members)], 0)


def join_groups(mixed, group):
    micro_count = mixed.shape[0] // GROUPS
    return jnp.concatenate([mixed[m * GROUPS + group] for m in range(micro_count)], 0)


def attend_out(mixed, entering, packed, vectors, w_out):
    middle = entering[...].astype(jnp.float32) + vectors[5:6, :]
    for group in range(GROUPS):
        rows = slice(group * WIDTH, (group + 1) * WIDTH)
        middle += dot(join_groups(mixed, group), w_out[rows, :], 1, 0)
    return middle


def start_copies(stored, packed, landed, panels):
    members, width = packed.shape[0], packed.shape[2]
    up_rows = width // members
    down_rows = panels * up_rows
    per_panel = members // panels

    def copy(index, rows, sources):
        here = (slice(None) if sources is None else sources, rows)
        return pltpu.make_async_copy(stored.at[here], packed.at[here], landed.at[index])

    out = copy(0, pl.ds(2 * down_rows, up_rows), None)
    ups, downs = [], []
    for panel in range(panels):
        ups.append(copy(1 + panel, pl.ds(down_rows + panel * up_rows, up_rows), None))
        downs.append(
            copy(1 + panels + panel, pl.ds(0, down_rows), pl.ds(panel * per_panel, per_panel))
        )
    return out, ups, downs


def feed_forward_body(mixed, entering, stored, vectors, up_bias, result, packed, landed):
    members, width = packed.shape[0], packed.shape[2]
    panels = up_bias.shape[0]
    up_rows = width // members
    down_rows = panels * up_rows
    out, ups, downs = start_copies(stored, packed, landed, panels)
    for copy in [out] + ups + downs:
        copy.start()
    out.wait()
    middle = attend_out(mixed, entering, packed, vectors, weight_panel(packed, 2 * down_rows))
    normed, _, _ = normalize(middle, vectors[1:2, :], vectors[6:7, :])
    normed = normed.astype(jnp.bfloat16)
    parts = []
    for panel in range(panels):
        ups[panel].wait()
        hidden = dot(normed, weight_panel(packed, down_rows + panel * up_rows), 1, 0)
        hidden = hidden + up_bias[panel : panel + 1, :]
        parts.append(jax.nn.gelu(hidden).astype(jnp.bfloat16))
    active = jnp.concatenate(parts, 1)
    total = middle + vectors[7:8, :]
    for member in range(members):
        if member % (members // panels) == 0:
            downs[member // (members // panels)].wait()
        columns = slice(member * down_rows, (member + 1) * down_rows)
        total += dot(active[:, columns], packed[member, :down_rows, :], 1, 0)
    result[...] = total.astype(jnp.bfloat16)


def feed_specs(count):
    specs = [pl.BlockSpec(memory_space=pltpu.VMEM) for _ in range(count)]
    specs[2] = pl.BlockSpec(memory_space=pl.ANY)
    return specs


def feed_scratch(packed, up_bias):
    return [
        pltpu.VMEM(packed.shape, packed.dtype),
        pltpu.SemaphoreType.DMA((1 + 2 * up_bias.shape[0],)),
    ]


def feed_forward(mixed, entering, packed, vectors, up_bias):
    rows, width = entering.shape
    return pl.pallas_call(
        feed_forward_body,
        in_specs=feed_specs(5),
        out_specs=pl.BlockSpec(memory_space=pltpu.VMEM),
        scratch_shapes=feed_scratch(packed, up_bias),
        out_shape=jax.ShapeDtypeStruct((rows, width), jnp.bfloat16),
        compiler_params=pltpu.CompilerParams(vmem_limit_bytes=48 << 20),
        cost_estimate=pl.CostEstimate(
            flops=18 * rows * width * width,
            bytes_accessed=18 * width * width,
            transcendentals=4 * rows * width,
        ),
    )(mixed, entering, packed, vectors, up_bias)


def feed_back_body(mixed, entering, stored, vectors, up_bias, grad_low, *outs):
    packed, landed = outs[-2:]
    outs = outs[:-2]
    last = len(outs) == 6
    grad_mixed, grad_middle = outs[:2]
    members, width = packed.shape[0], packed.shape[2]
    panels = up_bias.shape[0]
    up_rows = width // members
    down_rows = panels * up_rows
    micro_count = mixed.shape[0] // GROUPS
    local_rows = mixed.shape[1]
    out, ups, downs = start_copies(stored, packed, landed, panels)
    out.start()
    for panel in range(panels):
        ups[panel].start()
        downs[panel].start()
    out.wait()
    w_out = weight_panel(packed, 2 * down_rows)
    middle = attend_out(mixed, entering, packed, vectors, w_out)
    normed, unit, spread_two = normalize(middle, vectors[1:2, :], vectors[6:7, :])
    normed = normed.astype(jnp.bfloat16)
    grads = grad_low[...]
    grad_normed = jnp.zeros(middle.shape, jnp.float32)
    per_panel = members // panels
    for panel in range(panels):
        columns = slice(panel * width, (panel + 1) * width)
        ups[panel].wait()
        w_up = weight_panel(packed, down_rows + panel * up_rows)
        hidden = dot(normed, w_up, 1, 0) + up_bias[panel : panel + 1, :]
        square = hidden * hidden
        bend = jnp.tanh(GELU_SCALE * (hidden + GELU_CUBE * (square * hidden)))
        slope = 0.5 * (1.0 + bend) + 0.5 * hidden * (1.0 - bend * bend) * (
            GELU_SCALE * (1.0 + 3.0 * GELU_CUBE * square)
        )
        downs[panel].wait()
        w_down = jnp.concatenate(
            [packed[i, :down_rows, :] for i in range(panel * per_panel, (panel + 1) * per_panel)],
            0,
        )
        grad_hidden = (dot(grads, w_down, 1, 1) * slope).astype(jnp.bfloat16)
        grad_normed += dot(grad_hidden, w_up, 1, 1)
        if last:
            outs[2][:, columns] = grad_hidden
            outs[5][panel : panel + 1, :] = jnp.sum(
                grad_hidden.astype(jnp.float32), 0, keepdims=True
            )
        else:
            outs[2][:, columns] = (0.5 * hidden * (1.0 + bend)).astype(jnp.bfloat16)
    grad_top = grads.astype(jnp.float32)
    grad_norm, d_gain, d_shift = normalize_back(grad_normed, unit, spread_two, vectors[1:2, :])
    grad_sum = grad_top + grad_norm
    grad_middle[...] = grad_sum
    grad_attn = grad_sum.astype(jnp.bfloat16)
    for group in range(GROUPS):
        part = dot(grad_attn, w_out[group * WIDTH : (group + 1) * WIDTH, :], 1, 1)
        part = part.astype(jnp.bfloat16)
        for m in range(micro_count):
            grad_mixed[m * GROUPS + group] = part[m * local_rows : (m + 1) * local_rows]
    if last:
        outs[3][...] = grad_attn
        sums = outs[4]
        sums[0:1, :] = d_gain[None]
        sums[1:2, :] = d_shift[None]
        sums[2:3, :] = jnp.sum(grad_attn.astype(jnp.float32), 0, keepdims=True)
        sums[3:4, :] = jnp.sum(grad_top, 0, keepdims=True)
    else:
        outs[3][...] = normed.astype(jnp.float32).T.astype(jnp.bfloat16)
        for group in range(GROUPS):
            part = join_groups(mixed, group).astype(jnp.float32).T.astype(jnp.bfloat16)
            outs[4][group * WIDTH : (group + 1) * WIDTH, :] = part


def feed_back(mixed, entering, packed, vectors, up_bias, grad_low, last):
    rows, width = entering.shape
    hidden_width = up_bias.size
    shapes = [(mixed.shape, jnp.bfloat16), ((rows, width), jnp.float32)]
    shapes.append(((rows, hidden_width), jnp.bfloat16))
    if last:
        shapes.append(((rows, width), jnp.bfloat16))
        shapes += [((4, width), jnp.float32), (up_bias.shape, jnp.float32)]
    else:
        shapes += [((width, rows), jnp.bfloat16)] * 2
    return pl.pallas_call(
        feed_back_body,
        in_specs=feed_specs(6),
        scratch_shapes=feed_scratch(packed, up_bias),
        out_specs=[pl.BlockSpec(memory_space=pltpu.VMEM)] * len(shapes),
        out_shape=[jax.ShapeDtypeStruct(*shape) for shape in shapes],
        compiler_params=pltpu.CompilerParams(vmem_limit_bytes=56 << 20),
        cost_estimate=pl.CostEstimate(
            flops=28 * rows * width * width,
            bytes_accessed=24 * width * width,
            transcendentals=4 * rows * width,
        ),
    )(mixed, entering, packed, vectors, up_bias, grad_low)


def qkv_grads_body(owners, ids, own, other, grad_joined, *outs):
    pieces, sums, both = outs[:-2], outs[-2], outs[-1]
    first_core = ids[0] == 0
    grads = grad_joined[...]
    half = own.shape[1]
    own_grads = dot(own[...], grads, 0, 0).astype(jnp.bfloat16)
    other_grads = dot(other[...], grads, 0, 0).astype(jnp.bfloat16)
    both[:half, :] = jnp.where(first_core, own_grads, other_grads)
    both[half:, :] = jnp.where(first_core, other_grads, own_grads)
    count = len(pieces)
    rows = pieces[0].shape[0] // owners
    for shift in range(count):
        place = lax.rem(ids[2] + shift, count) * rows
        for owner in range(owners):
            start = pl.multiple_of(owner * rows * count + place, rows)
            pieces[shift][owner * rows : (owner + 1) * rows, :] = both[pl.ds(start, rows), :]
    sums[...] = jnp.sum(grads.astype(jnp.float32), 0, keepdims=True)


def qkv_grads(ids, own, other, grad_joined, count, owners):
    rows, half = own.shape
    width = grad_joined.shape[1]
    piece = jax.ShapeDtypeStruct((2 * half // count, width), jnp.bfloat16)
    return pl.pallas_call(
        functools.partial(qkv_grads_body, owners),
        in_specs=[pl.BlockSpec(memory_space=pltpu.SMEM)]
        + [pl.BlockSpec(memory_space=pltpu.VMEM)] * 3,
        out_specs=[pl.BlockSpec(memory_space=pltpu.VMEM)] * (count + 1),
        out_shape=[piece] * count + [jax.ShapeDtypeStruct((1, width), jnp.float32)],
        scratch_shapes=[pltpu.VMEM((2 * half, width), jnp.bfloat16)],
        compiler_params=pltpu.CompilerParams(vmem_limit_bytes=48 << 20),
        cost_estimate=pl.CostEstimate(
            flops=4 * rows * half * width, bytes_accessed=6 * rows * half, transcendentals=0
        ),
    )(ids, own, other, grad_joined)


def unpack_body(core_id, own, other, g_qkv, g_out, g_up, g_down, vectors):
    first_core = core_id[0] == 0
    count = own.shape[0]
    width = own.shape[2]
    joint_rows = JOINT_ROWS
    piece_rows = own.shape[1] - joint_rows - 16
    up_rows = g_up.shape[0] // 2
    down_rows = g_down.shape[0] // 2
    sums = jnp.zeros(vectors.shape, jnp.float32)
    for core in range(2):
        pick = first_core if core == 0 else jnp.logical_not(first_core)
        joint = jnp.concatenate(
            [
                jnp.where(pick, own[i, :joint_rows, :], other[i, :joint_rows, :])
                for i in range(count)
            ],
            0,
        ).astype(jnp.float32)
        g_down[core * down_rows : (core + 1) * down_rows, :] = joint[:down_rows]
        place = down_rows
        for panel in range(g_up.shape[1] // width):
            g_up[core * up_rows : (core + 1) * up_rows, panel * width : (panel + 1) * width] = (
                joint[place : place + up_rows]
            )
            place += up_rows
        g_out[core * up_rows : (core + 1) * up_rows, :] = joint[place : place + up_rows]
        for i in range(count):
            x_id, group = i // 2, (i % 2) * 2 + core
            piece = jnp.where(pick, own[i, joint_rows:, :], other[i, joint_rows:, :])
            piece = piece.astype(jnp.float32)
            for part in range(3):
                start = part * width + group * WIDTH
                g_qkv[x_id * piece_rows : (x_id + 1) * piece_rows, start : start + WIDTH] = piece[
                    :piece_rows, part * WIDTH : (part + 1) * WIDTH
                ]
            sums += piece[piece_rows : piece_rows + 4, :]
    vectors[...] = sums


def unpack(core_id, own, other, shard, hidden_width, hidden_shard):
    width = own.shape[2]
    return pl.pallas_call(
        unpack_body,
        in_specs=[pl.BlockSpec(memory_space=pltpu.SMEM)]
        + [pl.BlockSpec(memory_space=pltpu.VMEM)] * 2,
        out_specs=[pl.BlockSpec(memory_space=pltpu.VMEM)] * 5,
        out_shape=[
            jax.ShapeDtypeStruct((shard, 3 * width), jnp.float32),
            jax.ShapeDtypeStruct((shard, width), jnp.float32),
            jax.ShapeDtypeStruct((shard, hidden_width), jnp.float32),
            jax.ShapeDtypeStruct((hidden_shard, width), jnp.float32),
            jax.ShapeDtypeStruct((4, width), jnp.float32),
        ],
        compiler_params=pltpu.CompilerParams(vmem_limit_bytes=48 << 20),
        cost_estimate=pl.CostEstimate(flops=0, bytes_accessed=12 << 20, transcendentals=0),
    )(core_id, own, other)


def normalize(values, gain_row, shift_row):
    center = values - jnp.mean(values, -1, keepdims=True)
    spread = lax.rsqrt(jnp.mean(center * center, -1, keepdims=True) + epsilon)
    unit_rows = center * spread
    return (unit_rows * gain_row + shift_row, unit_rows, spread)


def normalize_back(grad_out, unit_rows, spread, gain_row):
    grad_unit = grad_out * gain_row
    grad_in = spread * (
        grad_unit
        - jnp.mean(grad_unit, -1, keepdims=True)
        - unit_rows * jnp.mean(grad_unit * unit_rows, -1, keepdims=True)
    )
    return (grad_in, jnp.sum(grad_out * unit_rows, 0), jnp.sum(grad_out, 0))


def exchange(value, axes):
    return lax.all_to_all(value, axes, 0, 0, tiled=True)


def swap(value):
    return lax.ppermute(value, "core", [(0, 1), (1, 0)])


def in_order(own, other):
    first = lax.axis_index("core") == 0
    return jnp.where(first, own, other), jnp.where(first, other, own)


def pack_weights(attn_out, mlp_in, mlp_out):
    core_id = lax.axis_index("core")
    width = attn_out.shape[2]
    out_half, up_half, down_half = (
        lax.dynamic_slice_in_dim(
            weight[0], core_id * (weight.shape[1] // 2), weight.shape[1] // 2, 0
        )
        for weight in (attn_out, mlp_in, mlp_out)
    )
    panels = [up_half[:, start : start + width] for start in range(0, mlp_in.shape[2], width)]
    return jnp.concatenate([down_half] + panels + [out_half], 0)


def ring_pairs(axis, shift):
    count = lax.axis_size(axis)
    return [(source, (source + shift) % count) for source in range(count)]


def gather_ring(value, axis):
    return [value] + [
        lax.ppermute(value, axis, ring_pairs(axis, -shift))
        for shift in range(1, lax.axis_size(axis))
    ]


def sum_pieces(pieces, axis):
    total = pieces[0].astype(jnp.float32)
    for shift in range(1, len(pieces)):
        received = lax.ppermute(pieces[shift], axis, ring_pairs(axis, shift))
        total = total + received.astype(jnp.float32)
    return total.astype(jnp.bfloat16)


def sum_low(value):
    return jnp.sum(value.astype(jnp.float32), 0).astype(jnp.bfloat16)


def spread(value, axes):
    count = lax.axis_size(axes)
    return exchange(jnp.broadcast_to(value[None], (count,) + value.shape), axes)


def shards(
    inputs,
    cotangent,
    plan,
    block_table,
    attn_in,
    attn_out,
    mlp_in,
    mlp_out,
    norm_gains,
    biases,
    mlp_bias,
):
    shard = norm_gains.shape[2]
    core_id = lax.axis_index("core")
    group_id = lax.axis_index("yh") * 2 + core_id
    fsdp_id = lax.axis_index("fsdp")
    section_id = lax.axis_index("section")
    sections = lax.axis_size("section")
    fsdp_count = lax.axis_size("fsdp")

    small = jnp.concatenate([norm_gains[0], biases[0], mlp_bias.reshape(-1, shard)], 0)
    small = small.reshape(-1, 3 * WIDTH)
    own_columns = lax.dynamic_index_in_dim(
        attn_in[0].reshape(shard, 3, GROUPS, WIDTH), group_id, 2, keepdims=False
    ).reshape(shard, 3 * WIDTH)
    small_all = spread(small, "fsdp").reshape(fsdp_count, -1, shard).astype(jnp.float32)
    w_group = gather_ring(own_columns, "fsdp")
    small_all, w_group[1], w_group[3] = lax.optimization_barrier(
        (small_all, w_group[1], w_group[3])
    )
    packed = pack_weights(attn_out, mlp_in, mlp_out)
    packed = lax.all_gather(packed, ("fsdp", "core"), axis=0)
    model_width = attn_out.shape[2]
    half = model_width // 2
    vector_rows = small_all[:, :8].transpose(1, 0, 2).reshape(8, model_width)
    gain_rows, bias_rows = vector_rows[:2], vector_rows[2:]
    up_rows = small_all[:, 8:].reshape(-1, model_width)
    own_bias = lax.dynamic_index_in_dim(small_all, group_id, 0, keepdims=False)
    group_bias = jnp.concatenate([own_bias[3], jnp.zeros_like(own_bias[3]), own_bias[4]])[None]

    micro_count, _, local_rows, _ = inputs.shape
    rows = micro_count * local_rows
    fresh = jnp.stack(
        [lax.dynamic_index_in_dim(inputs, plan[step], 0, keepdims=False) for step in range(micro_count)]
    ).reshape(rows, model_width)
    top_grad = cotangent.reshape(rows, model_width)
    core_number = core_id.astype(jnp.int32)[None]
    numbers = jnp.stack([core_id, fsdp_id, lax.axis_index("x")]).astype(jnp.int32)

    def forward(entering):
        stream = entering.astype(jnp.float32)
        normed, unit_one, spread_one = normalize(stream, gain_rows[0], bias_rows[0])
        halves = normed.astype(jnp.bfloat16).reshape(micro_count, 1, local_rows, 2, half)
        halves = jnp.broadcast_to(
            halves.transpose(0, 1, 3, 2, 4), (micro_count, 2, 2, local_rows, half)
        )
        own = exchange(halves.reshape(-1, local_rows, half), CTX).reshape(-1, half)
        own, weights = lax.optimization_barrier((own, w_group))
        other = swap(own)
        joined, mixed_heads, log_total = attend(
            block_table, numbers, own, other, weights, group_bias
        )
        mixed = exchange(mixed_heads.reshape(-1, local_rows, WIDTH), CTX)
        result = feed_forward(mixed, entering, packed, vector_rows, up_rows)
        return result, (entering, unit_one, spread_one, own, other, joined, log_total, mixed)

    def backward(grad_low, saved, kept):
        entering, unit_one, spread_one, own, other, joined, log_total, mixed = saved
        last = kept is not None
        grad_mixed, grad_middle, *extra = feed_back(
            mixed, entering, packed, vector_rows, up_rows, grad_low, last
        )
        grad_heads = exchange(grad_mixed.reshape(-1, local_rows, WIDTH), CTX).reshape(-1, WIDTH)
        if last:
            grad_hidden, grad_attn, sums, up_sums = extra
            active_pair, normed_pair, mixed_pair = kept
            low_pair, hidden_pair, attn_pair = (
                (value, swap(value)) for value in (grad_low, grad_hidden, grad_attn)
            )
            joint = weight_grads(
                core_number,
                [active_pair, low_pair, normed_pair, hidden_pair, mixed_pair, attn_pair],
                fsdp_count,
            )
            grad_heads, joint = lax.optimization_barrier((grad_heads, joint))
            share = lax.psum_scatter(
                joint.reshape(-1, model_width),
                "fsdp",
                scatter_dimension=0,
                tiled=True,
            )
        grad_joined, grad_own, grad_other = attend_back(
            block_table, numbers, joined, grad_heads, log_total, w_group
        )
        received = swap(grad_other)
        summed = (grad_own.astype(jnp.float32) + received.astype(jnp.float32)).astype(jnp.bfloat16)
        returned = exchange(summed.reshape(-1, local_rows, half), CTX)
        returned = returned.reshape(micro_count, 2, 2, local_rows, half).astype(jnp.float32)
        grad_normed = (returned[:, 0] + returned[:, 1]).transpose(0, 2, 1, 3)
        grad_normed = grad_normed.reshape(rows, model_width)
        grad_norm_one, d_gain_one, d_shift_one = normalize_back(
            grad_normed, unit_one, spread_one, gain_rows[0]
        )
        grad_in = (grad_middle + grad_norm_one).astype(jnp.bfloat16)
        if not last:
            return grad_in, extra
        x_count = lax.axis_size("x")
        *pieces, joined_sums = qkv_grads(numbers, own, other, grad_joined, x_count, fsdp_count)
        joined_sums = joined_sums[0]
        qkv_share = sum_pieces(pieces, "x")
        share, qkv_share = lax.optimization_barrier((share, qkv_share))
        piece_rows = shard // x_count
        owner_pieces = [
            lax.dynamic_slice_in_dim(
                qkv_share, (fsdp_id + shift) % fsdp_count * piece_rows, piece_rows, 0
            )
            for shift in range(fsdp_count)
        ]
        qkv_piece = sum_pieces(owner_pieces, "fsdp")
        vectors = jnp.stack([d_gain_one, sums[0], d_shift_one, sums[2], sums[1], sums[3]])
        d_up_bias = up_sums.reshape(-1)
        return grad_in, share, qkv_piece, joined_sums, vectors, d_up_bias

    forward_pairs = [(i, i + 1) for i in range(sections - 1)]
    entering = fresh
    for _ in range(sections - 1):
        result, _ = forward(entering)
        received = lax.ppermute(result, "section", forward_pairs)
        entering = jnp.where(section_id == 0, fresh, received)
    layer_out, saved = forward(entering)

    back_pairs = [(i + 1, i) for i in range(sections - 1)]
    grad_low = top_grad
    for _ in range(sections - 1):
        result, kept = backward(grad_low, saved, None)
        received = lax.ppermute(result, "section", back_pairs)
        grad_low = jnp.where(section_id == sections - 1, top_grad, received)
        kept = [(value, swap(value)) for value in kept]
        grad_low, kept = lax.optimization_barrier((grad_low, kept))
    input_grad, share, qkv_piece, joined_sums, vectors, d_up_bias = backward(grad_low, saved, kept)

    ours = jnp.arange(fsdp_count)[:, None] == group_id
    vector_parts = jnp.concatenate(
        [
            vectors.reshape(6, -1, shard).transpose(1, 0, 2).reshape(-1, 6 * shard),
            jnp.where(ours, joined_sums[None, :WIDTH], 0.0),
            jnp.where(ours, joined_sums[None, 2 * WIDTH :], 0.0),
            d_up_bias.reshape(fsdp_count, -1),
        ],
        1,
    )
    vector_parts = vector_parts.astype(jnp.bfloat16).reshape(fsdp_count, 4, 3 * WIDTH)
    vector_share = sum_low(exchange(vector_parts, "fsdp"))
    vector_share = jnp.pad(vector_share, ((0, 12), (0, 0)))
    qkv_piece = jnp.concatenate([qkv_piece, vector_share], 0)
    qkv_piece = jnp.pad(qkv_piece, ((0, 0), (0, model_width - 3 * WIDTH)))
    joint_piece = sum_low(exchange(share.reshape(8, -1, model_width), ("x", "yh")))
    joint_piece, layer_out = lax.optimization_barrier((joint_piece, layer_out))
    both = spread(jnp.concatenate([joint_piece, qkv_piece], 0), ("x", "yh"))
    g_qkv, g_out, g_up, g_down, vector_sum = unpack(
        core_number, both, swap(both), shard, mlp_in.shape[2], mlp_out.shape[1]
    )
    vector_sum = vector_sum[:, : 3 * WIDTH].reshape(-1)
    own_vectors = vector_sum[: 8 * shard].reshape(8, shard)
    own_up_bias = vector_sum[8 * shard :]
    order = (2, 6, 7, 3, 4, 5)
    g_biases = jnp.stack([own_vectors[place] for place in order])
    out_shape = (1, micro_count, 1, local_rows, model_width)
    return (
        layer_out.reshape(out_shape),
        input_grad.reshape(out_shape),
        g_qkv[None],
        g_out[None],
        g_up[None],
        g_down[None],
        own_vectors[None, :2],
        g_biases[None],
        own_up_bias[None],
    )


def solution(mesh):
    fine = Mesh(
        mesh.devices.reshape(2, 4, 2, 2, 4), ("section", "x", "yh", "core", "fsdp")
    )
    rows = P(None, "fsdp", CTX, None)
    weight = P("section", "fsdp", None)
    vector = P("section", None, "fsdp")
    row = P("section", "fsdp")
    out_rows = P("section", None, "fsdp", CTX, None)
    return jax.shard_map(
        shards,
        mesh=fine,
        in_specs=(rows, rows, P(), P(), weight, weight, weight, weight, vector, vector, row),
        out_specs=(out_rows, out_rows, weight, weight, weight, weight, vector, vector, row),
        check_vma=False,
    )
```

```python
import functools

import jax
import jax.numpy as jnp
from jax import lax
from jax.experimental import pallas as pl
from jax.experimental.pallas import tpu as pltpu
from jax.sharding import Mesh
from jax.sharding import PartitionSpec as P

HEADS = 12
HDIM = 64
GROUPS = 4
GROUP_HEADS = HEADS // GROUPS
WIDTH = GROUP_HEADS * HDIM
QUERY_BLOCK = 256
EXTRA = 32
JOINT_ROWS = 112
CTX = ("x", "yh", "core")

epsilon = 1e-05
neg_fill = -1e30
GELU_SCALE = (2.0 / 3.141592653589793) ** 0.5
GELU_CUBE = 0.044715


def dot(left_side, right_side, left_dim, right_dim):
    return lax.dot_general(
        left_side,
        right_side,
        (((left_dim,), (right_dim,)), ((), ())),
        preferred_element_type=jnp.float32,
    )


def head_columns(part, head):
    start = part * WIDTH + head * HDIM
    return slice(start, start + HDIM)


def whole(*shape):
    return pl.BlockSpec(shape, lambda i, *unused: (0,) * len(shape))


def sort_rows(target, source, table, back):
    blocks = table.shape[0]
    size = source.shape[0] // blocks
    for block in range(blocks):
        fixed = slice(block * size, (block + 1) * size)
        moved = pl.ds(pl.multiple_of(table[block] * size, size), size)
        if back:
            target[fixed, :] = source[moved, :]
        else:
            target[moved, :] = source[fixed, :]


def place_weight(target, members, ids):
    count, rows = len(members), members[0].shape[0]
    for shift, member in enumerate(members):
        place = lax.rem(ids[1] + shift - 2 * ids[0] + count, count)
        target[pl.ds(pl.multiple_of(place * rows, rows), rows), :] = member[...]


def mask_scores(scores):
    count = scores.shape[0] - QUERY_BLOCK
    tile = (QUERY_BLOCK, QUERY_BLOCK)
    visible = lax.broadcasted_iota(jnp.int32, tile, 0) <= lax.broadcasted_iota(jnp.int32, tile, 1)
    masked = jnp.where(visible, scores[count:], neg_fill)
    return jnp.concatenate([scores[:count], masked], 0) if count else masked


def attend_body(
    table, ids, own, other, w0, w1, w2, w3, bias, joined, mixed, log_total, weight, scratch, sorted_out
):
    step = pl.program_id(0)
    half = own.shape[1]

    @pl.when(step == 0)
    def _():
        place_weight(weight, (w0, w1, w2, w3), ids)
        product = dot(own[...], weight[:half, :], 1, 0) + dot(other[...], weight[half:, :], 1, 0)
        scratch[...] = (product + bias[...]).astype(jnp.bfloat16)
        sort_rows(joined, scratch, table, False)

    def block(index):
        rows = slice(index * QUERY_BLOCK, (index + 1) * QUERY_BLOCK)
        seen = slice(0, (index + 1) * QUERY_BLOCK)
        parts = []
        for head in range(GROUP_HEADS):
            queries = joined[rows, head_columns(0, head)] * jnp.bfloat16(HDIM ** (-0.5))
            keys = joined[seen, head_columns(1, head)]
            values = joined[seen, head_columns(2, head)]
            scores = mask_scores(dot(keys, queries, 1, 1))
            top = jnp.max(scores, 0, keepdims=True)
            powers = jnp.exp(scores - top)
            total = jnp.sum(powers, 0, keepdims=True)
            parts.append(dot(values, powers.astype(jnp.bfloat16), 0, 0) / total)
            log_total[head : head + 1, rows] = top + jnp.log(total)
        sorted_out[rows, :] = jnp.concatenate(parts, 0).T.astype(jnp.bfloat16)

    for index in range(own.shape[0] // QUERY_BLOCK):
        pl.when(step == index)(lambda index=index: block(index))

    @pl.when(step == pl.num_programs(0) - 1)
    def _():
        sort_rows(mixed, sorted_out, table, True)


def attend(table, ids, own, other, weights, bias):
    count, half = own.shape
    return pl.pallas_call(
        attend_body,
        grid_spec=pltpu.PrefetchScalarGridSpec(
            num_scalar_prefetch=2,
            grid=(count // QUERY_BLOCK,),
            in_specs=[whole(count, half)] * 2
            + [whole(*weight.shape) for weight in weights]
            + [whole(1, 3 * WIDTH)],
            out_specs=[whole(count, 3 * WIDTH), whole(count, WIDTH), whole(8, count)],
            scratch_shapes=[
                pltpu.VMEM((2 * half, 3 * WIDTH), jnp.bfloat16),
                pltpu.VMEM((count, 3 * WIDTH), jnp.bfloat16),
                pltpu.VMEM((count, WIDTH), jnp.bfloat16),
            ],
        ),
        out_shape=[
            jax.ShapeDtypeStruct((count, 3 * WIDTH), jnp.bfloat16),
            jax.ShapeDtypeStruct((count, WIDTH), jnp.bfloat16),
            jax.ShapeDtypeStruct((8, count), jnp.float32),
        ],
        compiler_params=pltpu.CompilerParams(vmem_limit_bytes=48 << 20),
        cost_estimate=pl.CostEstimate(
            flops=4 * count * count * WIDTH,
            bytes_accessed=8 * count * WIDTH,
            transcendentals=count * count * GROUP_HEADS,
        ),
    )(table, ids, own, other, *weights, bias)


def attend_back_body(
    table,
    ids,
    joined,
    grad_mixed,
    log_total,
    w0,
    w1,
    w2,
    w3,
    grad_joined,
    grad_own,
    grad_other,
    weight,
    sorted_grads,
    sorted_out,
    key_sums,
    value_sums,
):
    step = pl.program_id(0)
    half = grad_own.shape[1]

    @pl.when(step == 0)
    def _():
        place_weight(weight, (w0, w1, w2, w3), ids)
        sort_rows(sorted_grads, grad_mixed, table, False)
        key_sums[...] = jnp.zeros_like(key_sums)
        value_sums[...] = jnp.zeros_like(value_sums)

    def block(index):
        rows = slice(index * QUERY_BLOCK, (index + 1) * QUERY_BLOCK)
        seen = slice(0, (index + 1) * QUERY_BLOCK)
        parts = []
        for head in range(GROUP_HEADS):
            queries = joined[rows, head_columns(0, head)] * jnp.bfloat16(HDIM ** (-0.5))
            keys = joined[seen, head_columns(1, head)]
            values = joined[seen, head_columns(2, head)]
            grads = sorted_grads[rows, head_columns(0, head)]
            scores = mask_scores(dot(keys, queries, 1, 1))
            weights = jnp.exp(scores - log_total[head : head + 1, rows])
            grad_weights = dot(values, grads, 1, 1)
            inner_sum = jnp.sum(weights * grad_weights, 0, keepdims=True)
            grad_scores = (weights * (grad_weights - inner_sum)).astype(jnp.bfloat16)
            value_sums[head, seen, :] += dot(weights.astype(jnp.bfloat16), grads, 1, 0)
            key_sums[head, seen, :] += dot(grad_scores, queries, 1, 0)
            parts.append(dot(keys, grad_scores, 0, 0) * (HDIM ** (-0.5)))
        sorted_out[rows, :WIDTH] = jnp.concatenate(parts, 0).T.astype(jnp.bfloat16)

    for index in range(joined.shape[0] // QUERY_BLOCK):
        pl.when(step == index)(lambda index=index: block(index))

    @pl.when(step == pl.num_programs(0) - 1)
    def _():
        for head in range(GROUP_HEADS):
            sorted_out[:, head_columns(1, head)] = key_sums[head].astype(jnp.bfloat16)
            sorted_out[:, head_columns(2, head)] = value_sums[head].astype(jnp.bfloat16)
        sort_rows(grad_joined, sorted_out, table, True)
        grad_own[...] = dot(grad_joined[...], weight[:half, :], 1, 1).astype(jnp.bfloat16)
        grad_other[...] = dot(grad_joined[...], weight[half:, :], 1, 1).astype(jnp.bfloat16)


def attend_back(table, ids, joined, grad_mixed, log_total, weights):
    count = joined.shape[0]
    half = len(weights) * weights[0].shape[0] // 2
    return pl.pallas_call(
        attend_back_body,
        grid_spec=pltpu.PrefetchScalarGridSpec(
            num_scalar_prefetch=2,
            grid=(count // QUERY_BLOCK,),
            in_specs=[whole(count, 3 * WIDTH), whole(count, WIDTH), whole(8, count)]
            + [whole(*weight.shape) for weight in weights],
            out_specs=[whole(count, 3 * WIDTH), whole(count, half), whole(count, half)],
            scratch_shapes=[
                pltpu.VMEM((2 * half, 3 * WIDTH), jnp.bfloat16),
                pltpu.VMEM((count, WIDTH), jnp.bfloat16),
                pltpu.VMEM((count, 3 * WIDTH), jnp.bfloat16),
                pltpu.VMEM((GROUP_HEADS, count, HDIM), jnp.float32),
                pltpu.VMEM((GROUP_HEADS, count, HDIM), jnp.float32),
            ],
        ),
        out_shape=[
            jax.ShapeDtypeStruct((count, 3 * WIDTH), jnp.bfloat16),
            jax.ShapeDtypeStruct((count, half), jnp.bfloat16),
            jax.ShapeDtypeStruct((count, half), jnp.bfloat16),
        ],
        compiler_params=pltpu.CompilerParams(vmem_limit_bytes=48 << 20),
        cost_estimate=pl.CostEstimate(
            flops=10 * count * count * WIDTH,
            bytes_accessed=16 * count * WIDTH,
            transcendentals=count * count * GROUP_HEADS,
        ),
    )(table, ids, joined, grad_mixed, log_total, *weights)


def weight_grads_body(
    core_id,
    active,
    active_other,
    grad_low,
    grad_low_other,
    normed_two,
    normed_two_other,
    grad_hidden,
    grad_hidden_other,
    mixed,
    mixed_other,
    grad_attn,
    grad_attn_other,
    joint,
):
    down_rows, up_rows = active.shape[1], normed_two.shape[0]
    width = grad_low.shape[1]
    product = dot(active[...], grad_low[...], 0, 0)
    product += dot(active_other[...], grad_low_other[...], 0, 0)
    joint[0, :down_rows, :] = product.astype(jnp.bfloat16)
    place = down_rows
    for panel in range(grad_hidden.shape[1] // width):
        columns = slice(panel * width, (panel + 1) * width)
        product = dot(normed_two[...], grad_hidden[:, columns], 1, 0)
        product += dot(normed_two_other[...], grad_hidden_other[:, columns], 1, 0)
        joint[0, place : place + up_rows, :] = product.astype(jnp.bfloat16)
        place += up_rows
    product = dot(mixed[...], grad_attn[...], 1, 0)
    product += dot(mixed_other[...], grad_attn_other[...], 1, 0)
    joint[0, place : place + up_rows, :] = product.astype(jnp.bfloat16)
    place += up_rows
    joint[0, place:, :] = jnp.zeros_like(joint[0, place:, :])


def weight_grads(core_id, pairs, members):
    rows, hidden_width = pairs[0][0].shape
    width = pairs[1][0].shape[1]
    down_rows, up_rows = hidden_width // members // 2, width // members // 2
    out_rows = 2 * down_rows + up_rows + EXTRA
    flat = pl.BlockSpec((rows, width), lambda i, core: (0, 0))
    tall = pl.BlockSpec((up_rows, rows), lambda i, core: (2 * i + core[0], 0))
    specs = [
        pl.BlockSpec((rows, down_rows), lambda i, core: (0, 2 * i + core[0])),
        flat,
        tall,
        pl.BlockSpec((rows, hidden_width), lambda i, core: (0, 0)),
        tall,
        flat,
    ]
    return pl.pallas_call(
        weight_grads_body,
        grid_spec=pltpu.PrefetchScalarGridSpec(
            num_scalar_prefetch=1,
            grid=(members,),
            in_specs=[spec for spec in specs for _ in range(2)],
            out_specs=pl.BlockSpec((1, out_rows, width), lambda i, core: (i, 0, 0)),
        ),
        out_shape=jax.ShapeDtypeStruct((members, out_rows, width), jnp.bfloat16),
        compiler_params=pltpu.CompilerParams(vmem_limit_bytes=48 << 20),
        cost_estimate=pl.CostEstimate(
            flops=2 * rows * width * (2 * hidden_width + width),
            bytes_accessed=2 * members * out_rows * width,
            transcendentals=0,
        ),
    )(core_id, *[value for pair in pairs for value in pair])


def weight_panel(packed, start):
    members, width = packed.shape[0], packed.shape[2]
    rows = width // members
    return jnp.concatenate([packed[i, start : start + rows, :] for i in range(members)], 0)


def join_groups(mixed, group):
    micro_count = mixed.shape[0] // GROUPS
    return jnp.concatenate([mixed[m * GROUPS + group] for m in range(micro_count)], 0)


def attend_out(mixed, entering, packed, vectors, w_out):
    middle = entering[...].astype(jnp.float32) + vectors[5:6, :]
    for group in range(GROUPS):
        rows = slice(group * WIDTH, (group + 1) * WIDTH)
        middle += dot(join_groups(mixed, group), w_out[rows, :], 1, 0)
    return middle


def start_copies(stored, packed, landed, panels):
    members, width = packed.shape[0], packed.shape[2]
    up_rows = width // members
    down_rows = panels * up_rows
    per_panel = members // panels

    def copy(index, rows, sources):
        here = (slice(None) if sources is None else sources, rows)
        return pltpu.make_async_copy(stored.at[here], packed.at[here], landed.at[index])

    out = copy(0, pl.ds(2 * down_rows, up_rows), None)
    ups, downs = [], []
    for panel in range(panels):
        ups.append(copy(1 + panel, pl.ds(down_rows + panel * up_rows, up_rows), None))
        downs.append(
            copy(1 + panels + panel, pl.ds(0, down_rows), pl.ds(panel * per_panel, per_panel))
        )
    return out, ups, downs


def feed_forward_body(mixed, entering, stored, vectors, up_bias, result, packed, landed):
    members, width = packed.shape[0], packed.shape[2]
    panels = up_bias.shape[0]
    up_rows = width // members
    down_rows = panels * up_rows
    out, ups, downs = start_copies(stored, packed, landed, panels)
    for copy in [out] + ups + downs:
        copy.start()
    out.wait()
    middle = attend_out(mixed, entering, packed, vectors, weight_panel(packed, 2 * down_rows))
    normed, _, _ = normalize(middle, vectors[1:2, :], vectors[6:7, :])
    normed = normed.astype(jnp.bfloat16)
    parts = []
    for panel in range(panels):
        ups[panel].wait()
        hidden = dot(normed, weight_panel(packed, down_rows + panel * up_rows), 1, 0)
        hidden = hidden + up_bias[panel : panel + 1, :]
        parts.append(jax.nn.gelu(hidden).astype(jnp.bfloat16))
    active = jnp.concatenate(parts, 1)
    total = middle + vectors[7:8, :]
    for member in range(members):
        if member % (members // panels) == 0:
            downs[member // (members // panels)].wait()
        columns = slice(member * down_rows, (member + 1) * down_rows)
        total += dot(active[:, columns], packed[member, :down_rows, :], 1, 0)
    result[...] = total.astype(jnp.bfloat16)


def feed_specs(count):
    specs = [pl.BlockSpec(memory_space=pltpu.VMEM) for _ in range(count)]
    specs[2] = pl.BlockSpec(memory_space=pl.ANY)
    return specs


def feed_scratch(packed, up_bias):
    return [
        pltpu.VMEM(packed.shape, packed.dtype),
        pltpu.SemaphoreType.DMA((1 + 2 * up_bias.shape[0],)),
    ]


def feed_forward(mixed, entering, packed, vectors, up_bias):
    rows, width = entering.shape
    return pl.pallas_call(
        feed_forward_body,
        in_specs=feed_specs(5),
        out_specs=pl.BlockSpec(memory_space=pltpu.VMEM),
        scratch_shapes=feed_scratch(packed, up_bias),
        out_shape=jax.ShapeDtypeStruct((rows, width), jnp.bfloat16),
        compiler_params=pltpu.CompilerParams(vmem_limit_bytes=48 << 20),
        cost_estimate=pl.CostEstimate(
            flops=18 * rows * width * width,
            bytes_accessed=18 * width * width,
            transcendentals=4 * rows * width,
        ),
    )(mixed, entering, packed, vectors, up_bias)


def feed_back_end(grads, grad_normed, unit, spread_two, vectors, w_out, grad_mixed, grad_middle):
    local_rows = grad_mixed.shape[1]
    grad_top = grads.astype(jnp.float32)
    grad_norm, d_gain, d_shift = normalize_back(grad_normed, unit, spread_two, vectors[1:2, :])
    grad_sum = grad_top + grad_norm
    grad_middle[...] = grad_sum
    grad_attn = grad_sum.astype(jnp.bfloat16)
    for group in range(GROUPS):
        part = dot(grad_attn, w_out[group * WIDTH : (group + 1) * WIDTH, :], 1, 1)
        part = part.astype(jnp.bfloat16)
        for m in range(grad_mixed.shape[0] // GROUPS):
            grad_mixed[m * GROUPS + group] = part[m * local_rows : (m + 1) * local_rows]
    return grad_attn, d_gain, d_shift


def down_panel(packed, panel, panels):
    members, width = packed.shape[0], packed.shape[2]
    each = members // panels
    rows = panels * width // members
    return jnp.concatenate(
        [packed[i, :rows, :] for i in range(panel * each, (panel + 1) * each)], 0
    )


def feed_back_first_body(
    mixed,
    entering,
    packed,
    vectors,
    up_bias,
    grad_low,
    grad_mixed,
    grad_middle,
    active,
    normed_tall,
    mixed_tall,
    slopes,
    units,
    spreads,
):
    members, width = packed.shape[0], packed.shape[2]
    panels = up_bias.shape[0]
    up_rows = width // members
    down_rows = panels * up_rows
    w_out = weight_panel(packed, 2 * down_rows)
    middle = attend_out(mixed, entering, packed, vectors, w_out)
    normed, unit, spread_two = normalize(middle, vectors[1:2, :], vectors[6:7, :])
    normed = normed.astype(jnp.bfloat16)
    grads = grad_low[...]
    grad_normed = jnp.zeros(middle.shape, jnp.float32)
    for panel in range(panels):
        columns = slice(panel * width, (panel + 1) * width)
        w_up = weight_panel(packed, down_rows + panel * up_rows)
        hidden = dot(normed, w_up, 1, 0) + up_bias[panel : panel + 1, :]
        square = hidden * hidden
        bend = jnp.tanh(GELU_SCALE * (hidden + GELU_CUBE * (square * hidden)))
        slope = 0.5 * (1.0 + bend) + 0.5 * hidden * (1.0 - bend * bend) * (
            GELU_SCALE * (1.0 + 3.0 * GELU_CUBE * square)
        )
        slopes[:, columns] = slope
        active[:, columns] = (0.5 * hidden * (1.0 + bend)).astype(jnp.bfloat16)
        w_down = down_panel(packed, panel, panels)
        grad_hidden = (dot(grads, w_down, 1, 1) * slope).astype(jnp.bfloat16)
        grad_normed += dot(grad_hidden, w_up, 1, 1)
    feed_back_end(grads, grad_normed, unit, spread_two, vectors, w_out, grad_mixed, grad_middle)
    units[...] = unit
    spreads[...] = jnp.broadcast_to(spread_two, spreads.shape)
    normed_tall[...] = normed.astype(jnp.float32).T.astype(jnp.bfloat16)
    for group in range(GROUPS):
        part = join_groups(mixed, group).astype(jnp.float32).T.astype(jnp.bfloat16)
        mixed_tall[group * WIDTH : (group + 1) * WIDTH, :] = part


def feed_back_last_body(
    packed,
    vectors,
    grad_low,
    slopes,
    units,
    spreads,
    grad_mixed,
    grad_middle,
    grad_hidden,
    grad_attn,
    sums,
    up_sums,
):
    members, width = packed.shape[0], packed.shape[2]
    panels = up_sums.shape[0]
    up_rows = width // members
    down_rows = panels * up_rows
    w_out = weight_panel(packed, 2 * down_rows)
    grads = grad_low[...]
    grad_normed = jnp.zeros(units.shape, jnp.float32)
    for panel in range(panels):
        columns = slice(panel * width, (panel + 1) * width)
        w_up = weight_panel(packed, down_rows + panel * up_rows)
        w_down = down_panel(packed, panel, panels)
        part = (dot(grads, w_down, 1, 1) * slopes[:, columns]).astype(jnp.bfloat16)
        grad_normed += dot(part, w_up, 1, 1)
        grad_hidden[:, columns] = part
        up_sums[panel : panel + 1, :] = jnp.sum(part.astype(jnp.float32), 0, keepdims=True)
    attn, d_gain, d_shift = feed_back_end(
        grads, grad_normed, units[...], spreads[:, :1], vectors, w_out, grad_mixed, grad_middle
    )
    grad_attn[...] = attn
    sums[0:1, :] = d_gain[None]
    sums[1:2, :] = d_shift[None]
    sums[2:3, :] = jnp.sum(attn.astype(jnp.float32), 0, keepdims=True)
    sums[3:4, :] = jnp.sum(grads.astype(jnp.float32), 0, keepdims=True)


def feed_back(body, args, shapes):
    rows, width = shapes[1][0]
    return pl.pallas_call(
        body,
        in_specs=[pl.BlockSpec(memory_space=pltpu.VMEM)] * len(args),
        out_specs=[pl.BlockSpec(memory_space=pltpu.VMEM)] * len(shapes),
        out_shape=[jax.ShapeDtypeStruct(*shape) for shape in shapes],
        compiler_params=pltpu.CompilerParams(vmem_limit_bytes=56 << 20),
        cost_estimate=pl.CostEstimate(
            flops=28 * rows * width * width,
            bytes_accessed=24 * width * width,
            transcendentals=4 * rows * width,
        ),
    )(*args)


def norm_back_body(returned, entering, grad_middle, vectors, grad_in, sums):
    parts = []
    for m in range(returned.shape[0] // GROUPS):
        halves = [
            returned[m * GROUPS + core].astype(jnp.float32)
            + returned[m * GROUPS + 2 + core].astype(jnp.float32)
            for core in range(2)
        ]
        parts.append(jnp.concatenate(halves, 1))
    grad_normed = jnp.concatenate(parts, 0)
    gain = vectors[0:1, :]
    _, unit, spread_one = normalize(entering[...].astype(jnp.float32), gain, vectors[2:3, :])
    grad_norm, d_gain, d_shift = normalize_back(grad_normed, unit, spread_one, gain)
    grad_in[...] = (grad_middle[...] + grad_norm).astype(jnp.bfloat16)
    sums[0:1, :] = d_gain[None]
    sums[1:2, :] = d_shift[None]


def norm_back(returned, entering, grad_middle, vectors):
    rows, width = entering.shape
    return pl.pallas_call(
        norm_back_body,
        in_specs=[pl.BlockSpec(memory_space=pltpu.VMEM)] * 4,
        out_specs=[pl.BlockSpec(memory_space=pltpu.VMEM)] * 2,
        out_shape=[
            jax.ShapeDtypeStruct((rows, width), jnp.bfloat16),
            jax.ShapeDtypeStruct((2, width), jnp.float32),
        ],
        compiler_params=pltpu.CompilerParams(vmem_limit_bytes=32 << 20),
        cost_estimate=pl.CostEstimate(
            flops=20 * rows * width, bytes_accessed=10 * rows * width, transcendentals=rows
        ),
    )(returned, entering, grad_middle, vectors)


def qkv_grads_body(owners, ids, own, other, grad_joined, *outs):
    pieces, sums, both = outs[:-2], outs[-2], outs[-1]
    first_core = ids[0] == 0
    grads = grad_joined[...]
    half = own.shape[1]
    own_grads = dot(own[...], grads, 0, 0).astype(jnp.bfloat16)
    other_grads = dot(other[...], grads, 0, 0).astype(jnp.bfloat16)
    both[:half, :] = jnp.where(first_core, own_grads, other_grads)
    both[half:, :] = jnp.where(first_core, other_grads, own_grads)
    count = len(pieces)
    rows = pieces[0].shape[0] // owners
    for shift in range(count):
        place = lax.rem(ids[2] + shift, count) * rows
        for owner in range(owners):
            start = pl.multiple_of(owner * rows * count + place, rows)
            pieces[shift][owner * rows : (owner + 1) * rows, :] = both[pl.ds(start, rows), :]
    sums[...] = jnp.sum(grads.astype(jnp.float32), 0, keepdims=True)


def qkv_grads(ids, own, other, grad_joined, count, owners):
    rows, half = own.shape
    width = grad_joined.shape[1]
    piece = jax.ShapeDtypeStruct((2 * half // count, width), jnp.bfloat16)
    return pl.pallas_call(
        functools.partial(qkv_grads_body, owners),
        in_specs=[pl.BlockSpec(memory_space=pltpu.SMEM)]
        + [pl.BlockSpec(memory_space=pltpu.VMEM)] * 3,
        out_specs=[pl.BlockSpec(memory_space=pltpu.VMEM)] * (count + 1),
        out_shape=[piece] * count + [jax.ShapeDtypeStruct((1, width), jnp.float32)],
        scratch_shapes=[pltpu.VMEM((2 * half, width), jnp.bfloat16)],
        compiler_params=pltpu.CompilerParams(vmem_limit_bytes=48 << 20),
        cost_estimate=pl.CostEstimate(
            flops=4 * rows * half * width, bytes_accessed=6 * rows * half, transcendentals=0
        ),
    )(ids, own, other, grad_joined)


def unpack_body(core_id, own, other, g_qkv, g_out, g_up, g_down, vectors):
    first_core = core_id[0] == 0
    count = own.shape[0]
    width = own.shape[2]
    joint_rows = JOINT_ROWS
    piece_rows = own.shape[1] - joint_rows - 16
    up_rows = g_up.shape[0] // 2
    down_rows = g_down.shape[0] // 2
    sums = jnp.zeros(vectors.shape, jnp.float32)
    for core in range(2):
        pick = first_core if core == 0 else jnp.logical_not(first_core)
        joint = jnp.concatenate(
            [
                jnp.where(pick, own[i, :joint_rows, :], other[i, :joint_rows, :])
                for i in range(count)
            ],
            0,
        ).astype(jnp.float32)
        g_down[core * down_rows : (core + 1) * down_rows, :] = joint[:down_rows]
        place = down_rows
        for panel in range(g_up.shape[1] // width):
            g_up[core * up_rows : (core + 1) * up_rows, panel * width : (panel + 1) * width] = (
                joint[place : place + up_rows]
            )
            place += up_rows
        g_out[core * up_rows : (core + 1) * up_rows, :] = joint[place : place + up_rows]
        for i in range(count):
            x_id, group = i // 2, (i % 2) * 2 + core
            piece = jnp.where(pick, own[i, joint_rows:, :], other[i, joint_rows:, :])
            piece = piece.astype(jnp.float32)
            for part in range(3):
                start = part * width + group * WIDTH
                g_qkv[x_id * piece_rows : (x_id + 1) * piece_rows, start : start + WIDTH] = piece[
                    :piece_rows, part * WIDTH : (part + 1) * WIDTH
                ]
            sums += piece[piece_rows : piece_rows + 4, :]
    vectors[...] = sums


def unpack(core_id, own, other, shard, hidden_width, hidden_shard):
    width = own.shape[2]
    return pl.pallas_call(
        unpack_body,
        in_specs=[pl.BlockSpec(memory_space=pltpu.SMEM)]
        + [pl.BlockSpec(memory_space=pltpu.VMEM)] * 2,
        out_specs=[pl.BlockSpec(memory_space=pltpu.VMEM)] * 5,
        out_shape=[
            jax.ShapeDtypeStruct((shard, 3 * width), jnp.float32),
            jax.ShapeDtypeStruct((shard, width), jnp.float32),
            jax.ShapeDtypeStruct((shard, hidden_width), jnp.float32),
            jax.ShapeDtypeStruct((hidden_shard, width), jnp.float32),
            jax.ShapeDtypeStruct((4, width), jnp.float32),
        ],
        compiler_params=pltpu.CompilerParams(vmem_limit_bytes=48 << 20),
        cost_estimate=pl.CostEstimate(flops=0, bytes_accessed=12 << 20, transcendentals=0),
    )(core_id, own, other)


def normalize(values, gain_row, shift_row):
    center = values - jnp.mean(values, -1, keepdims=True)
    spread = lax.rsqrt(jnp.mean(center * center, -1, keepdims=True) + epsilon)
    unit_rows = center * spread
    return (unit_rows * gain_row + shift_row, unit_rows, spread)


def normalize_back(grad_out, unit_rows, spread, gain_row):
    grad_unit = grad_out * gain_row
    grad_in = spread * (
        grad_unit
        - jnp.mean(grad_unit, -1, keepdims=True)
        - unit_rows * jnp.mean(grad_unit * unit_rows, -1, keepdims=True)
    )
    return (grad_in, jnp.sum(grad_out * unit_rows, 0), jnp.sum(grad_out, 0))


def exchange(value, axes):
    return lax.all_to_all(value, axes, 0, 0, tiled=True)


def swap(value):
    return lax.ppermute(value, "core", [(0, 1), (1, 0)])


def in_order(own, other):
    first = lax.axis_index("core") == 0
    return jnp.where(first, own, other), jnp.where(first, other, own)


def pack_weights(attn_out, mlp_in, mlp_out):
    core_id = lax.axis_index("core")
    width = attn_out.shape[2]
    out_half, up_half, down_half = (
        lax.dynamic_slice_in_dim(
            weight[0], core_id * (weight.shape[1] // 2), weight.shape[1] // 2, 0
        )
        for weight in (attn_out, mlp_in, mlp_out)
    )
    panels = [up_half[:, start : start + width] for start in range(0, mlp_in.shape[2], width)]
    return jnp.concatenate([down_half] + panels + [out_half], 0)


def ring_pairs(axis, shift):
    count = lax.axis_size(axis)
    return [(source, (source + shift) % count) for source in range(count)]


def gather_ring(value, axis):
    return [value] + [
        lax.ppermute(value, axis, ring_pairs(axis, -shift))
        for shift in range(1, lax.axis_size(axis))
    ]


def sum_pieces(pieces, axis):
    total = pieces[0].astype(jnp.float32)
    for shift in range(1, len(pieces)):
        received = lax.ppermute(pieces[shift], axis, ring_pairs(axis, shift))
        total = total + received.astype(jnp.float32)
    return total.astype(jnp.bfloat16)


def sum_low(value):
    return jnp.sum(value.astype(jnp.float32), 0).astype(jnp.bfloat16)


def spread(value, axes):
    count = lax.axis_size(axes)
    return exchange(jnp.broadcast_to(value[None], (count,) + value.shape), axes)


def shards(
    inputs,
    cotangent,
    plan,
    block_table,
    attn_in,
    attn_out,
    mlp_in,
    mlp_out,
    norm_gains,
    biases,
    mlp_bias,
):
    shard = norm_gains.shape[2]
    core_id = lax.axis_index("core")
    group_id = lax.axis_index("yh") * 2 + core_id
    fsdp_id = lax.axis_index("fsdp")
    section_id = lax.axis_index("section")
    sections = lax.axis_size("section")
    fsdp_count = lax.axis_size("fsdp")

    small = jnp.concatenate([norm_gains[0], biases[0], mlp_bias.reshape(-1, shard)], 0)
    small = small.reshape(-1, 3 * WIDTH)
    own_columns = lax.dynamic_index_in_dim(
        attn_in[0].reshape(shard, 3, GROUPS, WIDTH), group_id, 2, keepdims=False
    ).reshape(shard, 3 * WIDTH)
    small_all = spread(small, "fsdp").reshape(fsdp_count, -1, shard).astype(jnp.float32)
    w_group = gather_ring(own_columns, "fsdp")
    small_all, w_group[1], w_group[3] = lax.optimization_barrier(
        (small_all, w_group[1], w_group[3])
    )
    packed = pack_weights(attn_out, mlp_in, mlp_out)
    packed = lax.all_gather(packed, ("fsdp", "core"), axis=0)
    model_width = attn_out.shape[2]
    hidden_width = mlp_in.shape[2]
    half = model_width // 2
    vector_rows = small_all[:, :8].transpose(1, 0, 2).reshape(8, model_width)
    gain_rows, bias_rows = vector_rows[:2], vector_rows[2:]
    up_rows = small_all[:, 8:].reshape(-1, model_width)
    own_bias = lax.dynamic_index_in_dim(small_all, group_id, 0, keepdims=False)
    group_bias = jnp.concatenate([own_bias[3], jnp.zeros_like(own_bias[3]), own_bias[4]])[None]

    micro_count, _, local_rows, _ = inputs.shape
    rows = micro_count * local_rows
    fresh = jnp.stack(
        [lax.dynamic_index_in_dim(inputs, plan[step], 0, keepdims=False) for step in range(micro_count)]
    ).reshape(rows, model_width)
    top_grad = cotangent.reshape(rows, model_width)
    core_number = core_id.astype(jnp.int32)[None]
    numbers = jnp.stack([core_id, fsdp_id, lax.axis_index("x")]).astype(jnp.int32)

    def forward(entering):
        stream = entering.astype(jnp.float32)
        normed, _, _ = normalize(stream, gain_rows[0], bias_rows[0])
        halves = normed.astype(jnp.bfloat16).reshape(micro_count, 1, local_rows, 2, half)
        halves = jnp.broadcast_to(
            halves.transpose(0, 1, 3, 2, 4), (micro_count, 2, 2, local_rows, half)
        )
        own = exchange(halves.reshape(-1, local_rows, half), CTX).reshape(-1, half)
        own, weights = lax.optimization_barrier((own, w_group))
        other = swap(own)
        joined, mixed_heads, log_total = attend(
            block_table, numbers, own, other, weights, group_bias
        )
        mixed = exchange(mixed_heads.reshape(-1, local_rows, WIDTH), CTX)
        result = feed_forward(mixed, entering, packed, vector_rows, up_rows)
        return result, (entering, own, other, joined, log_total, mixed)

    def backward(grad_low, saved, kept):
        entering, own, other, joined, log_total, mixed = saved
        last = kept is not None
        low, full = jnp.bfloat16, jnp.float32
        shapes = [(mixed.shape, low), ((rows, model_width), full), ((rows, hidden_width), low)]
        if last:
            pairs, plain = kept
            shapes += [((rows, model_width), low), ((4, model_width), full), (up_rows.shape, full)]
            grad_mixed, grad_middle, *extra = feed_back(
                feed_back_last_body, (packed, vector_rows, grad_low, *plain), shapes
            )
        else:
            shapes += [((model_width, rows), low)] * 2
            shapes += [((rows, hidden_width), full), ((rows, model_width), full), ((rows, 128), full)]
            grad_mixed, grad_middle, *extra = feed_back(
                feed_back_first_body,
                (mixed, entering, packed, vector_rows, up_rows, grad_low),
                shapes,
            )
        grad_heads = exchange(grad_mixed.reshape(-1, local_rows, WIDTH), CTX).reshape(-1, WIDTH)
        if last:
            grad_hidden, grad_attn, sums, up_sums = extra
            active_pair, normed_pair, mixed_pair = pairs
            low_pair, hidden_pair, attn_pair = (
                (value, swap(value)) for value in (grad_low, grad_hidden, grad_attn)
            )
            joint = weight_grads(
                core_number,
                [active_pair, low_pair, normed_pair, hidden_pair, mixed_pair, attn_pair],
                fsdp_count,
            )
            grad_heads, joint = lax.optimization_barrier((grad_heads, joint))
            share = lax.psum_scatter(
                joint.reshape(-1, model_width),
                "fsdp",
                scatter_dimension=0,
                tiled=True,
            )
        grad_joined, grad_own, grad_other = attend_back(
            block_table, numbers, joined, grad_heads, log_total, w_group
        )
        received = swap(grad_other)
        summed = (grad_own.astype(jnp.float32) + received.astype(jnp.float32)).astype(jnp.bfloat16)
        returned = exchange(summed.reshape(-1, local_rows, half), CTX)
        grad_in, norm_sums = norm_back(returned, entering, grad_middle, vector_rows)
        if not last:
            return grad_in, extra
        x_count = lax.axis_size("x")
        *pieces, joined_sums = qkv_grads(numbers, own, other, grad_joined, x_count, fsdp_count)
        joined_sums = joined_sums[0]
        qkv_share = sum_pieces(pieces, "x")
        share, qkv_share = lax.optimization_barrier((share, qkv_share))
        piece_rows = shard // x_count
        owner_pieces = [
            lax.dynamic_slice_in_dim(
                qkv_share, (fsdp_id + shift) % fsdp_count * piece_rows, piece_rows, 0
            )
            for shift in range(fsdp_count)
        ]
        qkv_piece = sum_pieces(owner_pieces, "fsdp")
        vectors = jnp.stack(
            [norm_sums[0], sums[0], norm_sums[1], sums[2], sums[1], sums[3]]
        )
        d_up_bias = up_sums.reshape(-1)
        return grad_in, share, qkv_piece, joined_sums, vectors, d_up_bias

    forward_pairs = [(i, i + 1) for i in range(sections - 1)]
    entering = fresh
    for _ in range(sections - 1):
        result, _ = forward(entering)
        received = lax.ppermute(result, "section", forward_pairs)
        entering = jnp.where(section_id == 0, fresh, received)
    layer_out, saved = forward(entering)

    back_pairs = [(i + 1, i) for i in range(sections - 1)]
    grad_low = top_grad
    for _ in range(sections - 1):
        result, kept = backward(grad_low, saved, None)
        received = lax.ppermute(result, "section", back_pairs)
        grad_low = jnp.where(section_id == sections - 1, top_grad, received)
        pairs = [(value, swap(value)) for value in kept[:3]]
        grad_low, pairs = lax.optimization_barrier((grad_low, pairs))
        kept = (pairs, kept[3:])
    input_grad, share, qkv_piece, joined_sums, vectors, d_up_bias = backward(grad_low, saved, kept)

    ours = jnp.arange(fsdp_count)[:, None] == group_id
    vector_parts = jnp.concatenate(
        [
            vectors.reshape(6, -1, shard).transpose(1, 0, 2).reshape(-1, 6 * shard),
            jnp.where(ours, joined_sums[None, :WIDTH], 0.0),
            jnp.where(ours, joined_sums[None, 2 * WIDTH :], 0.0),
            d_up_bias.reshape(fsdp_count, -1),
        ],
        1,
    )
    vector_parts = vector_parts.astype(jnp.bfloat16).reshape(fsdp_count, 4, 3 * WIDTH)
    vector_share = sum_low(exchange(vector_parts, "fsdp"))
    vector_share = jnp.pad(vector_share, ((0, 12), (0, 0)))
    qkv_piece = jnp.concatenate([qkv_piece, vector_share], 0)
    qkv_piece = jnp.pad(qkv_piece, ((0, 0), (0, model_width - 3 * WIDTH)))
    joint_piece = sum_low(exchange(share.reshape(8, -1, model_width), ("x", "yh")))
    joint_piece, layer_out = lax.optimization_barrier((joint_piece, layer_out))
    both = spread(jnp.concatenate([joint_piece, qkv_piece], 0), ("x", "yh"))
    g_qkv, g_out, g_up, g_down, vector_sum = unpack(
        core_number, both, swap(both), shard, mlp_in.shape[2], mlp_out.shape[1]
    )
    vector_sum = vector_sum[:, : 3 * WIDTH].reshape(-1)
    own_vectors = vector_sum[: 8 * shard].reshape(8, shard)
    own_up_bias = vector_sum[8 * shard :]
    order = (2, 6, 7, 3, 4, 5)
    g_biases = jnp.stack([own_vectors[place] for place in order])
    out_shape = (1, micro_count, 1, local_rows, model_width)
    return (
        layer_out.reshape(out_shape),
        input_grad.reshape(out_shape),
        g_qkv[None],
        g_out[None],
        g_up[None],
        g_down[None],
        own_vectors[None, :2],
        g_biases[None],
        own_up_bias[None],
    )


def solution(mesh):
    fine = Mesh(
        mesh.devices.reshape(2, 4, 2, 2, 4), ("section", "x", "yh", "core", "fsdp")
    )
    rows = P(None, "fsdp", CTX, None)
    weight = P("section", "fsdp", None)
    vector = P("section", None, "fsdp")
    row = P("section", "fsdp")
    out_rows = P("section", None, "fsdp", CTX, None)
    return jax.shard_map(
        shards,
        mesh=fine,
        in_specs=(rows, rows, P(), P(), weight, weight, weight, weight, vector, vector, row),
        out_specs=(out_rows, out_rows, weight, weight, weight, weight, vector, vector, row),
        check_vma=False,
    )
```

```python
import functools

import jax
import jax.numpy as jnp
from jax import lax
from jax.experimental import pallas as pl
from jax.experimental.pallas import tpu as pltpu
from jax.sharding import Mesh
from jax.sharding import PartitionSpec as P

HEADS = 12
HDIM = 64
GROUPS = 4
GROUP_HEADS = HEADS // GROUPS
WIDTH = GROUP_HEADS * HDIM
QUERY_BLOCK = 256
VECTOR_ROWS = 4
CTX = ("x", "yh", "core")

epsilon = 1e-05
neg_fill = -1e30
GELU_SCALE = (2.0 / 3.141592653589793) ** 0.5
GELU_CUBE = 0.044715


def dot(left_side, right_side, left_dim, right_dim):
    return lax.dot_general(
        left_side,
        right_side,
        (((left_dim,), (right_dim,)), ((), ())),
        preferred_element_type=jnp.float32,
    )


def head_columns(part, head):
    start = part * WIDTH + head * HDIM
    return slice(start, start + HDIM)


def whole(*shape):
    return pl.BlockSpec(shape, lambda i, *unused: (0,) * len(shape))


def sort_rows(target, source, table, back):
    blocks = table.shape[0]
    size = source.shape[0] // blocks
    for block in range(blocks):
        fixed = slice(block * size, (block + 1) * size)
        moved = pl.ds(pl.multiple_of(table[block] * size, size), size)
        if back:
            target[fixed, :] = source[moved, :]
        else:
            target[moved, :] = source[fixed, :]


def place_weight(target, members, ids):
    count, rows = len(members), members[0].shape[0]
    for shift, member in enumerate(members):
        place = lax.rem(ids[1] + shift - 2 * ids[0] + count, count)
        target[pl.ds(pl.multiple_of(place * rows, rows), rows), :] = member[...]


def mask_scores(scores):
    count = scores.shape[0] - QUERY_BLOCK
    tile = (QUERY_BLOCK, QUERY_BLOCK)
    visible = lax.broadcasted_iota(jnp.int32, tile, 0) <= lax.broadcasted_iota(jnp.int32, tile, 1)
    masked = jnp.where(visible, scores[count:], neg_fill)
    return jnp.concatenate([scores[:count], masked], 0) if count else masked


def attend_body(
    table, ids, own, other, w0, w1, w2, w3, bias, joined, mixed, log_total, weight, scratch, sorted_out
):
    step = pl.program_id(0)
    half = own.shape[1]

    @pl.when(step == 0)
    def _():
        place_weight(weight, (w0, w1, w2, w3), ids)
        product = dot(own[...], weight[:half, :], 1, 0) + dot(other[...], weight[half:, :], 1, 0)
        scratch[...] = (product + bias[...]).astype(jnp.bfloat16)
        sort_rows(joined, scratch, table, False)

    def block(index):
        rows = slice(index * QUERY_BLOCK, (index + 1) * QUERY_BLOCK)
        seen = slice(0, (index + 1) * QUERY_BLOCK)
        parts = []
        for head in range(GROUP_HEADS):
            queries = joined[rows, head_columns(0, head)] * jnp.bfloat16(HDIM ** (-0.5))
            keys = joined[seen, head_columns(1, head)]
            values = joined[seen, head_columns(2, head)]
            scores = mask_scores(dot(keys, queries, 1, 1))
            top = jnp.max(scores, 0, keepdims=True)
            powers = jnp.exp(scores - top)
            total = jnp.sum(powers, 0, keepdims=True)
            parts.append(dot(values, powers.astype(jnp.bfloat16), 0, 0) / total)
            log_total[head : head + 1, rows] = top + jnp.log(total)
        sorted_out[rows, :] = jnp.concatenate(parts, 0).T.astype(jnp.bfloat16)

    for index in range(own.shape[0] // QUERY_BLOCK):
        pl.when(step == index)(lambda index=index: block(index))

    @pl.when(step == pl.num_programs(0) - 1)
    def _():
        sort_rows(mixed, sorted_out, table, True)


def attend(table, ids, own, other, weights, bias):
    count, half = own.shape
    return pl.pallas_call(
        attend_body,
        grid_spec=pltpu.PrefetchScalarGridSpec(
            num_scalar_prefetch=2,
            grid=(count // QUERY_BLOCK,),
            in_specs=[whole(count, half)] * 2
            + [whole(*weight.shape) for weight in weights]
            + [whole(1, 3 * WIDTH)],
            out_specs=[whole(count, 3 * WIDTH), whole(count, WIDTH), whole(8, count)],
            scratch_shapes=[
                pltpu.VMEM((2 * half, 3 * WIDTH), jnp.bfloat16),
                pltpu.VMEM((count, 3 * WIDTH), jnp.bfloat16),
                pltpu.VMEM((count, WIDTH), jnp.bfloat16),
            ],
        ),
        out_shape=[
            jax.ShapeDtypeStruct((count, 3 * WIDTH), jnp.bfloat16),
            jax.ShapeDtypeStruct((count, WIDTH), jnp.bfloat16),
            jax.ShapeDtypeStruct((8, count), jnp.float32),
        ],
        compiler_params=pltpu.CompilerParams(vmem_limit_bytes=48 << 20),
        cost_estimate=pl.CostEstimate(
            flops=4 * count * count * WIDTH,
            bytes_accessed=8 * count * WIDTH,
            transcendentals=count * count * GROUP_HEADS,
        ),
    )(table, ids, own, other, *weights, bias)


def attend_back_body(
    table,
    ids,
    joined,
    grad_mixed,
    log_total,
    w0,
    w1,
    w2,
    w3,
    grad_joined,
    grad_own,
    grad_other,
    weight,
    sorted_grads,
    sorted_out,
    key_sums,
    value_sums,
):
    step = pl.program_id(0)
    half = grad_own.shape[1]

    @pl.when(step == 0)
    def _():
        place_weight(weight, (w0, w1, w2, w3), ids)
        sort_rows(sorted_grads, grad_mixed, table, False)
        key_sums[...] = jnp.zeros_like(key_sums)
        value_sums[...] = jnp.zeros_like(value_sums)

    def block(index):
        rows = slice(index * QUERY_BLOCK, (index + 1) * QUERY_BLOCK)
        seen = slice(0, (index + 1) * QUERY_BLOCK)
        parts = []
        for head in range(GROUP_HEADS):
            queries = joined[rows, head_columns(0, head)] * jnp.bfloat16(HDIM ** (-0.5))
            keys = joined[seen, head_columns(1, head)]
            values = joined[seen, head_columns(2, head)]
            grads = sorted_grads[rows, head_columns(0, head)]
            scores = mask_scores(dot(keys, queries, 1, 1))
            weights = jnp.exp(scores - log_total[head : head + 1, rows])
            grad_weights = dot(values, grads, 1, 1)
            inner_sum = jnp.sum(weights * grad_weights, 0, keepdims=True)
            grad_scores = (weights * (grad_weights - inner_sum)).astype(jnp.bfloat16)
            value_sums[head, seen, :] += dot(weights.astype(jnp.bfloat16), grads, 1, 0)
            key_sums[head, seen, :] += dot(grad_scores, queries, 1, 0)
            parts.append(dot(keys, grad_scores, 0, 0) * (HDIM ** (-0.5)))
        sorted_out[rows, :WIDTH] = jnp.concatenate(parts, 0).T.astype(jnp.bfloat16)

    for index in range(joined.shape[0] // QUERY_BLOCK):
        pl.when(step == index)(lambda index=index: block(index))

    @pl.when(step == pl.num_programs(0) - 1)
    def _():
        for head in range(GROUP_HEADS):
            sorted_out[:, head_columns(1, head)] = key_sums[head].astype(jnp.bfloat16)
            sorted_out[:, head_columns(2, head)] = value_sums[head].astype(jnp.bfloat16)
        sort_rows(grad_joined, sorted_out, table, True)
        grad_own[...] = dot(grad_joined[...], weight[:half, :], 1, 1).astype(jnp.bfloat16)
        grad_other[...] = dot(grad_joined[...], weight[half:, :], 1, 1).astype(jnp.bfloat16)


def attend_back(table, ids, joined, grad_mixed, log_total, weights):
    count = joined.shape[0]
    half = len(weights) * weights[0].shape[0] // 2
    return pl.pallas_call(
        attend_back_body,
        grid_spec=pltpu.PrefetchScalarGridSpec(
            num_scalar_prefetch=2,
            grid=(count // QUERY_BLOCK,),
            in_specs=[whole(count, 3 * WIDTH), whole(count, WIDTH), whole(8, count)]
            + [whole(*weight.shape) for weight in weights],
            out_specs=[whole(count, 3 * WIDTH), whole(count, half), whole(count, half)],
            scratch_shapes=[
                pltpu.VMEM((2 * half, 3 * WIDTH), jnp.bfloat16),
                pltpu.VMEM((count, WIDTH), jnp.bfloat16),
                pltpu.VMEM((count, 3 * WIDTH), jnp.bfloat16),
                pltpu.VMEM((GROUP_HEADS, count, HDIM), jnp.float32),
                pltpu.VMEM((GROUP_HEADS, count, HDIM), jnp.float32),
            ],
        ),
        out_shape=[
            jax.ShapeDtypeStruct((count, 3 * WIDTH), jnp.bfloat16),
            jax.ShapeDtypeStruct((count, half), jnp.bfloat16),
            jax.ShapeDtypeStruct((count, half), jnp.bfloat16),
        ],
        compiler_params=pltpu.CompilerParams(vmem_limit_bytes=48 << 20),
        cost_estimate=pl.CostEstimate(
            flops=10 * count * count * WIDTH,
            bytes_accessed=16 * count * WIDTH,
            transcendentals=count * count * GROUP_HEADS,
        ),
    )(table, ids, joined, grad_mixed, log_total, *weights)


def weight_grads_body(
    core_id,
    active,
    active_other,
    grad_low,
    grad_low_other,
    normed_two,
    normed_two_other,
    grad_hidden,
    grad_hidden_other,
    mixed,
    mixed_other,
    grad_attn,
    grad_attn_other,
    joint,
):
    down_rows, up_rows = active.shape[1], normed_two.shape[0]
    width = grad_low.shape[1]
    product = dot(active[...], grad_low[...], 0, 0)
    product += dot(active_other[...], grad_low_other[...], 0, 0)
    joint[0, :down_rows, :] = product.astype(jnp.bfloat16)
    place = down_rows
    for panel in range(grad_hidden.shape[1] // width):
        columns = slice(panel * width, (panel + 1) * width)
        product = dot(normed_two[...], grad_hidden[:, columns], 1, 0)
        product += dot(normed_two_other[...], grad_hidden_other[:, columns], 1, 0)
        joint[0, place : place + up_rows, :] = product.astype(jnp.bfloat16)
        place += up_rows
    product = dot(mixed[...], grad_attn[...], 1, 0)
    product += dot(mixed_other[...], grad_attn_other[...], 1, 0)
    joint[0, place : place + up_rows, :] = product.astype(jnp.bfloat16)


def weight_grads(core_id, pairs, members):
    rows, hidden_width = pairs[0][0].shape
    width = pairs[1][0].shape[1]
    down_rows, up_rows = hidden_width // members // 2, width // members // 2
    out_rows = 2 * down_rows + up_rows
    flat = pl.BlockSpec((rows, width), lambda i, core: (0, 0))
    tall = pl.BlockSpec((up_rows, rows), lambda i, core: (2 * i + core[0], 0))
    specs = [
        pl.BlockSpec((rows, down_rows), lambda i, core: (0, 2 * i + core[0])),
        flat,
        tall,
        pl.BlockSpec((rows, hidden_width), lambda i, core: (0, 0)),
        tall,
        flat,
    ]
    return pl.pallas_call(
        weight_grads_body,
        grid_spec=pltpu.PrefetchScalarGridSpec(
            num_scalar_prefetch=1,
            grid=(members,),
            in_specs=[spec for spec in specs for _ in range(2)],
            out_specs=pl.BlockSpec((1, out_rows, width), lambda i, core: (i, 0, 0)),
        ),
        out_shape=jax.ShapeDtypeStruct((members, out_rows, width), jnp.bfloat16),
        compiler_params=pltpu.CompilerParams(vmem_limit_bytes=48 << 20),
        cost_estimate=pl.CostEstimate(
            flops=2 * rows * width * (2 * hidden_width + width),
            bytes_accessed=2 * members * out_rows * width,
            transcendentals=0,
        ),
    )(core_id, *[value for pair in pairs for value in pair])


def weight_panel(packed, start):
    members, width = packed.shape[0], packed.shape[2]
    rows = width // members
    return jnp.concatenate([packed[i, start : start + rows, :] for i in range(members)], 0)


def join_groups(mixed, group):
    micro_count = mixed.shape[0] // GROUPS
    return jnp.concatenate([mixed[m * GROUPS + group] for m in range(micro_count)], 0)


def attend_out(mixed, entering, packed, vectors, w_out):
    middle = entering[...].astype(jnp.float32) + vectors[5:6, :]
    for group in range(GROUPS):
        rows = slice(group * WIDTH, (group + 1) * WIDTH)
        middle += dot(join_groups(mixed, group), w_out[rows, :], 1, 0)
    return middle


def start_copies(stored, packed, landed, panels):
    members, width = packed.shape[0], packed.shape[2]
    up_rows = width // members
    down_rows = panels * up_rows
    per_panel = members // panels

    def copy(index, rows, sources):
        here = (slice(None) if sources is None else sources, rows)
        return pltpu.make_async_copy(stored.at[here], packed.at[here], landed.at[index])

    out = copy(0, pl.ds(2 * down_rows, up_rows), None)
    ups, downs = [], []
    for panel in range(panels):
        ups.append(copy(1 + panel, pl.ds(down_rows + panel * up_rows, up_rows), None))
        downs.append(
            copy(1 + panels + panel, pl.ds(0, down_rows), pl.ds(panel * per_panel, per_panel))
        )
    return out, ups, downs


def feed_forward_body(mixed, entering, stored, vectors, up_bias, result, packed, landed):
    members, width = packed.shape[0], packed.shape[2]
    panels = up_bias.shape[0]
    up_rows = width // members
    down_rows = panels * up_rows
    out, ups, downs = start_copies(stored, packed, landed, panels)
    for copy in [out] + ups + downs:
        copy.start()
    out.wait()
    middle = attend_out(mixed, entering, packed, vectors, weight_panel(packed, 2 * down_rows))
    normed, _, _ = normalize(middle, vectors[1:2, :], vectors[6:7, :])
    normed = normed.astype(jnp.bfloat16)
    parts = []
    for panel in range(panels):
        ups[panel].wait()
        hidden = dot(normed, weight_panel(packed, down_rows + panel * up_rows), 1, 0)
        hidden = hidden + up_bias[panel : panel + 1, :]
        parts.append(jax.nn.gelu(hidden).astype(jnp.bfloat16))
    active = jnp.concatenate(parts, 1)
    total = middle + vectors[7:8, :]
    for member in range(members):
        if member % (members // panels) == 0:
            downs[member // (members // panels)].wait()
        columns = slice(member * down_rows, (member + 1) * down_rows)
        total += dot(active[:, columns], packed[member, :down_rows, :], 1, 0)
    result[...] = total.astype(jnp.bfloat16)


def feed_specs(count):
    specs = [pl.BlockSpec(memory_space=pltpu.VMEM) for _ in range(count)]
    specs[2] = pl.BlockSpec(memory_space=pl.ANY)
    return specs


def feed_scratch(packed, up_bias):
    return [
        pltpu.VMEM(packed.shape, packed.dtype),
        pltpu.SemaphoreType.DMA((1 + 2 * up_bias.shape[0],)),
    ]


def feed_forward(mixed, entering, packed, vectors, up_bias):
    rows, width = entering.shape
    return pl.pallas_call(
        feed_forward_body,
        in_specs=feed_specs(5),
        out_specs=pl.BlockSpec(memory_space=pltpu.VMEM),
        scratch_shapes=feed_scratch(packed, up_bias),
        out_shape=jax.ShapeDtypeStruct((rows, width), jnp.bfloat16),
        compiler_params=pltpu.CompilerParams(vmem_limit_bytes=48 << 20),
        cost_estimate=pl.CostEstimate(
            flops=18 * rows * width * width,
            bytes_accessed=18 * width * width,
            transcendentals=4 * rows * width,
        ),
    )(mixed, entering, packed, vectors, up_bias)


def feed_back_end(grads, grad_normed, unit, spread_two, vectors, w_out, grad_mixed, grad_middle):
    local_rows = grad_mixed.shape[1]
    grad_top = grads.astype(jnp.float32)
    grad_norm, d_gain, d_shift = normalize_back(grad_normed, unit, spread_two, vectors[1:2, :])
    grad_sum = grad_top + grad_norm
    grad_middle[...] = grad_sum
    grad_attn = grad_sum.astype(jnp.bfloat16)
    for group in range(GROUPS):
        part = dot(grad_attn, w_out[group * WIDTH : (group + 1) * WIDTH, :], 1, 1)
        part = part.astype(jnp.bfloat16)
        for m in range(grad_mixed.shape[0] // GROUPS):
            grad_mixed[m * GROUPS + group] = part[m * local_rows : (m + 1) * local_rows]
    return grad_attn, d_gain, d_shift


def down_panel(packed, panel, panels):
    members, width = packed.shape[0], packed.shape[2]
    each = members // panels
    rows = panels * width // members
    return jnp.concatenate(
        [packed[i, :rows, :] for i in range(panel * each, (panel + 1) * each)], 0
    )


def feed_back_first_body(
    mixed,
    entering,
    packed,
    vectors,
    up_bias,
    grad_low,
    grad_mixed,
    grad_middle,
    active,
    normed_tall,
    mixed_tall,
    slopes,
    units,
    spreads,
):
    members, width = packed.shape[0], packed.shape[2]
    panels = up_bias.shape[0]
    up_rows = width // members
    down_rows = panels * up_rows
    w_out = weight_panel(packed, 2 * down_rows)
    middle = attend_out(mixed, entering, packed, vectors, w_out)
    normed, unit, spread_two = normalize(middle, vectors[1:2, :], vectors[6:7, :])
    normed = normed.astype(jnp.bfloat16)
    grads = grad_low[...]
    grad_normed = jnp.zeros(middle.shape, jnp.float32)
    for panel in range(panels):
        columns = slice(panel * width, (panel + 1) * width)
        w_up = weight_panel(packed, down_rows + panel * up_rows)
        hidden = dot(normed, w_up, 1, 0) + up_bias[panel : panel + 1, :]
        square = hidden * hidden
        bend = jnp.tanh(GELU_SCALE * (hidden + GELU_CUBE * (square * hidden)))
        slope = 0.5 * (1.0 + bend) + 0.5 * hidden * (1.0 - bend * bend) * (
            GELU_SCALE * (1.0 + 3.0 * GELU_CUBE * square)
        )
        slopes[:, columns] = slope
        active[:, columns] = (0.5 * hidden * (1.0 + bend)).astype(jnp.bfloat16)
        w_down = down_panel(packed, panel, panels)
        grad_hidden = (dot(grads, w_down, 1, 1) * slope).astype(jnp.bfloat16)
        grad_normed += dot(grad_hidden, w_up, 1, 1)
    feed_back_end(grads, grad_normed, unit, spread_two, vectors, w_out, grad_mixed, grad_middle)
    units[...] = unit
    spreads[...] = jnp.broadcast_to(spread_two, spreads.shape)
    normed_tall[...] = normed.astype(jnp.float32).T.astype(jnp.bfloat16)
    for group in range(GROUPS):
        part = join_groups(mixed, group).astype(jnp.float32).T.astype(jnp.bfloat16)
        mixed_tall[group * WIDTH : (group + 1) * WIDTH, :] = part


def feed_back_last_body(
    packed,
    vectors,
    grad_low,
    slopes,
    units,
    spreads,
    grad_mixed,
    grad_middle,
    grad_hidden,
    grad_attn,
    sums,
    up_sums,
):
    members, width = packed.shape[0], packed.shape[2]
    panels = up_sums.shape[0]
    up_rows = width // members
    down_rows = panels * up_rows
    w_out = weight_panel(packed, 2 * down_rows)
    grads = grad_low[...]
    grad_normed = jnp.zeros(units.shape, jnp.float32)
    for panel in range(panels):
        columns = slice(panel * width, (panel + 1) * width)
        w_up = weight_panel(packed, down_rows + panel * up_rows)
        w_down = down_panel(packed, panel, panels)
        part = (dot(grads, w_down, 1, 1) * slopes[:, columns]).astype(jnp.bfloat16)
        grad_normed += dot(part, w_up, 1, 1)
        grad_hidden[:, columns] = part
        up_sums[panel : panel + 1, :] = jnp.sum(part.astype(jnp.float32), 0, keepdims=True)
    attn, d_gain, d_shift = feed_back_end(
        grads, grad_normed, units[...], spreads[:, :1], vectors, w_out, grad_mixed, grad_middle
    )
    grad_attn[...] = attn
    sums[0:1, :] = d_gain[None]
    sums[1:2, :] = d_shift[None]
    sums[2:3, :] = jnp.sum(attn.astype(jnp.float32), 0, keepdims=True)
    sums[3:4, :] = jnp.sum(grads.astype(jnp.float32), 0, keepdims=True)


def feed_back(body, args, shapes):
    rows, width = shapes[1][0]
    return pl.pallas_call(
        body,
        in_specs=[pl.BlockSpec(memory_space=pltpu.VMEM)] * len(args),
        out_specs=[pl.BlockSpec(memory_space=pltpu.VMEM)] * len(shapes),
        out_shape=[jax.ShapeDtypeStruct(*shape) for shape in shapes],
        compiler_params=pltpu.CompilerParams(vmem_limit_bytes=56 << 20),
        cost_estimate=pl.CostEstimate(
            flops=28 * rows * width * width,
            bytes_accessed=24 * width * width,
            transcendentals=4 * rows * width,
        ),
    )(*args)


def norm_back_body(returned, entering, grad_middle, vectors, grad_in, sums):
    parts = []
    for m in range(returned.shape[0] // GROUPS):
        halves = [
            returned[m * GROUPS + core].astype(jnp.float32)
            + returned[m * GROUPS + 2 + core].astype(jnp.float32)
            for core in range(2)
        ]
        parts.append(jnp.concatenate(halves, 1))
    grad_normed = jnp.concatenate(parts, 0)
    gain = vectors[0:1, :]
    _, unit, spread_one = normalize(entering[...].astype(jnp.float32), gain, vectors[2:3, :])
    grad_norm, d_gain, d_shift = normalize_back(grad_normed, unit, spread_one, gain)
    grad_in[...] = (grad_middle[...] + grad_norm).astype(jnp.bfloat16)
    sums[0:1, :] = d_gain[None]
    sums[1:2, :] = d_shift[None]


def norm_back(returned, entering, grad_middle, vectors):
    rows, width = entering.shape
    return pl.pallas_call(
        norm_back_body,
        in_specs=[pl.BlockSpec(memory_space=pltpu.VMEM)] * 4,
        out_specs=[pl.BlockSpec(memory_space=pltpu.VMEM)] * 2,
        out_shape=[
            jax.ShapeDtypeStruct((rows, width), jnp.bfloat16),
            jax.ShapeDtypeStruct((2, width), jnp.float32),
        ],
        compiler_params=pltpu.CompilerParams(vmem_limit_bytes=32 << 20),
        cost_estimate=pl.CostEstimate(
            flops=20 * rows * width, bytes_accessed=10 * rows * width, transcendentals=rows
        ),
    )(returned, entering, grad_middle, vectors)


def qkv_grads_body(owners, ids, own, other, grad_joined, *outs):
    pieces, sums, both = outs[:-2], outs[-2], outs[-1]
    first_core = ids[0] == 0
    grads = grad_joined[...]
    half = own.shape[1]
    own_grads = dot(own[...], grads, 0, 0).astype(jnp.bfloat16)
    other_grads = dot(other[...], grads, 0, 0).astype(jnp.bfloat16)
    both[:half, :] = jnp.where(first_core, own_grads, other_grads)
    both[half:, :] = jnp.where(first_core, other_grads, own_grads)
    count = len(pieces)
    rows = pieces[0].shape[0] // owners
    for shift in range(count):
        place = lax.rem(ids[2] + shift, count) * rows
        for owner in range(owners):
            start = pl.multiple_of(owner * rows * count + place, rows)
            pieces[shift][owner * rows : (owner + 1) * rows, :] = both[pl.ds(start, rows), :]
    sums[...] = jnp.sum(grads.astype(jnp.float32), 0, keepdims=True)


def qkv_grads(ids, own, other, grad_joined, count, owners):
    rows, half = own.shape
    width = grad_joined.shape[1]
    piece = jax.ShapeDtypeStruct((2 * half // count, width), jnp.bfloat16)
    return pl.pallas_call(
        functools.partial(qkv_grads_body, owners),
        in_specs=[pl.BlockSpec(memory_space=pltpu.SMEM)]
        + [pl.BlockSpec(memory_space=pltpu.VMEM)] * 3,
        out_specs=[pl.BlockSpec(memory_space=pltpu.VMEM)] * (count + 1),
        out_shape=[piece] * count + [jax.ShapeDtypeStruct((1, width), jnp.float32)],
        scratch_shapes=[pltpu.VMEM((2 * half, width), jnp.bfloat16)],
        compiler_params=pltpu.CompilerParams(vmem_limit_bytes=48 << 20),
        cost_estimate=pl.CostEstimate(
            flops=4 * rows * half * width, bytes_accessed=6 * rows * half, transcendentals=0
        ),
    )(ids, own, other, grad_joined)


def unpack_body(core_id, own, other, g_qkv, g_out, g_up, g_down, vectors):
    first_core = core_id[0] == 0
    count = own.shape[0]
    width = own.shape[2]
    piece_rows = g_qkv.shape[0] // (count // 2)
    joint_end = own.shape[1] - VECTOR_ROWS
    up_rows = g_up.shape[0] // 2
    down_rows = g_down.shape[0] // 2
    sums = jnp.zeros(vectors.shape, jnp.float32)
    for core in range(2):
        pick = first_core if core == 0 else jnp.logical_not(first_core)
        blocks = [jnp.where(pick, own[i], other[i]).astype(jnp.float32) for i in range(count)]
        joint = jnp.concatenate([block[piece_rows:joint_end] for block in blocks], 0)
        g_down[core * down_rows : (core + 1) * down_rows, :] = joint[:down_rows]
        place = down_rows
        for panel in range(g_up.shape[1] // width):
            g_up[core * up_rows : (core + 1) * up_rows, panel * width : (panel + 1) * width] = (
                joint[place : place + up_rows]
            )
            place += up_rows
        g_out[core * up_rows : (core + 1) * up_rows, :] = joint[place : place + up_rows]
        for i, block in enumerate(blocks):
            x_id, group = i // 2, (i % 2) * 2 + core
            for part in range(3):
                start = part * width + group * WIDTH
                g_qkv[x_id * piece_rows : (x_id + 1) * piece_rows, start : start + WIDTH] = block[
                    :piece_rows, part * WIDTH : (part + 1) * WIDTH
                ]
            sums += block[joint_end:]
    vectors[...] = sums


def unpack(core_id, own, other, shard, hidden_width, hidden_shard):
    width = own.shape[2]
    return pl.pallas_call(
        unpack_body,
        in_specs=[pl.BlockSpec(memory_space=pltpu.SMEM)]
        + [pl.BlockSpec(memory_space=pltpu.VMEM)] * 2,
        out_specs=[pl.BlockSpec(memory_space=pltpu.VMEM)] * 5,
        out_shape=[
            jax.ShapeDtypeStruct((shard, 3 * width), jnp.float32),
            jax.ShapeDtypeStruct((shard, width), jnp.float32),
            jax.ShapeDtypeStruct((shard, hidden_width), jnp.float32),
            jax.ShapeDtypeStruct((hidden_shard, width), jnp.float32),
            jax.ShapeDtypeStruct((4, width), jnp.float32),
        ],
        compiler_params=pltpu.CompilerParams(vmem_limit_bytes=48 << 20),
        cost_estimate=pl.CostEstimate(flops=0, bytes_accessed=12 << 20, transcendentals=0),
    )(core_id, own, other)


def normalize(values, gain_row, shift_row):
    center = values - jnp.mean(values, -1, keepdims=True)
    spread = lax.rsqrt(jnp.mean(center * center, -1, keepdims=True) + epsilon)
    unit_rows = center * spread
    return (unit_rows * gain_row + shift_row, unit_rows, spread)


def normalize_back(grad_out, unit_rows, spread, gain_row):
    grad_unit = grad_out * gain_row
    grad_in = spread * (
        grad_unit
        - jnp.mean(grad_unit, -1, keepdims=True)
        - unit_rows * jnp.mean(grad_unit * unit_rows, -1, keepdims=True)
    )
    return (grad_in, jnp.sum(grad_out * unit_rows, 0), jnp.sum(grad_out, 0))


def exchange(value, axes):
    return lax.all_to_all(value, axes, 0, 0, tiled=True)


def swap(value):
    return lax.ppermute(value, "core", [(0, 1), (1, 0)])


def in_order(own, other):
    first = lax.axis_index("core") == 0
    return jnp.where(first, own, other), jnp.where(first, other, own)


def pack_weights(attn_out, mlp_in, mlp_out):
    core_id = lax.axis_index("core")
    width = attn_out.shape[2]
    out_half, up_half, down_half = (
        lax.dynamic_slice_in_dim(
            weight[0], core_id * (weight.shape[1] // 2), weight.shape[1] // 2, 0
        )
        for weight in (attn_out, mlp_in, mlp_out)
    )
    panels = [up_half[:, start : start + width] for start in range(0, mlp_in.shape[2], width)]
    return jnp.concatenate([down_half] + panels + [out_half], 0)


def ring_pairs(axis, shift):
    count = lax.axis_size(axis)
    return [(source, (source + shift) % count) for source in range(count)]


def gather_ring(value, axis):
    return [value] + [
        lax.ppermute(value, axis, ring_pairs(axis, -shift))
        for shift in range(1, lax.axis_size(axis))
    ]


def sum_pieces(pieces, axis):
    total = pieces[0].astype(jnp.float32)
    for shift in range(1, len(pieces)):
        received = lax.ppermute(pieces[shift], axis, ring_pairs(axis, shift))
        total = total + received.astype(jnp.float32)
    return total.astype(jnp.bfloat16)


def sum_low(value):
    return jnp.sum(value.astype(jnp.float32), 0).astype(jnp.bfloat16)


def spread(value, axes):
    count = lax.axis_size(axes)
    return exchange(jnp.broadcast_to(value[None], (count,) + value.shape), axes)


def shards(
    inputs,
    cotangent,
    plan,
    block_table,
    attn_in,
    attn_out,
    mlp_in,
    mlp_out,
    norm_gains,
    biases,
    mlp_bias,
):
    shard = norm_gains.shape[2]
    core_id = lax.axis_index("core")
    group_id = lax.axis_index("yh") * 2 + core_id
    fsdp_id = lax.axis_index("fsdp")
    section_id = lax.axis_index("section")
    sections = lax.axis_size("section")
    fsdp_count = lax.axis_size("fsdp")

    small = jnp.concatenate([norm_gains[0], biases[0], mlp_bias.reshape(-1, shard)], 0)
    small = small.reshape(-1, 3 * WIDTH)
    own_columns = lax.dynamic_index_in_dim(
        attn_in[0].reshape(shard, 3, GROUPS, WIDTH), group_id, 2, keepdims=False
    ).reshape(shard, 3 * WIDTH)
    small_all = spread(small, "fsdp").reshape(fsdp_count, -1, shard).astype(jnp.float32)
    w_group = gather_ring(own_columns, "fsdp")
    small_all, w_group[1], w_group[3] = lax.optimization_barrier(
        (small_all, w_group[1], w_group[3])
    )
    packed = pack_weights(attn_out, mlp_in, mlp_out)
    packed = lax.all_gather(packed, ("fsdp", "core"), axis=0)
    model_width = attn_out.shape[2]
    hidden_width = mlp_in.shape[2]
    half = model_width // 2
    vector_rows = small_all[:, :8].transpose(1, 0, 2).reshape(8, model_width)
    gain_rows, bias_rows = vector_rows[:2], vector_rows[2:]
    up_rows = small_all[:, 8:].reshape(-1, model_width)
    own_bias = lax.dynamic_index_in_dim(small_all, group_id, 0, keepdims=False)
    group_bias = jnp.concatenate([own_bias[3], jnp.zeros_like(own_bias[3]), own_bias[4]])[None]

    micro_count, _, local_rows, _ = inputs.shape
    rows = micro_count * local_rows
    fresh = jnp.stack(
        [lax.dynamic_index_in_dim(inputs, plan[step], 0, keepdims=False) for step in range(micro_count)]
    ).reshape(rows, model_width)
    top_grad = cotangent.reshape(rows, model_width)
    core_number = core_id.astype(jnp.int32)[None]
    numbers = jnp.stack([core_id, fsdp_id, lax.axis_index("x")]).astype(jnp.int32)

    def forward(entering):
        stream = entering.astype(jnp.float32)
        normed, _, _ = normalize(stream, gain_rows[0], bias_rows[0])
        halves = normed.astype(jnp.bfloat16).reshape(micro_count, 1, local_rows, 2, half)
        halves = jnp.broadcast_to(
            halves.transpose(0, 1, 3, 2, 4), (micro_count, 2, 2, local_rows, half)
        )
        own = exchange(halves.reshape(-1, local_rows, half), CTX).reshape(-1, half)
        own, weights = lax.optimization_barrier((own, w_group))
        other = swap(own)
        joined, mixed_heads, log_total = attend(
            block_table, numbers, own, other, weights, group_bias
        )
        mixed = exchange(mixed_heads.reshape(-1, local_rows, WIDTH), CTX)
        result = feed_forward(mixed, entering, packed, vector_rows, up_rows)
        return result, (entering, own, other, joined, log_total, mixed)

    def backward(grad_low, saved, kept):
        entering, own, other, joined, log_total, mixed = saved
        last = kept is not None
        low, full = jnp.bfloat16, jnp.float32
        shapes = [(mixed.shape, low), ((rows, model_width), full), ((rows, hidden_width), low)]
        if last:
            pairs, plain = kept
            shapes += [((rows, model_width), low), ((4, model_width), full), (up_rows.shape, full)]
            grad_mixed, grad_middle, *extra = feed_back(
                feed_back_last_body, (packed, vector_rows, grad_low, *plain), shapes
            )
        else:
            shapes += [((model_width, rows), low)] * 2
            shapes += [((rows, hidden_width), full), ((rows, model_width), full), ((rows, 128), full)]
            grad_mixed, grad_middle, *extra = feed_back(
                feed_back_first_body,
                (mixed, entering, packed, vector_rows, up_rows, grad_low),
                shapes,
            )
        grad_heads = exchange(grad_mixed.reshape(-1, local_rows, WIDTH), CTX).reshape(-1, WIDTH)
        if last:
            grad_hidden, grad_attn, sums, up_sums = extra
            active_pair, normed_pair, mixed_pair = pairs
            low_pair, hidden_pair, attn_pair = (
                (value, swap(value)) for value in (grad_low, grad_hidden, grad_attn)
            )
            joint = weight_grads(
                core_number,
                [active_pair, low_pair, normed_pair, hidden_pair, mixed_pair, attn_pair],
                fsdp_count,
            )
            grad_heads, joint = lax.optimization_barrier((grad_heads, joint))
            share = lax.psum_scatter(
                joint.reshape(-1, model_width),
                "fsdp",
                scatter_dimension=0,
                tiled=True,
            )
        grad_joined, grad_own, grad_other = attend_back(
            block_table, numbers, joined, grad_heads, log_total, w_group
        )
        received = swap(grad_other)
        summed = (grad_own.astype(jnp.float32) + received.astype(jnp.float32)).astype(jnp.bfloat16)
        returned = exchange(summed.reshape(-1, local_rows, half), CTX)
        grad_in, norm_sums = norm_back(returned, entering, grad_middle, vector_rows)
        if not last:
            return grad_in, extra
        x_count = lax.axis_size("x")
        *pieces, joined_sums = qkv_grads(numbers, own, other, grad_joined, x_count, fsdp_count)
        joined_sums = joined_sums[0]
        qkv_share = sum_pieces(pieces, "x")
        share, qkv_share = lax.optimization_barrier((share, qkv_share))
        piece_rows = shard // x_count
        owner_pieces = [
            lax.dynamic_slice_in_dim(
                qkv_share, (fsdp_id + shift) % fsdp_count * piece_rows, piece_rows, 0
            )
            for shift in range(fsdp_count)
        ]
        qkv_piece = sum_pieces(owner_pieces, "fsdp")
        vectors = jnp.stack(
            [norm_sums[0], sums[0], norm_sums[1], sums[2], sums[1], sums[3]]
        )
        d_up_bias = up_sums.reshape(-1)
        return grad_in, share, qkv_piece, joined_sums, vectors, d_up_bias

    forward_pairs = [(i, i + 1) for i in range(sections - 1)]
    entering = fresh
    for _ in range(sections - 1):
        result, _ = forward(entering)
        received = lax.ppermute(result, "section", forward_pairs)
        entering = jnp.where(section_id == 0, fresh, received)
    layer_out, saved = forward(entering)

    back_pairs = [(i + 1, i) for i in range(sections - 1)]
    grad_low = top_grad
    for _ in range(sections - 1):
        result, kept = backward(grad_low, saved, None)
        received = lax.ppermute(result, "section", back_pairs)
        grad_low = jnp.where(section_id == sections - 1, top_grad, received)
        pairs = [(value, swap(value)) for value in kept[:3]]
        grad_low, pairs = lax.optimization_barrier((grad_low, pairs))
        kept = (pairs, kept[3:])
    input_grad, share, qkv_piece, joined_sums, vectors, d_up_bias = backward(grad_low, saved, kept)

    ours = jnp.arange(fsdp_count)[:, None] == group_id
    vector_parts = jnp.concatenate(
        [
            vectors.reshape(6, -1, shard).transpose(1, 0, 2).reshape(-1, 6 * shard),
            jnp.where(ours, joined_sums[None, :WIDTH], 0.0),
            jnp.where(ours, joined_sums[None, 2 * WIDTH :], 0.0),
            d_up_bias.reshape(fsdp_count, -1),
        ],
        1,
    )
    vector_parts = vector_parts.astype(jnp.bfloat16).reshape(fsdp_count, 4, 3 * WIDTH)
    vector_share = sum_low(exchange(vector_parts, "fsdp"))
    wide = ((0, 0), (0, model_width - 3 * WIDTH))
    qkv_piece, vector_share = jnp.pad(qkv_piece, wide), jnp.pad(vector_share, wide)
    joint_piece = sum_low(exchange(share.reshape(8, -1, model_width), ("x", "yh")))
    joint_piece, layer_out = lax.optimization_barrier((joint_piece, layer_out))
    both = spread(jnp.concatenate([qkv_piece, joint_piece, vector_share], 0), ("x", "yh"))
    g_qkv, g_out, g_up, g_down, vector_sum = unpack(
        core_number, both, swap(both), shard, mlp_in.shape[2], mlp_out.shape[1]
    )
    vector_sum = vector_sum[:, : 3 * WIDTH].reshape(-1)
    own_vectors = vector_sum[: 8 * shard].reshape(8, shard)
    own_up_bias = vector_sum[8 * shard :]
    order = (2, 6, 7, 3, 4, 5)
    g_biases = jnp.stack([own_vectors[place] for place in order])
    out_shape = (1, micro_count, 1, local_rows, model_width)
    return (
        layer_out.reshape(out_shape),
        input_grad.reshape(out_shape),
        g_qkv[None],
        g_out[None],
        g_up[None],
        g_down[None],
        own_vectors[None, :2],
        g_biases[None],
        own_up_bias[None],
    )


def solution(mesh):
    fine = Mesh(
        mesh.devices.reshape(2, 4, 2, 2, 4), ("section", "x", "yh", "core", "fsdp")
    )
    rows = P(None, "fsdp", CTX, None)
    weight = P("section", "fsdp", None)
    vector = P("section", None, "fsdp")
    row = P("section", "fsdp")
    out_rows = P("section", None, "fsdp", CTX, None)
    return jax.shard_map(
        shards,
        mesh=fine,
        in_specs=(rows, rows, P(), P(), weight, weight, weight, weight, vector, vector, row),
        out_specs=(out_rows, out_rows, weight, weight, weight, weight, vector, vector, row),
        check_vma=False,
    )
```

```python
import functools

import jax
import jax.numpy as jnp
from jax import lax
from jax.experimental import pallas as pl
from jax.experimental.pallas import tpu as pltpu
from jax.sharding import Mesh
from jax.sharding import PartitionSpec as P

HEADS = 12
HDIM = 64
GROUPS = 4
GROUP_HEADS = HEADS // GROUPS
WIDTH = GROUP_HEADS * HDIM
QUERY_BLOCK = 256
VECTOR_ROWS = 4
CTX = ("x", "yh", "core")

epsilon = 1e-05
neg_fill = -1e30
GELU_SCALE = (2.0 / 3.141592653589793) ** 0.5
GELU_CUBE = 0.044715


def dot(left_side, right_side, left_dim, right_dim):
    return lax.dot_general(
        left_side,
        right_side,
        (((left_dim,), (right_dim,)), ((), ())),
        preferred_element_type=jnp.float32,
    )


def head_columns(part, head):
    start = part * WIDTH + head * HDIM
    return slice(start, start + HDIM)


def whole(*shape):
    return pl.BlockSpec(shape, lambda i, *unused: (0,) * len(shape))


def sort_rows(target, source, table, back):
    blocks = table.shape[0]
    size = source.shape[0] // blocks
    for block in range(blocks):
        fixed = slice(block * size, (block + 1) * size)
        moved = pl.ds(pl.multiple_of(table[block] * size, size), size)
        if back:
            target[fixed, :] = source[moved, :]
        else:
            target[moved, :] = source[fixed, :]


def place_weight(target, members, ids):
    count, rows = len(members), members[0].shape[0]
    for shift, member in enumerate(members):
        place = lax.rem(ids[1] + shift - 2 * ids[0] + count, count)
        target[pl.ds(pl.multiple_of(place * rows, rows), rows), :] = member[...]


def mask_scores(scores):
    count = scores.shape[0] - QUERY_BLOCK
    tile = (QUERY_BLOCK, QUERY_BLOCK)
    visible = lax.broadcasted_iota(jnp.int32, tile, 0) <= lax.broadcasted_iota(jnp.int32, tile, 1)
    masked = jnp.where(visible, scores[count:], neg_fill)
    return jnp.concatenate([scores[:count], masked], 0) if count else masked


def attend_body(
    table, ids, own, other, w0, w1, w2, w3, bias, joined, mixed, log_total, weight, scratch, sorted_out
):
    step = pl.program_id(0)
    half = own.shape[1]

    @pl.when(step == 0)
    def _():
        place_weight(weight, (w0, w1, w2, w3), ids)
        product = dot(own[...], weight[:half, :], 1, 0) + dot(other[...], weight[half:, :], 1, 0)
        scratch[...] = (product + bias[...]).astype(jnp.bfloat16)
        sort_rows(joined, scratch, table, False)

    def block(index):
        rows = slice(index * QUERY_BLOCK, (index + 1) * QUERY_BLOCK)
        seen = slice(0, (index + 1) * QUERY_BLOCK)
        parts = []
        for head in range(GROUP_HEADS):
            queries = joined[rows, head_columns(0, head)] * jnp.bfloat16(HDIM ** (-0.5))
            keys = joined[seen, head_columns(1, head)]
            values = joined[seen, head_columns(2, head)]
            scores = mask_scores(dot(keys, queries, 1, 1))
            top = jnp.max(scores, 0, keepdims=True)
            powers = jnp.exp(scores - top)
            total = jnp.sum(powers, 0, keepdims=True)
            parts.append(dot(values, powers.astype(jnp.bfloat16), 0, 0) / total)
            log_total[head : head + 1, rows] = top + jnp.log(total)
        sorted_out[rows, :] = jnp.concatenate(parts, 0).T.astype(jnp.bfloat16)

    for index in range(own.shape[0] // QUERY_BLOCK):
        pl.when(step == index)(lambda index=index: block(index))

    @pl.when(step == pl.num_programs(0) - 1)
    def _():
        sort_rows(mixed, sorted_out, table, True)


def attend(table, ids, own, other, weights, bias):
    count, half = own.shape
    return pl.pallas_call(
        attend_body,
        grid_spec=pltpu.PrefetchScalarGridSpec(
            num_scalar_prefetch=2,
            grid=(count // QUERY_BLOCK,),
            in_specs=[whole(count, half)] * 2
            + [whole(*weight.shape) for weight in weights]
            + [whole(1, 3 * WIDTH)],
            out_specs=[whole(count, 3 * WIDTH), whole(count, WIDTH), whole(8, count)],
            scratch_shapes=[
                pltpu.VMEM((2 * half, 3 * WIDTH), jnp.bfloat16),
                pltpu.VMEM((count, 3 * WIDTH), jnp.bfloat16),
                pltpu.VMEM((count, WIDTH), jnp.bfloat16),
            ],
        ),
        out_shape=[
            jax.ShapeDtypeStruct((count, 3 * WIDTH), jnp.bfloat16),
            jax.ShapeDtypeStruct((count, WIDTH), jnp.bfloat16),
            jax.ShapeDtypeStruct((8, count), jnp.float32),
        ],
        compiler_params=pltpu.CompilerParams(vmem_limit_bytes=48 << 20),
        cost_estimate=pl.CostEstimate(
            flops=4 * count * count * WIDTH,
            bytes_accessed=8 * count * WIDTH,
            transcendentals=count * count * GROUP_HEADS,
        ),
    )(table, ids, own, other, *weights, bias)


def attend_back_body(
    table,
    ids,
    joined,
    grad_mixed,
    log_total,
    w0,
    w1,
    w2,
    w3,
    grad_joined,
    grad_own,
    grad_other,
    weight,
    sorted_grads,
    sorted_out,
    key_sums,
    value_sums,
):
    step = pl.program_id(0)
    half = grad_own.shape[1]

    @pl.when(step == 0)
    def _():
        place_weight(weight, (w0, w1, w2, w3), ids)
        sort_rows(sorted_grads, grad_mixed, table, False)
        key_sums[...] = jnp.zeros_like(key_sums)
        value_sums[...] = jnp.zeros_like(value_sums)

    def block(index):
        rows = slice(index * QUERY_BLOCK, (index + 1) * QUERY_BLOCK)
        seen = slice(0, (index + 1) * QUERY_BLOCK)
        parts = []
        for head in range(GROUP_HEADS):
            queries = joined[rows, head_columns(0, head)] * jnp.bfloat16(HDIM ** (-0.5))
            keys = joined[seen, head_columns(1, head)]
            values = joined[seen, head_columns(2, head)]
            grads = sorted_grads[rows, head_columns(0, head)]
            scores = mask_scores(dot(keys, queries, 1, 1))
            weights = jnp.exp(scores - log_total[head : head + 1, rows])
            grad_weights = dot(values, grads, 1, 1)
            inner_sum = jnp.sum(weights * grad_weights, 0, keepdims=True)
            grad_scores = (weights * (grad_weights - inner_sum)).astype(jnp.bfloat16)
            value_sums[head, seen, :] += dot(weights.astype(jnp.bfloat16), grads, 1, 0)
            key_sums[head, seen, :] += dot(grad_scores, queries, 1, 0)
            parts.append(dot(keys, grad_scores, 0, 0) * (HDIM ** (-0.5)))
        sorted_out[rows, :WIDTH] = jnp.concatenate(parts, 0).T.astype(jnp.bfloat16)

    for index in range(joined.shape[0] // QUERY_BLOCK):
        pl.when(step == index)(lambda index=index: block(index))

    @pl.when(step == pl.num_programs(0) - 1)
    def _():
        for head in range(GROUP_HEADS):
            sorted_out[:, head_columns(1, head)] = key_sums[head].astype(jnp.bfloat16)
            sorted_out[:, head_columns(2, head)] = value_sums[head].astype(jnp.bfloat16)
        sort_rows(grad_joined, sorted_out, table, True)
        grad_own[...] = dot(grad_joined[...], weight[:half, :], 1, 1).astype(jnp.bfloat16)
        grad_other[...] = dot(grad_joined[...], weight[half:, :], 1, 1).astype(jnp.bfloat16)


def attend_back(table, ids, joined, grad_mixed, log_total, weights):
    count = joined.shape[0]
    half = len(weights) * weights[0].shape[0] // 2
    return pl.pallas_call(
        attend_back_body,
        grid_spec=pltpu.PrefetchScalarGridSpec(
            num_scalar_prefetch=2,
            grid=(count // QUERY_BLOCK,),
            in_specs=[whole(count, 3 * WIDTH), whole(count, WIDTH), whole(8, count)]
            + [whole(*weight.shape) for weight in weights],
            out_specs=[whole(count, 3 * WIDTH), whole(count, half), whole(count, half)],
            scratch_shapes=[
                pltpu.VMEM((2 * half, 3 * WIDTH), jnp.bfloat16),
                pltpu.VMEM((count, WIDTH), jnp.bfloat16),
                pltpu.VMEM((count, 3 * WIDTH), jnp.bfloat16),
                pltpu.VMEM((GROUP_HEADS, count, HDIM), jnp.float32),
                pltpu.VMEM((GROUP_HEADS, count, HDIM), jnp.float32),
            ],
        ),
        out_shape=[
            jax.ShapeDtypeStruct((count, 3 * WIDTH), jnp.bfloat16),
            jax.ShapeDtypeStruct((count, half), jnp.bfloat16),
            jax.ShapeDtypeStruct((count, half), jnp.bfloat16),
        ],
        compiler_params=pltpu.CompilerParams(vmem_limit_bytes=48 << 20),
        cost_estimate=pl.CostEstimate(
            flops=10 * count * count * WIDTH,
            bytes_accessed=16 * count * WIDTH,
            transcendentals=count * count * GROUP_HEADS,
        ),
    )(table, ids, joined, grad_mixed, log_total, *weights)


def weight_grads_body(
    core_id,
    active,
    active_other,
    grad_low,
    grad_low_other,
    normed_two,
    normed_two_other,
    grad_hidden,
    grad_hidden_other,
    mixed,
    mixed_other,
    grad_attn,
    grad_attn_other,
    joint,
):
    down_rows, up_rows = active.shape[1], normed_two.shape[0]
    width = grad_low.shape[1]
    product = dot(active[...], grad_low[...], 0, 0)
    product += dot(active_other[...], grad_low_other[...], 0, 0)
    joint[0, :down_rows, :] = product.astype(jnp.bfloat16)
    place = down_rows
    for panel in range(grad_hidden.shape[1] // width):
        columns = slice(panel * width, (panel + 1) * width)
        product = dot(normed_two[...], grad_hidden[:, columns], 1, 0)
        product += dot(normed_two_other[...], grad_hidden_other[:, columns], 1, 0)
        joint[0, place : place + up_rows, :] = product.astype(jnp.bfloat16)
        place += up_rows
    product = dot(mixed[...], grad_attn[...], 1, 0)
    product += dot(mixed_other[...], grad_attn_other[...], 1, 0)
    joint[0, place : place + up_rows, :] = product.astype(jnp.bfloat16)


def weight_grads(core_id, pairs, members):
    rows, hidden_width = pairs[0][0].shape
    width = pairs[1][0].shape[1]
    down_rows, up_rows = hidden_width // members // 2, width // members // 2
    out_rows = 2 * down_rows + up_rows
    flat = pl.BlockSpec((rows, width), lambda i, core: (0, 0))
    tall = pl.BlockSpec((up_rows, rows), lambda i, core: (2 * i + core[0], 0))
    specs = [
        pl.BlockSpec((rows, down_rows), lambda i, core: (0, 2 * i + core[0])),
        flat,
        tall,
        pl.BlockSpec((rows, hidden_width), lambda i, core: (0, 0)),
        tall,
        flat,
    ]
    return pl.pallas_call(
        weight_grads_body,
        grid_spec=pltpu.PrefetchScalarGridSpec(
            num_scalar_prefetch=1,
            grid=(members,),
            in_specs=[spec for spec in specs for _ in range(2)],
            out_specs=pl.BlockSpec((1, out_rows, width), lambda i, core: (i, 0, 0)),
        ),
        out_shape=jax.ShapeDtypeStruct((members, out_rows, width), jnp.bfloat16),
        compiler_params=pltpu.CompilerParams(vmem_limit_bytes=48 << 20),
        cost_estimate=pl.CostEstimate(
            flops=2 * rows * width * (2 * hidden_width + width),
            bytes_accessed=2 * members * out_rows * width,
            transcendentals=0,
        ),
    )(core_id, *[value for pair in pairs for value in pair])


def weight_panel(packed, start):
    members, width = packed.shape[0], packed.shape[2]
    rows = width // members
    return jnp.concatenate([packed[i, start : start + rows, :] for i in range(members)], 0)


def join_groups(mixed, group):
    micro_count = mixed.shape[0] // GROUPS
    return jnp.concatenate([mixed[m * GROUPS + group] for m in range(micro_count)], 0)


def attend_out(mixed, entering, packed, vectors, w_out):
    middle = entering[...].astype(jnp.float32) + vectors[5:6, :]
    for group in range(GROUPS):
        rows = slice(group * WIDTH, (group + 1) * WIDTH)
        middle += dot(join_groups(mixed, group), w_out[rows, :], 1, 0)
    return middle


def start_copies(stored, packed, landed, panels):
    members, width = packed.shape[0], packed.shape[2]
    up_rows = width // members
    down_rows = panels * up_rows
    per_panel = members // panels

    def copy(index, rows, sources):
        here = (slice(None) if sources is None else sources, rows)
        return pltpu.make_async_copy(stored.at[here], packed.at[here], landed.at[index])

    out = copy(0, pl.ds(2 * down_rows, up_rows), None)
    ups, downs = [], []
    for panel in range(panels):
        ups.append(copy(1 + panel, pl.ds(down_rows + panel * up_rows, up_rows), None))
        downs.append(
            copy(1 + panels + panel, pl.ds(0, down_rows), pl.ds(panel * per_panel, per_panel))
        )
    return out, ups, downs


def feed_forward_body(mixed, entering, stored, vectors, up_bias, result, packed, landed):
    members, width = packed.shape[0], packed.shape[2]
    panels = up_bias.shape[0]
    up_rows = width // members
    down_rows = panels * up_rows
    out, ups, downs = start_copies(stored, packed, landed, panels)
    for copy in [out] + ups + downs:
        copy.start()
    out.wait()
    middle = attend_out(mixed, entering, packed, vectors, weight_panel(packed, 2 * down_rows))
    normed, _, _ = normalize(middle, vectors[1:2, :], vectors[6:7, :])
    normed = normed.astype(jnp.bfloat16)
    parts = []
    for panel in range(panels):
        ups[panel].wait()
        hidden = dot(normed, weight_panel(packed, down_rows + panel * up_rows), 1, 0)
        hidden = hidden + up_bias[panel : panel + 1, :]
        parts.append(jax.nn.gelu(hidden).astype(jnp.bfloat16))
    active = jnp.concatenate(parts, 1)
    total = middle + vectors[7:8, :]
    for member in range(members):
        if member % (members // panels) == 0:
            downs[member // (members // panels)].wait()
        columns = slice(member * down_rows, (member + 1) * down_rows)
        total += dot(active[:, columns], packed[member, :down_rows, :], 1, 0)
    result[...] = total.astype(jnp.bfloat16)


def feed_specs(count):
    specs = [pl.BlockSpec(memory_space=pltpu.VMEM) for _ in range(count)]
    specs[2] = pl.BlockSpec(memory_space=pl.ANY)
    return specs


def feed_scratch(packed, up_bias):
    return [
        pltpu.VMEM(packed.shape, packed.dtype),
        pltpu.SemaphoreType.DMA((1 + 2 * up_bias.shape[0],)),
    ]


def feed_forward(mixed, entering, packed, vectors, up_bias):
    rows, width = entering.shape
    return pl.pallas_call(
        feed_forward_body,
        in_specs=feed_specs(5),
        out_specs=pl.BlockSpec(memory_space=pltpu.VMEM),
        scratch_shapes=feed_scratch(packed, up_bias),
        out_shape=jax.ShapeDtypeStruct((rows, width), jnp.bfloat16),
        compiler_params=pltpu.CompilerParams(vmem_limit_bytes=48 << 20),
        cost_estimate=pl.CostEstimate(
            flops=18 * rows * width * width,
            bytes_accessed=18 * width * width,
            transcendentals=4 * rows * width,
        ),
    )(mixed, entering, packed, vectors, up_bias)


def feed_back_end(grads, grad_normed, unit, spread_two, vectors, w_out, grad_mixed, grad_middle):
    local_rows = grad_mixed.shape[1]
    grad_top = grads.astype(jnp.float32)
    grad_norm, d_gain, d_shift = normalize_back(grad_normed, unit, spread_two, vectors[1:2, :])
    grad_sum = grad_top + grad_norm
    grad_middle[...] = grad_sum
    grad_attn = grad_sum.astype(jnp.bfloat16)
    for group in range(GROUPS):
        part = dot(grad_attn, w_out[group * WIDTH : (group + 1) * WIDTH, :], 1, 1)
        part = part.astype(jnp.bfloat16)
        for m in range(grad_mixed.shape[0] // GROUPS):
            grad_mixed[m * GROUPS + group] = part[m * local_rows : (m + 1) * local_rows]
    return grad_attn, d_gain, d_shift


def down_panel(packed, panel, panels):
    members, width = packed.shape[0], packed.shape[2]
    each = members // panels
    rows = panels * width // members
    return jnp.concatenate(
        [packed[i, :rows, :] for i in range(panel * each, (panel + 1) * each)], 0
    )


def feed_back_first_body(
    mixed,
    entering,
    packed,
    vectors,
    up_bias,
    grad_low,
    grad_mixed,
    grad_middle,
    active,
    normed_tall,
    mixed_tall,
    slopes,
    units,
    spreads,
):
    members, width = packed.shape[0], packed.shape[2]
    panels = up_bias.shape[0]
    up_rows = width // members
    down_rows = panels * up_rows
    w_out = weight_panel(packed, 2 * down_rows)
    middle = attend_out(mixed, entering, packed, vectors, w_out)
    normed, unit, spread_two = normalize(middle, vectors[1:2, :], vectors[6:7, :])
    normed = normed.astype(jnp.bfloat16)
    grads = grad_low[...]
    grad_normed = jnp.zeros(middle.shape, jnp.float32)
    for panel in range(panels):
        columns = slice(panel * width, (panel + 1) * width)
        w_up = weight_panel(packed, down_rows + panel * up_rows)
        hidden = dot(normed, w_up, 1, 0) + up_bias[panel : panel + 1, :]
        square = hidden * hidden
        bend = jnp.tanh(GELU_SCALE * (hidden + GELU_CUBE * (square * hidden)))
        slope = 0.5 * (1.0 + bend) + 0.5 * hidden * (1.0 - bend * bend) * (
            GELU_SCALE * (1.0 + 3.0 * GELU_CUBE * square)
        )
        slopes[:, columns] = slope
        active[:, columns] = (0.5 * hidden * (1.0 + bend)).astype(jnp.bfloat16)
        w_down = down_panel(packed, panel, panels)
        grad_hidden = (dot(grads, w_down, 1, 1) * slope).astype(jnp.bfloat16)
        grad_normed += dot(grad_hidden, w_up, 1, 1)
    feed_back_end(grads, grad_normed, unit, spread_two, vectors, w_out, grad_mixed, grad_middle)
    units[...] = unit
    spreads[...] = jnp.broadcast_to(spread_two, spreads.shape)
    normed_tall[...] = normed.astype(jnp.float32).T.astype(jnp.bfloat16)
    for group in range(GROUPS):
        part = join_groups(mixed, group).astype(jnp.float32).T.astype(jnp.bfloat16)
        mixed_tall[group * WIDTH : (group + 1) * WIDTH, :] = part


def feed_back_last_body(
    packed,
    vectors,
    grad_low,
    slopes,
    units,
    spreads,
    grad_mixed,
    grad_middle,
    grad_hidden,
    grad_attn,
    sums,
    up_sums,
):
    members, width = packed.shape[0], packed.shape[2]
    panels = up_sums.shape[0]
    up_rows = width // members
    down_rows = panels * up_rows
    w_out = weight_panel(packed, 2 * down_rows)
    grads = grad_low[...]
    grad_normed = jnp.zeros(units.shape, jnp.float32)
    for panel in range(panels):
        columns = slice(panel * width, (panel + 1) * width)
        w_up = weight_panel(packed, down_rows + panel * up_rows)
        w_down = down_panel(packed, panel, panels)
        part = (dot(grads, w_down, 1, 1) * slopes[:, columns]).astype(jnp.bfloat16)
        grad_normed += dot(part, w_up, 1, 1)
        grad_hidden[:, columns] = part
        up_sums[panel : panel + 1, :] = jnp.sum(part.astype(jnp.float32), 0, keepdims=True)
    attn, d_gain, d_shift = feed_back_end(
        grads, grad_normed, units[...], spreads[:, :1], vectors, w_out, grad_mixed, grad_middle
    )
    grad_attn[...] = attn
    sums[0:1, :] = d_gain[None]
    sums[1:2, :] = d_shift[None]
    sums[2:3, :] = jnp.sum(attn.astype(jnp.float32), 0, keepdims=True)
    sums[3:4, :] = jnp.sum(grads.astype(jnp.float32), 0, keepdims=True)


def feed_back(body, args, shapes):
    rows, width = shapes[1][0]
    return pl.pallas_call(
        body,
        in_specs=[pl.BlockSpec(memory_space=pltpu.VMEM)] * len(args),
        out_specs=[pl.BlockSpec(memory_space=pltpu.VMEM)] * len(shapes),
        out_shape=[jax.ShapeDtypeStruct(*shape) for shape in shapes],
        compiler_params=pltpu.CompilerParams(vmem_limit_bytes=56 << 20),
        cost_estimate=pl.CostEstimate(
            flops=28 * rows * width * width,
            bytes_accessed=24 * width * width,
            transcendentals=4 * rows * width,
        ),
    )(*args)


def norm_back_body(returned, entering, grad_middle, vectors, grad_in, sums):
    parts = []
    for m in range(returned.shape[0] // GROUPS):
        halves = [
            returned[m * GROUPS + core].astype(jnp.float32)
            + returned[m * GROUPS + 2 + core].astype(jnp.float32)
            for core in range(2)
        ]
        parts.append(jnp.concatenate(halves, 1))
    grad_normed = jnp.concatenate(parts, 0)
    gain = vectors[0:1, :]
    _, unit, spread_one = normalize(entering[...].astype(jnp.float32), gain, vectors[2:3, :])
    grad_norm, d_gain, d_shift = normalize_back(grad_normed, unit, spread_one, gain)
    grad_in[...] = (grad_middle[...] + grad_norm).astype(jnp.bfloat16)
    sums[0:1, :] = d_gain[None]
    sums[1:2, :] = d_shift[None]


def norm_back(returned, entering, grad_middle, vectors):
    rows, width = entering.shape
    return pl.pallas_call(
        norm_back_body,
        in_specs=[pl.BlockSpec(memory_space=pltpu.VMEM)] * 4,
        out_specs=[pl.BlockSpec(memory_space=pltpu.VMEM)] * 2,
        out_shape=[
            jax.ShapeDtypeStruct((rows, width), jnp.bfloat16),
            jax.ShapeDtypeStruct((2, width), jnp.float32),
        ],
        compiler_params=pltpu.CompilerParams(vmem_limit_bytes=32 << 20),
        cost_estimate=pl.CostEstimate(
            flops=20 * rows * width, bytes_accessed=10 * rows * width, transcendentals=rows
        ),
    )(returned, entering, grad_middle, vectors)


def qkv_grads_body(owners, ids, own, other, grad_joined, *outs):
    pieces, sums, both = outs[:-2], outs[-2], outs[-1]
    first_core = ids[0] == 0
    grads = grad_joined[...]
    half = own.shape[1]
    own_grads = dot(own[...], grads, 0, 0).astype(jnp.bfloat16)
    other_grads = dot(other[...], grads, 0, 0).astype(jnp.bfloat16)
    both[:half, :] = jnp.where(first_core, own_grads, other_grads)
    both[half:, :] = jnp.where(first_core, other_grads, own_grads)
    count = len(pieces)
    rows = pieces[0].shape[0] // owners
    for shift in range(count):
        place = lax.rem(ids[2] + shift, count) * rows
        for owner in range(owners):
            start = pl.multiple_of(owner * rows * count + place, rows)
            pieces[shift][owner * rows : (owner + 1) * rows, :] = both[pl.ds(start, rows), :]
    sums[...] = jnp.sum(grads.astype(jnp.float32), 0, keepdims=True)


def qkv_grads(ids, own, other, grad_joined, count, owners):
    rows, half = own.shape
    width = grad_joined.shape[1]
    piece = jax.ShapeDtypeStruct((2 * half // count, width), jnp.bfloat16)
    return pl.pallas_call(
        functools.partial(qkv_grads_body, owners),
        in_specs=[pl.BlockSpec(memory_space=pltpu.SMEM)]
        + [pl.BlockSpec(memory_space=pltpu.VMEM)] * 3,
        out_specs=[pl.BlockSpec(memory_space=pltpu.VMEM)] * (count + 1),
        out_shape=[piece] * count + [jax.ShapeDtypeStruct((1, width), jnp.float32)],
        scratch_shapes=[pltpu.VMEM((2 * half, width), jnp.bfloat16)],
        compiler_params=pltpu.CompilerParams(vmem_limit_bytes=48 << 20),
        cost_estimate=pl.CostEstimate(
            flops=4 * rows * half * width, bytes_accessed=6 * rows * half, transcendentals=0
        ),
    )(ids, own, other, grad_joined)


def unpack_body(core_id, own, other, g_qkv, g_out, g_up, g_down, vectors):
    first_core = core_id[0] == 0
    count = own.shape[0]
    width = own.shape[2]
    piece_rows = g_qkv.shape[0] // (count // 2)
    joint_end = own.shape[1] - VECTOR_ROWS
    up_rows = g_up.shape[0] // 2
    down_rows = g_down.shape[0] // 2
    sums = jnp.zeros(vectors.shape, jnp.float32)
    for core in range(2):
        pick = first_core if core == 0 else jnp.logical_not(first_core)
        blocks = [jnp.where(pick, own[i], other[i]).astype(jnp.float32) for i in range(count)]
        joint = jnp.concatenate([block[piece_rows:joint_end] for block in blocks], 0)
        g_down[core * down_rows : (core + 1) * down_rows, :] = joint[:down_rows]
        place = down_rows
        for panel in range(g_up.shape[1] // width):
            g_up[core * up_rows : (core + 1) * up_rows, panel * width : (panel + 1) * width] = (
                joint[place : place + up_rows]
            )
            place += up_rows
        g_out[core * up_rows : (core + 1) * up_rows, :] = joint[place : place + up_rows]
        for i, block in enumerate(blocks):
            x_id, group = i // 2, (i % 2) * 2 + core
            for part in range(3):
                start = part * width + group * WIDTH
                g_qkv[x_id * piece_rows : (x_id + 1) * piece_rows, start : start + WIDTH] = block[
                    :piece_rows, part * WIDTH : (part + 1) * WIDTH
                ]
            sums += block[joint_end:]
    vectors[...] = sums


def unpack(core_id, own, other, shard, hidden_width, hidden_shard):
    width = own.shape[2]
    return pl.pallas_call(
        unpack_body,
        in_specs=[pl.BlockSpec(memory_space=pltpu.SMEM)]
        + [pl.BlockSpec(memory_space=pltpu.VMEM)] * 2,
        out_specs=[pl.BlockSpec(memory_space=pltpu.VMEM)] * 5,
        out_shape=[
            jax.ShapeDtypeStruct((shard, 3 * width), jnp.float32),
            jax.ShapeDtypeStruct((shard, width), jnp.float32),
            jax.ShapeDtypeStruct((shard, hidden_width), jnp.float32),
            jax.ShapeDtypeStruct((hidden_shard, width), jnp.float32),
            jax.ShapeDtypeStruct((4, width), jnp.float32),
        ],
        compiler_params=pltpu.CompilerParams(vmem_limit_bytes=48 << 20),
        cost_estimate=pl.CostEstimate(flops=0, bytes_accessed=12 << 20, transcendentals=0),
    )(core_id, own, other)


def normalize(values, gain_row, shift_row):
    center = values - jnp.mean(values, -1, keepdims=True)
    spread = lax.rsqrt(jnp.mean(center * center, -1, keepdims=True) + epsilon)
    unit_rows = center * spread
    return (unit_rows * gain_row + shift_row, unit_rows, spread)


def normalize_back(grad_out, unit_rows, spread, gain_row):
    grad_unit = grad_out * gain_row
    grad_in = spread * (
        grad_unit
        - jnp.mean(grad_unit, -1, keepdims=True)
        - unit_rows * jnp.mean(grad_unit * unit_rows, -1, keepdims=True)
    )
    return (grad_in, jnp.sum(grad_out * unit_rows, 0), jnp.sum(grad_out, 0))


def exchange(value, axes):
    return lax.all_to_all(value, axes, 0, 0, tiled=True)


def swap(value):
    return lax.ppermute(value, "core", [(0, 1), (1, 0)])


def in_order(own, other):
    first = lax.axis_index("core") == 0
    return jnp.where(first, own, other), jnp.where(first, other, own)


def pack_weights(attn_out, mlp_in, mlp_out):
    core_id = lax.axis_index("core")
    width = attn_out.shape[2]
    out_half, up_half, down_half = (
        lax.dynamic_slice_in_dim(
            weight[0], core_id * (weight.shape[1] // 2), weight.shape[1] // 2, 0
        )
        for weight in (attn_out, mlp_in, mlp_out)
    )
    panels = [up_half[:, start : start + width] for start in range(0, mlp_in.shape[2], width)]
    return jnp.concatenate([down_half] + panels + [out_half], 0)


def ring_pairs(axis, shift):
    count = lax.axis_size(axis)
    return [(source, (source + shift) % count) for source in range(count)]


def gather_ring(value, axis):
    return [value] + [
        lax.ppermute(value, axis, ring_pairs(axis, -shift))
        for shift in range(1, lax.axis_size(axis))
    ]


def sum_pieces(pieces, axis):
    total = pieces[0].astype(jnp.float32)
    for shift in range(1, len(pieces)):
        received = lax.ppermute(pieces[shift], axis, ring_pairs(axis, shift))
        total = total + received.astype(jnp.float32)
    return total.astype(jnp.bfloat16)


def sum_low(value):
    return jnp.sum(value.astype(jnp.float32), 0).astype(jnp.bfloat16)


def spread(value, axes):
    count = lax.axis_size(axes)
    return exchange(jnp.broadcast_to(value[None], (count,) + value.shape), axes)


def shards(
    inputs,
    cotangent,
    plan,
    block_table,
    attn_in,
    attn_out,
    mlp_in,
    mlp_out,
    norm_gains,
    biases,
    mlp_bias,
):
    shard = norm_gains.shape[2]
    core_id = lax.axis_index("core")
    group_id = lax.axis_index("yh") * 2 + core_id
    fsdp_id = lax.axis_index("fsdp")
    section_id = lax.axis_index("section")
    sections = lax.axis_size("section")
    fsdp_count = lax.axis_size("fsdp")

    small = jnp.concatenate([norm_gains[0], biases[0], mlp_bias.reshape(-1, shard)], 0)
    small = small.reshape(-1, 3 * WIDTH)
    own_columns = lax.dynamic_index_in_dim(
        attn_in[0].reshape(shard, 3, GROUPS, WIDTH), group_id, 2, keepdims=False
    ).reshape(shard, 3 * WIDTH)
    small_all = spread(small, "fsdp").reshape(fsdp_count, -1, shard).astype(jnp.float32)
    w_group = gather_ring(own_columns, "fsdp")
    small_all, w_group[2] = lax.optimization_barrier((small_all, w_group[2]))
    packed = pack_weights(attn_out, mlp_in, mlp_out)
    packed = lax.all_gather(packed, ("fsdp", "core"), axis=0)
    model_width = attn_out.shape[2]
    hidden_width = mlp_in.shape[2]
    half = model_width // 2
    vector_rows = small_all[:, :8].transpose(1, 0, 2).reshape(8, model_width)
    gain_rows, bias_rows = vector_rows[:2], vector_rows[2:]
    up_rows = small_all[:, 8:].reshape(-1, model_width)
    own_bias = lax.dynamic_index_in_dim(small_all, group_id, 0, keepdims=False)
    group_bias = jnp.concatenate([own_bias[3], jnp.zeros_like(own_bias[3]), own_bias[4]])[None]

    micro_count, _, local_rows, _ = inputs.shape
    rows = micro_count * local_rows
    fresh = jnp.stack(
        [lax.dynamic_index_in_dim(inputs, plan[step], 0, keepdims=False) for step in range(micro_count)]
    ).reshape(rows, model_width)
    top_grad = cotangent.reshape(rows, model_width)
    core_number = core_id.astype(jnp.int32)[None]
    numbers = jnp.stack([core_id, fsdp_id, lax.axis_index("x")]).astype(jnp.int32)

    def forward(entering):
        stream = entering.astype(jnp.float32)
        normed, _, _ = normalize(stream, gain_rows[0], bias_rows[0])
        halves = normed.astype(jnp.bfloat16).reshape(micro_count, 1, local_rows, 2, half)
        halves = jnp.broadcast_to(
            halves.transpose(0, 1, 3, 2, 4), (micro_count, 2, 2, local_rows, half)
        )
        own = exchange(halves.reshape(-1, local_rows, half), CTX).reshape(-1, half)
        own, weights = lax.optimization_barrier((own, w_group))
        other = swap(own)
        joined, mixed_heads, log_total = attend(
            block_table, numbers, own, other, weights, group_bias
        )
        mixed = exchange(mixed_heads.reshape(-1, local_rows, WIDTH), CTX)
        result = feed_forward(mixed, entering, packed, vector_rows, up_rows)
        return result, (entering, own, other, joined, log_total, mixed)

    def backward(grad_low, saved, kept):
        entering, own, other, joined, log_total, mixed = saved
        last = kept is not None
        low, full = jnp.bfloat16, jnp.float32
        shapes = [(mixed.shape, low), ((rows, model_width), full), ((rows, hidden_width), low)]
        if last:
            pairs, plain = kept
            shapes += [((rows, model_width), low), ((4, model_width), full), (up_rows.shape, full)]
            grad_mixed, grad_middle, *extra = feed_back(
                feed_back_last_body, (packed, vector_rows, grad_low, *plain), shapes
            )
        else:
            shapes += [((model_width, rows), low)] * 2
            shapes += [((rows, hidden_width), full), ((rows, model_width), full), ((rows, 128), full)]
            grad_mixed, grad_middle, *extra = feed_back(
                feed_back_first_body,
                (mixed, entering, packed, vector_rows, up_rows, grad_low),
                shapes,
            )
        grad_heads = exchange(grad_mixed.reshape(-1, local_rows, WIDTH), CTX).reshape(-1, WIDTH)
        if last:
            grad_hidden, grad_attn, sums, up_sums = extra
            active_pair, normed_pair, mixed_pair = pairs
            low_pair, hidden_pair, attn_pair = (
                (value, swap(value)) for value in (grad_low, grad_hidden, grad_attn)
            )
            joint = weight_grads(
                core_number,
                [active_pair, low_pair, normed_pair, hidden_pair, mixed_pair, attn_pair],
                fsdp_count,
            )
            grad_heads, joint = lax.optimization_barrier((grad_heads, joint))
            share = lax.psum_scatter(
                joint.reshape(-1, model_width),
                "fsdp",
                scatter_dimension=0,
                tiled=True,
            )
        grad_joined, grad_own, grad_other = attend_back(
            block_table, numbers, joined, grad_heads, log_total, w_group
        )
        received = swap(grad_other)
        summed = (grad_own.astype(jnp.float32) + received.astype(jnp.float32)).astype(jnp.bfloat16)
        returned = exchange(summed.reshape(-1, local_rows, half), CTX)
        grad_in, norm_sums = norm_back(returned, entering, grad_middle, vector_rows)
        if not last:
            return grad_in, extra
        x_count = lax.axis_size("x")
        *pieces, joined_sums = qkv_grads(numbers, own, other, grad_joined, x_count, fsdp_count)
        joined_sums = joined_sums[0]
        qkv_share = sum_pieces(pieces, "x")
        share, qkv_share = lax.optimization_barrier((share, qkv_share))
        piece_rows = shard // x_count
        owner_pieces = [
            lax.dynamic_slice_in_dim(
                qkv_share, (fsdp_id + shift) % fsdp_count * piece_rows, piece_rows, 0
            )
            for shift in range(fsdp_count)
        ]
        qkv_piece = sum_pieces(owner_pieces, "fsdp")
        vectors = jnp.stack(
            [norm_sums[0], sums[0], norm_sums[1], sums[2], sums[1], sums[3]]
        )
        d_up_bias = up_sums.reshape(-1)
        return grad_in, share, qkv_piece, joined_sums, vectors, d_up_bias

    forward_pairs = [(i, i + 1) for i in range(sections - 1)]
    entering = fresh
    for _ in range(sections - 1):
        result, _ = forward(entering)
        received = lax.ppermute(result, "section", forward_pairs)
        entering = jnp.where(section_id == 0, fresh, received)
    layer_out, saved = forward(entering)

    back_pairs = [(i + 1, i) for i in range(sections - 1)]
    grad_low = top_grad
    for _ in range(sections - 1):
        result, kept = backward(grad_low, saved, None)
        received = lax.ppermute(result, "section", back_pairs)
        grad_low = jnp.where(section_id == sections - 1, top_grad, received)
        pairs = [(value, swap(value)) for value in kept[:3]]
        grad_low, pairs = lax.optimization_barrier((grad_low, pairs))
        kept = (pairs, kept[3:])
    input_grad, share, qkv_piece, joined_sums, vectors, d_up_bias = backward(grad_low, saved, kept)

    ours = jnp.arange(fsdp_count)[:, None] == group_id
    vector_parts = jnp.concatenate(
        [
            vectors.reshape(6, -1, shard).transpose(1, 0, 2).reshape(-1, 6 * shard),
            jnp.where(ours, joined_sums[None, :WIDTH], 0.0),
            jnp.where(ours, joined_sums[None, 2 * WIDTH :], 0.0),
            d_up_bias.reshape(fsdp_count, -1),
        ],
        1,
    )
    vector_parts = vector_parts.astype(jnp.bfloat16).reshape(fsdp_count, 4, 3 * WIDTH)
    vector_share = sum_low(exchange(vector_parts, "fsdp"))
    wide = ((0, 0), (0, model_width - 3 * WIDTH))
    qkv_piece, vector_share = jnp.pad(qkv_piece, wide), jnp.pad(vector_share, wide)
    joint_piece = sum_low(exchange(share.reshape(8, -1, model_width), ("x", "yh")))
    joint_piece, layer_out = lax.optimization_barrier((joint_piece, layer_out))
    both = spread(jnp.concatenate([qkv_piece, joint_piece, vector_share], 0), ("x", "yh"))
    g_qkv, g_out, g_up, g_down, vector_sum = unpack(
        core_number, both, swap(both), shard, mlp_in.shape[2], mlp_out.shape[1]
    )
    vector_sum = vector_sum[:, : 3 * WIDTH].reshape(-1)
    own_vectors = vector_sum[: 8 * shard].reshape(8, shard)
    own_up_bias = vector_sum[8 * shard :]
    order = (2, 6, 7, 3, 4, 5)
    g_biases = jnp.stack([own_vectors[place] for place in order])
    out_shape = (1, micro_count, 1, local_rows, model_width)
    return (
        layer_out.reshape(out_shape),
        input_grad.reshape(out_shape),
        g_qkv[None],
        g_out[None],
        g_up[None],
        g_down[None],
        own_vectors[None, :2],
        g_biases[None],
        own_up_bias[None],
    )


def solution(mesh):
    fine = Mesh(
        mesh.devices.reshape(2, 4, 2, 2, 4), ("section", "x", "yh", "core", "fsdp")
    )
    rows = P(None, "fsdp", CTX, None)
    weight = P("section", "fsdp", None)
    vector = P("section", None, "fsdp")
    row = P("section", "fsdp")
    out_rows = P("section", None, "fsdp", CTX, None)
    return jax.shard_map(
        shards,
        mesh=fine,
        in_specs=(rows, rows, P(), P(), weight, weight, weight, weight, vector, vector, row),
        out_specs=(out_rows, out_rows, weight, weight, weight, weight, vector, vector, row),
        check_vma=False,
    )
```
